32 devices in a mesh: replica: 8 (over z, x), tensor: 4 (over y, core).
Axes of the slice: x: 2, y: 2, z: 4, core: 2. Of those that a mesh axis runs over, the one named last changes fastest.
Arguments:
- tokens: bfloat16 [96, 1536], P(('replica', 'tensor')), may hold values from -6 to 6
- attn_gain: float32 [1536], replicated, may hold values from 0.5 to 1.5
- qkv_weight: bfloat16 [1536, 2560], P(None, 'tensor'), may hold values from -0.15625 to 0.15625
- out_weight: bfloat16 [1536, 1536], P('tensor'), may hold values from -0.15625 to 0.15625
- moe_gain: float32 [1536], replicated, may hold values from 0.5 to 1.5
- router: bfloat16 [1536, 8], replicated, may hold values from -0.15625 to 0.15625
- expert_gate_up: bfloat16 [1536, 2, 4096], P(None, None, 'tensor'), may hold values from -0.15625 to 0.15625
- expert_down: bfloat16 [4096, 1536], P('tensor'), may hold values from -0.25 to 0.25
- kv_cache: bfloat16 [192, 2, 128, 512], P(('replica', 'tensor')), may hold values from -240 to 240
- page_table: int32 [64, 2], P('replica'), may hold values from 0 to 21, as said below
- home_len: int32 [64], P('replica'), may hold values from 1 to 256
- guest_source: int32 [32], P(('replica', 'tensor')), may hold values from 0 to 7, as said below
- guest_pages: int32 [32, 2], P(('replica', 'tensor')), may hold values from 4 to 5, as said below
- guest_len: int32 [32], P(('replica', 'tensor')), may hold values from 1 to 256
- routes: int32 [96, 6], P('replica'), may hold values from 0 to 7, all different within a row
Outputs:
- layer_out: bfloat16 [96, 1536], P(('replica', 'tensor'))
The draws below stay inside these ranges and needn't reach their ends.
Inputs may be any that keep to these rules, and one draw needn't show every extreme that they name: `page_table`: the home requests of one replica name different pages, together each of a device's first 4 pages exactly once. `guest_source`: never the guest's own replica; among the guests of one slot and one tensor index, each replica is named exactly once. `guest_pages`: each row names 2 different pages, none of them named by a home request, and guests of different slots name different pages.
All inputs are finite; a program needn't handle non-finite values.
Results may differ from the reference program's by a relative error of at most 0.022.
Values may be sent and summed in bfloat16 or wider, within the bound.
No kernel may reach another device: no remote copies, remote signals or barrier semaphores. Data moves between devices by JAX's collectives and lax.ppermute only.
A program may use at most 64 MiB of HBM per device.

```python
import jax
import jax.numpy as jnp
from jax import lax

D = 1536
HEADS = 12
KVH = 4
HD = 128
MOE_FF = 512
TOP = 6
EXPERTS = 8
PAGE = 128
MAXP = 2
HOME_DEV = 2
GUEST_DEV = 1
PAGES_DEV = 6
ROWS_DEV = 3
TOKENS_REP = 12
ROWS = 96
HOMES_REP = 8
POOL = 24
REPLICAS = 8
GUESTS = 32
GROUP = 3
QKV = 2560
UNITS = 4096


def draw_kv_cache(key, part):
    shape = (REPLICAS * POOL, 2, PAGE, KVH * HD)
    base = jnp.clip(jax.random.normal(key, shape, jnp.float32), -6.0, 6.0)
    return base.astype(jnp.bfloat16)


def draw_page_table(key, part):
    per_device = HOME_DEV * MAXP
    replica_keys = jax.random.split(key, REPLICAS)
    items = jax.vmap(lambda single: jax.random.permutation(single, HOMES_REP * MAXP))(replica_keys)
    pages = items // per_device * PAGES_DEV + items % per_device
    return pages.reshape(REPLICAS * HOMES_REP, MAXP).astype(jnp.int32)


def draw_guest_source(key, part):
    lanes = GUESTS // REPLICAS
    lane_keys = jax.random.split(key, lanes)
    orders = jax.vmap(lambda single: jax.random.permutation(single, REPLICAS))(lane_keys).astype(jnp.int32)
    places = jnp.argsort(orders, axis=1).astype(jnp.int32)
    following = jnp.take_along_axis(orders, (places + 1) % REPLICAS, axis=1)
    return following.T.reshape(GUESTS).astype(jnp.int32)


def draw_guest_pages(key, part):
    row_keys = jax.random.split(key, GUESTS)
    orders = jax.vmap(lambda single: jax.random.permutation(single, MAXP))(row_keys).astype(jnp.int32)
    slot = jnp.arange(GUESTS, dtype=jnp.int32) % GUEST_DEV
    return (HOME_DEV * MAXP + slot[:, None] * MAXP + orders).astype(jnp.int32)


def set_ends(array, rng, least, top_value):
    extent = array.shape
    place = [jax.random.randint(jax.random.fold_in(rng, axis), (), 0, extent[axis]) for axis in range(len(extent))]
    array = array.at[tuple(place)].set(least)
    longest = extent.index(max(extent))
    place[longest] = (place[longest] + 1) % extent[longest]
    return array.at[tuple(place)].set(top_value)


def block_levels(rng, extent, shards, least, top_value):
    def one(axis_at, blocks):
        draws = jax.random.uniform(jax.random.fold_in(jax.random.fold_in(rng, 6), axis_at), (blocks,), jnp.float32, least / len(shards), top_value / len(shards))
        return jnp.repeat(jnp.exp(draws), extent[axis_at] // blocks).reshape((-1,) + (1,) * (len(extent) - axis_at - 1))

    level = one(*shards[0])
    for cut in shards[1:]:
        level = level * one(*cut)
    return level


def choose_distinct(key, rows, count, top, lift):
    ranking = jax.random.permutation(jax.random.fold_in(key, 1), count)
    favour = ranking
    for power in range(3):
        favour = favour * favour // count
    favour = favour * lift // count
    chance = jax.random.randint(jax.random.fold_in(key, 2), (rows, count), 0, 4096) + favour
    sure = jax.random.permutation(jax.random.fold_in(key, 3), rows)[jnp.arange(count) % rows]
    chance = jnp.where(jnp.arange(rows)[:, None] == sure[None, :], 1 << 14, chance)
    priority = chance * count + jnp.arange(count)
    return lax.top_k(priority.astype(jnp.int32), top)[1].astype(jnp.int32)


def bell_draw(stream_key, dims, spread, bound, shards=(), kind=jnp.bfloat16):
    result = spread * jax.random.normal(stream_key, dims, jnp.float32)
    if shards:
        result = result * block_levels(stream_key, dims, shards, -0.22, 0.18)
    return jnp.clip(result, -bound, bound).astype(kind)


def setup_inputs(seed: int = 0) -> dict:
    streams_of = jax.random.split(jax.random.key(seed), 16)
    tokens = bell_draw(streams_of[0], (ROWS, D), 1.0, 6.0, ((0, 32),))
    attn_gain = jnp.clip(1.0 + 0.1 * jax.random.normal(streams_of[1], (D,), jnp.float32), 0.5, 1.5)
    qkv_weight = bell_draw(streams_of[2], (D, QKV), D ** -0.5, 0.15625, ((1, 4),))
    out_weight = bell_draw(streams_of[3], (HEADS * HD, D), (HEADS * HD) ** -0.5, 0.15625, ((0, 4),))
    moe_gain = jnp.clip(1.0 + 0.1 * jax.random.normal(streams_of[4], (D,), jnp.float32), 0.5, 1.5)
    router = bell_draw(streams_of[5], (D, EXPERTS), D ** -0.5, 0.15625)
    expert_gate_up = bell_draw(streams_of[6], (D, 2, UNITS), D ** -0.5, 0.15625, ((2, 4),))
    expert_down = bell_draw(streams_of[7], (UNITS, D), MOE_FF ** -0.5, 0.25, ((0, 4),))
    kv_cache = draw_kv_cache(jax.random.fold_in(streams_of[15], 71), 0)
    page_table = draw_page_table(jax.random.fold_in(streams_of[15], 71), 0)
    home_len = set_ends(jax.random.randint(streams_of[10], (REPLICAS * HOMES_REP,), 1, MAXP * PAGE + 1), jax.random.fold_in(streams_of[10], 1), 1, MAXP * PAGE).astype(jnp.int32)
    guest_source = draw_guest_source(jax.random.fold_in(streams_of[15], 71), 0)
    guest_pages = draw_guest_pages(jax.random.fold_in(streams_of[15], 71), 0)
    guest_len = set_ends(jax.random.randint(streams_of[13], (GUESTS,), 1, MAXP * PAGE + 1), jax.random.fold_in(streams_of[13], 1), 1, MAXP * PAGE).astype(jnp.int32)
    routes = choose_distinct(streams_of[14], ROWS, EXPERTS, TOP, 6144)
    return dict(tokens=tokens, attn_gain=attn_gain, qkv_weight=qkv_weight, out_weight=out_weight, moe_gain=moe_gain, router=router, expert_gate_up=expert_gate_up, expert_down=expert_down, kv_cache=kv_cache, page_table=page_table, home_len=home_len, guest_source=guest_source, guest_pages=guest_pages, guest_len=guest_len, routes=routes)


def normed_rows(values, gain):
    widened = values.astype(jnp.float32)
    inverse = lax.rsqrt(lax.optimization_barrier(jnp.mean(widened * widened, axis=-1, keepdims=True)) + 1e-05)
    return (widened * inverse * gain).astype(jnp.bfloat16)

def reference(tokens, attn_gain, qkv_weight, out_weight, moe_gain, router, expert_gate_up, expert_down, kv_cache, page_table, home_len, guest_source, guest_pages, guest_len, routes):
    projected = jnp.dot(normed_rows(tokens, attn_gain), qkv_weight, preferred_element_type=jnp.float32).astype(jnp.bfloat16)
    row_ids = jnp.arange(ROWS, dtype=jnp.int32)
    replica_of = row_ids // TOKENS_REP
    column_of = row_ids % TOKENS_REP // ROWS_DEV
    slot_of = row_ids % ROWS_DEV
    is_home = slot_of < HOME_DEV
    home_index = replica_of * HOMES_REP + column_of * HOME_DEV + jnp.minimum(slot_of, HOME_DEV - 1)
    guest_index = row_ids // ROWS_DEV * GUEST_DEV + jnp.maximum(slot_of - HOME_DEV, 0)
    home_ids = replica_of[:, None] * POOL + page_table[home_index]
    guest_ids = guest_source[guest_index][:, None] * POOL + column_of[:, None] * PAGES_DEV + guest_pages[guest_index]
    page_ids = jnp.where(is_home[:, None], home_ids, guest_ids).astype(jnp.int32)
    lengths = jnp.where(is_home, home_len[home_index], guest_len[guest_index]).astype(jnp.int32)
    qwidth = HEADS * HD
    kwidth = KVH * HD
    queries = projected[:, :qwidth].reshape(REPLICAS, TOKENS_REP, KVH, GROUP, HD)
    fresh_keys = projected[:, qwidth:qwidth + kwidth].reshape(REPLICAS, TOKENS_REP, KVH, HD)
    fresh_values = projected[:, qwidth + kwidth:].reshape(REPLICAS, TOKENS_REP, KVH, HD)
    flat_cache = kv_cache.reshape(REPLICAS * POOL, 2, PAGE, KVH, HD)
    positions = jnp.arange(MAXP * PAGE, dtype=jnp.int32)
    scale = HD ** (-0.5)
    highest = lax.Precision.HIGHEST

    def attend(block):
        query, fresh_key, fresh_value, block_ids, block_len = block
        pages = flat_cache[block_ids]
        key_rows = pages[:, :, 0].reshape(TOKENS_REP, MAXP * PAGE, KVH, HD).astype(jnp.float32)
        value_rows = pages[:, :, 1].reshape(TOKENS_REP, MAXP * PAGE, KVH, HD).astype(jnp.float32)
        wide_query = query.astype(jnp.float32)
        scores = jnp.einsum('rkgd,rjkd->rkgj', wide_query, key_rows, precision=highest) * scale
        usable = (positions[None, :] < block_len[:, None])[:, None, None, :]
        scores = jnp.where(usable, scores, -1e+30)
        peak = lax.optimization_barrier(jnp.max(scores, axis=-1))
        weights = jnp.where(usable, jnp.exp(scores - peak[..., None]), 0.0)
        total = lax.optimization_barrier(jnp.sum(weights, axis=-1))
        rounded = lax.optimization_barrier(weights.astype(jnp.bfloat16)).astype(jnp.float32)
        summed = jnp.einsum('rkgj,rjkd->rkgd', rounded, value_rows, precision=highest)
        own_score = jnp.einsum('rkgd,rkd->rkg', wide_query, fresh_key.astype(jnp.float32), precision=highest) * scale
        top = jnp.maximum(peak, own_score)
        factor = jnp.exp(peak - top)
        newest = jnp.exp(own_score - top)
        numerator = summed * factor[..., None] + newest[..., None] * fresh_value.astype(jnp.float32)[:, :, None, :]
        denominator = total * factor + newest
        mixed = numerator / denominator[..., None]
        return mixed.reshape(TOKENS_REP, HEADS * HD).astype(jnp.bfloat16)
    attended = lax.map(attend, (queries, fresh_keys, fresh_values, page_ids.reshape(REPLICAS, TOKENS_REP, MAXP), lengths.reshape(REPLICAS, TOKENS_REP)))
    attended = attended.reshape(ROWS, HEADS * HD)
    hidden = (tokens.astype(jnp.float32) + jnp.dot(attended, out_weight, preferred_element_type=jnp.float32)).astype(jnp.bfloat16)
    normed = normed_rows(hidden, moe_gain)
    logits = jnp.dot(normed, router, preferred_element_type=jnp.float32)
    weights = jax.nn.softmax(jnp.take_along_axis(logits, routes, axis=1), axis=1)
    expert_weight = lax.optimization_barrier(jnp.sum(weights[:, :, None] * (routes[:, :, None] == jnp.arange(EXPERTS, dtype=jnp.int32)[None, None, :]), axis=1))
    per_unit = jnp.repeat(expert_weight, MOE_FF, axis=1)
    gate = jnp.dot(normed, expert_gate_up[:, 0, :], preferred_element_type=jnp.float32)
    upper = jnp.dot(normed, expert_gate_up[:, 1, :], preferred_element_type=jnp.float32)
    activated = (jax.nn.silu(gate) * upper * per_unit).astype(jnp.bfloat16)
    return (hidden.astype(jnp.float32) + jnp.dot(activated, expert_down, preferred_element_type=jnp.float32)).astype(jnp.bfloat16)
```

```python
import jax
import jax.numpy as jnp
from jax import lax
from jax.sharding import PartitionSpec as P

HEADS = 12
KVH = 4
HD = 128
MOE_FF = 512


def normed_rows(values, gain):
    widened = values.astype(jnp.float32)
    inverse = lax.rsqrt(jnp.mean(widened * widened, axis=-1, keepdims=True) + 1e-05)
    return (widened * inverse * gain).astype(jnp.bfloat16)


def shifted(value, axis, shift):
    size = lax.axis_size(axis)
    return lax.ppermute(value, axis, [(i, (i - shift) % size) for i in range(size)])


def gathered(value, axis):
    size = lax.axis_size(axis)
    return [value] + [shifted(value, axis, shift) for shift in range(1, size)]


def scattered(blocks, axis):
    size = lax.axis_size(axis)
    me = lax.axis_index(axis)
    parts = [lax.dynamic_index_in_dim(blocks, me, 0, keepdims=False)]
    for shift in range(1, size):
        block = lax.dynamic_index_in_dim(blocks, (me - shift) % size, 0, keepdims=False)
        parts.append(shifted(block, axis, shift))
    return parts


def placed_in_order(parts, axis):
    size = len(parts)
    me = lax.axis_index(axis)
    return lax.dynamic_slice_in_dim(jnp.stack(parts + parts), (size - me) % size, size, 0)


def shards(
    tokens,
    attn_gain,
    qkv_weight,
    out_weight,
    moe_gain,
    router,
    expert_gate_up,
    expert_down,
    kv_cache,
    page_table,
    home_len,
    guest_source,
    guest_pages,
    guest_len,
    routes,
):
    size = lax.axis_size("tensor")
    me = lax.axis_index("tensor")
    replica = lax.axis_index("replica")
    rows_dev, width = tokens.shape
    home_dev = page_table.shape[0] // size
    top = routes.shape[1]
    npages, _, page_len, _ = kv_cache.shape
    maxp = page_table.shape[1]
    home_pages = home_dev * maxp
    group = HEADS // KVH
    qwidth = HEADS * HD
    kwidth = KVH * HD

    own_routes = lax.dynamic_slice_in_dim(routes, me * rows_dev, rows_dev, 0)
    numbers = jnp.concatenate(
        [own_routes[home_dev:], guest_source[:, None], guest_len[:, None], guest_pages], axis=1
    ).astype(jnp.bfloat16)
    message = jnp.concatenate([tokens[home_dev:], numbers], axis=1)
    offers = jnp.stack(gathered(message, "replica"))
    chosen = offers[:, :, width + top] == replica.astype(jnp.bfloat16)
    served = jnp.sum(
        jnp.where(chosen[:, :, None], offers.astype(jnp.float32), 0.0), axis=0
    ).astype(jnp.bfloat16)
    served_numbers = served[:, width:].astype(jnp.int32)
    near_len = served_numbers[0, top + 1]
    near_pages = served_numbers[0, top + 2 :]

    mine = jnp.concatenate(
        [
            jnp.concatenate([tokens[:home_dev], own_routes[:home_dev].astype(jnp.bfloat16)], axis=1),
            served[:, : width + top],
        ],
        axis=0,
    )
    everyone = placed_in_order(gathered(mine, "tensor"), "tensor").reshape(size * rows_dev, -1)
    all_rows = everyone[:, :width]
    all_routes = everyone[:, width:].astype(jnp.int32)

    ids = jnp.arange(size * npages, dtype=jnp.int32)
    home_ids = jnp.arange(size * home_dev, dtype=jnp.int32)
    home_rows = home_ids // home_dev * rows_dev + home_ids % home_dev
    match = page_table[None] == ids[:, None, None]
    page_row = jnp.where(
        ids % npages < home_pages,
        jnp.sum(jnp.where(match, home_rows[None, :, None], 0), axis=(1, 2)),
        ids // npages * rows_dev + home_dev,
    )
    onehot = (page_row[:, None] == jnp.arange(size * rows_dev)[None]).astype(jnp.bfloat16)
    page_rows = jnp.dot(
        onehot, normed_rows(all_rows, attn_gain), preferred_element_type=jnp.float32
    ).astype(jnp.bfloat16)
    projected = jnp.dot(page_rows, qkv_weight, preferred_element_type=jnp.float32).astype(
        jnp.bfloat16
    )
    joined = (
        placed_in_order(scattered(projected.reshape(size, npages, -1), "tensor"), "tensor")
        .transpose(1, 0, 2)
        .reshape(npages, -1)
    )
    query = joined[:, :qwidth].reshape(npages, KVH, group, HD)
    fresh_key = joined[:, qwidth : qwidth + kwidth].reshape(npages, KVH, HD)
    fresh_value = joined[:, qwidth + kwidth :].reshape(npages, KVH, HD)

    own_ids = me * npages + jnp.arange(npages, dtype=jnp.int32)
    own_match = page_table[None] == own_ids[:, None, None]
    starts = jnp.arange(maxp, dtype=jnp.int32) * page_len
    home_left = jnp.sum(
        jnp.where(own_match, home_len[None, :, None] - starts[None, None, :], 0), axis=(1, 2)
    )
    home_first = jnp.any(own_match[:, :, 0], axis=1)
    guest_match = near_pages[None, :] == jnp.arange(npages, dtype=jnp.int32)[:, None]
    guest_left = jnp.sum(jnp.where(guest_match, near_len - starts[None, :], 0), axis=1)
    is_home = jnp.arange(npages) < home_pages
    left = jnp.where(is_home, home_left, guest_left)
    first = jnp.where(is_home, home_first, guest_match[:, 0])
    keys = kv_cache[:, 0].reshape(npages, page_len, KVH, HD)
    values = kv_cache[:, 1].reshape(npages, page_len, KVH, HD)
    scores = (
        jnp.einsum("jkgd,jpkd->jkgp", query, keys, preferred_element_type=jnp.float32)
        * HD ** (-0.5)
    )
    usable = (jnp.arange(page_len)[None] < left[:, None])[:, None, None, :]
    scores = jnp.where(usable, scores, -1e30)
    own = (
        jnp.einsum("jkgd,jkd->jkg", query, fresh_key, preferred_element_type=jnp.float32)
        * HD ** (-0.5)
    )
    own = jnp.where(first[:, None, None], own, -1e30)
    peak = jnp.maximum(jnp.max(scores, axis=-1), own)
    weights = jnp.where(usable, jnp.exp(scores - peak[..., None]), 0.0)
    newest = jnp.where(first[:, None, None], jnp.exp(own - peak), 0.0)
    total = jnp.sum(weights, axis=-1) + newest
    summed = jnp.einsum(
        "jkgp,jpkd->jkgd",
        weights.astype(jnp.bfloat16),
        values,
        preferred_element_type=jnp.float32,
    ) + newest[..., None] * fresh_value.astype(jnp.float32)[:, :, None, :]
    used = total > 0.0
    safe = jnp.where(used, total, 1.0)
    mixed = (summed / safe[..., None]).reshape(npages, qwidth)
    level = jnp.where(used, peak + jnp.log(safe), -1e30).reshape(npages, HEADS)
    levels = jnp.repeat(level, HD, axis=1)
    part = qwidth // size
    terms = jnp.concatenate(
        [mixed.reshape(npages, size, part), levels.reshape(npages, size, part)], axis=2
    ).transpose(1, 0, 2)
    terms = placed_in_order(scattered(terms, "tensor"), "tensor").reshape(size * npages, 2 * part)

    guest_ids = (
        jnp.arange(size, dtype=jnp.int32)[:, None] * npages
        + home_pages
        + jnp.arange(maxp, dtype=jnp.int32)[None]
    )
    row_pages = jnp.concatenate(
        [page_table.reshape(size, home_dev, maxp), guest_ids[:, None]], axis=1
    ).reshape(size * rows_dev, maxp)
    both = jnp.take(terms, row_pages, axis=0)
    mixes, lows = both[..., :part], both[..., part:]
    highest = jnp.max(lows, axis=1, keepdims=True)
    factors = jnp.exp(lows - highest)
    attended = (jnp.sum(mixes * factors, axis=1) / jnp.sum(factors, axis=1)).astype(jnp.bfloat16)

    partial = jnp.dot(attended, out_weight, preferred_element_type=jnp.float32).astype(jnp.bfloat16)
    attn_sum = sum(piece.astype(jnp.float32) for piece in gathered(partial, "tensor"))
    hidden = (all_rows.astype(jnp.float32) + attn_sum).astype(jnp.bfloat16)

    normed = normed_rows(hidden, moe_gain)
    logits = jnp.dot(normed, router, preferred_element_type=jnp.float32)
    experts = router.shape[1]
    routed = jnp.any(
        all_routes[:, :, None] == jnp.arange(experts, dtype=jnp.int32)[None, None], axis=1
    )
    expert_weight = jax.nn.softmax(jnp.where(routed, logits, -jnp.inf), axis=1)
    units = expert_gate_up.shape[2]
    unit_owner = (me * units + jnp.arange(units, dtype=jnp.int32)) // MOE_FF
    per_unit = jnp.sum(
        expert_weight[:, :, None]
        * (unit_owner[None, None, :] == jnp.arange(experts, dtype=jnp.int32)[None, :, None]),
        axis=1,
    )
    gates = jnp.einsum("td,dgu->tgu", normed, expert_gate_up, preferred_element_type=jnp.float32)
    activated = (jax.nn.silu(gates[:, 0]) * gates[:, 1] * per_unit).astype(jnp.bfloat16)
    down = jnp.dot(activated, expert_down, preferred_element_type=jnp.float32).astype(jnp.bfloat16)
    pieces = scattered(down.reshape(size, rows_dev, width), "tensor")
    own_hidden = lax.dynamic_slice_in_dim(hidden, me * rows_dev, rows_dev, 0)
    finished = (
        own_hidden.astype(jnp.float32) + sum(piece.astype(jnp.float32) for piece in pieces)
    ).astype(jnp.bfloat16)

    returned = jnp.stack(gathered(finished[home_dev:], "replica"))
    replicas = lax.axis_size("replica")
    back = (guest_source - replica) % replicas
    picked = jnp.arange(replicas, dtype=jnp.int32)[:, None] == back[None]
    guest_rows = jnp.sum(
        jnp.where(picked[:, :, None], returned.astype(jnp.float32), 0.0), axis=0
    ).astype(jnp.bfloat16)
    return jnp.concatenate([finished[:home_dev], guest_rows], axis=0)


def solution(mesh):
    placed = (
        P(("replica", "tensor"), None),
        P(),
        P(None, "tensor"),
        P("tensor", None),
        P(),
        P(),
        P(None, None, "tensor"),
        P("tensor", None),
        P(("replica", "tensor"), None, None, None),
        P("replica", None),
        P("replica"),
        P(("replica", "tensor")),
        P(("replica", "tensor"), None),
        P(("replica", "tensor")),
        P("replica", None),
    )
    return jax.shard_map(
        shards,
        mesh=mesh,
        in_specs=placed,
        out_specs=P(("replica", "tensor"), None),
        check_vma=False,
    )
```

```python
import jax
import jax.numpy as jnp
from jax import lax
from jax.sharding import PartitionSpec as P

HEADS = 12
KVH = 4
HD = 128
MOE_FF = 512


def normed_rows(values, gain):
    widened = values.astype(jnp.float32)
    inverse = lax.rsqrt(jnp.mean(widened * widened, axis=-1, keepdims=True) + 1e-05)
    return (widened * inverse * gain).astype(jnp.bfloat16)


def shifted(value, axis, shift):
    size = lax.axis_size(axis)
    return lax.ppermute(value, axis, [(i, (i - shift) % size) for i in range(size)])


def gathered(value, axis):
    size = lax.axis_size(axis)
    return [value] + [shifted(value, axis, shift) for shift in range(1, size)]


def scattered(blocks, axis):
    size = lax.axis_size(axis)
    me = lax.axis_index(axis)
    parts = [lax.dynamic_index_in_dim(blocks, me, 0, keepdims=False)]
    for shift in range(1, size):
        block = lax.dynamic_index_in_dim(blocks, (me - shift) % size, 0, keepdims=False)
        parts.append(shifted(block, axis, shift))
    return parts


def placed_in_order(parts, axis):
    size = len(parts)
    me = lax.axis_index(axis)
    return lax.dynamic_slice_in_dim(jnp.stack(parts + parts), (size - me) % size, size, 0)


def shards(
    tokens,
    attn_gain,
    qkv_weight,
    out_weight,
    moe_gain,
    router,
    expert_gate_up,
    expert_down,
    kv_cache,
    page_table,
    home_len,
    guest_source,
    guest_pages,
    guest_len,
    routes,
):
    size = lax.axis_size("tensor")
    me = lax.axis_index("tensor")
    replica = lax.axis_index("replica")
    rows_dev, width = tokens.shape
    home_dev = page_table.shape[0] // size
    top = routes.shape[1]
    npages, _, page_len, _ = kv_cache.shape
    maxp = page_table.shape[1]
    home_pages = home_dev * maxp
    group = HEADS // KVH
    qwidth = HEADS * HD
    kwidth = KVH * HD

    replicas = lax.axis_size("replica")
    both_axes = ("replica", "tensor")
    own_routes = lax.dynamic_slice_in_dim(routes, me * rows_dev, rows_dev, 0)
    numbers = jnp.concatenate(
        [own_routes[home_dev:], guest_source[:, None], guest_len[:, None], guest_pages], axis=1
    )
    home_message = jnp.concatenate(
        [
            tokens[:home_dev],
            jnp.pad(own_routes[:home_dev], ((0, 0), (0, numbers.shape[1] - top))).astype(
                jnp.bfloat16
            ),
        ],
        axis=1,
    )
    guest_message = jnp.pad(
        jnp.concatenate([tokens[home_dev:], numbers.astype(jnp.bfloat16)], axis=1),
        ((0, home_dev - guest_source.shape[0]), (0, 0)),
    )
    here = jnp.arange(replicas, dtype=jnp.int32) == replica
    sent = jnp.where(here[:, None, None, None], home_message, guest_message[None, None])
    sent = jnp.broadcast_to(sent, (replicas, size) + home_message.shape)
    came = lax.all_to_all(
        sent.reshape((-1,) + home_message.shape), both_axes, 0, 0, tiled=True
    ).reshape(sent.shape)
    homes = lax.dynamic_index_in_dim(came, replica, 0, keepdims=False)
    offers = came[:, :, 0]
    chosen = (offers[:, :, width + top] == replica.astype(jnp.bfloat16)) & ~here[:, None]
    served = jnp.sum(
        jnp.where(chosen[:, :, None], offers.astype(jnp.float32), 0.0), axis=0
    ).astype(jnp.bfloat16)
    own_served = lax.dynamic_index_in_dim(served, me, 0, keepdims=False)
    served_numbers = own_served[width:].astype(jnp.int32)
    near_len = served_numbers[top + 1]
    near_pages = served_numbers[top + 2 :]
    everyone = jnp.concatenate([homes, served[:, None]], axis=1).reshape(size * rows_dev, -1)
    all_rows = everyone[:, :width]
    all_routes = everyone[:, width : width + top].astype(jnp.int32)

    ids = jnp.arange(size * npages, dtype=jnp.int32)
    home_ids = jnp.arange(size * home_dev, dtype=jnp.int32)
    home_rows = home_ids // home_dev * rows_dev + home_ids % home_dev
    match = page_table[None] == ids[:, None, None]
    page_row = jnp.where(
        ids % npages < home_pages,
        jnp.sum(jnp.where(match, home_rows[None, :, None], 0), axis=(1, 2)),
        ids // npages * rows_dev + home_dev,
    )
    onehot = (page_row[:, None] == jnp.arange(size * rows_dev)[None]).astype(jnp.bfloat16)
    page_rows = jnp.dot(
        onehot, normed_rows(all_rows, attn_gain), preferred_element_type=jnp.float32
    ).astype(jnp.bfloat16)
    projected = jnp.dot(page_rows, qkv_weight, preferred_element_type=jnp.float32).astype(
        jnp.bfloat16
    )
    joined = (
        placed_in_order(scattered(projected.reshape(size, npages, -1), "tensor"), "tensor")
        .transpose(1, 0, 2)
        .reshape(npages, -1)
    )
    query = joined[:, :qwidth].reshape(npages, KVH, group, HD)
    fresh_key = joined[:, qwidth : qwidth + kwidth].reshape(npages, KVH, HD)
    fresh_value = joined[:, qwidth + kwidth :].reshape(npages, KVH, HD)

    own_ids = me * npages + jnp.arange(npages, dtype=jnp.int32)
    own_match = page_table[None] == own_ids[:, None, None]
    starts = jnp.arange(maxp, dtype=jnp.int32) * page_len
    home_left = jnp.sum(
        jnp.where(own_match, home_len[None, :, None] - starts[None, None, :], 0), axis=(1, 2)
    )
    home_first = jnp.any(own_match[:, :, 0], axis=1)
    guest_match = near_pages[None, :] == jnp.arange(npages, dtype=jnp.int32)[:, None]
    guest_left = jnp.sum(jnp.where(guest_match, near_len - starts[None, :], 0), axis=1)
    is_home = jnp.arange(npages) < home_pages
    left = jnp.where(is_home, home_left, guest_left)
    first = jnp.where(is_home, home_first, guest_match[:, 0])
    keys = kv_cache[:, 0].reshape(npages, page_len, KVH, HD)
    values = kv_cache[:, 1].reshape(npages, page_len, KVH, HD)
    scores = (
        jnp.einsum("jkgd,jpkd->jkgp", query, keys, preferred_element_type=jnp.float32)
        * HD ** (-0.5)
    )
    usable = (jnp.arange(page_len)[None] < left[:, None])[:, None, None, :]
    scores = jnp.where(usable, scores, -1e30)
    own = (
        jnp.einsum("jkgd,jkd->jkg", query, fresh_key, preferred_element_type=jnp.float32)
        * HD ** (-0.5)
    )
    own = jnp.where(first[:, None, None], own, -1e30)
    peak = jnp.maximum(jnp.max(scores, axis=-1), own)
    weights = jnp.where(usable, jnp.exp(scores - peak[..., None]), 0.0)
    newest = jnp.where(first[:, None, None], jnp.exp(own - peak), 0.0)
    total = jnp.sum(weights, axis=-1) + newest
    summed = jnp.einsum(
        "jkgp,jpkd->jkgd",
        weights.astype(jnp.bfloat16),
        values,
        preferred_element_type=jnp.float32,
    ) + newest[..., None] * fresh_value.astype(jnp.float32)[:, :, None, :]
    used = total > 0.0
    safe = jnp.where(used, total, 1.0)
    mixed = (summed / safe[..., None]).reshape(npages, qwidth)
    level = jnp.where(used, peak + jnp.log(safe), -1e30).reshape(npages, HEADS)
    levels = jnp.repeat(level, HD, axis=1)
    part = qwidth // size
    terms = jnp.concatenate(
        [mixed.reshape(npages, size, part), levels.reshape(npages, size, part)], axis=2
    ).transpose(1, 0, 2)
    terms = placed_in_order(scattered(terms, "tensor"), "tensor").reshape(size * npages, 2 * part)

    guest_ids = (
        jnp.arange(size, dtype=jnp.int32)[:, None] * npages
        + home_pages
        + jnp.arange(maxp, dtype=jnp.int32)[None]
    )
    row_pages = jnp.concatenate(
        [page_table.reshape(size, home_dev, maxp), guest_ids[:, None]], axis=1
    ).reshape(size * rows_dev, maxp)
    both = jnp.take(terms, row_pages, axis=0)
    mixes, lows = both[..., :part], both[..., part:]
    highest = jnp.max(lows, axis=1, keepdims=True)
    factors = jnp.exp(lows - highest)
    attended = (jnp.sum(mixes * factors, axis=1) / jnp.sum(factors, axis=1)).astype(jnp.bfloat16)

    partial = jnp.dot(attended, out_weight, preferred_element_type=jnp.float32).astype(jnp.bfloat16)
    attn_sum = sum(piece.astype(jnp.float32) for piece in gathered(partial, "tensor"))
    hidden = (all_rows.astype(jnp.float32) + attn_sum).astype(jnp.bfloat16)

    normed = normed_rows(hidden, moe_gain)
    logits = jnp.dot(normed, router, preferred_element_type=jnp.float32)
    experts = router.shape[1]
    routed = jnp.any(
        all_routes[:, :, None] == jnp.arange(experts, dtype=jnp.int32)[None, None], axis=1
    )
    expert_weight = jax.nn.softmax(jnp.where(routed, logits, -jnp.inf), axis=1)
    units = expert_gate_up.shape[2]
    unit_owner = (me * units + jnp.arange(units, dtype=jnp.int32)) // MOE_FF
    per_unit = jnp.sum(
        expert_weight[:, :, None]
        * (unit_owner[None, None, :] == jnp.arange(experts, dtype=jnp.int32)[None, :, None]),
        axis=1,
    )
    gates = jnp.einsum("td,dgu->tgu", normed, expert_gate_up, preferred_element_type=jnp.float32)
    activated = (jax.nn.silu(gates[:, 0]) * gates[:, 1] * per_unit).astype(jnp.bfloat16)
    down = jnp.dot(activated, expert_down, preferred_element_type=jnp.float32)
    down = down.reshape(size, rows_dev, width)
    owner = (jnp.arange(size, dtype=jnp.int32) == me)[:, None, None]
    down = down + jnp.where(owner, hidden.astype(jnp.float32).reshape(down.shape), 0.0)
    down = down.astype(jnp.bfloat16)
    guest_down = jnp.pad(
        down[:, home_dev:], ((0, 0), (0, home_dev - guest_source.shape[0]), (0, 0))
    )
    sent = jnp.where(here[:, None, None, None], down[None, :, :home_dev], guest_down[None])
    came = lax.all_to_all(
        sent.reshape(replicas * size, home_dev, width), both_axes, 0, 0, tiled=True
    ).reshape(sent.shape)
    homes = lax.dynamic_index_in_dim(came, replica, 0, keepdims=False)
    guests = lax.dynamic_index_in_dim(came, guest_source[0], 0, keepdims=False)[:, :1]
    finished = jnp.concatenate([homes, guests], axis=1)
    return jnp.sum(finished.astype(jnp.float32), axis=0).astype(jnp.bfloat16)


def solution(mesh):
    placed = (
        P(("replica", "tensor"), None),
        P(),
        P(None, "tensor"),
        P("tensor", None),
        P(),
        P(),
        P(None, None, "tensor"),
        P("tensor", None),
        P(("replica", "tensor"), None, None, None),
        P("replica", None),
        P("replica"),
        P(("replica", "tensor")),
        P(("replica", "tensor"), None),
        P(("replica", "tensor")),
        P("replica", None),
    )
    return jax.shard_map(
        shards,
        mesh=mesh,
        in_specs=placed,
        out_specs=P(("replica", "tensor"), None),
        check_vma=False,
    )
```

```python
import functools

import jax
import jax.numpy as jnp
from jax import lax
from jax.experimental import pallas as pl
from jax.experimental.pallas import tpu as pltpu
from jax.sharding import PartitionSpec as P

HEADS = 12
KVH = 4
HD = 128
MOE_FF = 512
LANES = 128
SUB = 8
CORES = 2
EMPTY = -1e30

VMEM = pl.BlockSpec(memory_space=pltpu.VMEM)
SMEM = pl.BlockSpec(memory_space=pltpu.SMEM)
PARAMS = pltpu.CompilerParams(vmem_limit_bytes=16 * 2**20)


def resident(array):
    return pltpu.with_memory_space_constraint(array, pltpu.VMEM)


def normed(values, gain):
    inverse = lax.rsqrt(jnp.mean(values * values, axis=-1, keepdims=True) + 1e-05)
    return (values * inverse * gain).astype(jnp.bfloat16)


def steps(size):
    ways = [(chips, core) for chips in range(size // CORES) for core in range(CORES)]
    return ways[1:]


def partner(me, size, way):
    chips, core = way
    chip = lax.rem(me // CORES + chips, size // CORES)
    return chip * CORES + (lax.rem(me, CORES) + core) % CORES


def from_partner(value, size, way):
    chips, core = way
    pairs = []
    for me in range(size):
        chip = (me // CORES + chips) % (size // CORES)
        pairs.append((chip * CORES + (me + core) % CORES, me))
    return lax.ppermute(value, "tensor", pairs)


def back_way(size, way):
    return ((size // CORES - way[0]) % (size // CORES), way[1])


def lanes_of(numbers, lane):
    row = jnp.zeros(lane.shape, jnp.float32)
    for place, number in enumerate(numbers):
        row = jnp.where(lane == place, number.astype(jnp.float32), row)
    return row


def at_lane(rows, lane, place):
    return jnp.sum(jnp.where(lane == place, rows, 0.0), axis=-1, keepdims=True)


def offer_kernel(tokens, routes, source, pages, length, offers):
    me = lax.axis_index("tensor")
    rows_dev, width = tokens.shape
    top = routes.shape[0]
    lane = lax.broadcasted_iota(jnp.int32, (1, LANES), 1)
    row = (me + 1) * rows_dev - 1
    numbers = [routes[place, row] for place in range(top)]
    numbers += [length[0]] + [pages[0, place] for place in range(pages.shape[1])] + [source[0]]
    tail = lanes_of(numbers, lane)
    token = tokens[...].astype(jnp.float32)[rows_dev - 1 :]
    for place in range(offers.shape[0]):
        offers[place, :, :width] = token
        offers[place, :, width:] = tail


def choose_kernel(maxp, offers, tokens, routes, message):
    me = lax.axis_index("tensor")
    replica = lax.axis_index("replica")
    rows_dev, width = tokens.shape
    top = routes.shape[0]
    lane = lax.broadcasted_iota(jnp.int32, (1, LANES), 1)
    served = jnp.zeros((1, width + LANES), jnp.float32)
    for place in range(offers.shape[0]):
        offer = offers[place]
        source = at_lane(offer[:, width:], lane, top + 1 + maxp)
        far = jnp.where(place == replica, 0.0, 1.0)
        wanted = jnp.where(source == replica.astype(jnp.float32), far, 0.0)
        served = jnp.where(wanted > 0.5, offer, served)
    home = rows_dev - 1
    tails = []
    for slot in range(home):
        row = me * rows_dev + slot
        tails.append(lanes_of([routes[place, row] for place in range(top)], lane))
    homes = jnp.concatenate(
        [tokens[...].astype(jnp.float32)[:home], jnp.concatenate(tails, axis=0)], axis=1
    )
    message[...] = jnp.concatenate([homes, served], axis=0).astype(jnp.bfloat16)


def project_kernel(size, npages, *refs):
    blocks = refs[:size]
    gain, weight, table, rows_ref = refs[size : size + 4]
    outs = refs[size + 4 : 2 * size + 4]
    gathered, products, paged = refs[2 * size + 4 :]
    me = lax.axis_index("tensor")
    rows_dev = blocks[0].shape[0]
    width = weight.shape[0]
    maxp, homes = table.shape
    home_dev = homes // size
    for way, block in zip([(0, 0)] + steps(size), blocks):
        owner = partner(me, size, way)
        gathered[pl.ds(owner, 1)] = block[...].astype(jnp.float32)[None]
    for owner in range(size):
        rows_ref[owner * rows_dev : (owner + 1) * rows_dev] = gathered[owner]
    rows = rows_ref[:, :width]
    products[...] = jnp.dot(normed(rows, gain[...]), weight[...], preferred_element_type=jnp.float32)
    for home in range(homes):
        row = home // home_dev * rows_dev + home % home_dev
        for place in range(maxp):
            page = table[place, home]
            paged[pl.ds(page // npages * SUB + lax.rem(page, npages), 1)] = products[row : row + 1]
    for owner in range(size):
        row = (owner + 1) * rows_dev - 1
        for page in range(home_dev * maxp, npages):
            paged[owner * SUB + page : owner * SUB + page + 1] = products[row : row + 1]
    for way, out in zip([(0, 0)] + steps(size), outs):
        start = pl.multiple_of(partner(me, size, way) * SUB, SUB)
        out[...] = paged[pl.ds(start, SUB)][:npages].astype(jnp.bfloat16)


def attend_kernel(size, top, *refs):
    blocks = refs[:size]
    cache, message, table, lengths = refs[size : size + 4]
    outs = refs[size + 4 : 2 * size + 4]
    gathered, terms, left, first = refs[2 * size + 4 :]
    me = lax.axis_index("tensor")
    npages, _, page_len, _ = cache.shape
    maxp, homes = table.shape
    home_pages = homes // size * maxp
    group = HEADS // KVH
    qwidth, kwidth = HEADS * HD, KVH * HD
    width = message.shape[1] - LANES
    for way, block in zip([(0, 0)] + steps(size), blocks):
        gathered[pl.ds(partner(me, size, way), 1), :npages] = block[...].astype(jnp.float32)[None]
    joined = jnp.concatenate([gathered[owner] for owner in range(size)], axis=1)

    for home in range(homes):
        for place in range(maxp):
            page = table[place, home]
            left[page] = lengths[home] - place * page_len
            first[page] = jnp.int32(place == 0)
    lane = lax.broadcasted_iota(jnp.int32, (1, LANES), 1)
    numbers = message[...].astype(jnp.float32)[-1:, width:]
    near_len = at_lane(numbers, lane, top)
    near_pages = [at_lane(numbers, lane, top + 1 + place) for place in range(maxp)]
    row = lax.broadcasted_iota(jnp.int32, (SUB, page_len), 0)
    spot = lax.broadcasted_iota(jnp.int32, (SUB, page_len), 1).astype(jnp.float32)
    line = lax.broadcasted_iota(jnp.int32, (SUB, 1), 0)
    usable, leads = [], jnp.zeros((SUB, 1), jnp.float32)
    for page in range(npages):
        if page < home_pages:
            count = left[me * npages + page].astype(jnp.float32)
            lead = first[me * npages + page].astype(jnp.float32)
        else:
            count = jnp.zeros((1, 1), jnp.float32)
            for place in range(maxp):
                named = near_pages[place] == float(page)
                count = jnp.where(named, near_len - float(place * page_len), count)
            lead = jnp.where(near_pages[0] == float(page), 1.0, 0.0)
        usable.append(jnp.where((row == page) & (spot < count), 1.0, 0.0))
        leads = jnp.where(line == page, lead, leads)
    usable = jnp.concatenate(usable, axis=1)
    usable = jnp.concatenate([usable] * group, axis=0) > 0.5
    leads = jnp.concatenate([leads] * group, axis=0) > 0.5

    mixes, levels = [], []
    for kv in range(KVH):
        heads = range(kv * group, (kv + 1) * group)
        query = jnp.concatenate([joined[:, h * HD : (h + 1) * HD] for h in heads], axis=0)
        fresh_key = joined[:, qwidth + kv * HD : qwidth + (kv + 1) * HD]
        fresh_value = joined[:, qwidth + kwidth + kv * HD : qwidth + kwidth + (kv + 1) * HD]
        columns = slice(kv * HD, (kv + 1) * HD)
        keys = cache[:, 0, :, columns].reshape(npages * page_len, HD)
        values = cache[:, 1, :, columns].reshape(npages * page_len, HD)
        scores = lax.dot_general(
            query.astype(jnp.bfloat16),
            keys,
            (((1,), (1,)), ((), ())),
            preferred_element_type=jnp.float32,
        ) * HD ** (-0.5)
        scores = jnp.where(usable, scores, EMPTY)
        own = jnp.sum(
            query * jnp.concatenate([fresh_key] * group, axis=0), axis=-1, keepdims=True
        ) * HD ** (-0.5)
        own = jnp.where(leads, own, EMPTY)
        peak = jnp.maximum(jnp.max(scores, axis=-1, keepdims=True), own)
        weights = jnp.where(usable, jnp.exp(scores - peak), 0.0)
        newest = jnp.where(leads, jnp.exp(own - peak), 0.0)
        total = jnp.sum(weights, axis=-1, keepdims=True) + newest
        summed = jnp.dot(
            weights.astype(jnp.bfloat16), values, preferred_element_type=jnp.float32
        ) + newest * jnp.concatenate([fresh_value] * group, axis=0)
        used = total > 0.0
        safe = jnp.where(used, total, 1.0)
        mixed = summed / safe
        level = jnp.broadcast_to(jnp.where(used, peak + jnp.log(safe), EMPTY), mixed.shape)
        for part in range(group):
            mixes.append(mixed[part * SUB : (part + 1) * SUB])
            levels.append(level[part * SUB : (part + 1) * SUB])
    mixes = jnp.concatenate(mixes, axis=1)
    levels = jnp.concatenate(levels, axis=1)
    part = qwidth // size
    for owner in range(size):
        columns = slice(owner * part, (owner + 1) * part)
        terms[owner] = jnp.concatenate([mixes[:, columns], levels[:, columns]], axis=1)
    for way, out in zip([(0, 0)] + steps(size), outs):
        out[...] = terms[pl.ds(partner(me, size, way), 1)][0, :npages]


def out_kernel(size, npages, *refs):
    blocks = refs[:size]
    weight, table, out = refs[size : size + 3]
    terms, rows = refs[size + 3 :]
    me = lax.axis_index("tensor")
    maxp, homes = table.shape
    home_dev = homes // size
    part = weight.shape[0]
    rows_dev = home_dev + 1
    for way, block in zip([(0, 0)] + steps(size), blocks):
        start = pl.multiple_of(partner(me, size, way) * SUB, SUB)
        terms[pl.ds(start, npages)] = block[...]
    for row in range(size * rows_dev):
        owner, slot = row // rows_dev, row % rows_dev
        for place in range(maxp):
            if slot < home_dev:
                page = table[place, owner * home_dev + slot]
                start = page // npages * SUB + lax.rem(page, npages)
            else:
                start = owner * SUB + home_dev * maxp + place
            rows[place, row : row + 1] = terms[pl.ds(start, 1)]
    levels = [rows[place, :, part:] for place in range(maxp)]
    highest = functools.reduce(jnp.maximum, levels)
    factors = [jnp.exp(level - highest) for level in levels]
    total = sum(factors)
    mixed = sum(rows[place, :, :part] * factors[place] for place in range(maxp)) / total
    out[...] = jnp.dot(
        mixed.astype(jnp.bfloat16), weight[...], preferred_element_type=jnp.float32
    ).astype(jnp.bfloat16)


def expert_kernel(size, top, experts, pieces, *refs):
    sums = refs[:pieces]
    rows_ref, gain, router, gate_up, down = refs[pieces : pieces + 5]
    outs = refs[pieces + 5 : pieces + 5 + size]
    own_hidden, finished = refs[pieces + 5 + size :]
    me = lax.axis_index("tensor")
    count = rows_ref.shape[0]
    width = rows_ref.shape[1] - LANES
    rows_dev = count // size
    units = down.shape[0]
    total = functools.reduce(jnp.add, [piece[...].astype(jnp.float32) for piece in sums])
    hidden = (rows_ref[:, :width] + total).astype(jnp.bfloat16).astype(jnp.float32)
    norm = normed(hidden, gain[...])
    lane = lax.broadcasted_iota(jnp.int32, (count, LANES), 1)
    numbers = rows_ref[:, width:]
    logits = lax.dot_general(
        norm, router[...], (((1,), (1,)), ((), ())), preferred_element_type=jnp.float32
    )
    logits = jnp.concatenate(
        [logits, jnp.zeros((count, LANES - experts), jnp.float32)], axis=1
    )
    routed = jnp.zeros((count, LANES), jnp.float32)
    for place in range(top):
        route = at_lane(numbers, lane, place)
        routed = jnp.where(lane.astype(jnp.float32) == route, 1.0, routed)
    logits = jnp.where(routed > 0.5, logits, EMPTY)
    shares = jnp.where(
        routed > 0.5, jnp.exp(logits - jnp.max(logits, axis=-1, keepdims=True)), 0.0
    )
    shares = shares / jnp.sum(shares, axis=-1, keepdims=True)

    here = lax.broadcasted_iota(jnp.int32, (LANES, 2 * LANES), 0)
    there = lax.broadcasted_iota(jnp.int32, (LANES, 2 * LANES), 1)
    evens = jnp.where(there == 2 * here, 1.0, 0.0).astype(jnp.bfloat16)
    odds = jnp.where(there == 2 * here + 1, 1.0, 0.0).astype(jnp.bfloat16)
    padded = 16 * pl.cdiv(count, 16)
    wide = norm
    if padded > count:
        extra = jnp.zeros((padded - count, width), jnp.float32)
        wide = jnp.concatenate([norm.astype(jnp.float32), extra], axis=0).astype(jnp.bfloat16)
    blocks = width // LANES
    tall = jnp.concatenate([wide[:, b * LANES : (b + 1) * LANES] for b in range(blocks)], axis=0)
    to_gate = jnp.dot(tall, evens, preferred_element_type=jnp.float32).astype(jnp.bfloat16)
    to_up = jnp.dot(tall, odds, preferred_element_type=jnp.float32).astype(jnp.bfloat16)
    both = jnp.zeros((2 * padded, units), jnp.float32)
    for b in range(blocks):
        lines = slice(b * padded, (b + 1) * padded)
        left = jnp.concatenate([to_gate[lines], to_up[lines]], axis=0)
        both += jnp.dot(
            left,
            gate_up[2 * b * LANES : 2 * (b + 1) * LANES],
            preferred_element_type=jnp.float32,
        )
    gate, up = both[:count], both[padded : padded + count]
    activated = gate / (1.0 + jnp.exp(-gate)) * up
    step = min(units, MOE_FF)
    scaled = []
    for start in range(0, units, step):
        expert = (me * units + start) // MOE_FF
        share = at_lane(shares, lane, expert)
        scaled.append(activated[:, start : start + step] * share)
    scaled = jnp.concatenate(scaled, axis=1).astype(jnp.bfloat16)
    partial = jnp.dot(scaled, down[...], preferred_element_type=jnp.float32)
    for owner in range(size):
        lines = slice(owner * rows_dev, (owner + 1) * rows_dev)
        finished[owner, :, :width] = partial[lines]
        finished[owner, :, width:] = hidden[lines]
    for way, out in zip([(0, 0)] + steps(size), outs):
        out[...] = finished[pl.ds(partner(me, size, way), 1)][0, :, :width].astype(out.dtype)
    own_hidden[...] = finished[pl.ds(me, 1)][0, :, width:]


def finish_kernel(size, replicas, *refs):
    pieces = refs[:size]
    hidden, out, offers = refs[size:]
    total = functools.reduce(jnp.add, [piece[...].astype(jnp.float32) for piece in pieces])
    rows = hidden[...] + total
    out[...] = rows
    for place in range(replicas):
        offers[place] = rows[-1:]


def return_kernel(rows, offers, source, out):
    guest = offers[pl.ds(source[0], 1)][0]
    out[...] = jnp.concatenate([rows[...][:-1], guest], axis=0).astype(jnp.bfloat16)


def shape(dims, dtype=jnp.float32):
    return jax.ShapeDtypeStruct(dims, dtype)


def shards(
    tokens,
    attn_gain,
    qkv_weight,
    out_weight,
    moe_gain,
    router,
    expert_gate_up,
    expert_down,
    kv_cache,
    page_table,
    home_len,
    guest_source,
    guest_pages,
    guest_len,
    routes,
):
    size = lax.axis_size("tensor")
    replicas = lax.axis_size("replica")
    rows_dev, width = tokens.shape
    npages = kv_cache.shape[0]
    maxp = page_table.shape[1]
    top = routes.shape[1]
    units = expert_down.shape[0]
    part = out_weight.shape[0]
    columns = qkv_weight.shape[1]
    count = size * rows_dev
    ways = steps(size)
    table = page_table.T
    paths = routes.T

    offers = pl.pallas_call(
        offer_kernel,
        out_shape=shape((replicas, 1, width + LANES)),
        in_specs=[VMEM, SMEM, SMEM, SMEM, SMEM],
        out_specs=VMEM,
        compiler_params=PARAMS,
        name="offer",
    )(tokens, paths, guest_source, guest_pages, guest_len)
    offers = lax.all_to_all(offers, "replica", 0, 0, tiled=True)
    message = pl.pallas_call(
        functools.partial(choose_kernel, maxp),
        out_shape=shape((rows_dev, width + LANES), jnp.bfloat16),
        in_specs=[VMEM, VMEM, SMEM],
        out_specs=VMEM,
        compiler_params=PARAMS,
        name="choose",
    )(offers, tokens, paths)
    messages = [message] + [from_partner(message, size, way) for way in ways]

    rows, *projected = pl.pallas_call(
        functools.partial(project_kernel, size, npages),
        out_shape=[shape((count, width + LANES))]
        + [shape((npages, columns), jnp.bfloat16)] * size,
        in_specs=[VMEM] * size + [VMEM, VMEM, SMEM],
        out_specs=[VMEM] * (size + 1),
        scratch_shapes=[
            pltpu.VMEM((size, rows_dev, width + LANES), jnp.float32),
            pltpu.VMEM((count, columns), jnp.float32),
            pltpu.VMEM((size * SUB, columns), jnp.float32),
        ],
        compiler_params=PARAMS,
        name="project",
    )(*messages, attn_gain.reshape(1, width), resident(qkv_weight), table)
    joined = [projected[0]] + [
        from_partner(block, size, back_way(size, way))
        for way, block in zip(ways, projected[1:])
    ]
    order = [(0, 0)] + [back_way(size, way) for way in ways]
    joined = [joined[order.index(way)] for way in [(0, 0)] + ways]

    terms = pl.pallas_call(
        functools.partial(attend_kernel, size, top),
        out_shape=[shape((npages, 2 * part))] * size,
        in_specs=[VMEM] * (size + 2) + [SMEM, SMEM],
        out_specs=[VMEM] * size,
        scratch_shapes=[
            pltpu.VMEM((size, SUB, columns), jnp.float32),
            pltpu.VMEM((size, SUB, 2 * part), jnp.float32),
            pltpu.SMEM((size * npages,), jnp.int32),
            pltpu.SMEM((size * npages,), jnp.int32),
        ],
        compiler_params=PARAMS,
        name="attend",
    )(*joined, resident(kv_cache), message, table, home_len)
    terms = [terms[0]] + [
        from_partner(block, size, back_way(size, way)) for way, block in zip(ways, terms[1:])
    ]
    terms = [terms[order.index(way)] for way in [(0, 0)] + ways]

    partial = pl.pallas_call(
        functools.partial(out_kernel, size, npages),
        out_shape=shape((count, width), jnp.bfloat16),
        in_specs=[VMEM] * (size + 1) + [SMEM],
        out_specs=VMEM,
        scratch_shapes=[
            pltpu.VMEM((size * SUB, 2 * part), jnp.float32),
            pltpu.VMEM((maxp, count, 2 * part), jnp.float32),
        ],
        compiler_params=PARAMS,
        name="out",
    )(*terms, resident(out_weight), table)
    mate = from_partner(partial, size, (0, 1))
    pair = (partial.astype(jnp.float32) + mate.astype(jnp.float32)).astype(jnp.bfloat16)
    sums = [pair] + [
        from_partner(pair, size, (chips, 0)) for chips in range(1, size // CORES)
    ]

    *pieces, hidden = pl.pallas_call(
        functools.partial(expert_kernel, size, top, router.shape[1], len(sums)),
        out_shape=[shape((rows_dev, width), jnp.bfloat16)] * size + [shape((rows_dev, width))],
        in_specs=[VMEM] * (len(sums) + 5),
        out_specs=[VMEM] * (size + 1),
        scratch_shapes=[pltpu.VMEM((size, rows_dev, 2 * width), jnp.float32)],
        compiler_params=PARAMS,
        name="experts",
    )(
        *sums,
        rows,
        moe_gain.reshape(1, width),
        router.T,
        resident(expert_gate_up.reshape(2 * width, units)),
        resident(expert_down),
    )
    pieces = [pieces[0]] + [
        from_partner(block, size, back_way(size, way)) for way, block in zip(ways, pieces[1:])
    ]
    finished, offers = pl.pallas_call(
        functools.partial(finish_kernel, size, replicas),
        out_shape=[shape((rows_dev, width)), shape((replicas, 1, width))],
        in_specs=[VMEM] * (size + 1),
        out_specs=[VMEM] * 2,
        compiler_params=PARAMS,
        name="finish",
    )(*pieces, hidden)
    offers = lax.all_to_all(offers, "replica", 0, 0, tiled=True)
    return pl.pallas_call(
        return_kernel,
        out_shape=shape((rows_dev, width), jnp.bfloat16),
        in_specs=[VMEM, VMEM, SMEM],
        out_specs=VMEM,
        compiler_params=PARAMS,
        name="give_back",
    )(finished, offers, guest_source)


def solution(mesh):
    placed = (
        P(("replica", "tensor"), None),
        P(),
        P(None, "tensor"),
        P("tensor", None),
        P(),
        P(),
        P(None, None, "tensor"),
        P("tensor", None),
        P(("replica", "tensor"), None, None, None),
        P("replica", None),
        P("replica"),
        P(("replica", "tensor")),
        P(("replica", "tensor"), None),
        P(("replica", "tensor")),
        P("replica", None),
    )
    return jax.shard_map(
        shards,
        mesh=mesh,
        in_specs=placed,
        out_specs=P(("replica", "tensor"), None),
        check_vma=False,
    )
```

```python
import functools

import jax
import jax.numpy as jnp
from jax import lax
from jax.experimental import pallas as pl
from jax.experimental.pallas import tpu as pltpu
from jax.sharding import PartitionSpec as P

HEADS = 12
KVH = 4
HD = 128
MOE_FF = 512
LANES = 128
SUB = 8
CORES = 2
EMPTY = -1e30

VMEM = pl.BlockSpec(memory_space=pltpu.VMEM)
SMEM = pl.BlockSpec(memory_space=pltpu.SMEM)
ANY = pl.BlockSpec(memory_space=pl.ANY)
PARAMS = pltpu.CompilerParams(vmem_limit_bytes=16 * 2**20)


def resident(array):
    return pltpu.with_memory_space_constraint(array, pltpu.VMEM)


def far(array):
    return pltpu.with_memory_space_constraint(array, pltpu.HBM)


def normed(values, gain):
    inverse = lax.rsqrt(jnp.mean(values * values, axis=-1, keepdims=True) + 1e-05)
    return (values * inverse * gain).astype(jnp.bfloat16)


def to_mate(value, size):
    return lax.ppermute(value, "tensor", [(me, me ^ 1) for me in range(size)])


def along(value, size, chips):
    pairs = [(me, (me + CORES * chips) % size) for me in range(size)]
    return lax.ppermute(value, "tensor", pairs)


def senders(me, size):
    chip, core = me // CORES, lax.rem(me, CORES)
    order = []
    for chips in range(size // CORES):
        start = lax.rem(chip + size // CORES - chips, size // CORES) * CORES
        order += [start + core, start + 1 - core]
    return order


def receivers(me, size):
    chip, core = me // CORES, lax.rem(me, CORES)
    starts = [lax.rem(chip + chips, size // CORES) * CORES for chips in range(size // CORES)]
    return [start + core for start in starts], [start + 1 - core for start in starts]


def exchanged(keep, give, size):
    came = to_mate(give, size)
    arrivals = [jnp.stack([keep[0], came[0]])]
    for chips in range(1, size // CORES):
        arrivals.append(along(jnp.stack([keep[chips], came[chips]]), size, chips))
    return arrivals


def doubled(block, replicas, loads=()):
    reach, near = 1, []
    while reach < replicas:
        came = lax.ppermute(block, "replica", [(me, me ^ reach) for me in range(replicas)])
        if len(near) < len(loads):
            near.append(loads[len(near)](block))
            block = joined_blocks(block, came, near[-1])
        else:
            block = jnp.concatenate([block, came], axis=0)
        reach *= 2
    return block, near


def lanes_of(numbers, lane):
    row = jnp.zeros(lane.shape, jnp.float32)
    for place, number in enumerate(numbers):
        row = jnp.where(lane == place, number.astype(jnp.float32), row)
    return row


def at_lane(rows, lane, place):
    return jnp.sum(jnp.where(lane == place, rows, 0.0), axis=-1, keepdims=True)


def offer_kernel(tokens, paths, source, pages, length, table, lens, *refs):
    offer, homes, table_out, lens_out, source_out, rows, paths_s, source_s, pages_s, length_s, sems = refs
    pairs = [
        (tokens, rows),
        (paths, paths_s),
        (source, source_s),
        (pages, pages_s),
        (length, length_s),
        (table, table_out),
        (lens, lens_out),
        (source, source_out),
    ]
    copies = [pltpu.make_async_copy(*pair, sems.at[i]) for i, pair in enumerate(pairs)]
    for copy in copies:
        copy.start()
    for copy in copies:
        copy.wait()
    me = lax.axis_index("tensor")
    rows_dev, width = rows.shape
    top = paths.shape[0]
    lane = lax.broadcasted_iota(jnp.int32, (1, LANES), 1)
    wide = rows[...].astype(jnp.float32)
    tails = []
    for slot in range(rows_dev):
        numbers = [paths_s[place, me * rows_dev + slot] for place in range(top)]
        if slot == rows_dev - 1:
            numbers += [length_s[0, 0]]
            numbers += [pages_s[0, place] for place in range(pages.shape[1])]
            numbers += [source_s[0, 0]]
        tails.append(lanes_of(numbers, lane))
    full = jnp.concatenate([wide, jnp.concatenate(tails, axis=0)], axis=1)
    homes[...] = full[:-1]
    offer[0] = full[-1:]


def choose_kernel(top, maxp, offers, homes, message):
    replica = lax.axis_index("replica").astype(jnp.float32)
    lane = lax.broadcasted_iota(jnp.int32, (1, LANES), 1)
    width = homes.shape[1] - LANES
    served = jnp.zeros((1, width + LANES), jnp.float32)
    for place in range(1, offers.shape[0]):
        offer = offers[place]
        source = at_lane(offer[:, width:], lane, top + 1 + maxp)
        served = jnp.where(source == replica, offer, served)
    message[...] = jnp.concatenate([homes[...], served], axis=0).astype(jnp.bfloat16)


def load_kernel(first, after, source, out, sems):
    pieces = sems.shape[0]
    each = out.shape[0] // pieces
    copies = []
    for place in range(pieces):
        lines = pl.ds(first + place * each, each)
        copies.append(
            pltpu.make_async_copy(
                source.at[lines], out.at[pl.ds(place * each, each)], sems.at[place]
            )
        )
    for copy in copies:
        copy.start()
    for copy in copies:
        copy.wait()


def loaded(after, array, first, count):
    pieces = 4 if count % 64 == 0 else 1
    return pl.pallas_call(
        functools.partial(load_kernel, first),
        out_shape=shape((count, array.shape[1]), array.dtype),
        in_specs=[ANY, ANY],
        out_specs=VMEM,
        scratch_shapes=[pltpu.SemaphoreType.DMA((pieces,))],
        compiler_params=PARAMS,
        cost_estimate=pl.CostEstimate(
            flops=0, bytes_accessed=count * array.shape[1] * 2, transcendentals=0
        ),
        name="load",
    )(after, far(array))


def join_kernel(own, came, before, out):
    half = own.shape[0]
    out[:half] = own[...]
    out[half:] = came[...]


def joined_blocks(own, came, before):
    return pl.pallas_call(
        join_kernel,
        out_shape=shape((2 * own.shape[0],) + own.shape[1:], own.dtype),
        in_specs=[VMEM, VMEM, ANY],
        out_specs=VMEM,
        compiler_params=PARAMS,
        name="join",
    )(own, came, before)


def blocks_kernel(first, after, source, out, sems):
    copies = []
    for place in range(out.shape[0]):
        columns = slice((first + place) * LANES, (first + place + 1) * LANES)
        copies.append(
            pltpu.make_async_copy(source.at[:, :, columns], out.at[place], sems.at[place])
        )
    for copy in copies:
        copy.start()
    for copy in copies:
        copy.wait()


def column_blocks(after, array, first, count):
    rows, two, _ = array.shape
    blocks = pl.pallas_call(
        functools.partial(blocks_kernel, first),
        out_shape=shape((count, rows, two, LANES), array.dtype),
        in_specs=[ANY, ANY],
        out_specs=VMEM,
        scratch_shapes=[pltpu.SemaphoreType.DMA((count,))],
        compiler_params=PARAMS,
        cost_estimate=pl.CostEstimate(
            flops=0, bytes_accessed=count * rows * two * LANES * 2, transcendentals=0
        ),
        name="load_blocks",
    )(after, far(array))
    return blocks.reshape(count, rows * two, LANES)


def project_kernel(size, npages, *refs):
    chips = size // CORES
    blocks = refs[:chips]
    gain, weight, table, _, rows_ref, keep, give, gathered, products, paged = refs[chips:]
    me = lax.axis_index("tensor")
    rows_dev = blocks[0].shape[1]
    width = weight.shape[0]
    maxp, homes = table.shape
    home_dev = homes // size
    for place, owner in enumerate(senders(me, size)):
        block = blocks[place // CORES][place % CORES]
        gathered[pl.ds(owner, 1)] = block.astype(jnp.float32)[None]
    for owner in range(size):
        rows_ref[owner * rows_dev : (owner + 1) * rows_dev] = gathered[owner]
    rows = rows_ref[:, :width]
    products[...] = jnp.dot(normed(rows, gain[...]), weight[...], preferred_element_type=jnp.float32)
    for home in range(homes):
        row = home // home_dev * rows_dev + home % home_dev
        for place in range(maxp):
            page = table[place, home]
            paged[pl.ds(page // npages * SUB + lax.rem(page, npages), 1)] = products[row : row + 1]
    for owner in range(size):
        row = (owner + 1) * rows_dev - 1
        for page in range(home_dev * maxp, npages):
            paged[owner * SUB + page : owner * SUB + page + 1] = products[row : row + 1]
    for out, ends in zip((keep, give), receivers(me, size)):
        for place, end in enumerate(ends):
            start = pl.multiple_of(end * SUB, SUB)
            out[place] = paged[pl.ds(start, SUB)][:npages].astype(jnp.bfloat16)


def attend_kernel(size, top, *refs):
    chips = size // CORES
    blocks = refs[:chips]
    cache, message, table, lengths, _, keep, give, gathered, terms, left, first = refs[chips:]
    me = lax.axis_index("tensor")
    npages, _, page_len, _ = cache.shape
    maxp, homes = table.shape
    home_pages = homes // size * maxp
    group = HEADS // KVH
    qwidth, kwidth = HEADS * HD, KVH * HD
    width = message.shape[1] - LANES
    for place, owner in enumerate(senders(me, size)):
        block = blocks[place // CORES][place % CORES]
        gathered[pl.ds(owner, 1), :npages] = block.astype(jnp.float32)[None]
    joined = jnp.concatenate([gathered[owner] for owner in range(size)], axis=1)

    for home in range(homes):
        for place in range(maxp):
            page = table[place, home]
            left[page] = lengths[home] - place * page_len
            first[page] = jnp.int32(place == 0)
    lane = lax.broadcasted_iota(jnp.int32, (1, LANES), 1)
    numbers = message[...].astype(jnp.float32)[-1:, width:]
    near_len = at_lane(numbers, lane, top)
    near_pages = [at_lane(numbers, lane, top + 1 + place) for place in range(maxp)]
    row = lax.broadcasted_iota(jnp.int32, (SUB, page_len), 0)
    spot = lax.broadcasted_iota(jnp.int32, (SUB, page_len), 1).astype(jnp.float32)
    line = lax.broadcasted_iota(jnp.int32, (SUB, 1), 0)
    usable, leads = [], jnp.zeros((SUB, 1), jnp.float32)
    for page in range(npages):
        if page < home_pages:
            count = left[me * npages + page].astype(jnp.float32)
            lead = first[me * npages + page].astype(jnp.float32)
        else:
            count = jnp.zeros((1, 1), jnp.float32)
            for place in range(maxp):
                named = near_pages[place] == float(page)
                count = jnp.where(named, near_len - float(place * page_len), count)
            lead = jnp.where(near_pages[0] == float(page), 1.0, 0.0)
        usable.append(jnp.where((row == page) & (spot < count), 1.0, 0.0))
        leads = jnp.where(line == page, lead, leads)
    usable = jnp.concatenate(usable, axis=1)
    usable = jnp.concatenate([usable] * HEADS, axis=0) > 0.5
    leads = jnp.concatenate([leads] * HEADS, axis=0) > 0.5

    query = jnp.concatenate([joined[:, h * HD : (h + 1) * HD] for h in range(HEADS)], axis=0)
    fresh_key, fresh_value = [
        jnp.concatenate(
            [joined[:, start + h // group * HD : start + (h // group + 1) * HD] for h in range(HEADS)],
            axis=0,
        )
        for start in (qwidth, qwidth + kwidth)
    ]
    lines = group * SUB
    narrow = query.astype(jnp.bfloat16)
    scores = []
    for kv in range(KVH):
        keys = cache[:, 0, :, kv * HD : (kv + 1) * HD].reshape(npages * page_len, HD)
        scores.append(
            lax.dot_general(
                narrow[kv * lines : (kv + 1) * lines],
                keys,
                (((1,), (1,)), ((), ())),
                preferred_element_type=jnp.float32,
            )
        )
    scores = jnp.concatenate(scores, axis=0) * HD ** (-0.5)
    scores = jnp.where(usable, scores, EMPTY)
    own = jnp.sum(query * fresh_key, axis=-1, keepdims=True) * HD ** (-0.5)
    own = jnp.where(leads, own, EMPTY)
    peak = jnp.maximum(jnp.max(scores, axis=-1, keepdims=True), own)
    weights = jnp.where(usable, jnp.exp(scores - peak), 0.0)
    newest = jnp.where(leads, jnp.exp(own - peak), 0.0)
    total = jnp.sum(weights, axis=-1, keepdims=True) + newest
    narrow = weights.astype(jnp.bfloat16)
    summed = []
    for kv in range(KVH):
        values = cache[:, 1, :, kv * HD : (kv + 1) * HD].reshape(npages * page_len, HD)
        summed.append(
            jnp.dot(
                narrow[kv * lines : (kv + 1) * lines], values, preferred_element_type=jnp.float32
            )
        )
    summed = jnp.concatenate(summed, axis=0) + newest * fresh_value
    used = total > 0.0
    safe = jnp.where(used, total, 1.0)
    mixed = summed / safe
    level = jnp.broadcast_to(jnp.where(used, peak + jnp.log(safe), EMPTY), mixed.shape)
    mixes = jnp.concatenate([mixed[h * SUB : (h + 1) * SUB] for h in range(HEADS)], axis=1)
    levels = jnp.concatenate([level[h * SUB : (h + 1) * SUB] for h in range(HEADS)], axis=1)
    part = qwidth // size
    for owner in range(size):
        columns = slice(owner * part, (owner + 1) * part)
        terms[owner] = jnp.concatenate([mixes[:, columns], levels[:, columns]], axis=1)
    for out, ends in zip((keep, give), receivers(me, size)):
        for place, end in enumerate(ends):
            out[place] = terms[pl.ds(end, 1)][0, :npages]


def out_kernel(size, npages, *refs):
    chips = size // CORES
    blocks = refs[:chips]
    weight, table, _, out, terms, rows = refs[chips:]
    me = lax.axis_index("tensor")
    maxp, homes = table.shape
    home_dev = homes // size
    part = weight.shape[0]
    rows_dev = home_dev + 1
    for place, owner in enumerate(senders(me, size)):
        start = pl.multiple_of(owner * SUB, SUB)
        terms[pl.ds(start, npages)] = blocks[place // CORES][place % CORES]
    for row in range(size * rows_dev):
        owner, slot = row // rows_dev, row % rows_dev
        for place in range(maxp):
            if slot < home_dev:
                page = table[place, owner * home_dev + slot]
                start = page // npages * SUB + lax.rem(page, npages)
            else:
                start = owner * SUB + home_dev * maxp + place
            rows[place, row : row + 1] = terms[pl.ds(start, 1)]
    levels = [rows[place, :, part:] for place in range(maxp)]
    highest = functools.reduce(jnp.maximum, levels)
    factors = [jnp.exp(level - highest) for level in levels]
    total = sum(factors)
    mixed = sum(rows[place, :, :part] * factors[place] for place in range(maxp)) / total
    out[...] = jnp.dot(
        mixed.astype(jnp.bfloat16), weight[...], preferred_element_type=jnp.float32
    ).astype(jnp.bfloat16)


def expert_kernel(size, top, experts, pieces, parts, *refs):
    sums = refs[:pieces]
    rows_ref, gain, router, down_0, down_1 = refs[pieces : pieces + 5]
    gate_up = refs[pieces + 5 : pieces + 5 + parts]
    keep, give, own_hidden, finished = refs[pieces + 5 + parts :]
    me = lax.axis_index("tensor")
    count = rows_ref.shape[0]
    width = rows_ref.shape[1] - LANES
    rows_dev = count // size
    half = down_0.shape[0]
    units = 2 * half
    total = functools.reduce(jnp.add, [piece[...].astype(jnp.float32) for piece in sums])
    hidden = (rows_ref[:, :width] + total).astype(jnp.bfloat16).astype(jnp.float32)
    norm = normed(hidden, gain[...])
    lane = lax.broadcasted_iota(jnp.int32, (count, LANES), 1)
    numbers = rows_ref[:, width:]
    logits = lax.dot_general(
        norm, router[...], (((1,), (1,)), ((), ())), preferred_element_type=jnp.float32
    )
    logits = jnp.concatenate(
        [logits, jnp.zeros((count, LANES - experts), jnp.float32)], axis=1
    )
    routed = jnp.zeros((count, LANES), jnp.float32)
    for place in range(top):
        route = at_lane(numbers, lane, place)
        routed = jnp.where(lane.astype(jnp.float32) == route, 1.0, routed)
    logits = jnp.where(routed > 0.5, logits, EMPTY)
    shares = jnp.where(
        routed > 0.5, jnp.exp(logits - jnp.max(logits, axis=-1, keepdims=True)), 0.0
    )
    shares = shares / jnp.sum(shares, axis=-1, keepdims=True)

    here = lax.broadcasted_iota(jnp.int32, (LANES, 2 * LANES), 0)
    there = lax.broadcasted_iota(jnp.int32, (LANES, 2 * LANES), 1)
    evens = jnp.where(there == 2 * here, 1.0, 0.0).astype(jnp.bfloat16)
    odds = jnp.where(there == 2 * here + 1, 1.0, 0.0).astype(jnp.bfloat16)
    padded = 16 * pl.cdiv(count, 16)
    wide = norm
    if padded > count:
        extra = jnp.zeros((padded - count, width), jnp.float32)
        wide = jnp.concatenate([norm.astype(jnp.float32), extra], axis=0).astype(jnp.bfloat16)
    blocks = width // LANES
    tall = jnp.concatenate([wide[:, b * LANES : (b + 1) * LANES] for b in range(blocks)], axis=0)
    to_gate = jnp.dot(tall, evens, preferred_element_type=jnp.float32).astype(jnp.bfloat16)
    to_up = jnp.dot(tall, odds, preferred_element_type=jnp.float32).astype(jnp.bfloat16)
    left = []
    for b in range(blocks):
        lines = slice(b * padded, (b + 1) * padded)
        left.append(jnp.concatenate([to_gate[lines], to_up[lines]], axis=0))
    left = jnp.concatenate(left, axis=1)
    both = []
    for piece in gate_up:
        right = jnp.concatenate([piece[place] for place in range(piece.shape[0])], axis=1)
        both.append(jnp.dot(left, right, preferred_element_type=jnp.float32))
    both = jnp.concatenate(both, axis=1)
    gate, up = both[:count], both[padded : padded + count]
    activated = gate / (1.0 + jnp.exp(-gate)) * up
    step = min(units, MOE_FF)
    scaled = []
    for start in range(0, units, step):
        expert = (me * units + start) // MOE_FF
        share = at_lane(shares, lane, expert)
        scaled.append(activated[:, start : start + step] * share)
    scaled = jnp.concatenate(scaled, axis=1).astype(jnp.bfloat16)
    partial = jnp.dot(scaled[:, :half], down_0[...], preferred_element_type=jnp.float32)
    partial += jnp.dot(scaled[:, half:], down_1[...], preferred_element_type=jnp.float32)
    for owner in range(size):
        lines = slice(owner * rows_dev, (owner + 1) * rows_dev)
        finished[owner, :, :width] = partial[lines]
        finished[owner, :, width:] = hidden[lines]
    for out, ends in zip((keep, give), receivers(me, size)):
        for place, end in enumerate(ends):
            out[place] = finished[pl.ds(end, 1)][0, :, :width].astype(out.dtype)
    own_hidden[...] = finished[pl.ds(me, 1)][0, :, width:]


def finish_kernel(pieces, *refs):
    hidden, out, offer = refs[pieces:]
    total = functools.reduce(jnp.add, [piece[...].astype(jnp.float32) for piece in refs[:pieces]])
    rows = hidden[...] + total
    out[...] = rows
    offer[0] = rows[-1:]


def return_kernel(rows, offers, source, out):
    guest = offers[pl.ds(source[0, 0] ^ lax.axis_index("replica"), 1)][0]
    out[...] = jnp.concatenate([rows[...][:-1], guest], axis=0).astype(jnp.bfloat16)


def shape(dims, dtype=jnp.float32):
    return jax.ShapeDtypeStruct(dims, dtype)


def shards(
    tokens,
    attn_gain,
    qkv_weight,
    out_weight,
    moe_gain,
    router,
    expert_gate_up,
    expert_down,
    kv_cache,
    page_table,
    home_len,
    guest_source,
    guest_pages,
    guest_len,
    routes,
):
    size = lax.axis_size("tensor")
    replicas = lax.axis_size("replica")
    rows_dev, width = tokens.shape
    npages = kv_cache.shape[0]
    maxp = page_table.shape[1]
    top = routes.shape[1]
    units = expert_down.shape[0]
    part = out_weight.shape[0]
    columns = qkv_weight.shape[1]
    count = size * rows_dev
    chips = size // CORES
    wide = width + LANES

    source, length = guest_source[:, None], guest_len[:, None]
    offer, homes, table, lens, source = pl.pallas_call(
        offer_kernel,
        out_shape=[
            shape((1, 1, wide)),
            shape((rows_dev - 1, wide)),
            shape(page_table.T.shape, jnp.int32),
            shape(home_len.shape, jnp.int32),
            shape(source.shape, jnp.int32),
        ],
        in_specs=[ANY] * 7,
        out_specs=[VMEM] * 5,
        scratch_shapes=[
            pltpu.VMEM(tokens.shape, tokens.dtype),
            pltpu.SMEM(routes.T.shape, jnp.int32),
            pltpu.SMEM(source.shape, jnp.int32),
            pltpu.SMEM(guest_pages.shape, jnp.int32),
            pltpu.SMEM(length.shape, jnp.int32),
            pltpu.SemaphoreType.DMA((8,)),
        ],
        compiler_params=PARAMS,
        name="offer",
    )(
        far(tokens),
        far(routes.T),
        source,
        far(guest_pages),
        length,
        far(page_table.T),
        far(home_len),
    )
    half = units // 2
    offers, (down_0, down_1, qkv_near) = doubled(
        offer,
        replicas,
        [
            lambda after: loaded(after, expert_down, 0, half),
            lambda after: loaded(after, expert_down, half, half),
            lambda after: loaded(after, qkv_weight, 0, width),
        ],
    )
    message = pl.pallas_call(
        functools.partial(choose_kernel, top, maxp),
        out_shape=shape((rows_dev, wide), jnp.bfloat16),
        in_specs=[VMEM, VMEM],
        out_specs=VMEM,
        compiler_params=PARAMS,
        name="choose",
    )(offers, homes)
    both = jnp.stack([message, to_mate(message, size)])
    messages = [both] + [along(both, size, step) for step in range(1, chips)]

    blocks = units // LANES
    parts = min(4, blocks)
    each = blocks // parts
    gate_up = [column_blocks(both, expert_gate_up, 0, each)]
    rows, keep, give = pl.pallas_call(
        functools.partial(project_kernel, size, npages),
        out_shape=[shape((count, wide))] + [shape((chips, npages, columns), jnp.bfloat16)] * 2,
        in_specs=[VMEM] * (chips + 2) + [SMEM, ANY],
        out_specs=[VMEM] * 3,
        scratch_shapes=[
            pltpu.VMEM((size, rows_dev, wide), jnp.float32),
            pltpu.VMEM((count, columns), jnp.float32),
            pltpu.VMEM((size * SUB, columns), jnp.float32),
        ],
        compiler_params=PARAMS,
        name="project",
    )(*messages, attn_gain.reshape(1, width), resident(qkv_near), table, gate_up[0])
    joined = exchanged(keep, give, size)

    if parts > 1:
        gate_up.append(column_blocks(keep, expert_gate_up, each, each))
    keep, give = pl.pallas_call(
        functools.partial(attend_kernel, size, top),
        out_shape=[shape((chips, npages, 2 * part))] * 2,
        in_specs=[VMEM] * (chips + 2) + [SMEM, SMEM, ANY],
        out_specs=[VMEM] * 2,
        scratch_shapes=[
            pltpu.VMEM((size, SUB, columns), jnp.float32),
            pltpu.VMEM((size, SUB, 2 * part), jnp.float32),
            pltpu.SMEM((size * npages,), jnp.int32),
            pltpu.SMEM((size * npages,), jnp.int32),
        ],
        compiler_params=PARAMS,
        name="attend",
    )(*joined, resident(kv_cache), message, table, lens, gate_up[-1])
    terms = exchanged(keep, give, size)

    if parts > 2:
        gate_up.append(column_blocks(keep, expert_gate_up, 2 * each, each))
    partial = pl.pallas_call(
        functools.partial(out_kernel, size, npages),
        out_shape=shape((count, width), jnp.bfloat16),
        in_specs=[VMEM] * (chips + 1) + [SMEM, ANY],
        out_specs=VMEM,
        scratch_shapes=[
            pltpu.VMEM((size * SUB, 2 * part), jnp.float32),
            pltpu.VMEM((maxp, count, 2 * part), jnp.float32),
        ],
        compiler_params=PARAMS,
        name="out",
    )(*terms, resident(out_weight), table, gate_up[-1])
    mate = to_mate(partial, size)
    pair = (partial.astype(jnp.float32) + mate.astype(jnp.float32)).astype(jnp.bfloat16)
    sums = [pair] + [along(pair, size, step) for step in range(1, chips)]

    if parts > 3:
        gate_up.append(column_blocks(partial, expert_gate_up, 3 * each, each))
    keep, give, hidden = pl.pallas_call(
        functools.partial(expert_kernel, size, top, router.shape[1], chips, parts),
        out_shape=[
            shape((chips, rows_dev, width)),
            shape((chips, rows_dev, width), jnp.bfloat16),
            shape((rows_dev, width)),
        ],
        in_specs=[VMEM] * (chips + 5 + parts),
        out_specs=[VMEM] * 3,
        scratch_shapes=[pltpu.VMEM((size, rows_dev, 2 * width), jnp.float32)],
        compiler_params=PARAMS,
        name="experts",
    )(
        *sums,
        rows,
        moe_gain.reshape(1, width),
        router.T,
        resident(down_0),
        resident(down_1),
        *[resident(piece) for piece in gate_up],
    )
    pairs = keep + to_mate(give, size).astype(jnp.float32)
    pieces = [pairs[0]] + [
        along(pairs[step].astype(jnp.bfloat16), size, step) for step in range(1, chips)
    ]
    finished, offer = pl.pallas_call(
        functools.partial(finish_kernel, len(pieces)),
        out_shape=[shape((rows_dev, width)), shape((1, 1, width))],
        in_specs=[VMEM] * (len(pieces) + 1),
        out_specs=[VMEM] * 2,
        compiler_params=PARAMS,
        name="finish",
    )(*pieces, hidden)
    return pl.pallas_call(
        return_kernel,
        out_shape=shape((rows_dev, width), jnp.bfloat16),
        in_specs=[VMEM, VMEM, SMEM],
        out_specs=VMEM,
        compiler_params=PARAMS,
        name="give_back",
    )(finished, doubled(offer, replicas)[0], source)


def solution(mesh):
    placed = (
        P(("replica", "tensor"), None),
        P(),
        P(None, "tensor"),
        P("tensor", None),
        P(),
        P(),
        P(None, None, "tensor"),
        P("tensor", None),
        P(("replica", "tensor"), None, None, None),
        P("replica", None),
        P("replica"),
        P(("replica", "tensor")),
        P(("replica", "tensor"), None),
        P(("replica", "tensor")),
        P("replica", None),
    )
    return jax.shard_map(
        shards,
        mesh=mesh,
        in_specs=placed,
        out_specs=P(("replica", "tensor"), None),
        check_vma=False,
    )
```

```python
import functools

import jax
import jax.numpy as jnp
from jax import lax
from jax.experimental import pallas as pl
from jax.experimental.pallas import tpu as pltpu
from jax.sharding import PartitionSpec as P

HEADS = 12
KVH = 4
HD = 128
MOE_FF = 512
LANES = 128
SUB = 8
CORES = 2
FAR = 1024
EMPTY = -1e30

VMEM = pl.BlockSpec(memory_space=pltpu.VMEM)
SMEM = pl.BlockSpec(memory_space=pltpu.SMEM)
ANY = pl.BlockSpec(memory_space=pl.ANY)
PARAMS = pltpu.CompilerParams(vmem_limit_bytes=16 * 2**20)


def resident(array):
    return pltpu.with_memory_space_constraint(array, pltpu.VMEM)


def far(array):
    return pltpu.with_memory_space_constraint(array, pltpu.HBM)


def normed(values, gain):
    inverse = lax.rsqrt(jnp.mean(values * values, axis=-1, keepdims=True) + 1e-05)
    return (values * inverse * gain).astype(jnp.bfloat16)


def ways(size):
    return [(chips, core) for chips in range(size // CORES) for core in range(CORES)][1:]


def target(me, size, way):
    chip = lax.rem(me // CORES + way[0], size // CORES)
    return chip * CORES + lax.rem(me + way[1], CORES)


def sender(me, size, way):
    chip = lax.rem(me // CORES + size // CORES - way[0], size // CORES)
    return chip * CORES + lax.rem(me + way[1], CORES)


def senders(me, size):
    return [me] + [sender(me, size, way) for way in ways(size)]


def targets(me, size):
    return [me] + [target(me, size, way) for way in ways(size)]


def exchanged(blocks):
    size = len(blocks)
    arrived = [blocks[0]]
    for way, block in zip(ways(size), blocks[1:]):
        pairs = []
        for me in range(size):
            chip = (me // CORES + way[0]) % (size // CORES)
            pairs.append((me, chip * CORES + (me + way[1]) % CORES))
        arrived.append(lax.ppermute(block, "tensor", pairs))
    return arrived


def lanes_of(numbers, lane):
    row = jnp.zeros(lane.shape, jnp.float32)
    for place, number in enumerate(numbers):
        row = jnp.where(lane == place, number.astype(jnp.float32), row)
    return row


def at_lane(rows, lane, place):
    return jnp.sum(jnp.where(lane == place, rows, 0.0), axis=-1, keepdims=True)


def offer_kernel(tokens, paths, pages, table, lens, packed, *refs):
    offers, homes, table_out, lens_out, tail_out, rows, paths_s, pages_s, sems = refs
    pairs = [
        (tokens, rows),
        (paths, paths_s),
        (pages, pages_s),
        (table, table_out),
        (lens, lens_out),
    ]
    copies = [pltpu.make_async_copy(*pair, sems.at[i]) for i, pair in enumerate(pairs)]
    for copy in copies:
        copy.start()
    for copy in copies:
        copy.wait()
    me = lax.axis_index("tensor")
    rows_dev, width = rows.shape
    top = paths.shape[0]
    lane = lax.broadcasted_iota(jnp.int32, (1, LANES), 1)
    wide = rows[...].astype(jnp.float32)
    tails = []
    for slot in range(rows_dev):
        numbers = [paths_s[place, me * rows_dev + slot] for place in range(top)]
        if slot == rows_dev - 1:
            numbers += [packed[0] % FAR]
            numbers += [pages_s[0, place] for place in range(pages.shape[1])]
            numbers += [packed[0] // FAR]
        tails.append(lanes_of(numbers, lane))
    tail_out[...] = tails[-1]
    full = jnp.concatenate([wide, jnp.concatenate(tails, axis=0)], axis=1)
    homes[...] = full[:-1].astype(jnp.bfloat16)
    guest = jnp.concatenate(
        [wide[-1:], tails[-1], jnp.zeros((1, LANES), jnp.float32)], axis=1
    )
    half = guest.shape[1] // 2
    block = jnp.concatenate([guest[:, :half], guest[:, half:]], axis=0).astype(jnp.bfloat16)
    for place in range(offers.shape[0]):
        offers[place] = block


def load_kernel(first, after, source, out, sems):
    pieces = sems.shape[0]
    each = out.shape[0] // pieces
    copies = []
    for place in range(pieces):
        lines = pl.ds(first + place * each, each)
        copies.append(
            pltpu.make_async_copy(
                source.at[lines], out.at[pl.ds(place * each, each)], sems.at[place]
            )
        )
    for copy in copies:
        copy.start()
    for copy in copies:
        copy.wait()


def loaded(after, array, first, count):
    pieces = 8 if count % 128 == 0 else 1
    return pl.pallas_call(
        functools.partial(load_kernel, first),
        out_shape=shape((count, array.shape[1]), array.dtype),
        in_specs=[ANY, ANY],
        out_specs=VMEM,
        scratch_shapes=[pltpu.SemaphoreType.DMA((pieces,))],
        compiler_params=PARAMS,
        cost_estimate=pl.CostEstimate(
            flops=0, bytes_accessed=count * array.shape[1] * 2, transcendentals=0
        ),
        name="load",
    )(after, far(array))


def blocks_kernel(first, after, source, out, sems):
    copies = []
    for place in range(out.shape[0]):
        columns = slice((first + place) * LANES, (first + place + 1) * LANES)
        copies.append(
            pltpu.make_async_copy(source.at[:, :, columns], out.at[place], sems.at[place])
        )
    for copy in copies:
        copy.start()
    for copy in copies:
        copy.wait()


def column_blocks(after, array, first, count):
    rows, two, _ = array.shape
    blocks = pl.pallas_call(
        functools.partial(blocks_kernel, first),
        out_shape=shape((count, rows, two, LANES), array.dtype),
        in_specs=[ANY, ANY],
        out_specs=VMEM,
        scratch_shapes=[pltpu.SemaphoreType.DMA((count,))],
        compiler_params=PARAMS,
        cost_estimate=pl.CostEstimate(
            flops=0, bytes_accessed=count * rows * two * LANES * 2, transcendentals=0
        ),
        name="load_blocks",
    )(after, far(array))
    return blocks.reshape(count, rows * two, LANES)


def project_kernel(size, npages, top, *refs):
    blocks, refs = refs[:size], refs[size:]
    offers, gain, weight, table = refs[:4]
    rows_ref = refs[6]
    outs = refs[7 : 7 + size]
    gathered, products, paged = refs[7 + size :]
    me = lax.axis_index("tensor")
    replica = lax.axis_index("replica").astype(jnp.float32)
    home_dev = blocks[0].shape[0]
    rows_dev = home_dev + 1
    width = weight.shape[0]
    maxp, homes = table.shape
    for owner, block in zip(senders(me, size), blocks):
        gathered[pl.ds(owner, 1)] = block[...].astype(jnp.float32)[None]
    came = offers[...].astype(jnp.float32)
    half = came.shape[2]
    lane = lax.broadcasted_iota(jnp.int32, (1, 1, half), 2)
    spot = width + top + 1 + maxp - half
    source = jnp.sum(jnp.where(lane == spot, came[:, 1:], 0.0), axis=2, keepdims=True)
    picked = jnp.where(source == replica, came, 0.0)
    picked = jnp.sum(picked.reshape(-1, size, 2, half), axis=0)
    for owner in range(size):
        start = owner * rows_dev
        rows_ref[start : start + home_dev] = gathered[owner]
        guest = jnp.concatenate([picked[owner, :1], picked[owner, 1:]], axis=1)
        rows_ref[start + home_dev : start + rows_dev] = guest[:, : width + LANES]
    rows = rows_ref[:, :width]
    products[...] = jnp.dot(normed(rows, gain[...]), weight[...], preferred_element_type=jnp.float32)
    for home in range(homes):
        row = home // home_dev * rows_dev + home % home_dev
        for place in range(maxp):
            page = table[place, home]
            paged[pl.ds(page // npages * SUB + lax.rem(page, npages), 1)] = products[row : row + 1]
    for owner in range(size):
        row = (owner + 1) * rows_dev - 1
        for page in range(home_dev * maxp, npages):
            paged[owner * SUB + page : owner * SUB + page + 1] = products[row : row + 1]
    for end, out in zip(targets(me, size), outs):
        start = pl.multiple_of(end * SUB, SUB)
        out[...] = paged[pl.ds(start, SUB)][:npages].astype(jnp.bfloat16)


def attend_kernel(size, top, *refs):
    blocks, refs = refs[:size], refs[size:]
    cache, rows_ref, table, lengths = refs[:4]
    outs = refs[5 : 5 + size]
    gathered, terms, left, first = refs[5 + size :]
    me = lax.axis_index("tensor")
    npages, _, page_len, _ = cache.shape
    maxp, homes = table.shape
    home_pages = homes // size * maxp
    group = HEADS // KVH
    qwidth, kwidth = HEADS * HD, KVH * HD
    width = rows_ref.shape[1] - LANES
    rows_dev = rows_ref.shape[0] // size
    for owner, block in zip(senders(me, size), blocks):
        gathered[pl.ds(owner, 1), :npages] = block[...].astype(jnp.float32)[None]
    joined = jnp.concatenate([gathered[owner] for owner in range(size)], axis=1)

    for home in range(homes):
        for place in range(maxp):
            page = table[place, home]
            left[page] = lengths[home] - place * page_len
            first[page] = jnp.int32(place == 0)
    lane = lax.broadcasted_iota(jnp.int32, (1, LANES), 1)
    tails = rows_ref[:, width:]
    place = lax.broadcasted_iota(jnp.int32, tails.shape, 0)
    own = place == (me + 1) * rows_dev - 1
    numbers = jnp.sum(jnp.where(own, tails, 0.0), axis=0, keepdims=True)
    near_len = at_lane(numbers, lane, top)
    near_pages = [at_lane(numbers, lane, top + 1 + place) for place in range(maxp)]
    row = lax.broadcasted_iota(jnp.int32, (SUB, page_len), 0)
    spot = lax.broadcasted_iota(jnp.int32, (SUB, page_len), 1).astype(jnp.float32)
    line = lax.broadcasted_iota(jnp.int32, (SUB, 1), 0)
    usable, leads = [], jnp.zeros((SUB, 1), jnp.float32)
    for page in range(npages):
        if page < home_pages:
            count = left[me * npages + page].astype(jnp.float32)
            lead = first[me * npages + page].astype(jnp.float32)
        else:
            count = jnp.zeros((1, 1), jnp.float32)
            for place in range(maxp):
                named = near_pages[place] == float(page)
                count = jnp.where(named, near_len - float(place * page_len), count)
            lead = jnp.where(near_pages[0] == float(page), 1.0, 0.0)
        usable.append(jnp.where((row == page) & (spot < count), 1.0, 0.0))
        leads = jnp.where(line == page, lead, leads)
    usable = jnp.concatenate(usable, axis=1)
    usable = jnp.concatenate([usable] * HEADS, axis=0) > 0.5
    leads = jnp.concatenate([leads] * HEADS, axis=0) > 0.5

    query = jnp.concatenate([joined[:, h * HD : (h + 1) * HD] for h in range(HEADS)], axis=0)
    fresh_key, fresh_value = [
        jnp.concatenate(
            [joined[:, start + h // group * HD : start + (h // group + 1) * HD] for h in range(HEADS)],
            axis=0,
        )
        for start in (qwidth, qwidth + kwidth)
    ]
    lines = group * SUB
    narrow = query.astype(jnp.bfloat16)
    scores = []
    for kv in range(KVH):
        keys = cache[:, 0, :, kv * HD : (kv + 1) * HD].reshape(npages * page_len, HD)
        scores.append(
            lax.dot_general(
                narrow[kv * lines : (kv + 1) * lines],
                keys,
                (((1,), (1,)), ((), ())),
                preferred_element_type=jnp.float32,
            )
        )
    scores = jnp.concatenate(scores, axis=0) * HD ** (-0.5)
    scores = jnp.where(usable, scores, EMPTY)
    own = jnp.sum(query * fresh_key, axis=-1, keepdims=True) * HD ** (-0.5)
    own = jnp.where(leads, own, EMPTY)
    peak = jnp.maximum(jnp.max(scores, axis=-1, keepdims=True), own)
    weights = jnp.where(usable, jnp.exp(scores - peak), 0.0)
    newest = jnp.where(leads, jnp.exp(own - peak), 0.0)
    total = jnp.sum(weights, axis=-1, keepdims=True) + newest
    narrow = weights.astype(jnp.bfloat16)
    summed = []
    for kv in range(KVH):
        values = cache[:, 1, :, kv * HD : (kv + 1) * HD].reshape(npages * page_len, HD)
        summed.append(
            jnp.dot(
                narrow[kv * lines : (kv + 1) * lines], values, preferred_element_type=jnp.float32
            )
        )
    summed = jnp.concatenate(summed, axis=0) + newest * fresh_value
    used = total > 0.0
    safe = jnp.where(used, total, 1.0)
    mixed = summed / safe
    level = jnp.broadcast_to(jnp.where(used, peak + jnp.log(safe), EMPTY), mixed.shape)
    mixes = jnp.concatenate([mixed[h * SUB : (h + 1) * SUB] for h in range(HEADS)], axis=1)
    levels = jnp.concatenate([level[h * SUB : (h + 1) * SUB] for h in range(HEADS)], axis=1)
    part = qwidth // size
    for owner in range(size):
        columns = slice(owner * part, (owner + 1) * part)
        terms[owner] = jnp.concatenate([mixes[:, columns], levels[:, columns]], axis=1)
    for end, out in zip(targets(me, size), outs):
        out[...] = terms[pl.ds(end, 1)][0, :npages]


def out_kernel(size, npages, *refs):
    blocks, refs = refs[:size], refs[size:]
    weight, table, _, out, terms, rows = refs
    me = lax.axis_index("tensor")
    maxp, homes = table.shape
    home_dev = homes // size
    part = weight.shape[0]
    rows_dev = home_dev + 1
    for owner, block in zip(senders(me, size), blocks):
        terms[pl.ds(pl.multiple_of(owner * SUB, SUB), npages)] = block[...]
    for row in range(size * rows_dev):
        owner, slot = row // rows_dev, row % rows_dev
        for place in range(maxp):
            if slot < home_dev:
                page = table[place, owner * home_dev + slot]
                start = page // npages * SUB + lax.rem(page, npages)
            else:
                start = owner * SUB + home_dev * maxp + place
            rows[place, row : row + 1] = terms[pl.ds(start, 1)]
    levels = [rows[place, :, part:] for place in range(maxp)]
    highest = functools.reduce(jnp.maximum, levels)
    factors = [jnp.exp(level - highest) for level in levels]
    total = sum(factors)
    mixed = sum(rows[place, :, :part] * factors[place] for place in range(maxp)) / total
    out[...] = jnp.dot(
        mixed.astype(jnp.bfloat16), weight[...], preferred_element_type=jnp.float32
    ).astype(jnp.bfloat16)


def expert_kernel(size, top, experts, parts, *refs):
    sums, refs = refs[:size], refs[size:]
    rows_ref, gain, router, down = refs[:4]
    gate_up, refs = refs[4 : 4 + parts], refs[4 + parts :]
    homes, guests, finished = refs[:size], refs[size], refs[size + 1]
    me = lax.axis_index("tensor")
    count = rows_ref.shape[0]
    width = rows_ref.shape[1] - LANES
    rows_dev = count // size
    units = down.shape[0]
    total = functools.reduce(jnp.add, [piece[...].astype(jnp.float32) for piece in sums])
    hidden = (rows_ref[:, :width] + total).astype(jnp.bfloat16).astype(jnp.float32)
    norm = normed(hidden, gain[...])
    lane = lax.broadcasted_iota(jnp.int32, (count, LANES), 1)
    numbers = rows_ref[:, width:]
    logits = lax.dot_general(
        norm, router[...], (((1,), (1,)), ((), ())), preferred_element_type=jnp.float32
    )
    logits = jnp.concatenate(
        [logits, jnp.zeros((count, LANES - experts), jnp.float32)], axis=1
    )
    routed = jnp.zeros((count, LANES), jnp.float32)
    for place in range(top):
        route = at_lane(numbers, lane, place)
        routed = jnp.where(lane.astype(jnp.float32) == route, 1.0, routed)
    logits = jnp.where(routed > 0.5, logits, EMPTY)
    shares = jnp.where(
        routed > 0.5, jnp.exp(logits - jnp.max(logits, axis=-1, keepdims=True)), 0.0
    )
    shares = shares / jnp.sum(shares, axis=-1, keepdims=True)

    here = lax.broadcasted_iota(jnp.int32, (LANES, 2 * LANES), 0)
    there = lax.broadcasted_iota(jnp.int32, (LANES, 2 * LANES), 1)
    evens = jnp.where(there == 2 * here, 1.0, 0.0).astype(jnp.bfloat16)
    odds = jnp.where(there == 2 * here + 1, 1.0, 0.0).astype(jnp.bfloat16)
    padded = 16 * pl.cdiv(count, 16)
    wide = norm
    if padded > count:
        extra = jnp.zeros((padded - count, width), jnp.float32)
        wide = jnp.concatenate([norm.astype(jnp.float32), extra], axis=0).astype(jnp.bfloat16)
    blocks = width // LANES
    tall = jnp.concatenate([wide[:, b * LANES : (b + 1) * LANES] for b in range(blocks)], axis=0)
    to_gate = jnp.dot(tall, evens, preferred_element_type=jnp.float32).astype(jnp.bfloat16)
    to_up = jnp.dot(tall, odds, preferred_element_type=jnp.float32).astype(jnp.bfloat16)
    left = []
    for b in range(blocks):
        lines = slice(b * padded, (b + 1) * padded)
        left.append(jnp.concatenate([to_gate[lines], to_up[lines]], axis=0))
    left = jnp.concatenate(left, axis=1)
    both = []
    for piece in gate_up:
        right = jnp.concatenate([piece[place] for place in range(piece.shape[0])], axis=1)
        both.append(jnp.dot(left, right, preferred_element_type=jnp.float32))
    both = jnp.concatenate(both, axis=1)
    gate, up = both[:count], both[padded : padded + count]
    activated = gate / (1.0 + jnp.exp(-gate)) * up
    step = min(units, MOE_FF)
    scaled = []
    for start in range(0, units, step):
        expert = (me * units + start) // MOE_FF
        share = at_lane(shares, lane, expert)
        scaled.append(activated[:, start : start + step] * share)
    scaled = jnp.concatenate(scaled, axis=1).astype(jnp.bfloat16)
    partial = jnp.dot(scaled, down[...], preferred_element_type=jnp.float32)
    for owner in range(size):
        lines = slice(owner * rows_dev, (owner + 1) * rows_dev)
        mine = jnp.where(me == owner, 1.0, 0.0)
        finished[owner] = partial[lines] + hidden[lines] * mine
    for end, out in zip(targets(me, size), homes):
        out[...] = finished[pl.ds(end, 1)][0, :-1].astype(jnp.bfloat16)
    half = width // 2
    for owner in range(size):
        guest = finished[owner, rows_dev - 1 :]
        block = jnp.concatenate([guest[:, :half], guest[:, half:]], axis=0).astype(jnp.bfloat16)
        for place in range(owner, guests.shape[0], size):
            guests[place] = block


def finish_kernel(size, spot, *refs):
    pieces, refs = refs[:size], refs[size:]
    guests, tail, out = refs
    homes = functools.reduce(jnp.add, [piece[...].astype(jnp.float32) for piece in pieces])
    came = guests[...].astype(jnp.float32)
    lane = lax.broadcasted_iota(jnp.int32, (1, LANES), 1)
    source = at_lane(tail[...], lane, spot).reshape(1, 1, 1)
    place = lax.broadcasted_iota(jnp.int32, (came.shape[0], 1, 1), 0) // size
    guest = jnp.sum(jnp.where(place.astype(jnp.float32) == source, came, 0.0), axis=0)
    guest = jnp.concatenate([guest[:1], guest[1:]], axis=1)
    out[...] = jnp.concatenate([homes, guest], axis=0).astype(jnp.bfloat16)


def shape(dims, dtype=jnp.float32):
    return jax.ShapeDtypeStruct(dims, dtype)


def shards(
    tokens,
    attn_gain,
    qkv_weight,
    out_weight,
    moe_gain,
    router,
    expert_gate_up,
    expert_down,
    kv_cache,
    page_table,
    home_len,
    guest_source,
    guest_pages,
    guest_len,
    routes,
):
    size = lax.axis_size("tensor")
    replicas = lax.axis_size("replica")
    rows_dev, width = tokens.shape
    npages = kv_cache.shape[0]
    maxp = page_table.shape[1]
    top = routes.shape[1]
    units = expert_down.shape[0]
    part = out_weight.shape[0]
    columns = qkv_weight.shape[1]
    count = size * rows_dev
    home_dev = rows_dev - 1
    wide = width + LANES
    everyone = size * replicas
    blocks = units // LANES
    parts = min(4, blocks)
    each = blocks // parts

    packed = guest_source * FAR + guest_len
    offers, homes, table, lens, tail = pl.pallas_call(
        offer_kernel,
        out_shape=[
            shape((everyone, 2, (wide + LANES) // 2), jnp.bfloat16),
            shape((home_dev, wide), jnp.bfloat16),
            shape(page_table.T.shape, jnp.int32),
            shape(home_len.shape, jnp.int32),
            shape((1, LANES)),
        ],
        in_specs=[ANY] * 5 + [SMEM],
        out_specs=[VMEM] * 5,
        scratch_shapes=[
            pltpu.VMEM(tokens.shape, tokens.dtype),
            pltpu.SMEM(routes.T.shape, jnp.int32),
            pltpu.SMEM(guest_pages.shape, jnp.int32),
            pltpu.SemaphoreType.DMA((5,)),
        ],
        compiler_params=PARAMS,
        name="offer",
    )(far(tokens), far(routes.T), far(guest_pages), far(page_table.T), far(home_len), packed)
    came = lax.all_to_all(offers, ("replica", "tensor"), 0, 0, tiled=True)
    messages = exchanged([homes] * size)
    qkv_near = loaded(homes, qkv_weight, 0, width)
    down_near = loaded(homes, expert_down, 0, units)
    gate_up = [column_blocks(homes, expert_gate_up, 0, each)]

    rows, *projected = pl.pallas_call(
        functools.partial(project_kernel, size, npages, top),
        out_shape=[shape((count, wide))] + [shape((npages, columns), jnp.bfloat16)] * size,
        in_specs=[VMEM] * (size + 3) + [SMEM, ANY, ANY],
        out_specs=[VMEM] * (size + 1),
        scratch_shapes=[
            pltpu.VMEM((size, home_dev, wide), jnp.float32),
            pltpu.VMEM((count, columns), jnp.float32),
            pltpu.VMEM((size * SUB, columns), jnp.float32),
        ],
        compiler_params=PARAMS,
        name="project",
    )(
        *messages,
        came,
        attn_gain.reshape(1, width),
        resident(qkv_near),
        table,
        gate_up[0],
        down_near,
    )
    joined = exchanged(projected)

    if parts > 1:
        gate_up.append(column_blocks(rows, expert_gate_up, each, each))
    terms = pl.pallas_call(
        functools.partial(attend_kernel, size, top),
        out_shape=[shape((npages, 2 * part))] * size,
        in_specs=[VMEM] * (size + 2) + [SMEM, SMEM, ANY],
        out_specs=[VMEM] * size,
        scratch_shapes=[
            pltpu.VMEM((size, SUB, columns), jnp.float32),
            pltpu.VMEM((size, SUB, 2 * part), jnp.float32),
            pltpu.SMEM((size * npages,), jnp.int32),
            pltpu.SMEM((size * npages,), jnp.int32),
        ],
        compiler_params=PARAMS,
        name="attend",
    )(*joined, resident(kv_cache), rows, table, lens, gate_up[-1])
    arrived = exchanged(terms)

    if parts > 2:
        gate_up.append(column_blocks(terms[0], expert_gate_up, 2 * each, each))
    partial = pl.pallas_call(
        functools.partial(out_kernel, size, npages),
        out_shape=shape((count, width), jnp.bfloat16),
        in_specs=[VMEM] * (size + 1) + [SMEM, ANY],
        out_specs=VMEM,
        scratch_shapes=[
            pltpu.VMEM((size * SUB, 2 * part), jnp.float32),
            pltpu.VMEM((maxp, count, 2 * part), jnp.float32),
        ],
        compiler_params=PARAMS,
        name="out",
    )(*arrived, resident(out_weight), table, gate_up[-1])
    sums = exchanged([partial] * size)

    if parts > 3:
        gate_up.append(column_blocks(partial, expert_gate_up, 3 * each, each))
    *pieces, guests = pl.pallas_call(
        functools.partial(expert_kernel, size, top, router.shape[1], parts),
        out_shape=[shape((home_dev, width), jnp.bfloat16)] * size
        + [shape((everyone, 2, width // 2), jnp.bfloat16)],
        in_specs=[VMEM] * (size + 4 + parts),
        out_specs=[VMEM] * (size + 1),
        scratch_shapes=[pltpu.VMEM((size, rows_dev, width), jnp.float32)],
        compiler_params=PARAMS,
        name="experts",
    )(
        *sums,
        rows,
        moe_gain.reshape(1, width),
        router.T,
        resident(down_near),
        *[resident(piece) for piece in gate_up],
    )
    guests = lax.all_to_all(guests, ("replica", "tensor"), 0, 0, tiled=True)
    pieces = exchanged(pieces)
    return pl.pallas_call(
        functools.partial(finish_kernel, size, top + 1 + maxp),
        out_shape=shape((rows_dev, width), jnp.bfloat16),
        in_specs=[VMEM] * (size + 2),
        out_specs=VMEM,
        compiler_params=PARAMS,
        name="finish",
    )(*pieces, guests, tail)


def solution(mesh):
    placed = (
        P(("replica", "tensor"), None),
        P(),
        P(None, "tensor"),
        P("tensor", None),
        P(),
        P(),
        P(None, None, "tensor"),
        P("tensor", None),
        P(("replica", "tensor"), None, None, None),
        P("replica", None),
        P("replica"),
        P(("replica", "tensor")),
        P(("replica", "tensor"), None),
        P(("replica", "tensor")),
        P("replica", None),
    )
    return jax.shard_map(
        shards,
        mesh=mesh,
        in_specs=placed,
        out_specs=P(("replica", "tensor"), None),
        check_vma=False,
    )
```

```python
import functools

import jax
import jax.numpy as jnp
from jax import lax
from jax.experimental import pallas as pl
from jax.experimental.pallas import tpu as pltpu
from jax.sharding import PartitionSpec as P

HEADS = 12
KVH = 4
HD = 128
MOE_FF = 512
LANES = 128
SUB = 8
CORES = 2
FAR = 1024
EMPTY = -1e30

VMEM = pl.BlockSpec(memory_space=pltpu.VMEM)
SMEM = pl.BlockSpec(memory_space=pltpu.SMEM)
ANY = pl.BlockSpec(memory_space=pl.ANY)
PARAMS = pltpu.CompilerParams(vmem_limit_bytes=16 * 2**20)


def resident(array):
    return pltpu.with_memory_space_constraint(array, pltpu.VMEM)


def far(array):
    return pltpu.with_memory_space_constraint(array, pltpu.HBM)


def normed(values, gain):
    inverse = lax.rsqrt(jnp.mean(values * values, axis=-1, keepdims=True) + 1e-05)
    return (values * inverse * gain).astype(jnp.bfloat16)


def ways(size):
    return [(chips, core) for chips in range(size // CORES) for core in range(CORES)][1:]


def target(me, size, way):
    chip = lax.rem(me // CORES + way[0], size // CORES)
    return chip * CORES + lax.rem(me + way[1], CORES)


def sender(me, size, way):
    chip = lax.rem(me // CORES + size // CORES - way[0], size // CORES)
    return chip * CORES + lax.rem(me + way[1], CORES)


def senders(me, size):
    return [me] + [sender(me, size, way) for way in ways(size)]


def targets(me, size):
    return [me] + [target(me, size, way) for way in ways(size)]


def exchanged(blocks):
    size = len(blocks)
    arrived = [blocks[0]]
    for way, block in zip(ways(size), blocks[1:]):
        pairs = []
        for me in range(size):
            chip = (me // CORES + way[0]) % (size // CORES)
            pairs.append((me, chip * CORES + (me + way[1]) % CORES))
        arrived.append(lax.ppermute(block, "tensor", pairs))
    return arrived


def lanes_of(numbers, lane):
    row = jnp.zeros(lane.shape, jnp.float32)
    for place, number in enumerate(numbers):
        row = jnp.where(lane == place, number.astype(jnp.float32), row)
    return row


def at_lane(rows, lane, place):
    return jnp.sum(jnp.where(lane == place, rows, 0.0), axis=-1, keepdims=True)


def offer_kernel(tokens, paths, pages, table, lens, packed, *refs):
    offers, homes, table_out, lens_out, tail_out, rows, paths_s, pages_s, sems = refs
    pairs = [
        (tokens, rows),
        (paths, paths_s),
        (pages, pages_s),
        (table, table_out),
        (lens, lens_out),
    ]
    copies = [pltpu.make_async_copy(*pair, sems.at[i]) for i, pair in enumerate(pairs)]
    for copy in copies:
        copy.start()
    for copy in copies:
        copy.wait()
    me = lax.axis_index("tensor")
    rows_dev, width = rows.shape
    top = paths.shape[0]
    lane = lax.broadcasted_iota(jnp.int32, (1, LANES), 1)
    wide = rows[...].astype(jnp.float32)
    tails = []
    for slot in range(rows_dev):
        numbers = [paths_s[place, me * rows_dev + slot] for place in range(top)]
        if slot == rows_dev - 1:
            numbers += [packed[0] % FAR]
            numbers += [pages_s[0, place] for place in range(pages.shape[1])]
            numbers += [packed[0] // FAR]
        tails.append(lanes_of(numbers, lane))
    tail_out[...] = tails[-1]
    full = jnp.concatenate([wide, jnp.concatenate(tails, axis=0)], axis=1)
    homes[...] = full[:-1].astype(jnp.bfloat16)
    guest = jnp.concatenate(
        [wide[-1:], tails[-1], jnp.zeros((1, LANES), jnp.float32)], axis=1
    )
    half = guest.shape[1] // 2
    block = jnp.concatenate([guest[:, :half], guest[:, half:]], axis=0).astype(jnp.bfloat16)
    for place in range(offers.shape[0]):
        offers[place] = block


def load_kernel(plans, *refs):
    sources, outs, sems = refs[1 : 1 + len(plans)], refs[1 + len(plans) : -1], refs[-1]
    copies = []

    def copy(source, out):
        copies.append(pltpu.make_async_copy(source, out, sems.at[len(copies)]))

    for (first, count, pieces), source, out in zip(plans, sources, outs):
        each = source.shape[0] // pieces if len(out.shape) == 4 else count // pieces
        for piece in range(pieces):
            lines = pl.ds(piece * each, each)
            if len(out.shape) == 4:
                for place in range(count):
                    columns = pl.ds((first + place) * LANES, LANES)
                    copy(source.at[lines, :, columns], out.at[place, lines])
            else:
                copy(source.at[pl.ds(first + piece * each, each)], out.at[lines])
    for made in copies:
        made.start()
    for made in copies:
        made.wait()


def loaded(after, *wanted):
    shapes, plans, copies = [], [], 0
    for array, first, count in wanted:
        if array.ndim == 3:
            shapes.append(shape((count,) + array.shape[:2] + (LANES,), array.dtype))
            plans.append((first, count, 2))
            copies += 2 * count
        else:
            shapes.append(shape((count, array.shape[1]), array.dtype))
            plans.append((first, count, 4))
            copies += 4
    parts = pl.pallas_call(
        functools.partial(load_kernel, tuple(plans)),
        out_shape=shapes,
        in_specs=[ANY] * (1 + len(wanted)),
        out_specs=[VMEM] * len(wanted),
        scratch_shapes=[pltpu.SemaphoreType.DMA((copies,))],
        compiler_params=PARAMS,
        cost_estimate=pl.CostEstimate(
            flops=0, bytes_accessed=sum(2 * part.size for part in shapes), transcendentals=0
        ),
        name="load",
    )(after, *[far(array) for array, _, _ in wanted])
    return [
        part.reshape(part.shape[0], -1, LANES) if part.ndim == 4 else part for part in parts
    ]


def project_kernel(size, npages, top, *refs):
    blocks, refs = refs[:size], refs[size:]
    offers, gain, weight, table = refs[:4]
    rows_ref = refs[5]
    outs = refs[6 : 6 + size]
    gathered, products, paged = refs[6 + size :]
    me = lax.axis_index("tensor")
    replica = lax.axis_index("replica").astype(jnp.float32)
    home_dev = blocks[0].shape[0]
    rows_dev = home_dev + 1
    width = weight.shape[0]
    maxp, homes = table.shape
    for owner, block in zip(senders(me, size), blocks):
        gathered[pl.ds(owner, 1)] = block[...].astype(jnp.float32)[None]
    came = offers[...].astype(jnp.float32)
    half = came.shape[2]
    lane = lax.broadcasted_iota(jnp.int32, (1, 1, half), 2)
    spot = width + top + 1 + maxp - half
    source = jnp.sum(jnp.where(lane == spot, came[:, 1:], 0.0), axis=2, keepdims=True)
    picked = jnp.where(source == replica, came, 0.0)
    picked = jnp.sum(picked.reshape(-1, size, 2, half), axis=0)
    for owner in range(size):
        start = owner * rows_dev
        rows_ref[start : start + home_dev] = gathered[owner]
        guest = jnp.concatenate([picked[owner, :1], picked[owner, 1:]], axis=1)
        rows_ref[start + home_dev : start + rows_dev] = guest[:, : width + LANES]
    rows = rows_ref[:, :width]
    products[...] = jnp.dot(normed(rows, gain[...]), weight[...], preferred_element_type=jnp.float32)
    for home in range(homes):
        row = home // home_dev * rows_dev + home % home_dev
        for place in range(maxp):
            page = table[place, home]
            paged[pl.ds(page // npages * SUB + lax.rem(page, npages), 1)] = products[row : row + 1]
    for owner in range(size):
        row = (owner + 1) * rows_dev - 1
        for page in range(home_dev * maxp, npages):
            paged[owner * SUB + page : owner * SUB + page + 1] = products[row : row + 1]
    for end, out in zip(targets(me, size), outs):
        start = pl.multiple_of(end * SUB, SUB)
        out[...] = paged[pl.ds(start, SUB)][:npages].astype(jnp.bfloat16)


def attend_kernel(size, top, *refs):
    blocks, refs = refs[:size], refs[size:]
    cache, rows_ref, table, lengths = refs[:4]
    outs = refs[5 : 5 + size]
    gathered, terms, left, first = refs[5 + size :]
    me = lax.axis_index("tensor")
    npages, _, page_len, _ = cache.shape
    maxp, homes = table.shape
    home_pages = homes // size * maxp
    group = HEADS // KVH
    qwidth, kwidth = HEADS * HD, KVH * HD
    width = rows_ref.shape[1] - LANES
    rows_dev = rows_ref.shape[0] // size
    for owner, block in zip(senders(me, size), blocks):
        gathered[pl.ds(owner, 1), :npages] = block[...].astype(jnp.float32)[None]
    joined = jnp.concatenate([gathered[owner] for owner in range(size)], axis=1)

    for home in range(homes):
        for place in range(maxp):
            page = table[place, home]
            left[page] = lengths[home] - place * page_len
            first[page] = jnp.int32(place == 0)
    lane = lax.broadcasted_iota(jnp.int32, (1, LANES), 1)
    tails = rows_ref[:, width:]
    place = lax.broadcasted_iota(jnp.int32, tails.shape, 0)
    own = place == (me + 1) * rows_dev - 1
    numbers = jnp.sum(jnp.where(own, tails, 0.0), axis=0, keepdims=True)
    near_len = at_lane(numbers, lane, top)
    near_pages = [at_lane(numbers, lane, top + 1 + place) for place in range(maxp)]
    row = lax.broadcasted_iota(jnp.int32, (SUB, page_len), 0)
    spot = lax.broadcasted_iota(jnp.int32, (SUB, page_len), 1).astype(jnp.float32)
    line = lax.broadcasted_iota(jnp.int32, (SUB, 1), 0)
    usable, leads = [], jnp.zeros((SUB, 1), jnp.float32)
    for page in range(npages):
        if page < home_pages:
            count = left[me * npages + page].astype(jnp.float32)
            lead = first[me * npages + page].astype(jnp.float32)
        else:
            count = jnp.zeros((1, 1), jnp.float32)
            for place in range(maxp):
                named = near_pages[place] == float(page)
                count = jnp.where(named, near_len - float(place * page_len), count)
            lead = jnp.where(near_pages[0] == float(page), 1.0, 0.0)
        usable.append(jnp.where((row == page) & (spot < count), 1.0, 0.0))
        leads = jnp.where(line == page, lead, leads)
    usable = jnp.concatenate(usable, axis=1)
    usable = jnp.concatenate([usable] * HEADS, axis=0) > 0.5
    leads = jnp.concatenate([leads] * HEADS, axis=0) > 0.5

    query = jnp.concatenate([joined[:, h * HD : (h + 1) * HD] for h in range(HEADS)], axis=0)
    fresh_key, fresh_value = [
        jnp.concatenate(
            [joined[:, start + h // group * HD : start + (h // group + 1) * HD] for h in range(HEADS)],
            axis=0,
        )
        for start in (qwidth, qwidth + kwidth)
    ]
    lines = group * SUB
    narrow = query.astype(jnp.bfloat16)
    scores = []
    for kv in range(KVH):
        keys = cache[:, 0, :, kv * HD : (kv + 1) * HD].reshape(npages * page_len, HD)
        scores.append(
            lax.dot_general(
                narrow[kv * lines : (kv + 1) * lines],
                keys,
                (((1,), (1,)), ((), ())),
                preferred_element_type=jnp.float32,
            )
        )
    scores = jnp.concatenate(scores, axis=0) * HD ** (-0.5)
    scores = jnp.where(usable, scores, EMPTY)
    own = jnp.sum(query * fresh_key, axis=-1, keepdims=True) * HD ** (-0.5)
    own = jnp.where(leads, own, EMPTY)
    peak = jnp.maximum(jnp.max(scores, axis=-1, keepdims=True), own)
    weights = jnp.where(usable, jnp.exp(scores - peak), 0.0)
    newest = jnp.where(leads, jnp.exp(own - peak), 0.0)
    total = jnp.sum(weights, axis=-1, keepdims=True) + newest
    narrow = weights.astype(jnp.bfloat16)
    summed = []
    for kv in range(KVH):
        values = cache[:, 1, :, kv * HD : (kv + 1) * HD].reshape(npages * page_len, HD)
        summed.append(
            jnp.dot(
                narrow[kv * lines : (kv + 1) * lines], values, preferred_element_type=jnp.float32
            )
        )
    summed = jnp.concatenate(summed, axis=0) + newest * fresh_value
    used = total > 0.0
    safe = jnp.where(used, total, 1.0)
    mixed = summed / safe
    level = jnp.broadcast_to(jnp.where(used, peak + jnp.log(safe), EMPTY), mixed.shape)
    mixes = jnp.concatenate([mixed[h * SUB : (h + 1) * SUB] for h in range(HEADS)], axis=1)
    levels = jnp.concatenate([level[h * SUB : (h + 1) * SUB] for h in range(HEADS)], axis=1)
    part = qwidth // size
    for owner in range(size):
        columns = slice(owner * part, (owner + 1) * part)
        terms[owner] = jnp.concatenate([mixes[:, columns], levels[:, columns]], axis=1)
    for end, out in zip(targets(me, size), outs):
        out[...] = terms[pl.ds(end, 1)][0, :npages]


def out_kernel(size, npages, *refs):
    blocks, refs = refs[:size], refs[size:]
    weight, table, _, out, terms, rows = refs
    me = lax.axis_index("tensor")
    maxp, homes = table.shape
    home_dev = homes // size
    part = weight.shape[0]
    rows_dev = home_dev + 1
    for owner, block in zip(senders(me, size), blocks):
        terms[pl.ds(pl.multiple_of(owner * SUB, SUB), npages)] = block[...]
    for row in range(size * rows_dev):
        owner, slot = row // rows_dev, row % rows_dev
        for place in range(maxp):
            if slot < home_dev:
                page = table[place, owner * home_dev + slot]
                start = page // npages * SUB + lax.rem(page, npages)
            else:
                start = owner * SUB + home_dev * maxp + place
            rows[place, row : row + 1] = terms[pl.ds(start, 1)]
    levels = [rows[place, :, part:] for place in range(maxp)]
    highest = functools.reduce(jnp.maximum, levels)
    factors = [jnp.exp(level - highest) for level in levels]
    total = sum(factors)
    mixed = sum(rows[place, :, :part] * factors[place] for place in range(maxp)) / total
    out[...] = jnp.dot(
        mixed.astype(jnp.bfloat16), weight[...], preferred_element_type=jnp.float32
    ).astype(jnp.bfloat16)


def expert_kernel(size, top, experts, parts, lows, *refs):
    sums, refs = refs[:size], refs[size:]
    rows_ref, gain, router = refs[:3]
    gate_up, refs = refs[3 : 3 + parts], refs[3 + parts :]
    down, refs = refs[:lows], refs[lows:]
    homes, guests, finished = refs[:size], refs[size], refs[size + 1]
    me = lax.axis_index("tensor")
    count = rows_ref.shape[0]
    width = rows_ref.shape[1] - LANES
    rows_dev = count // size
    units = sum(piece.shape[0] for piece in down)
    total = functools.reduce(jnp.add, [piece[...].astype(jnp.float32) for piece in sums])
    hidden = (rows_ref[:, :width] + total).astype(jnp.bfloat16).astype(jnp.float32)
    norm = normed(hidden, gain[...])
    lane = lax.broadcasted_iota(jnp.int32, (count, LANES), 1)
    numbers = rows_ref[:, width:]
    logits = lax.dot_general(
        norm, router[...], (((1,), (1,)), ((), ())), preferred_element_type=jnp.float32
    )
    logits = jnp.concatenate(
        [logits, jnp.zeros((count, LANES - experts), jnp.float32)], axis=1
    )
    routed = jnp.zeros((count, LANES), jnp.float32)
    for place in range(top):
        route = at_lane(numbers, lane, place)
        routed = jnp.where(lane.astype(jnp.float32) == route, 1.0, routed)
    logits = jnp.where(routed > 0.5, logits, EMPTY)
    shares = jnp.where(
        routed > 0.5, jnp.exp(logits - jnp.max(logits, axis=-1, keepdims=True)), 0.0
    )
    shares = shares / jnp.sum(shares, axis=-1, keepdims=True)

    here = lax.broadcasted_iota(jnp.int32, (LANES, 2 * LANES), 0)
    there = lax.broadcasted_iota(jnp.int32, (LANES, 2 * LANES), 1)
    evens = jnp.where(there == 2 * here, 1.0, 0.0).astype(jnp.bfloat16)
    odds = jnp.where(there == 2 * here + 1, 1.0, 0.0).astype(jnp.bfloat16)
    padded = 16 * pl.cdiv(count, 16)
    wide = norm
    if padded > count:
        extra = jnp.zeros((padded - count, width), jnp.float32)
        wide = jnp.concatenate([norm.astype(jnp.float32), extra], axis=0).astype(jnp.bfloat16)
    blocks = width // LANES
    tall = jnp.concatenate([wide[:, b * LANES : (b + 1) * LANES] for b in range(blocks)], axis=0)
    to_gate = jnp.dot(tall, evens, preferred_element_type=jnp.float32).astype(jnp.bfloat16)
    to_up = jnp.dot(tall, odds, preferred_element_type=jnp.float32).astype(jnp.bfloat16)
    left = []
    for b in range(blocks):
        lines = slice(b * padded, (b + 1) * padded)
        left.append(jnp.concatenate([to_gate[lines], to_up[lines]], axis=0))
    left = jnp.concatenate(left, axis=1)
    both = []
    for piece in gate_up:
        right = jnp.concatenate([piece[place] for place in range(piece.shape[0])], axis=1)
        both.append(jnp.dot(left, right, preferred_element_type=jnp.float32))
    both = jnp.concatenate(both, axis=1)
    gate, up = both[:count], both[padded : padded + count]
    activated = gate / (1.0 + jnp.exp(-gate)) * up
    step = min(units, MOE_FF)
    scaled = []
    for start in range(0, units, step):
        expert = (me * units + start) // MOE_FF
        share = at_lane(shares, lane, expert)
        scaled.append(activated[:, start : start + step] * share)
    scaled = jnp.concatenate(scaled, axis=1).astype(jnp.bfloat16)
    partial, start = 0.0, 0
    for piece in down:
        left = scaled[:, start : start + piece.shape[0]]
        partial += jnp.dot(left, piece[...], preferred_element_type=jnp.float32)
        start += piece.shape[0]
    for owner in range(size):
        lines = slice(owner * rows_dev, (owner + 1) * rows_dev)
        mine = jnp.where(me == owner, 1.0, 0.0)
        finished[owner] = partial[lines] + hidden[lines] * mine
    for end, out in zip(targets(me, size), homes):
        out[...] = finished[pl.ds(end, 1)][0, :-1].astype(jnp.bfloat16)
    half = width // 2
    for owner in range(size):
        guest = finished[owner, rows_dev - 1 :]
        block = jnp.concatenate([guest[:, :half], guest[:, half:]], axis=0).astype(jnp.bfloat16)
        for place in range(owner, guests.shape[0], size):
            guests[place] = block


def finish_kernel(size, spot, *refs):
    pieces, refs = refs[:size], refs[size:]
    guests, tail, out = refs
    homes = functools.reduce(jnp.add, [piece[...].astype(jnp.float32) for piece in pieces])
    came = guests[...].astype(jnp.float32)
    lane = lax.broadcasted_iota(jnp.int32, (1, LANES), 1)
    source = at_lane(tail[...], lane, spot).reshape(1, 1, 1)
    place = lax.broadcasted_iota(jnp.int32, (came.shape[0], 1, 1), 0) // size
    guest = jnp.sum(jnp.where(place.astype(jnp.float32) == source, came, 0.0), axis=0)
    guest = jnp.concatenate([guest[:1], guest[1:]], axis=1)
    out[...] = jnp.concatenate([homes, guest], axis=0).astype(jnp.bfloat16)


def shape(dims, dtype=jnp.float32):
    return jax.ShapeDtypeStruct(dims, dtype)


def shards(
    tokens,
    attn_gain,
    qkv_weight,
    out_weight,
    moe_gain,
    router,
    expert_gate_up,
    expert_down,
    kv_cache,
    page_table,
    home_len,
    guest_source,
    guest_pages,
    guest_len,
    routes,
):
    size = lax.axis_size("tensor")
    replicas = lax.axis_size("replica")
    rows_dev, width = tokens.shape
    npages = kv_cache.shape[0]
    maxp = page_table.shape[1]
    top = routes.shape[1]
    units = expert_down.shape[0]
    part = out_weight.shape[0]
    columns = qkv_weight.shape[1]
    count = size * rows_dev
    home_dev = rows_dev - 1
    wide = width + LANES
    everyone = size * replicas
    blocks = units // LANES
    gate_up, down = [], []

    def load_more(after, ups, downs):
        first, last = ups[0] * blocks // 8, ups[1] * blocks // 8
        wanted = []
        if last > first:
            wanted.append((expert_gate_up, first, last - first))
        if downs[1] > downs[0]:
            wanted.append((expert_down, downs[0] * units // 8, (downs[1] - downs[0]) * units // 8))
        if not wanted:
            return after
        got = loaded(after, *wanted)
        for part in got:
            (gate_up if part.ndim == 3 else down).append(part)
        return got[0]

    packed = guest_source * FAR + guest_len
    offers, homes, table, lens, tail = pl.pallas_call(
        offer_kernel,
        out_shape=[
            shape((everyone, 2, (wide + LANES) // 2), jnp.bfloat16),
            shape((home_dev, wide), jnp.bfloat16),
            shape(page_table.T.shape, jnp.int32),
            shape(home_len.shape, jnp.int32),
            shape((1, LANES)),
        ],
        in_specs=[ANY] * 5 + [SMEM],
        out_specs=[VMEM] * 5,
        scratch_shapes=[
            pltpu.VMEM(tokens.shape, tokens.dtype),
            pltpu.SMEM(routes.T.shape, jnp.int32),
            pltpu.SMEM(guest_pages.shape, jnp.int32),
            pltpu.SemaphoreType.DMA((5,)),
        ],
        compiler_params=PARAMS,
        name="offer",
    )(far(tokens), far(routes.T), far(guest_pages), far(page_table.T), far(home_len), packed)
    came = lax.all_to_all(offers, ("replica", "tensor"), 0, 0, tiled=True)
    messages = exchanged([homes] * size)
    (qkv_near,) = loaded(homes, (qkv_weight, 0, width))
    before = load_more(homes, (0, 1), (0, 0))

    rows, *projected = pl.pallas_call(
        functools.partial(project_kernel, size, npages, top),
        out_shape=[shape((count, wide))] + [shape((npages, columns), jnp.bfloat16)] * size,
        in_specs=[VMEM] * (size + 3) + [SMEM, ANY],
        out_specs=[VMEM] * (size + 1),
        scratch_shapes=[
            pltpu.VMEM((size, home_dev, wide), jnp.float32),
            pltpu.VMEM((count, columns), jnp.float32),
            pltpu.VMEM((size * SUB, columns), jnp.float32),
        ],
        compiler_params=PARAMS,
        name="project",
    )(
        *messages,
        came,
        attn_gain.reshape(1, width),
        resident(qkv_near),
        table,
        before,
    )
    joined = exchanged(projected)

    before = load_more(rows, (1, 3), (0, 2))
    terms = pl.pallas_call(
        functools.partial(attend_kernel, size, top),
        out_shape=[shape((npages, 2 * part))] * size,
        in_specs=[VMEM] * (size + 2) + [SMEM, SMEM, ANY],
        out_specs=[VMEM] * size,
        scratch_shapes=[
            pltpu.VMEM((size, SUB, columns), jnp.float32),
            pltpu.VMEM((size, SUB, 2 * part), jnp.float32),
            pltpu.SMEM((size * npages,), jnp.int32),
            pltpu.SMEM((size * npages,), jnp.int32),
        ],
        compiler_params=PARAMS,
        name="attend",
    )(*joined, resident(kv_cache), rows, table, lens, before)
    arrived = exchanged(terms)

    before = load_more(terms[0], (3, 5), (2, 4))
    partial = pl.pallas_call(
        functools.partial(out_kernel, size, npages),
        out_shape=shape((count, width), jnp.bfloat16),
        in_specs=[VMEM] * (size + 1) + [SMEM, ANY],
        out_specs=VMEM,
        scratch_shapes=[
            pltpu.VMEM((size * SUB, 2 * part), jnp.float32),
            pltpu.VMEM((maxp, count, 2 * part), jnp.float32),
        ],
        compiler_params=PARAMS,
        name="out",
    )(*arrived, resident(out_weight), table, before)
    sums = exchanged([partial] * size)

    load_more(partial, (5, 8), (4, 8))
    *pieces, guests = pl.pallas_call(
        functools.partial(
            expert_kernel, size, top, router.shape[1], len(gate_up), len(down)
        ),
        out_shape=[shape((home_dev, width), jnp.bfloat16)] * size
        + [shape((everyone, 2, width // 2), jnp.bfloat16)],
        in_specs=[VMEM] * (size + 3 + len(gate_up) + len(down)),
        out_specs=[VMEM] * (size + 1),
        scratch_shapes=[pltpu.VMEM((size, rows_dev, width), jnp.float32)],
        compiler_params=PARAMS,
        name="experts",
    )(
        *sums,
        rows,
        moe_gain.reshape(1, width),
        router.T,
        *[resident(piece) for piece in gate_up + down],
    )
    guests = lax.all_to_all(guests, ("replica", "tensor"), 0, 0, tiled=True)
    pieces = exchanged(pieces)
    return pl.pallas_call(
        functools.partial(finish_kernel, size, top + 1 + maxp),
        out_shape=shape((rows_dev, width), jnp.bfloat16),
        in_specs=[VMEM] * (size + 2),
        out_specs=VMEM,
        compiler_params=PARAMS,
        name="finish",
    )(*pieces, guests, tail)


def solution(mesh):
    placed = (
        P(("replica", "tensor"), None),
        P(),
        P(None, "tensor"),
        P("tensor", None),
        P(),
        P(),
        P(None, None, "tensor"),
        P("tensor", None),
        P(("replica", "tensor"), None, None, None),
        P("replica", None),
        P("replica"),
        P(("replica", "tensor")),
        P(("replica", "tensor"), None),
        P(("replica", "tensor")),
        P("replica", None),
    )
    return jax.shard_map(
        shards,
        mesh=mesh,
        in_specs=placed,
        out_specs=P(("replica", "tensor"), None),
        check_vma=False,
    )
```

```python
import functools

import jax
import jax.numpy as jnp
from jax import lax
from jax.experimental import pallas as pl
from jax.experimental.pallas import tpu as pltpu
from jax.sharding import PartitionSpec as P

HEADS = 12
KVH = 4
HD = 128
MOE_FF = 512
LANES = 128
SUB = 8
CORES = 2
FAR = 1024
EMPTY = -1e30
STEP = 16
MAXP = 2

VMEM = pl.BlockSpec(memory_space=pltpu.VMEM)
SMEM = pl.BlockSpec(memory_space=pltpu.SMEM)
ANY = pl.BlockSpec(memory_space=pl.ANY)
PARAMS = pltpu.CompilerParams(vmem_limit_bytes=16 * 2**20)


def resident(array):
    return pltpu.with_memory_space_constraint(array, pltpu.VMEM)


def far(array):
    return pltpu.with_memory_space_constraint(array, pltpu.HBM)


def normed(values, gain):
    inverse = lax.rsqrt(jnp.mean(values * values, axis=-1, keepdims=True) + 1e-05)
    return (values * inverse * gain).astype(jnp.bfloat16)


def ways(size):
    return [(chips, core) for chips in range(size // CORES) for core in range(CORES)][1:]


def target(me, size, way):
    chip = lax.rem(me // CORES + way[0], size // CORES)
    return chip * CORES + lax.rem(me + way[1], CORES)


def sender(me, size, way):
    chip = lax.rem(me // CORES + size // CORES - way[0], size // CORES)
    return chip * CORES + lax.rem(me + way[1], CORES)


def senders(me, size):
    return [me] + [sender(me, size, way) for way in ways(size)]


def targets(me, size):
    return [me] + [target(me, size, way) for way in ways(size)]


def exchanged(blocks):
    size = len(blocks)
    arrived = [blocks[0]]
    for way, block in zip(ways(size), blocks[1:]):
        pairs = []
        for me in range(size):
            chip = (me // CORES + way[0]) % (size // CORES)
            pairs.append((me, chip * CORES + (me + way[1]) % CORES))
        arrived.append(lax.ppermute(block, "tensor", pairs))
    return arrived


def to_step(rows):
    extra = -rows.shape[0] % STEP
    if not extra:
        return rows
    filler = jnp.zeros((extra, rows.shape[1]), jnp.float32)
    return jnp.concatenate([rows.astype(jnp.float32), filler], axis=0).astype(rows.dtype)


def lanes_of(numbers, lane):
    row = jnp.zeros(lane.shape, jnp.float32)
    for place, number in enumerate(numbers):
        row = jnp.where(lane == place, number.astype(jnp.float32), row)
    return row


def at_lane(rows, lane, place):
    return jnp.sum(jnp.where(lane == place, rows, 0.0), axis=-1, keepdims=True)


def page_hits(plan, pages):
    return [jnp.where(plan[place : place + 1] == pages, 1.0, 0.0) for place in range(MAXP)]


def offer_kernel(tokens, paths, pages, table, lens, packed, *refs):
    offers, homes, plan, tail_out, rows, paths_s, pages_s, table_v, lens_v, sems = refs
    pairs = [
        (tokens, rows),
        (paths, paths_s),
        (pages, pages_s),
        (table, table_v),
        (lens, lens_v.at[0]),
    ]
    copies = [pltpu.make_async_copy(*pair, sems.at[i]) for i, pair in enumerate(pairs)]
    for copy in copies:
        copy.start()
    for copy in copies:
        copy.wait()
    me = lax.axis_index("tensor")
    rows_dev, width = rows.shape
    top = paths.shape[0]
    lane = lax.broadcasted_iota(jnp.int32, (1, LANES), 1)
    wide = rows[...].astype(jnp.float32)
    tails = []
    for slot in range(rows_dev):
        numbers = [paths_s[place, me * rows_dev + slot] for place in range(top)]
        if slot == rows_dev - 1:
            numbers += [packed[0] % FAR]
            numbers += [pages_s[0, place] for place in range(MAXP)]
            numbers += [packed[0] // FAR]
        tails.append(lanes_of(numbers, lane))
    tail_out[...] = tails[-1]
    full = jnp.concatenate([wide, jnp.concatenate(tails, axis=0)], axis=1)
    homes[...] = full[:-1].astype(jnp.bfloat16)
    guest = jnp.concatenate(
        [wide[-1:], tails[-1], jnp.zeros((1, LANES), jnp.float32)], axis=1
    )
    half = guest.shape[1] // 2
    block = jnp.concatenate([guest[:, :half], guest[:, half:]], axis=0).astype(jnp.bfloat16)
    for place in range(offers.shape[0]):
        offers[place] = block

    count = table.shape[1]
    npages = plan.shape[0]
    size = count * MAXP // (npages - MAXP)
    filler = jnp.zeros((1, LANES - count), jnp.float32)
    spots = lane - count
    lines = []
    for place in range(MAXP):
        ids = table_v[place : place + 1].astype(jnp.float32)
        ids = jnp.concatenate([ids, filler], axis=1)
        guests = (spots * npages + npages - MAXP + place).astype(jnp.float32)
        guests = jnp.where(spots < size, guests, -1.0)
        lines.append(jnp.where(spots < 0, ids, guests))
    lines.append(jnp.concatenate([lens_v[...].astype(jnp.float32), filler], axis=1))
    lines.append(jnp.zeros((npages - MAXP - 1, LANES), jnp.float32))
    plan[...] = jnp.concatenate(lines, axis=0)


def load_kernel(plans, *refs):
    sources, outs, sems = refs[1 : 1 + len(plans)], refs[1 + len(plans) : -1], refs[-1]
    copies = []

    def copy(source, out):
        copies.append(pltpu.make_async_copy(source, out, sems.at[len(copies)]))

    for (first, count, pieces), source, out in zip(plans, sources, outs):
        each = source.shape[0] // pieces if len(out.shape) == 4 else count // pieces
        for piece in range(pieces):
            lines = pl.ds(piece * each, each)
            if len(out.shape) == 4:
                for place in range(count):
                    columns = pl.ds((first + place) * LANES, LANES)
                    copy(source.at[lines, :, columns], out.at[place, lines])
            else:
                copy(source.at[pl.ds(first + piece * each, each)], out.at[lines])
    for made in copies:
        made.start()
    for made in copies:
        made.wait()


def loaded(after, *wanted):
    shapes, plans, copies = [], [], 0
    for array, first, count in wanted:
        if array.ndim == 3:
            shapes.append(shape((count,) + array.shape[:2] + (LANES,), array.dtype))
            plans.append((first, count, 2))
            copies += 2 * count
        else:
            shapes.append(shape((count, array.shape[1]), array.dtype))
            plans.append((first, count, 4))
            copies += 4
    parts = pl.pallas_call(
        functools.partial(load_kernel, tuple(plans)),
        out_shape=shapes,
        in_specs=[ANY] * (1 + len(wanted)),
        out_specs=[VMEM] * len(wanted),
        scratch_shapes=[pltpu.SemaphoreType.DMA((copies,))],
        compiler_params=PARAMS,
        cost_estimate=pl.CostEstimate(
            flops=0, bytes_accessed=sum(2 * part.size for part in shapes), transcendentals=0
        ),
        name="load",
    )(after, *[far(array) for array, _, _ in wanted])
    return [
        part.reshape(part.shape[0], -1, LANES) if part.ndim == 4 else part for part in parts
    ]


def project_kernel(size, npages, top, *refs):
    blocks, refs = refs[:size], refs[size:]
    offers, gain, weight, plan, _, rows_ref = refs[:6]
    outs = refs[6 : 6 + size]
    gathered, paged = refs[6 + size :]
    me = lax.axis_index("tensor")
    replica = lax.axis_index("replica").astype(jnp.float32)
    home_dev = blocks[0].shape[0]
    homes = size * home_dev
    width, columns = weight.shape
    for owner, block in zip(senders(me, size), blocks):
        gathered[pl.ds(owner, 1)] = block[...].astype(jnp.float32)[None]
    came = offers[...].astype(jnp.float32)
    half = came.shape[2]
    lane = lax.broadcasted_iota(jnp.int32, (1, 1, half), 2)
    spot = width + top + 1 + MAXP - half
    source = jnp.sum(jnp.where(lane == spot, came[:, 1:], 0.0), axis=2, keepdims=True)
    picked = jnp.where(source == replica, came, 0.0)
    picked = jnp.sum(picked.reshape(-1, size, 2, half), axis=0)
    for owner in range(size):
        rows_ref[owner * home_dev : (owner + 1) * home_dev] = gathered[owner]
        guest = jnp.concatenate([picked[owner, :1], picked[owner, 1:]], axis=1)
        rows_ref[homes + owner : homes + owner + 1] = guest[:, : width + LANES]
    norm = to_step(normed(rows_ref[:, :width], gain[...]))
    products = jnp.dot(norm, weight[...], preferred_element_type=jnp.float32)
    line = lax.broadcasted_iota(jnp.int32, (size * SUB, LANES), 0)
    ids = line // SUB * npages + line % SUB
    ids = jnp.where(line % SUB < npages, ids, -2).astype(jnp.float32)
    hits = sum(page_hits(plan[...], ids))[:, : norm.shape[0]]
    paged[...] = jnp.dot(
        hits.astype(jnp.bfloat16), products.astype(jnp.bfloat16), preferred_element_type=jnp.float32
    )
    for end, out in zip(targets(me, size), outs):
        start = pl.multiple_of(end * SUB, SUB)
        out[...] = paged[pl.ds(start, SUB)][:npages].astype(jnp.bfloat16)


def attend_kernel(size, top, *refs):
    blocks, refs = refs[:size], refs[size:]
    cache, rows_ref, plan_ref, _ = refs[:4]
    outs = refs[4 : 4 + size]
    gathered, terms = refs[4 + size :]
    me = lax.axis_index("tensor")
    npages, _, page_len, _ = cache.shape
    home_pages = npages - MAXP
    homes = home_pages // MAXP * size
    group = HEADS // KVH
    qwidth, kwidth = HEADS * HD, KVH * HD
    width = rows_ref.shape[1] - LANES
    for owner, block in zip(senders(me, size), blocks):
        gathered[pl.ds(owner, 1), :npages] = block[...].astype(jnp.float32)[None]
    joined = jnp.concatenate([gathered[owner] for owner in range(size)], axis=1)

    plan = plan_ref[...]
    line = lax.broadcasted_iota(jnp.int32, (SUB, LANES), 0)
    hits = page_hits(plan, (me * npages + line).astype(jnp.float32))
    left = sum(
        hit * (plan[MAXP : MAXP + 1] - float(place * page_len)) for place, hit in enumerate(hits)
    )
    left = jnp.sum(left, axis=1, keepdims=True)
    leads = jnp.sum(hits[0], axis=1, keepdims=True)
    tails = rows_ref[:, width:]
    place = lax.broadcasted_iota(jnp.int32, tails.shape, 0)
    numbers = jnp.sum(jnp.where(place == homes + me, tails, 0.0), axis=0, keepdims=True)
    lane = lax.broadcasted_iota(jnp.int32, (1, LANES), 1)
    near_len = at_lane(numbers, lane, top)
    line = line[:, :1]
    near_left, near_lead = jnp.zeros((SUB, 1), jnp.float32), None
    for place in range(MAXP):
        named = at_lane(numbers, lane, top + 1 + place) == line.astype(jnp.float32)
        near_left = jnp.where(named, near_len - float(place * page_len), near_left)
        if place == 0:
            near_lead = jnp.where(named, 1.0, 0.0)
    left = jnp.where(line < home_pages, left, near_left)
    leads = jnp.where(line < home_pages, leads, near_lead)
    row = lax.broadcasted_iota(jnp.int32, (SUB, npages * page_len), 0)
    spot = lax.broadcasted_iota(jnp.int32, (SUB, npages * page_len), 1)
    inside = (spot - row * page_len).astype(jnp.float32)
    usable = jnp.where((inside >= 0.0) & (inside < jnp.minimum(left, float(page_len))), 1.0, 0.0)
    usable = jnp.concatenate([usable] * HEADS, axis=0) > 0.5
    leads = jnp.concatenate([leads] * HEADS, axis=0) > 0.5

    query = jnp.concatenate([joined[:, h * HD : (h + 1) * HD] for h in range(HEADS)], axis=0)
    fresh_key, fresh_value = [
        jnp.concatenate(
            [joined[:, start + h // group * HD : start + (h // group + 1) * HD] for h in range(HEADS)],
            axis=0,
        )
        for start in (qwidth, qwidth + kwidth)
    ]
    lines = group * SUB
    narrow = query.astype(jnp.bfloat16)
    scores = []
    for kv in range(KVH):
        keys = cache[:, 0, :, kv * HD : (kv + 1) * HD].reshape(npages * page_len, HD)
        scores.append(
            lax.dot_general(
                narrow[kv * lines : (kv + 1) * lines],
                keys,
                (((1,), (1,)), ((), ())),
                preferred_element_type=jnp.float32,
            )
        )
    scores = jnp.concatenate(scores, axis=0) * HD ** (-0.5)
    scores = jnp.where(usable, scores, EMPTY)
    own = jnp.sum(query * fresh_key, axis=-1, keepdims=True) * HD ** (-0.5)
    own = jnp.where(leads, own, EMPTY)
    peak = jnp.maximum(jnp.max(scores, axis=-1, keepdims=True), own)
    weights = jnp.where(usable, jnp.exp(scores - peak), 0.0)
    newest = jnp.where(leads, jnp.exp(own - peak), 0.0)
    total = jnp.sum(weights, axis=-1, keepdims=True) + newest
    narrow = weights.astype(jnp.bfloat16)
    summed = []
    for kv in range(KVH):
        values = cache[:, 1, :, kv * HD : (kv + 1) * HD].reshape(npages * page_len, HD)
        summed.append(
            jnp.dot(
                narrow[kv * lines : (kv + 1) * lines], values, preferred_element_type=jnp.float32
            )
        )
    summed = jnp.concatenate(summed, axis=0) + newest * fresh_value
    used = total > 0.0
    safe = jnp.where(used, total, 1.0)
    mixed = summed / safe
    level = jnp.where(used, peak + jnp.log(safe), EMPTY)
    lane = lax.broadcasted_iota(jnp.int32, (SUB, LANES), 1)
    levels = jnp.zeros((SUB, LANES), jnp.float32)
    for h in range(HEADS):
        levels = jnp.where(lane % STEP == h, level[h * SUB : (h + 1) * SUB], levels)
    upper = levels.astype(jnp.bfloat16).astype(jnp.float32)
    rest = levels - upper
    middle = rest.astype(jnp.bfloat16).astype(jnp.float32)
    levels = jnp.where(lane < STEP, upper, jnp.where(lane < 2 * STEP, middle, rest - middle))
    levels = jnp.where(lane < 3 * STEP, levels, 0.0)
    mixes = jnp.concatenate([mixed[h * SUB : (h + 1) * SUB] for h in range(HEADS)], axis=1)
    part = qwidth // size
    for owner in range(size):
        terms[owner] = jnp.concatenate([mixes[:, owner * part : (owner + 1) * part], levels], axis=1)
    for end, out in zip(targets(me, size), outs):
        out[...] = terms[pl.ds(end, 1)][0, :npages].astype(jnp.bfloat16)


def out_kernel(size, npages, *refs):
    blocks, refs = refs[:size], refs[size:]
    weight, plan, _, out = refs
    me = lax.axis_index("tensor")
    part = weight.shape[0]
    terms, ids = [], []
    line = lax.broadcasted_iota(jnp.int32, (SUB, LANES), 0)
    filler = jnp.zeros((SUB - npages, part + LANES), jnp.float32)
    for owner, block in zip(senders(me, size), blocks):
        terms += [block[...].astype(jnp.float32), filler]
        ids.append(jnp.where(line < npages, owner * npages + line, -2))
    terms = jnp.concatenate(terms, axis=0).astype(jnp.bfloat16)
    ids = jnp.concatenate(ids, axis=0).astype(jnp.float32)
    spread = lax.broadcasted_iota(jnp.int32, (LANES, part), 0)
    head = (lax.broadcasted_iota(jnp.int32, (LANES, part), 1) + me * part) // HD
    spread = jnp.where((spread % STEP == head) & (spread < 3 * STEP), 1.0, 0.0)
    spread = spread.astype(jnp.bfloat16)
    count = out.shape[0]
    rows = count + -count % STEP
    mixes, levels = [], []
    for hit in page_hits(plan[...], ids):
        picked = lax.dot_general(
            hit[:, :rows].astype(jnp.bfloat16),
            terms,
            (((0,), (0,)), ((), ())),
            preferred_element_type=jnp.float32,
        )
        mixes.append(picked[:, :part])
        levels.append(
            jnp.dot(
                picked[:, part:].astype(jnp.bfloat16), spread, preferred_element_type=jnp.float32
            )
        )
    highest = functools.reduce(jnp.maximum, levels)
    factors = [jnp.exp(level - highest) for level in levels]
    mixed = sum(mix * factor for mix, factor in zip(mixes, factors)) / sum(factors)
    products = jnp.dot(
        mixed.astype(jnp.bfloat16), weight[...], preferred_element_type=jnp.float32
    )
    out[...] = products[:count].astype(jnp.bfloat16)


def expert_kernel(size, top, experts, parts, lows, *refs):
    sums, refs = refs[:size], refs[size:]
    rows_ref, gain, router = refs[:3]
    gate_up, refs = refs[3 : 3 + parts], refs[3 + parts :]
    down, refs = refs[:lows], refs[lows:]
    homes, guests, finished, ends_ref = refs[:size], refs[size], refs[size + 1], refs[size + 2]
    me = lax.axis_index("tensor")
    count = rows_ref.shape[0]
    width = rows_ref.shape[1] - LANES
    rows_dev = count // size
    units = sum(piece.shape[0] for piece in down)
    total = functools.reduce(jnp.add, [piece[...].astype(jnp.float32) for piece in sums])
    hidden = (rows_ref[:, :width] + total).astype(jnp.bfloat16).astype(jnp.float32)
    norm = normed(hidden, gain[...])
    lane = lax.broadcasted_iota(jnp.int32, (count, LANES), 1)
    numbers = rows_ref[:, width:]
    logits = lax.dot_general(
        norm, router[...], (((1,), (1,)), ((), ())), preferred_element_type=jnp.float32
    )
    logits = jnp.concatenate(
        [logits, jnp.zeros((count, LANES - experts), jnp.float32)], axis=1
    )
    routed = jnp.zeros((count, LANES), jnp.float32)
    for place in range(top):
        route = at_lane(numbers, lane, place)
        routed = jnp.where(lane.astype(jnp.float32) == route, 1.0, routed)
    logits = jnp.where(routed > 0.5, logits, EMPTY)
    shares = jnp.where(
        routed > 0.5, jnp.exp(logits - jnp.max(logits, axis=-1, keepdims=True)), 0.0
    )
    shares = shares / jnp.sum(shares, axis=-1, keepdims=True)

    here = lax.broadcasted_iota(jnp.int32, (LANES, 2 * LANES), 0)
    there = lax.broadcasted_iota(jnp.int32, (LANES, 2 * LANES), 1)
    evens = jnp.where(there == 2 * here, 1.0, 0.0).astype(jnp.bfloat16)
    odds = jnp.where(there == 2 * here + 1, 1.0, 0.0).astype(jnp.bfloat16)
    wide = to_step(norm)
    padded = wide.shape[0]
    blocks = width // LANES
    tall = jnp.concatenate([wide[:, b * LANES : (b + 1) * LANES] for b in range(blocks)], axis=0)
    to_gate = jnp.dot(tall, evens, preferred_element_type=jnp.float32).astype(jnp.bfloat16)
    to_up = jnp.dot(tall, odds, preferred_element_type=jnp.float32).astype(jnp.bfloat16)
    left = []
    for b in range(blocks):
        lines = slice(b * padded, (b + 1) * padded)
        left.append(jnp.concatenate([to_gate[lines], to_up[lines]], axis=0))
    left = jnp.concatenate(left, axis=1)
    both = []
    for piece in gate_up:
        right = jnp.concatenate([piece[place] for place in range(piece.shape[0])], axis=1)
        both.append(jnp.dot(left, right, preferred_element_type=jnp.float32))
    both = jnp.concatenate(both, axis=1)
    gate, up = both[:count], both[padded : padded + count]
    activated = gate / (1.0 + jnp.exp(-gate)) * up
    step = min(units, MOE_FF)
    scaled = []
    for start in range(0, units, step):
        expert = (me * units + start) // MOE_FF
        share = at_lane(shares, lane, expert)
        scaled.append(activated[:, start : start + step] * share)
    scaled = jnp.concatenate(scaled, axis=1).astype(jnp.bfloat16)
    partial, start = 0.0, 0
    for piece in down:
        left = scaled[:, start : start + piece.shape[0]]
        partial += jnp.dot(left, piece[...], preferred_element_type=jnp.float32)
        start += piece.shape[0]
    home_dev = rows_dev - 1
    first = size * home_dev
    for owner in range(size):
        lines = slice(owner * home_dev, (owner + 1) * home_dev)
        mine = jnp.where(me == owner, 1.0, 0.0)
        finished[owner] = partial[lines] + hidden[lines] * mine
        line = slice(first + owner, first + owner + 1)
        ends_ref[owner : owner + 1] = partial[line] + hidden[line] * mine
    for end, out in zip(targets(me, size), homes):
        out[...] = finished[pl.ds(end, 1)][0].astype(jnp.bfloat16)
    half = width // 2
    for owner in range(size):
        guest = ends_ref[owner : owner + 1]
        block = jnp.concatenate([guest[:, :half], guest[:, half:]], axis=0).astype(jnp.bfloat16)
        for place in range(owner, guests.shape[0], size):
            guests[place] = block


def finish_kernel(size, spot, *refs):
    pieces, refs = refs[:size], refs[size:]
    guests, tail, out = refs
    homes = functools.reduce(jnp.add, [piece[...].astype(jnp.float32) for piece in pieces])
    came = guests[...].astype(jnp.float32)
    lane = lax.broadcasted_iota(jnp.int32, (1, LANES), 1)
    source = at_lane(tail[...], lane, spot).reshape(1, 1, 1)
    place = lax.broadcasted_iota(jnp.int32, (came.shape[0], 1, 1), 0) // size
    guest = jnp.sum(jnp.where(place.astype(jnp.float32) == source, came, 0.0), axis=0)
    guest = jnp.concatenate([guest[:1], guest[1:]], axis=1)
    out[...] = jnp.concatenate([homes, guest], axis=0).astype(jnp.bfloat16)


def shape(dims, dtype=jnp.float32):
    return jax.ShapeDtypeStruct(dims, dtype)


def shards(
    tokens,
    attn_gain,
    qkv_weight,
    out_weight,
    moe_gain,
    router,
    expert_gate_up,
    expert_down,
    kv_cache,
    page_table,
    home_len,
    guest_source,
    guest_pages,
    guest_len,
    routes,
):
    size = lax.axis_size("tensor")
    replicas = lax.axis_size("replica")
    rows_dev, width = tokens.shape
    npages = kv_cache.shape[0]
    top = routes.shape[1]
    units = expert_down.shape[0]
    part = out_weight.shape[0]
    columns = qkv_weight.shape[1]
    count = size * rows_dev
    home_dev = rows_dev - 1
    wide = width + LANES
    everyone = size * replicas
    blocks = units // LANES
    gate_up, down = [], []

    def load_more(after, ups, downs):
        first, last = ups[0] * blocks // 8, ups[1] * blocks // 8
        wanted = []
        if last > first:
            wanted.append((expert_gate_up, first, last - first))
        if downs[1] > downs[0]:
            wanted.append((expert_down, downs[0] * units // 8, (downs[1] - downs[0]) * units // 8))
        if not wanted:
            return after
        got = loaded(after, *wanted)
        for part in got:
            (gate_up if part.ndim == 3 else down).append(part)
        return got[0]

    packed = guest_source * FAR + guest_len
    offers, homes, plan, tail = pl.pallas_call(
        offer_kernel,
        out_shape=[
            shape((everyone, 2, (wide + LANES) // 2), jnp.bfloat16),
            shape((home_dev, wide), jnp.bfloat16),
            shape((npages, LANES)),
            shape((1, LANES)),
        ],
        in_specs=[ANY] * 5 + [SMEM],
        out_specs=[VMEM] * 4,
        scratch_shapes=[
            pltpu.VMEM(tokens.shape, tokens.dtype),
            pltpu.SMEM(routes.T.shape, jnp.int32),
            pltpu.SMEM(guest_pages.shape, jnp.int32),
            pltpu.VMEM(page_table.T.shape, jnp.int32),
            pltpu.VMEM((1,) + home_len.shape, jnp.int32),
            pltpu.SemaphoreType.DMA((5,)),
        ],
        compiler_params=PARAMS,
        name="offer",
    )(far(tokens), far(routes.T), far(guest_pages), far(page_table.T), far(home_len), packed)
    came = lax.all_to_all(offers, ("replica", "tensor"), 0, 0, tiled=True)
    messages = exchanged([homes] * size)
    (qkv_near,) = loaded(homes, (qkv_weight, 0, width))
    before = load_more(homes, (0, 1), (0, 0))

    rows, *projected = pl.pallas_call(
        functools.partial(project_kernel, size, npages, top),
        out_shape=[shape((count, wide))] + [shape((npages, columns), jnp.bfloat16)] * size,
        in_specs=[VMEM] * (size + 4) + [ANY],
        out_specs=[VMEM] * (size + 1),
        scratch_shapes=[
            pltpu.VMEM((size, home_dev, wide), jnp.float32),
            pltpu.VMEM((size * SUB, columns), jnp.float32),
        ],
        compiler_params=PARAMS,
        name="project",
    )(
        *messages,
        came,
        attn_gain.reshape(1, width),
        resident(qkv_near),
        plan,
        before,
    )
    joined = exchanged(projected)

    before = load_more(rows, (1, 3), (0, 2))
    terms = pl.pallas_call(
        functools.partial(attend_kernel, size, top),
        out_shape=[shape((npages, part + LANES), jnp.bfloat16)] * size,
        in_specs=[VMEM] * (size + 3) + [ANY],
        out_specs=[VMEM] * size,
        scratch_shapes=[
            pltpu.VMEM((size, SUB, columns), jnp.float32),
            pltpu.VMEM((size, SUB, part + LANES), jnp.float32),
        ],
        compiler_params=PARAMS,
        name="attend",
    )(*joined, resident(kv_cache), rows, plan, before)
    arrived = exchanged(terms)

    before = load_more(terms[0], (3, 5), (2, 4))
    partial = pl.pallas_call(
        functools.partial(out_kernel, size, npages),
        out_shape=shape((count, width), jnp.bfloat16),
        in_specs=[VMEM] * (size + 2) + [ANY],
        out_specs=VMEM,
        compiler_params=PARAMS,
        name="out",
    )(*arrived, resident(out_weight), plan, before)
    sums = exchanged([partial] * size)

    load_more(partial, (5, 8), (4, 8))
    *pieces, guests = pl.pallas_call(
        functools.partial(
            expert_kernel, size, top, router.shape[1], len(gate_up), len(down)
        ),
        out_shape=[shape((home_dev, width), jnp.bfloat16)] * size
        + [shape((everyone, 2, width // 2), jnp.bfloat16)],
        in_specs=[VMEM] * (size + 3 + len(gate_up) + len(down)),
        out_specs=[VMEM] * (size + 1),
        scratch_shapes=[
            pltpu.VMEM((size, home_dev, width), jnp.float32),
            pltpu.VMEM((size, width), jnp.float32),
        ],
        compiler_params=PARAMS,
        name="experts",
    )(
        *sums,
        rows,
        moe_gain.reshape(1, width),
        router.T,
        *[resident(piece) for piece in gate_up + down],
    )
    guests = lax.all_to_all(guests, ("replica", "tensor"), 0, 0, tiled=True)
    pieces = exchanged(pieces)
    return pl.pallas_call(
        functools.partial(finish_kernel, size, top + 1 + MAXP),
        out_shape=shape((rows_dev, width), jnp.bfloat16),
        in_specs=[VMEM] * (size + 2),
        out_specs=VMEM,
        compiler_params=PARAMS,
        name="finish",
    )(*pieces, guests, tail)


def solution(mesh):
    placed = (
        P(("replica", "tensor"), None),
        P(),
        P(None, "tensor"),
        P("tensor", None),
        P(),
        P(),
        P(None, None, "tensor"),
        P("tensor", None),
        P(("replica", "tensor"), None, None, None),
        P("replica", None),
        P("replica"),
        P(("replica", "tensor")),
        P(("replica", "tensor"), None),
        P(("replica", "tensor")),
        P("replica", None),
    )
    return jax.shard_map(
        shards,
        mesh=mesh,
        in_specs=placed,
        out_specs=P(("replica", "tensor"), None),
        check_vma=False,
    )
```

```python
import functools

import jax
import jax.numpy as jnp
from jax import lax
from jax.experimental import pallas as pl
from jax.experimental.pallas import tpu as pltpu
from jax.sharding import PartitionSpec as P

HEADS = 12
KVH = 4
HD = 128
MOE_FF = 512
LANES = 128
SUB = 8
CORES = 2
FAR = 1024
EMPTY = -1e30
STEP = 16
MAXP = 2

VMEM = pl.BlockSpec(memory_space=pltpu.VMEM)
SMEM = pl.BlockSpec(memory_space=pltpu.SMEM)
ANY = pl.BlockSpec(memory_space=pl.ANY)
PARAMS = pltpu.CompilerParams(vmem_limit_bytes=16 * 2**20)


def resident(array):
    return pltpu.with_memory_space_constraint(array, pltpu.VMEM)


def far(array):
    return pltpu.with_memory_space_constraint(array, pltpu.HBM)


def normed(values, gain):
    inverse = lax.rsqrt(jnp.mean(values * values, axis=-1, keepdims=True) + 1e-05)
    return (values * inverse * gain).astype(jnp.bfloat16)


def ways(size):
    return [(chips, core) for chips in range(size // CORES) for core in range(CORES)][1:]


def target(me, size, way):
    chip = lax.rem(me // CORES + way[0], size // CORES)
    return chip * CORES + lax.rem(me + way[1], CORES)


def sender(me, size, way):
    chip = lax.rem(me // CORES + size // CORES - way[0], size // CORES)
    return chip * CORES + lax.rem(me + way[1], CORES)


def senders(me, size):
    return [me] + [sender(me, size, way) for way in ways(size)]


def targets(me, size):
    return [me] + [target(me, size, way) for way in ways(size)]


def exchanged(blocks):
    size = len(blocks)
    arrived = [blocks[0]]
    for way, block in zip(ways(size), blocks[1:]):
        pairs = []
        for me in range(size):
            chip = (me // CORES + way[0]) % (size // CORES)
            pairs.append((me, chip * CORES + (me + way[1]) % CORES))
        arrived.append(lax.ppermute(block, "tensor", pairs))
    return arrived


def to_step(rows):
    extra = -rows.shape[0] % STEP
    if not extra:
        return rows
    filler = jnp.zeros((extra, rows.shape[1]), jnp.float32)
    return jnp.concatenate([rows.astype(jnp.float32), filler], axis=0).astype(rows.dtype)


def lanes_of(numbers, lane):
    row = jnp.zeros(lane.shape, jnp.float32)
    for place, number in enumerate(numbers):
        row = jnp.where(lane == place, number.astype(jnp.float32), row)
    return row


def at_lane(rows, lane, place):
    return jnp.sum(jnp.where(lane == place, rows, 0.0), axis=-1, keepdims=True)


def across(block, size):
    arrived = [block]
    for chips in range(1, size // CORES):
        pairs = [(me, (me + chips * CORES) % size) for me in range(size)]
        arrived.append(lax.ppermute(block, "tensor", pairs))
    return arrived


def page_hits(plan, pages):
    return [jnp.where(plan[place : place + 1] == pages, 1.0, 0.0) for place in range(MAXP)]


def offer_kernel(tokens, paths, pages, table, lens, packed, *refs):
    offers, homes, plan, tail_out, rows, paths_s, pages_s, table_v, lens_v, sems = refs
    pairs = [
        (tokens, rows),
        (paths, paths_s),
        (pages, pages_s),
        (table, table_v),
        (lens, lens_v.at[0]),
    ]
    copies = [pltpu.make_async_copy(*pair, sems.at[i]) for i, pair in enumerate(pairs)]
    for copy in copies:
        copy.start()
    for copy in copies:
        copy.wait()
    me = lax.axis_index("tensor")
    rows_dev, width = rows.shape
    top = paths.shape[0]
    lane = lax.broadcasted_iota(jnp.int32, (1, LANES), 1)
    wide = rows[...].astype(jnp.float32)
    tails = []
    for slot in range(rows_dev):
        numbers = [paths_s[place, me * rows_dev + slot] for place in range(top)]
        if slot == rows_dev - 1:
            numbers += [packed[0] % FAR]
            numbers += [pages_s[0, place] for place in range(MAXP)]
            numbers += [packed[0] // FAR]
        tails.append(lanes_of(numbers, lane))
    tail_out[...] = tails[-1]
    full = jnp.concatenate([wide, jnp.concatenate(tails, axis=0)], axis=1)
    homes[...] = full[:-1].astype(jnp.bfloat16)
    guest = jnp.concatenate(
        [wide[-1:], tails[-1], jnp.zeros((1, LANES), jnp.float32)], axis=1
    )
    half = guest.shape[1] // 2
    block = jnp.concatenate([guest[:, :half], guest[:, half:]], axis=0).astype(jnp.bfloat16)
    for place in range(offers.shape[0]):
        offers[place] = block

    count = table.shape[1]
    npages = plan.shape[0]
    size = count * MAXP // (npages - MAXP)
    filler = jnp.zeros((1, LANES - count), jnp.float32)
    spots = lane - count
    lines = []
    for place in range(MAXP):
        ids = table_v[place : place + 1].astype(jnp.float32)
        ids = jnp.concatenate([ids, filler], axis=1)
        guests = (spots * npages + npages - MAXP + place).astype(jnp.float32)
        guests = jnp.where(spots < size, guests, -1.0)
        lines.append(jnp.where(spots < 0, ids, guests))
    lines.append(jnp.concatenate([lens_v[...].astype(jnp.float32), filler], axis=1))
    lines.append(jnp.zeros((npages - MAXP - 1, LANES), jnp.float32))
    plan[...] = jnp.concatenate(lines, axis=0)


def load_kernel(plans, *refs):
    sources, outs, sems = refs[1 : 1 + len(plans)], refs[1 + len(plans) : -1], refs[-1]
    copies = []

    def copy(source, out):
        copies.append(pltpu.make_async_copy(source, out, sems.at[len(copies)]))

    for (first, count, pieces), source, out in zip(plans, sources, outs):
        each = source.shape[0] // pieces if len(out.shape) == 4 else count // pieces
        for piece in range(pieces):
            lines = pl.ds(piece * each, each)
            if len(out.shape) == 4:
                for place in range(count):
                    columns = pl.ds((first + place) * LANES, LANES)
                    copy(source.at[lines, :, columns], out.at[place, lines])
            else:
                copy(source.at[pl.ds(first + piece * each, each)], out.at[lines])
    for made in copies:
        made.start()
    for made in copies:
        made.wait()


def loaded(after, *wanted):
    shapes, plans, copies = [], [], 0
    for array, first, count in wanted:
        if array.ndim == 3:
            shapes.append(shape((count,) + array.shape[:2] + (LANES,), array.dtype))
            plans.append((first, count, 2))
            copies += 2 * count
        else:
            shapes.append(shape((count, array.shape[1]), array.dtype))
            plans.append((first, count, 4))
            copies += 4
    parts = pl.pallas_call(
        functools.partial(load_kernel, tuple(plans)),
        out_shape=shapes,
        in_specs=[ANY] * (1 + len(wanted)),
        out_specs=[VMEM] * len(wanted),
        scratch_shapes=[pltpu.SemaphoreType.DMA((copies,))],
        compiler_params=PARAMS,
        cost_estimate=pl.CostEstimate(
            flops=0, bytes_accessed=sum(2 * part.size for part in shapes), transcendentals=0
        ),
        name="load",
    )(after, *[far(array) for array, _, _ in wanted])
    return [
        part.reshape(part.shape[0], -1, LANES) if part.ndim == 4 else part for part in parts
    ]


def project_kernel(size, npages, top, *refs):
    blocks, refs = refs[:size], refs[size:]
    offers, gain, weight, plan, rows_ref = refs[:5]
    outs = refs[5 : 5 + size]
    gathered, paged = refs[5 + size :]
    me = lax.axis_index("tensor")
    replica = lax.axis_index("replica").astype(jnp.float32)
    home_dev = blocks[0].shape[0]
    homes = size * home_dev
    width, columns = weight.shape
    for owner, block in zip(senders(me, size), blocks):
        gathered[pl.ds(owner, 1)] = block[...].astype(jnp.float32)[None]
    came = offers[...].astype(jnp.float32)
    half = came.shape[2]
    lane = lax.broadcasted_iota(jnp.int32, (1, 1, half), 2)
    spot = width + top + 1 + MAXP - half
    source = jnp.sum(jnp.where(lane == spot, came[:, 1:], 0.0), axis=2, keepdims=True)
    picked = jnp.where(source == replica, came, 0.0)
    picked = jnp.sum(picked.reshape(-1, size, 2, half), axis=0)
    for owner in range(size):
        rows_ref[owner * home_dev : (owner + 1) * home_dev] = gathered[owner]
        guest = jnp.concatenate([picked[owner, :1], picked[owner, 1:]], axis=1)
        rows_ref[homes + owner : homes + owner + 1] = guest[:, : width + LANES]
    norm = to_step(normed(rows_ref[:, :width], gain[...]))
    products = jnp.dot(norm, weight[...], preferred_element_type=jnp.float32)
    line = lax.broadcasted_iota(jnp.int32, (size * SUB, LANES), 0)
    ids = line // SUB * npages + line % SUB
    ids = jnp.where(line % SUB < npages, ids, -2).astype(jnp.float32)
    hits = sum(page_hits(plan[...], ids))[:, : norm.shape[0]]
    paged[...] = jnp.dot(
        hits.astype(jnp.bfloat16), products.astype(jnp.bfloat16), preferred_element_type=jnp.float32
    )
    for end, out in zip(targets(me, size), outs):
        start = pl.multiple_of(end * SUB, SUB)
        out[...] = paged[pl.ds(start, SUB)][:npages].astype(jnp.bfloat16)


def attend_kernel(size, top, *refs):
    blocks, refs = refs[:size], refs[size:]
    cache, rows_ref, plan_ref, _ = refs[:4]
    outs = refs[4 : 4 + size]
    gathered, terms = refs[4 + size :]
    me = lax.axis_index("tensor")
    npages, _, page_len, _ = cache.shape
    home_pages = npages - MAXP
    homes = home_pages // MAXP * size
    group = HEADS // KVH
    qwidth, kwidth = HEADS * HD, KVH * HD
    width = rows_ref.shape[1] - LANES
    for owner, block in zip(senders(me, size), blocks):
        gathered[pl.ds(owner, 1), :npages] = block[...].astype(jnp.float32)[None]
    joined = jnp.concatenate([gathered[owner] for owner in range(size)], axis=1)

    plan = plan_ref[...]
    line = lax.broadcasted_iota(jnp.int32, (SUB, LANES), 0)
    hits = page_hits(plan, (me * npages + line).astype(jnp.float32))
    left = sum(
        hit * (plan[MAXP : MAXP + 1] - float(place * page_len)) for place, hit in enumerate(hits)
    )
    left = jnp.sum(left, axis=1, keepdims=True)
    leads = jnp.sum(hits[0], axis=1, keepdims=True)
    tails = rows_ref[:, width:]
    place = lax.broadcasted_iota(jnp.int32, tails.shape, 0)
    numbers = jnp.sum(jnp.where(place == homes + me, tails, 0.0), axis=0, keepdims=True)
    lane = lax.broadcasted_iota(jnp.int32, (1, LANES), 1)
    near_len = at_lane(numbers, lane, top)
    line = line[:, :1]
    near_left, near_lead = jnp.zeros((SUB, 1), jnp.float32), None
    for place in range(MAXP):
        named = at_lane(numbers, lane, top + 1 + place) == line.astype(jnp.float32)
        near_left = jnp.where(named, near_len - float(place * page_len), near_left)
        if place == 0:
            near_lead = jnp.where(named, 1.0, 0.0)
    left = jnp.where(line < home_pages, left, near_left)
    leads = jnp.where(line < home_pages, leads, near_lead)
    row = lax.broadcasted_iota(jnp.int32, (SUB, npages * page_len), 0)
    spot = lax.broadcasted_iota(jnp.int32, (SUB, npages * page_len), 1)
    inside = (spot - row * page_len).astype(jnp.float32)
    usable = jnp.where((inside >= 0.0) & (inside < jnp.minimum(left, float(page_len))), 1.0, 0.0)
    usable = jnp.concatenate([usable] * HEADS, axis=0) > 0.5
    leads = jnp.concatenate([leads] * HEADS, axis=0) > 0.5

    query = jnp.concatenate([joined[:, h * HD : (h + 1) * HD] for h in range(HEADS)], axis=0)
    fresh_key, fresh_value = [
        jnp.concatenate(
            [joined[:, start + h // group * HD : start + (h // group + 1) * HD] for h in range(HEADS)],
            axis=0,
        )
        for start in (qwidth, qwidth + kwidth)
    ]
    lines = group * SUB
    narrow = query.astype(jnp.bfloat16)
    scores = []
    for kv in range(KVH):
        keys = cache[:, 0, :, kv * HD : (kv + 1) * HD].reshape(npages * page_len, HD)
        scores.append(
            lax.dot_general(
                narrow[kv * lines : (kv + 1) * lines],
                keys,
                (((1,), (1,)), ((), ())),
                preferred_element_type=jnp.float32,
            )
        )
    scores = jnp.concatenate(scores, axis=0) * HD ** (-0.5)
    scores = jnp.where(usable, scores, EMPTY)
    own = jnp.sum(query * fresh_key, axis=-1, keepdims=True) * HD ** (-0.5)
    own = jnp.where(leads, own, EMPTY)
    peak = jnp.maximum(jnp.max(scores, axis=-1, keepdims=True), own)
    weights = jnp.where(usable, jnp.exp(scores - peak), 0.0)
    newest = jnp.where(leads, jnp.exp(own - peak), 0.0)
    total = jnp.sum(weights, axis=-1, keepdims=True) + newest
    narrow = weights.astype(jnp.bfloat16)
    summed = []
    for kv in range(KVH):
        values = cache[:, 1, :, kv * HD : (kv + 1) * HD].reshape(npages * page_len, HD)
        summed.append(
            jnp.dot(
                narrow[kv * lines : (kv + 1) * lines], values, preferred_element_type=jnp.float32
            )
        )
    summed = jnp.concatenate(summed, axis=0) + newest * fresh_value
    used = total > 0.0
    safe = jnp.where(used, total, 1.0)
    mixed = summed / safe
    level = jnp.where(used, peak + jnp.log(safe), EMPTY)
    lane = lax.broadcasted_iota(jnp.int32, (SUB, LANES), 1)
    levels = jnp.zeros((SUB, LANES), jnp.float32)
    for h in range(HEADS):
        levels = jnp.where(lane % STEP == h, level[h * SUB : (h + 1) * SUB], levels)
    upper = levels.astype(jnp.bfloat16).astype(jnp.float32)
    rest = levels - upper
    middle = rest.astype(jnp.bfloat16).astype(jnp.float32)
    levels = jnp.where(lane < STEP, upper, jnp.where(lane < 2 * STEP, middle, rest - middle))
    levels = jnp.where(lane < 3 * STEP, levels, 0.0)
    mixes = jnp.concatenate([mixed[h * SUB : (h + 1) * SUB] for h in range(HEADS)], axis=1)
    chips = size // CORES
    part = qwidth // chips
    for chip in range(chips):
        terms[chip] = jnp.concatenate([mixes[:, chip * part : (chip + 1) * part], levels], axis=1)
    for end, out in zip(targets(me, size), outs):
        out[...] = terms[pl.ds(end // CORES, 1)][0, :npages].astype(jnp.bfloat16)


def out_kernel(size, npages, *refs):
    blocks, refs = refs[:size], refs[size:]
    weight, mate_weight, plan, _, out = refs
    me = lax.axis_index("tensor")
    part = CORES * weight.shape[0]
    terms, ids = [], []
    line = lax.broadcasted_iota(jnp.int32, (SUB, LANES), 0)
    filler = jnp.zeros((SUB - npages, part + LANES), jnp.float32)
    for owner, block in zip(senders(me, size), blocks):
        terms += [block[...].astype(jnp.float32), filler]
        ids.append(jnp.where(line < npages, owner * npages + line, -2))
    terms = jnp.concatenate(terms, axis=0).astype(jnp.bfloat16)
    ids = jnp.concatenate(ids, axis=0).astype(jnp.float32)
    spread = lax.broadcasted_iota(jnp.int32, (LANES, part), 0)
    head = (lax.broadcasted_iota(jnp.int32, (LANES, part), 1) + me // CORES * part) // HD
    spread = jnp.where((spread % STEP == head) & (spread < 3 * STEP), 1.0, 0.0)
    spread = spread.astype(jnp.bfloat16)
    count = out.shape[0]
    rows = count + -count % STEP
    mixes, levels = [], []
    for hit in page_hits(plan[...], ids):
        picked = lax.dot_general(
            hit[:, :rows].astype(jnp.bfloat16),
            terms,
            (((0,), (0,)), ((), ())),
            preferred_element_type=jnp.float32,
        )
        mixes.append(picked[:, :part])
        levels.append(
            jnp.dot(
                picked[:, part:].astype(jnp.bfloat16), spread, preferred_element_type=jnp.float32
            )
        )
    highest = functools.reduce(jnp.maximum, levels)
    factors = [jnp.exp(level - highest) for level in levels]
    mixed = sum(mix * factor for mix, factor in zip(mixes, factors)) / sum(factors)
    halves = mixed[:, : part // CORES], mixed[:, part // CORES :]
    first = lax.rem(me, CORES) == 0
    own = jnp.where(first, halves[0], halves[1]).astype(jnp.bfloat16)
    other = jnp.where(first, halves[1], halves[0]).astype(jnp.bfloat16)
    products = jnp.dot(own, weight[...], preferred_element_type=jnp.float32)
    products += jnp.dot(other, mate_weight[...], preferred_element_type=jnp.float32)
    out[...] = products[:count].astype(jnp.bfloat16)


def expert_kernel(size, top, experts, parts, *refs):
    chips = size // CORES
    sums, refs = refs[:chips], refs[chips:]
    rows_ref, gain, router, down_far = refs[:4]
    gate_up, refs = refs[4 : 4 + parts], refs[4 + parts :]
    down, sems = refs[-2:]
    units = down.shape[0]
    each = units // sems.shape[0]
    copies = []
    for place in range(sems.shape[0]):
        lines = pl.ds(place * each, each)
        copies.append(pltpu.make_async_copy(down_far.at[lines], down.at[lines], sems.at[place]))
    for copy in copies:
        copy.start()
    homes, guests, finished, ends_ref = refs[:size], refs[size], refs[size + 1], refs[size + 2]
    me = lax.axis_index("tensor")
    count = rows_ref.shape[0]
    width = rows_ref.shape[1] - LANES
    rows_dev = count // size
    total = functools.reduce(jnp.add, [piece[...].astype(jnp.float32) for piece in sums])
    hidden = (rows_ref[:, :width] + total).astype(jnp.bfloat16).astype(jnp.float32)
    norm = normed(hidden, gain[...])
    lane = lax.broadcasted_iota(jnp.int32, (count, LANES), 1)
    numbers = rows_ref[:, width:]
    logits = lax.dot_general(
        norm, router[...], (((1,), (1,)), ((), ())), preferred_element_type=jnp.float32
    )
    logits = jnp.concatenate(
        [logits, jnp.zeros((count, LANES - experts), jnp.float32)], axis=1
    )
    routed = jnp.zeros((count, LANES), jnp.float32)
    for place in range(top):
        route = at_lane(numbers, lane, place)
        routed = jnp.where(lane.astype(jnp.float32) == route, 1.0, routed)
    logits = jnp.where(routed > 0.5, logits, EMPTY)
    shares = jnp.where(
        routed > 0.5, jnp.exp(logits - jnp.max(logits, axis=-1, keepdims=True)), 0.0
    )
    shares = shares / jnp.sum(shares, axis=-1, keepdims=True)

    here = lax.broadcasted_iota(jnp.int32, (LANES, 2 * LANES), 0)
    there = lax.broadcasted_iota(jnp.int32, (LANES, 2 * LANES), 1)
    evens = jnp.where(there == 2 * here, 1.0, 0.0).astype(jnp.bfloat16)
    odds = jnp.where(there == 2 * here + 1, 1.0, 0.0).astype(jnp.bfloat16)
    wide = to_step(norm)
    padded = wide.shape[0]
    blocks = width // LANES
    tall = jnp.concatenate([wide[:, b * LANES : (b + 1) * LANES] for b in range(blocks)], axis=0)
    to_gate = jnp.dot(tall, evens, preferred_element_type=jnp.float32).astype(jnp.bfloat16)
    to_up = jnp.dot(tall, odds, preferred_element_type=jnp.float32).astype(jnp.bfloat16)
    left = []
    for b in range(blocks):
        lines = slice(b * padded, (b + 1) * padded)
        left.append(jnp.concatenate([to_gate[lines], to_up[lines]], axis=0))
    left = jnp.concatenate(left, axis=1)
    both = []
    for piece in gate_up:
        right = jnp.concatenate([piece[place] for place in range(piece.shape[0])], axis=1)
        both.append(jnp.dot(left, right, preferred_element_type=jnp.float32))
    both = jnp.concatenate(both, axis=1)
    gate, up = both[:count], both[padded : padded + count]
    activated = gate / (1.0 + jnp.exp(-gate)) * up
    step = min(units, MOE_FF)
    scaled = []
    for start in range(0, units, step):
        expert = (me * units + start) // MOE_FF
        share = at_lane(shares, lane, expert)
        scaled.append(activated[:, start : start + step] * share)
    scaled = jnp.concatenate(scaled, axis=1).astype(jnp.bfloat16)
    for copy in copies:
        copy.wait()
    partial = jnp.dot(scaled, down[...], preferred_element_type=jnp.float32)
    home_dev = rows_dev - 1
    first = size * home_dev
    for owner in range(size):
        lines = slice(owner * home_dev, (owner + 1) * home_dev)
        mine = jnp.where(me == owner, 1.0, 0.0)
        finished[owner] = partial[lines] + hidden[lines] * mine
        line = slice(first + owner, first + owner + 1)
        ends_ref[owner : owner + 1] = partial[line] + hidden[line] * mine
    for end, out in zip(targets(me, size), homes):
        out[...] = finished[pl.ds(end, 1)][0].astype(jnp.bfloat16)
    half = width // 2
    for owner in range(size):
        guest = ends_ref[owner : owner + 1]
        block = jnp.concatenate([guest[:, :half], guest[:, half:]], axis=0).astype(jnp.bfloat16)
        for place in range(owner, guests.shape[0], size):
            guests[place] = block


def finish_kernel(size, spot, *refs):
    pieces, refs = refs[:size], refs[size:]
    guests, tail, out = refs
    homes = functools.reduce(jnp.add, [piece[...].astype(jnp.float32) for piece in pieces])
    came = guests[...].astype(jnp.float32)
    lane = lax.broadcasted_iota(jnp.int32, (1, LANES), 1)
    source = at_lane(tail[...], lane, spot).reshape(1, 1, 1)
    place = lax.broadcasted_iota(jnp.int32, (came.shape[0], 1, 1), 0) // size
    guest = jnp.sum(jnp.where(place.astype(jnp.float32) == source, came, 0.0), axis=0)
    guest = jnp.concatenate([guest[:1], guest[1:]], axis=1)
    out[...] = jnp.concatenate([homes, guest], axis=0).astype(jnp.bfloat16)


def shape(dims, dtype=jnp.float32):
    return jax.ShapeDtypeStruct(dims, dtype)


def shards(
    tokens,
    attn_gain,
    qkv_weight,
    out_weight,
    moe_gain,
    router,
    expert_gate_up,
    expert_down,
    kv_cache,
    page_table,
    home_len,
    guest_source,
    guest_pages,
    guest_len,
    routes,
):
    size = lax.axis_size("tensor")
    replicas = lax.axis_size("replica")
    rows_dev, width = tokens.shape
    npages = kv_cache.shape[0]
    top = routes.shape[1]
    units = expert_down.shape[0]
    part = out_weight.shape[0]
    columns = qkv_weight.shape[1]
    count = size * rows_dev
    home_dev = rows_dev - 1
    wide = width + LANES
    everyone = size * replicas
    blocks = units // LANES
    gate_up = []

    def load_more(after, first, last, *others):
        first, last = first * blocks // 8, last * blocks // 8
        wanted = [(expert_gate_up, first, last - first)] if last > first else []
        if not wanted and not others:
            return [after]
        got = loaded(after, *others, *wanted)
        gate_up.extend(got[len(others) :])
        return got

    packed = guest_source * FAR + guest_len
    offers, homes, plan, tail = pl.pallas_call(
        offer_kernel,
        out_shape=[
            shape((everyone, 2, (wide + LANES) // 2), jnp.bfloat16),
            shape((home_dev, wide), jnp.bfloat16),
            shape((npages, LANES)),
            shape((1, LANES)),
        ],
        in_specs=[ANY] * 5 + [SMEM],
        out_specs=[VMEM] * 4,
        scratch_shapes=[
            pltpu.VMEM(tokens.shape, tokens.dtype),
            pltpu.SMEM(routes.T.shape, jnp.int32),
            pltpu.SMEM(guest_pages.shape, jnp.int32),
            pltpu.VMEM(page_table.T.shape, jnp.int32),
            pltpu.VMEM((1,) + home_len.shape, jnp.int32),
            pltpu.SemaphoreType.DMA((5,)),
        ],
        compiler_params=PARAMS,
        name="offer",
    )(far(tokens), far(routes.T), far(guest_pages), far(page_table.T), far(home_len), packed)
    came = lax.all_to_all(offers, ("replica", "tensor"), 0, 0, tiled=True)
    messages = exchanged([homes] * size)
    (qkv_near,) = loaded(homes, (qkv_weight, 0, width))

    rows, *projected = pl.pallas_call(
        functools.partial(project_kernel, size, npages, top),
        out_shape=[shape((count, wide))] + [shape((npages, columns), jnp.bfloat16)] * size,
        in_specs=[VMEM] * (size + 4),
        out_specs=[VMEM] * (size + 1),
        scratch_shapes=[
            pltpu.VMEM((size, home_dev, wide), jnp.float32),
            pltpu.VMEM((size * SUB, columns), jnp.float32),
        ],
        compiler_params=PARAMS,
        name="project",
    )(
        *messages,
        came,
        attn_gain.reshape(1, width),
        resident(qkv_near),
        plan,
    )
    joined = exchanged(projected)

    before = load_more(rows, 0, 2)[0]
    late, _ = lax.optimization_barrier((out_weight, messages[-1]))
    out_mate = lax.ppermute(late, "tensor", [(me, me ^ 1) for me in range(size)])
    terms = pl.pallas_call(
        functools.partial(attend_kernel, size, top),
        out_shape=[shape((npages, CORES * part + LANES), jnp.bfloat16)] * size,
        in_specs=[VMEM] * (size + 3) + [ANY],
        out_specs=[VMEM] * size,
        scratch_shapes=[
            pltpu.VMEM((size, SUB, columns), jnp.float32),
            pltpu.VMEM((size // CORES, SUB, CORES * part + LANES), jnp.float32),
        ],
        compiler_params=PARAMS,
        name="attend",
    )(*joined, resident(kv_cache), rows, plan, before)
    arrived = exchanged(terms)

    before = load_more(terms[0], 2, 5)[0]
    partial = pl.pallas_call(
        functools.partial(out_kernel, size, npages),
        out_shape=shape((count, width), jnp.bfloat16),
        in_specs=[VMEM] * (size + 3) + [ANY],
        out_specs=VMEM,
        compiler_params=PARAMS,
        name="out",
    )(*arrived, resident(out_weight), resident(out_mate), plan, before)
    sums = across(partial, size)

    load_more(partial, 5, 8)
    *pieces, guests = pl.pallas_call(
        functools.partial(expert_kernel, size, top, router.shape[1], len(gate_up)),
        out_shape=[shape((home_dev, width), jnp.bfloat16)] * size
        + [shape((everyone, 2, width // 2), jnp.bfloat16)],
        in_specs=[VMEM] * (len(sums) + 3) + [ANY] + [VMEM] * len(gate_up),
        out_specs=[VMEM] * (size + 1),
        scratch_shapes=[
            pltpu.VMEM((size, home_dev, width), jnp.float32),
            pltpu.VMEM((size, width), jnp.float32),
            pltpu.VMEM((units, width), jnp.bfloat16),
            pltpu.SemaphoreType.DMA((8,)),
        ],
        compiler_params=PARAMS,
        name="experts",
    )(
        *sums,
        rows,
        moe_gain.reshape(1, width),
        router.T,
        far(expert_down),
        *[resident(piece) for piece in gate_up],
    )
    guests = lax.all_to_all(guests, ("replica", "tensor"), 0, 0, tiled=True)
    pieces = exchanged(pieces)
    return pl.pallas_call(
        functools.partial(finish_kernel, size, top + 1 + MAXP),
        out_shape=shape((rows_dev, width), jnp.bfloat16),
        in_specs=[VMEM] * (size + 2),
        out_specs=VMEM,
        compiler_params=PARAMS,
        name="finish",
    )(*pieces, guests, tail)


def solution(mesh):
    placed = (
        P(("replica", "tensor"), None),
        P(),
        P(None, "tensor"),
        P("tensor", None),
        P(),
        P(),
        P(None, None, "tensor"),
        P("tensor", None),
        P(("replica", "tensor"), None, None, None),
        P("replica", None),
        P("replica"),
        P(("replica", "tensor")),
        P(("replica", "tensor"), None),
        P(("replica", "tensor")),
        P("replica", None),
    )
    return jax.shard_map(
        shards,
        mesh=mesh,
        in_specs=placed,
        out_specs=P(("replica", "tensor"), None),
        check_vma=False,
    )
```

```python
import functools

import jax
import jax.numpy as jnp
from jax import lax
from jax.experimental import pallas as pl
from jax.experimental.pallas import tpu as pltpu
from jax.sharding import PartitionSpec as P

HEADS = 12
KVH = 4
HD = 128
MOE_FF = 512
LANES = 128
SUB = 8
CORES = 2
FAR = 1024
EMPTY = -1e30
STEP = 16
MAXP = 2

VMEM = pl.BlockSpec(memory_space=pltpu.VMEM)
SMEM = pl.BlockSpec(memory_space=pltpu.SMEM)
ANY = pl.BlockSpec(memory_space=pl.ANY)
PARAMS = pltpu.CompilerParams(vmem_limit_bytes=16 * 2**20)


def resident(array):
    return pltpu.with_memory_space_constraint(array, pltpu.VMEM)


def far(array):
    return pltpu.with_memory_space_constraint(array, pltpu.HBM)


def normed(values, gain):
    inverse = lax.rsqrt(jnp.mean(values * values, axis=-1, keepdims=True) + 1e-05)
    return (values * inverse * gain).astype(jnp.bfloat16)


def ways(size):
    return [(chips, core) for chips in range(size // CORES) for core in range(CORES)][1:]


def target(me, size, way):
    chip = lax.rem(me // CORES + way[0], size // CORES)
    return chip * CORES + lax.rem(me + way[1], CORES)


def sender(me, size, way):
    chip = lax.rem(me // CORES + size // CORES - way[0], size // CORES)
    return chip * CORES + lax.rem(me + way[1], CORES)


def senders(me, size):
    return [me] + [sender(me, size, way) for way in ways(size)]


def targets(me, size):
    return [me] + [target(me, size, way) for way in ways(size)]


def exchanged(blocks):
    size = len(blocks)
    arrived = [blocks[0]]
    for way, block in zip(ways(size), blocks[1:]):
        pairs = []
        for me in range(size):
            chip = (me // CORES + way[0]) % (size // CORES)
            pairs.append((me, chip * CORES + (me + way[1]) % CORES))
        arrived.append(lax.ppermute(block, "tensor", pairs))
    return arrived


def to_step(rows):
    extra = -rows.shape[0] % STEP
    if not extra:
        return rows
    filler = jnp.zeros((extra, rows.shape[1]), jnp.float32)
    return jnp.concatenate([rows.astype(jnp.float32), filler], axis=0).astype(rows.dtype)


def lanes_of(numbers, lane):
    row = jnp.zeros(lane.shape, jnp.float32)
    for place, number in enumerate(numbers):
        row = jnp.where(lane == place, number.astype(jnp.float32), row)
    return row


def at_lane(rows, lane, place):
    return jnp.sum(jnp.where(lane == place, rows, 0.0), axis=-1, keepdims=True)


def across(block, size):
    arrived = [block]
    for chips in range(1, size // CORES):
        pairs = [(me, (me + chips * CORES) % size) for me in range(size)]
        arrived.append(lax.ppermute(block, "tensor", pairs))
    return arrived


def page_hits(plan, pages):
    return [jnp.where(plan[place : place + 1] == pages, 1.0, 0.0) for place in range(MAXP)]


def offer_kernel(tokens, paths, pages, table, lens, packed, *refs):
    offers, homes, plan, tail_out, rows, paths_s, pages_s, table_v, lens_v, sems = refs
    pairs = [
        (tokens, rows),
        (paths, paths_s),
        (pages, pages_s),
        (table, table_v),
        (lens, lens_v.at[0]),
    ]
    copies = [pltpu.make_async_copy(*pair, sems.at[i]) for i, pair in enumerate(pairs)]
    for copy in copies:
        copy.start()
    for copy in copies:
        copy.wait()
    me = lax.axis_index("tensor")
    rows_dev, width = rows.shape
    top = paths.shape[0]
    lane = lax.broadcasted_iota(jnp.int32, (1, LANES), 1)
    wide = rows[...].astype(jnp.float32)
    tails = []
    for slot in range(rows_dev):
        numbers = [paths_s[place, me * rows_dev + slot] for place in range(top)]
        if slot == rows_dev - 1:
            numbers += [packed[0] % FAR]
            numbers += [pages_s[0, place] for place in range(MAXP)]
            numbers += [packed[0] // FAR]
        tails.append(lanes_of(numbers, lane))
    tail_out[...] = tails[-1]
    full = jnp.concatenate([wide, jnp.concatenate(tails, axis=0)], axis=1)
    homes[...] = full[:-1].astype(jnp.bfloat16)
    guest = jnp.concatenate(
        [wide[-1:], tails[-1], jnp.zeros((1, LANES), jnp.float32)], axis=1
    )
    half = guest.shape[1] // 2
    block = jnp.concatenate([guest[:, :half], guest[:, half:]], axis=0).astype(jnp.bfloat16)
    for place in range(offers.shape[0]):
        offers[place] = block

    count = table.shape[1]
    npages = plan.shape[0]
    size = count * MAXP // (npages - MAXP)
    filler = jnp.zeros((1, LANES - count), jnp.float32)
    spots = lane - count
    lines = []
    for place in range(MAXP):
        ids = table_v[place : place + 1].astype(jnp.float32)
        ids = jnp.concatenate([ids, filler], axis=1)
        guests = (spots * npages + npages - MAXP + place).astype(jnp.float32)
        guests = jnp.where(spots < size, guests, -1.0)
        lines.append(jnp.where(spots < 0, ids, guests))
    lines.append(jnp.concatenate([lens_v[...].astype(jnp.float32), filler], axis=1))
    lines.append(jnp.zeros((npages - MAXP - 1, LANES), jnp.float32))
    plan[...] = jnp.concatenate(lines, axis=0)


def load_kernel(plans, *refs):
    sources, outs, sems = refs[1 : 1 + len(plans)], refs[1 + len(plans) : -1], refs[-1]
    copies = []

    def copy(source, out):
        copies.append(pltpu.make_async_copy(source, out, sems.at[len(copies)]))

    for (first, count, pieces), source, out in zip(plans, sources, outs):
        each = source.shape[0] // pieces if len(out.shape) == 4 else count // pieces
        for piece in range(pieces):
            lines = pl.ds(piece * each, each)
            if len(out.shape) == 4:
                for place in range(count):
                    columns = pl.ds((first + place) * LANES, LANES)
                    copy(source.at[lines, :, columns], out.at[place, lines])
            else:
                copy(source.at[pl.ds(first + piece * each, each)], out.at[lines])
    for made in copies:
        made.start()
    for made in copies:
        made.wait()


def loaded(after, *wanted):
    shapes, plans, copies = [], [], 0
    for array, first, count in wanted:
        if array.ndim == 3:
            shapes.append(shape((count,) + array.shape[:2] + (LANES,), array.dtype))
            plans.append((first, count, 2))
            copies += 2 * count
        else:
            shapes.append(shape((count, array.shape[1]), array.dtype))
            plans.append((first, count, 4))
            copies += 4
    parts = pl.pallas_call(
        functools.partial(load_kernel, tuple(plans)),
        out_shape=shapes,
        in_specs=[ANY] * (1 + len(wanted)),
        out_specs=[VMEM] * len(wanted),
        scratch_shapes=[pltpu.SemaphoreType.DMA((copies,))],
        compiler_params=PARAMS,
        cost_estimate=pl.CostEstimate(
            flops=0, bytes_accessed=sum(2 * part.size for part in shapes), transcendentals=0
        ),
        name="load",
    )(after, *[far(array) for array, _, _ in wanted])
    return [
        part.reshape(part.shape[0], -1, LANES) if part.ndim == 4 else part for part in parts
    ]


def project_kernel(size, npages, top, *refs):
    blocks, refs = refs[:size], refs[size:]
    offers, gain, weight, plan, rows_ref = refs[:5]
    outs = refs[5 : 5 + size]
    gathered, paged = refs[5 + size :]
    me = lax.axis_index("tensor")
    replica = lax.axis_index("replica").astype(jnp.float32)
    home_dev = blocks[0].shape[0]
    homes = size * home_dev
    width, columns = weight.shape
    for owner, block in zip(senders(me, size), blocks):
        gathered[pl.ds(owner, 1)] = block[...].astype(jnp.float32)[None]
    came = offers[...].astype(jnp.float32)
    half = came.shape[2]
    lane = lax.broadcasted_iota(jnp.int32, (1, 1, half), 2)
    spot = width + top + 1 + MAXP - half
    source = jnp.sum(jnp.where(lane == spot, came[:, 1:], 0.0), axis=2, keepdims=True)
    picked = jnp.where(source == replica, came, 0.0)
    picked = jnp.sum(picked.reshape(-1, size, 2, half), axis=0)
    for owner in range(size):
        rows_ref[owner * home_dev : (owner + 1) * home_dev] = gathered[owner]
        guest = jnp.concatenate([picked[owner, :1], picked[owner, 1:]], axis=1)
        rows_ref[homes + owner : homes + owner + 1] = guest[:, : width + LANES]
    norm = to_step(normed(rows_ref[:, :width], gain[...]))
    products = jnp.dot(norm, weight[...], preferred_element_type=jnp.float32)
    line = lax.broadcasted_iota(jnp.int32, (size * SUB, LANES), 0)
    ids = line // SUB * npages + line % SUB
    ids = jnp.where(line % SUB < npages, ids, -2).astype(jnp.float32)
    hits = sum(page_hits(plan[...], ids))[:, : norm.shape[0]]
    paged[...] = jnp.dot(
        hits.astype(jnp.bfloat16), products.astype(jnp.bfloat16), preferred_element_type=jnp.float32
    )
    for end, out in zip(targets(me, size), outs):
        start = pl.multiple_of(end * SUB, SUB)
        out[...] = paged[pl.ds(start, SUB)][:npages].astype(jnp.bfloat16)


def attend_kernel(size, top, *refs):
    blocks, refs = refs[:size], refs[size:]
    cache, rows_ref, plan_ref, _ = refs[:4]
    outs = refs[4 : 4 + size]
    gathered, terms = refs[4 + size :]
    me = lax.axis_index("tensor")
    npages, _, page_len, _ = cache.shape
    home_pages = npages - MAXP
    homes = home_pages // MAXP * size
    group = HEADS // KVH
    qwidth, kwidth = HEADS * HD, KVH * HD
    width = rows_ref.shape[1] - LANES
    for owner, block in zip(senders(me, size), blocks):
        gathered[pl.ds(owner, 1), :npages] = block[...].astype(jnp.float32)[None]
    joined = jnp.concatenate([gathered[owner] for owner in range(size)], axis=1)

    plan = plan_ref[...]
    line = lax.broadcasted_iota(jnp.int32, (SUB, LANES), 0)
    hits = page_hits(plan, (me * npages + line).astype(jnp.float32))
    left = sum(
        hit * (plan[MAXP : MAXP + 1] - float(place * page_len)) for place, hit in enumerate(hits)
    )
    left = jnp.sum(left, axis=1, keepdims=True)
    leads = jnp.sum(hits[0], axis=1, keepdims=True)
    tails = rows_ref[:, width:]
    place = lax.broadcasted_iota(jnp.int32, tails.shape, 0)
    numbers = jnp.sum(jnp.where(place == homes + me, tails, 0.0), axis=0, keepdims=True)
    lane = lax.broadcasted_iota(jnp.int32, (1, LANES), 1)
    near_len = at_lane(numbers, lane, top)
    line = line[:, :1]
    near_left, near_lead = jnp.zeros((SUB, 1), jnp.float32), None
    for place in range(MAXP):
        named = at_lane(numbers, lane, top + 1 + place) == line.astype(jnp.float32)
        near_left = jnp.where(named, near_len - float(place * page_len), near_left)
        if place == 0:
            near_lead = jnp.where(named, 1.0, 0.0)
    left = jnp.where(line < home_pages, left, near_left)
    leads = jnp.where(line < home_pages, leads, near_lead)
    row = lax.broadcasted_iota(jnp.int32, (SUB, npages * page_len), 0)
    spot = lax.broadcasted_iota(jnp.int32, (SUB, npages * page_len), 1)
    inside = (spot - row * page_len).astype(jnp.float32)
    usable = jnp.where((inside >= 0.0) & (inside < jnp.minimum(left, float(page_len))), 1.0, 0.0)
    usable = jnp.concatenate([usable] * HEADS, axis=0) > 0.5
    leads = jnp.concatenate([leads] * HEADS, axis=0) > 0.5

    query = jnp.concatenate([joined[:, h * HD : (h + 1) * HD] for h in range(HEADS)], axis=0)
    fresh_key, fresh_value = [
        jnp.concatenate(
            [joined[:, start + h // group * HD : start + (h // group + 1) * HD] for h in range(HEADS)],
            axis=0,
        )
        for start in (qwidth, qwidth + kwidth)
    ]
    lines = group * SUB
    narrow = query.astype(jnp.bfloat16)
    scores = []
    for kv in range(KVH):
        keys = cache[:, 0, :, kv * HD : (kv + 1) * HD].reshape(npages * page_len, HD)
        scores.append(
            lax.dot_general(
                narrow[kv * lines : (kv + 1) * lines],
                keys,
                (((1,), (1,)), ((), ())),
                preferred_element_type=jnp.float32,
            )
        )
    scores = jnp.concatenate(scores, axis=0) * HD ** (-0.5)
    scores = jnp.where(usable, scores, EMPTY)
    own = jnp.sum(query * fresh_key, axis=-1, keepdims=True) * HD ** (-0.5)
    own = jnp.where(leads, own, EMPTY)
    peak = jnp.maximum(jnp.max(scores, axis=-1, keepdims=True), own)
    weights = jnp.where(usable, jnp.exp(scores - peak), 0.0)
    newest = jnp.where(leads, jnp.exp(own - peak), 0.0)
    total = jnp.sum(weights, axis=-1, keepdims=True) + newest
    narrow = weights.astype(jnp.bfloat16)
    summed = []
    for kv in range(KVH):
        values = cache[:, 1, :, kv * HD : (kv + 1) * HD].reshape(npages * page_len, HD)
        summed.append(
            jnp.dot(
                narrow[kv * lines : (kv + 1) * lines], values, preferred_element_type=jnp.float32
            )
        )
    summed = jnp.concatenate(summed, axis=0) + newest * fresh_value
    used = total > 0.0
    safe = jnp.where(used, total, 1.0)
    mixed = summed / safe
    level = jnp.where(used, peak + jnp.log(safe), EMPTY)
    lane = lax.broadcasted_iota(jnp.int32, (SUB, LANES), 1)
    levels = jnp.zeros((SUB, LANES), jnp.float32)
    for h in range(HEADS):
        levels = jnp.where(lane % STEP == h, level[h * SUB : (h + 1) * SUB], levels)
    upper = levels.astype(jnp.bfloat16).astype(jnp.float32)
    rest = levels - upper
    middle = rest.astype(jnp.bfloat16).astype(jnp.float32)
    levels = jnp.where(lane < STEP, upper, jnp.where(lane < 2 * STEP, middle, rest - middle))
    levels = jnp.where(lane < 3 * STEP, levels, 0.0)
    mixes = jnp.concatenate([mixed[h * SUB : (h + 1) * SUB] for h in range(HEADS)], axis=1)
    chips = size // CORES
    part = qwidth // chips
    for chip in range(chips):
        terms[chip] = jnp.concatenate([mixes[:, chip * part : (chip + 1) * part], levels], axis=1)
    for end, out in zip(targets(me, size), outs):
        out[...] = terms[pl.ds(end // CORES, 1)][0, :npages].astype(jnp.bfloat16)


def out_kernel(size, npages, *refs):
    blocks, refs = refs[:size], refs[size:]
    weight, mate_weight, plan, _, out = refs
    me = lax.axis_index("tensor")
    part = CORES * weight.shape[0]
    terms, ids = [], []
    line = lax.broadcasted_iota(jnp.int32, (SUB, LANES), 0)
    filler = jnp.zeros((SUB - npages, part + LANES), jnp.float32)
    for owner, block in zip(senders(me, size), blocks):
        terms += [block[...].astype(jnp.float32), filler]
        ids.append(jnp.where(line < npages, owner * npages + line, -2))
    terms = jnp.concatenate(terms, axis=0).astype(jnp.bfloat16)
    ids = jnp.concatenate(ids, axis=0).astype(jnp.float32)
    spread = lax.broadcasted_iota(jnp.int32, (LANES, part), 0)
    head = (lax.broadcasted_iota(jnp.int32, (LANES, part), 1) + me // CORES * part) // HD
    spread = jnp.where((spread % STEP == head) & (spread < 3 * STEP), 1.0, 0.0)
    spread = spread.astype(jnp.bfloat16)
    count = out.shape[0]
    rows = count + -count % STEP
    mixes, levels = [], []
    for hit in page_hits(plan[...], ids):
        picked = lax.dot_general(
            hit[:, :rows].astype(jnp.bfloat16),
            terms,
            (((0,), (0,)), ((), ())),
            preferred_element_type=jnp.float32,
        )
        mixes.append(picked[:, :part])
        levels.append(
            jnp.dot(
                picked[:, part:].astype(jnp.bfloat16), spread, preferred_element_type=jnp.float32
            )
        )
    highest = functools.reduce(jnp.maximum, levels)
    factors = [jnp.exp(level - highest) for level in levels]
    mixed = sum(mix * factor for mix, factor in zip(mixes, factors)) / sum(factors)
    halves = mixed[:, : part // CORES], mixed[:, part // CORES :]
    first = lax.rem(me, CORES) == 0
    own = jnp.where(first, halves[0], halves[1]).astype(jnp.bfloat16)
    other = jnp.where(first, halves[1], halves[0]).astype(jnp.bfloat16)
    products = jnp.dot(own, weight[...], preferred_element_type=jnp.float32)
    products += jnp.dot(other, mate_weight[...], preferred_element_type=jnp.float32)
    out[...] = products[:count].astype(jnp.bfloat16)


def expert_kernel(size, top, experts, parts, lows, *refs):
    chips = size // CORES
    sums, refs = refs[:chips], refs[chips:]
    rows_ref, gain, router = refs[:3]
    gate_up, refs = refs[3 : 3 + parts], refs[3 + parts :]
    down, refs = refs[:lows], refs[lows:]
    units = sum(piece.shape[0] for piece in down)
    homes, guests, finished, ends_ref = refs[:size], refs[size], refs[size + 1], refs[size + 2]
    me = lax.axis_index("tensor")
    count = rows_ref.shape[0]
    width = rows_ref.shape[1] - LANES
    rows_dev = count // size
    total = functools.reduce(jnp.add, [piece[...].astype(jnp.float32) for piece in sums])
    hidden = (rows_ref[:, :width] + total).astype(jnp.bfloat16).astype(jnp.float32)
    norm = normed(hidden, gain[...])
    lane = lax.broadcasted_iota(jnp.int32, (count, LANES), 1)
    numbers = rows_ref[:, width:]
    logits = lax.dot_general(
        norm, router[...], (((1,), (1,)), ((), ())), preferred_element_type=jnp.float32
    )
    logits = jnp.concatenate(
        [logits, jnp.zeros((count, LANES - experts), jnp.float32)], axis=1
    )
    routed = jnp.zeros((count, LANES), jnp.float32)
    for place in range(top):
        route = at_lane(numbers, lane, place)
        routed = jnp.where(lane.astype(jnp.float32) == route, 1.0, routed)
    logits = jnp.where(routed > 0.5, logits, EMPTY)
    shares = jnp.where(
        routed > 0.5, jnp.exp(logits - jnp.max(logits, axis=-1, keepdims=True)), 0.0
    )
    shares = shares / jnp.sum(shares, axis=-1, keepdims=True)

    here = lax.broadcasted_iota(jnp.int32, (LANES, 2 * LANES), 0)
    there = lax.broadcasted_iota(jnp.int32, (LANES, 2 * LANES), 1)
    evens = jnp.where(there == 2 * here, 1.0, 0.0).astype(jnp.bfloat16)
    odds = jnp.where(there == 2 * here + 1, 1.0, 0.0).astype(jnp.bfloat16)
    wide = to_step(norm)
    padded = wide.shape[0]
    blocks = width // LANES
    tall = jnp.concatenate([wide[:, b * LANES : (b + 1) * LANES] for b in range(blocks)], axis=0)
    to_gate = jnp.dot(tall, evens, preferred_element_type=jnp.float32).astype(jnp.bfloat16)
    to_up = jnp.dot(tall, odds, preferred_element_type=jnp.float32).astype(jnp.bfloat16)
    left = []
    for b in range(blocks):
        lines = slice(b * padded, (b + 1) * padded)
        left.append(jnp.concatenate([to_gate[lines], to_up[lines]], axis=0))
    left = jnp.concatenate(left, axis=1)
    both = []
    for piece in gate_up:
        right = jnp.concatenate([piece[place] for place in range(piece.shape[0])], axis=1)
        both.append(jnp.dot(left, right, preferred_element_type=jnp.float32))
    both = jnp.concatenate(both, axis=1)
    gate, up = both[:count], both[padded : padded + count]
    activated = gate / (1.0 + jnp.exp(-gate)) * up
    step = min(units, MOE_FF)
    scaled = []
    for start in range(0, units, step):
        expert = (me * units + start) // MOE_FF
        share = at_lane(shares, lane, expert)
        scaled.append(activated[:, start : start + step] * share)
    scaled = jnp.concatenate(scaled, axis=1).astype(jnp.bfloat16)
    partial, start = 0.0, 0
    for piece in down:
        left = scaled[:, start : start + piece.shape[0]]
        partial += jnp.dot(left, piece[...], preferred_element_type=jnp.float32)
        start += piece.shape[0]
    home_dev = rows_dev - 1
    first = size * home_dev
    for owner in range(size):
        lines = slice(owner * home_dev, (owner + 1) * home_dev)
        mine = jnp.where(me == owner, 1.0, 0.0)
        finished[owner] = partial[lines] + hidden[lines] * mine
        line = slice(first + owner, first + owner + 1)
        ends_ref[owner : owner + 1] = partial[line] + hidden[line] * mine
    for end, out in zip(targets(me, size), homes):
        out[...] = finished[pl.ds(end, 1)][0].astype(jnp.bfloat16)
    half = width // 2
    for owner in range(size):
        guest = ends_ref[owner : owner + 1]
        block = jnp.concatenate([guest[:, :half], guest[:, half:]], axis=0).astype(jnp.bfloat16)
        for place in range(owner, guests.shape[0], size):
            guests[place] = block


def finish_kernel(size, spot, *refs):
    pieces, refs = refs[:size], refs[size:]
    guests, tail, out = refs
    homes = functools.reduce(jnp.add, [piece[...].astype(jnp.float32) for piece in pieces])
    came = guests[...].astype(jnp.float32)
    lane = lax.broadcasted_iota(jnp.int32, (1, LANES), 1)
    source = at_lane(tail[...], lane, spot).reshape(1, 1, 1)
    place = lax.broadcasted_iota(jnp.int32, (came.shape[0], 1, 1), 0) // size
    guest = jnp.sum(jnp.where(place.astype(jnp.float32) == source, came, 0.0), axis=0)
    guest = jnp.concatenate([guest[:1], guest[1:]], axis=1)
    out[...] = jnp.concatenate([homes, guest], axis=0).astype(jnp.bfloat16)


def shape(dims, dtype=jnp.float32):
    return jax.ShapeDtypeStruct(dims, dtype)


def shards(
    tokens,
    attn_gain,
    qkv_weight,
    out_weight,
    moe_gain,
    router,
    expert_gate_up,
    expert_down,
    kv_cache,
    page_table,
    home_len,
    guest_source,
    guest_pages,
    guest_len,
    routes,
):
    size = lax.axis_size("tensor")
    replicas = lax.axis_size("replica")
    rows_dev, width = tokens.shape
    npages = kv_cache.shape[0]
    top = routes.shape[1]
    units = expert_down.shape[0]
    part = out_weight.shape[0]
    columns = qkv_weight.shape[1]
    count = size * rows_dev
    home_dev = rows_dev - 1
    wide = width + LANES
    everyone = size * replicas
    blocks = units // LANES
    gate_up, down = [], []

    def load_more(after, ups, downs):
        first, last = ups[0] * blocks // 8, ups[1] * blocks // 8
        wanted = []
        if last > first:
            wanted.append((expert_gate_up, first, last - first))
        if downs[1] > downs[0]:
            wanted.append((expert_down, downs[0] * units // 8, (downs[1] - downs[0]) * units // 8))
        if not wanted:
            return after
        got = loaded(after, *wanted)
        for part in got:
            (gate_up if part.ndim == 3 else down).append(part)
        return got[0]

    packed = guest_source * FAR + guest_len
    offers, homes, plan, tail = pl.pallas_call(
        offer_kernel,
        out_shape=[
            shape((everyone, 2, (wide + LANES) // 2), jnp.bfloat16),
            shape((home_dev, wide), jnp.bfloat16),
            shape((npages, LANES)),
            shape((1, LANES)),
        ],
        in_specs=[ANY] * 5 + [SMEM],
        out_specs=[VMEM] * 4,
        scratch_shapes=[
            pltpu.VMEM(tokens.shape, tokens.dtype),
            pltpu.SMEM(routes.T.shape, jnp.int32),
            pltpu.SMEM(guest_pages.shape, jnp.int32),
            pltpu.VMEM(page_table.T.shape, jnp.int32),
            pltpu.VMEM((1,) + home_len.shape, jnp.int32),
            pltpu.SemaphoreType.DMA((5,)),
        ],
        compiler_params=PARAMS,
        name="offer",
    )(far(tokens), far(routes.T), far(guest_pages), far(page_table.T), far(home_len), packed)
    came = lax.all_to_all(offers, ("replica", "tensor"), 0, 0, tiled=True)
    messages = exchanged([homes] * size)
    (qkv_near,) = loaded(homes, (qkv_weight, 0, width))

    rows, *projected = pl.pallas_call(
        functools.partial(project_kernel, size, npages, top),
        out_shape=[shape((count, wide))] + [shape((npages, columns), jnp.bfloat16)] * size,
        in_specs=[VMEM] * (size + 4),
        out_specs=[VMEM] * (size + 1),
        scratch_shapes=[
            pltpu.VMEM((size, home_dev, wide), jnp.float32),
            pltpu.VMEM((size * SUB, columns), jnp.float32),
        ],
        compiler_params=PARAMS,
        name="project",
    )(
        *messages,
        came,
        attn_gain.reshape(1, width),
        resident(qkv_near),
        plan,
    )
    joined = exchanged(projected)

    before = load_more(rows, (0, 2), (0, 2))
    late, _ = lax.optimization_barrier((out_weight, rows))
    out_mate = lax.ppermute(late, "tensor", [(me, me ^ 1) for me in range(size)])
    terms = pl.pallas_call(
        functools.partial(attend_kernel, size, top),
        out_shape=[shape((npages, CORES * part + LANES), jnp.bfloat16)] * size,
        in_specs=[VMEM] * (size + 3) + [ANY],
        out_specs=[VMEM] * size,
        scratch_shapes=[
            pltpu.VMEM((size, SUB, columns), jnp.float32),
            pltpu.VMEM((size // CORES, SUB, CORES * part + LANES), jnp.float32),
        ],
        compiler_params=PARAMS,
        name="attend",
    )(*joined, resident(kv_cache), rows, plan, before)
    arrived = exchanged(terms)

    before = load_more(terms[0], (2, 5), (2, 4))
    partial = pl.pallas_call(
        functools.partial(out_kernel, size, npages),
        out_shape=shape((count, width), jnp.bfloat16),
        in_specs=[VMEM] * (size + 3) + [ANY],
        out_specs=VMEM,
        compiler_params=PARAMS,
        name="out",
    )(*arrived, resident(out_weight), resident(out_mate), plan, before)
    sums = across(partial, size)

    load_more(partial, (5, 8), (4, 8))
    *pieces, guests = pl.pallas_call(
        functools.partial(
            expert_kernel, size, top, router.shape[1], len(gate_up), len(down)
        ),
        out_shape=[shape((home_dev, width), jnp.bfloat16)] * size
        + [shape((everyone, 2, width // 2), jnp.bfloat16)],
        in_specs=[VMEM] * (len(sums) + 3 + len(gate_up) + len(down)),
        out_specs=[VMEM] * (size + 1),
        scratch_shapes=[
            pltpu.VMEM((size, home_dev, width), jnp.float32),
            pltpu.VMEM((size, width), jnp.float32),
        ],
        compiler_params=PARAMS,
        name="experts",
    )(
        *sums,
        rows,
        moe_gain.reshape(1, width),
        router.T,
        *[resident(piece) for piece in gate_up + down],
    )
    guests = lax.all_to_all(guests, ("replica", "tensor"), 0, 0, tiled=True)
    pieces = exchanged(pieces)
    return pl.pallas_call(
        functools.partial(finish_kernel, size, top + 1 + MAXP),
        out_shape=shape((rows_dev, width), jnp.bfloat16),
        in_specs=[VMEM] * (size + 2),
        out_specs=VMEM,
        compiler_params=PARAMS,
        name="finish",
    )(*pieces, guests, tail)


def solution(mesh):
    placed = (
        P(("replica", "tensor"), None),
        P(),
        P(None, "tensor"),
        P("tensor", None),
        P(),
        P(),
        P(None, None, "tensor"),
        P("tensor", None),
        P(("replica", "tensor"), None, None, None),
        P("replica", None),
        P("replica"),
        P(("replica", "tensor")),
        P(("replica", "tensor"), None),
        P(("replica", "tensor")),
        P("replica", None),
    )
    return jax.shard_map(
        shards,
        mesh=mesh,
        in_specs=placed,
        out_specs=P(("replica", "tensor"), None),
        check_vma=False,
    )
```

```python
import functools

import jax
import jax.numpy as jnp
from jax import lax
from jax.experimental import pallas as pl
from jax.experimental.pallas import tpu as pltpu
from jax.sharding import PartitionSpec as P

HEADS = 12
KVH = 4
HD = 128
MOE_FF = 512
LANES = 128
SUB = 8
CORES = 2
FAR = 1024
EMPTY = -1e30
STEP = 16
MAXP = 2

VMEM = pl.BlockSpec(memory_space=pltpu.VMEM)
SMEM = pl.BlockSpec(memory_space=pltpu.SMEM)
ANY = pl.BlockSpec(memory_space=pl.ANY)
PARAMS = pltpu.CompilerParams(vmem_limit_bytes=16 * 2**20)


def resident(array):
    return pltpu.with_memory_space_constraint(array, pltpu.VMEM)


def far(array):
    return pltpu.with_memory_space_constraint(array, pltpu.HBM)


def normed(values, gain):
    inverse = lax.rsqrt(jnp.mean(values * values, axis=-1, keepdims=True) + 1e-05)
    return (values * inverse * gain).astype(jnp.bfloat16)


def ways(size):
    return [(chips, core) for chips in range(size // CORES) for core in range(CORES)][1:]


def target(me, size, way):
    chip = lax.rem(me // CORES + way[0], size // CORES)
    return chip * CORES + lax.rem(me + way[1], CORES)


def sender(me, size, way):
    chip = lax.rem(me // CORES + size // CORES - way[0], size // CORES)
    return chip * CORES + lax.rem(me + way[1], CORES)


def senders(me, size):
    return [me] + [sender(me, size, way) for way in ways(size)]


def targets(me, size):
    return [me] + [target(me, size, way) for way in ways(size)]


def exchanged(blocks):
    size = len(blocks)
    arrived = [blocks[0]]
    for way, block in zip(ways(size), blocks[1:]):
        pairs = []
        for me in range(size):
            chip = (me // CORES + way[0]) % (size // CORES)
            pairs.append((me, chip * CORES + (me + way[1]) % CORES))
        arrived.append(lax.ppermute(block, "tensor", pairs))
    return arrived


def to_step(rows):
    extra = -rows.shape[0] % STEP
    if not extra:
        return rows
    filler = jnp.zeros((extra, rows.shape[1]), jnp.float32)
    return jnp.concatenate([rows.astype(jnp.float32), filler], axis=0).astype(rows.dtype)


def lanes_of(numbers, lane):
    row = jnp.zeros(lane.shape, jnp.float32)
    for place, number in enumerate(numbers):
        row = jnp.where(lane == place, number.astype(jnp.float32), row)
    return row


def at_lane(rows, lane, place):
    return jnp.sum(jnp.where(lane == place, rows, 0.0), axis=-1, keepdims=True)


def across(block, size):
    arrived = [block]
    for chips in range(1, size // CORES):
        pairs = [(me, (me + chips * CORES) % size) for me in range(size)]
        arrived.append(lax.ppermute(block, "tensor", pairs))
    return arrived


def page_hits(plan, pages):
    return [jnp.where(plan[place : place + 1] == pages, 1.0, 0.0) for place in range(MAXP)]


def offer_kernel(tokens, paths, pages, table, lens, packed, *refs):
    offers, homes, plan, tail_out, rows, paths_s, pages_s, table_v, lens_v, sems = refs
    pairs = [
        (tokens, rows),
        (paths, paths_s),
        (pages, pages_s),
        (table, table_v),
        (lens, lens_v.at[0]),
    ]
    copies = [pltpu.make_async_copy(*pair, sems.at[i]) for i, pair in enumerate(pairs)]
    for copy in copies:
        copy.start()
    for copy in copies:
        copy.wait()
    me = lax.axis_index("tensor")
    rows_dev, width = rows.shape
    top = paths.shape[0]
    lane = lax.broadcasted_iota(jnp.int32, (1, LANES), 1)
    wide = rows[...].astype(jnp.float32)
    tails = []
    for slot in range(rows_dev):
        numbers = [paths_s[place, me * rows_dev + slot] for place in range(top)]
        if slot == rows_dev - 1:
            numbers += [packed[0] % FAR]
            numbers += [pages_s[0, place] for place in range(MAXP)]
            numbers += [packed[0] // FAR]
        tails.append(lanes_of(numbers, lane))
    tail_out[...] = tails[-1]
    full = jnp.concatenate([wide, jnp.concatenate(tails, axis=0)], axis=1)
    homes[...] = full[:-1].astype(jnp.bfloat16)
    guest = jnp.concatenate(
        [wide[-1:], tails[-1], jnp.zeros((1, LANES), jnp.float32)], axis=1
    )
    half = guest.shape[1] // 2
    block = jnp.concatenate([guest[:, :half], guest[:, half:]], axis=0).astype(jnp.bfloat16)
    for place in range(offers.shape[0]):
        offers[place] = block

    count = table.shape[1]
    npages = plan.shape[0]
    size = count * MAXP // (npages - MAXP)
    filler = jnp.zeros((1, LANES - count), jnp.float32)
    spots = lane - count
    lines = []
    for place in range(MAXP):
        ids = table_v[place : place + 1].astype(jnp.float32)
        ids = jnp.concatenate([ids, filler], axis=1)
        guests = (spots * npages + npages - MAXP + place).astype(jnp.float32)
        guests = jnp.where(spots < size, guests, -1.0)
        lines.append(jnp.where(spots < 0, ids, guests))
    lines.append(jnp.concatenate([lens_v[...].astype(jnp.float32), filler], axis=1))
    lines.append(jnp.zeros((npages - MAXP - 1, LANES), jnp.float32))
    plan[...] = jnp.concatenate(lines, axis=0)


def load_kernel(plans, *refs):
    sources, outs, sems = refs[1 : 1 + len(plans)], refs[1 + len(plans) : -1], refs[-1]
    copies = []

    def copy(source, out):
        copies.append(pltpu.make_async_copy(source, out, sems.at[len(copies)]))

    for (first, count, pieces), source, out in zip(plans, sources, outs):
        each = source.shape[0] // pieces if len(out.shape) == 4 else count // pieces
        for piece in range(pieces):
            lines = pl.ds(piece * each, each)
            if len(out.shape) == 4:
                for place in range(count):
                    columns = pl.ds((first + place) * LANES, LANES)
                    copy(source.at[lines, :, columns], out.at[place, lines])
            else:
                copy(source.at[pl.ds(first + piece * each, each)], out.at[lines])
    for made in copies:
        made.start()
    for made in copies:
        made.wait()


def loaded(after, *wanted):
    shapes, plans, copies = [], [], 0
    for array, first, count in wanted:
        if array.ndim == 3:
            shapes.append(shape((count,) + array.shape[:2] + (LANES,), array.dtype))
            plans.append((first, count, 2))
            copies += 2 * count
        else:
            shapes.append(shape((count, array.shape[1]), array.dtype))
            plans.append((first, count, 4))
            copies += 4
    parts = pl.pallas_call(
        functools.partial(load_kernel, tuple(plans)),
        out_shape=shapes,
        in_specs=[ANY] * (1 + len(wanted)),
        out_specs=[VMEM] * len(wanted),
        scratch_shapes=[pltpu.SemaphoreType.DMA((copies,))],
        compiler_params=PARAMS,
        cost_estimate=pl.CostEstimate(
            flops=0, bytes_accessed=sum(2 * part.size for part in shapes), transcendentals=0
        ),
        name="load",
    )(after, *[far(array) for array, _, _ in wanted])
    return [
        part.reshape(part.shape[0], -1, LANES) if part.ndim == 4 else part for part in parts
    ]


def project_kernel(size, npages, top, *refs):
    blocks, refs = refs[:size], refs[size:]
    offers, gain, weight, plan, rows_ref = refs[:5]
    outs = refs[5 : 5 + size]
    gathered, paged = refs[5 + size :]
    me = lax.axis_index("tensor")
    replica = lax.axis_index("replica").astype(jnp.float32)
    home_dev = blocks[0].shape[0]
    homes = size * home_dev
    width, columns = weight.shape
    for owner, block in zip(senders(me, size), blocks):
        gathered[pl.ds(owner, 1)] = block[...].astype(jnp.float32)[None]
    came = offers[...].astype(jnp.float32)
    half = came.shape[2]
    lane = lax.broadcasted_iota(jnp.int32, (1, 1, half), 2)
    spot = width + top + 1 + MAXP - half
    source = jnp.sum(jnp.where(lane == spot, came[:, 1:], 0.0), axis=2, keepdims=True)
    picked = jnp.where(source == replica, came, 0.0)
    picked = jnp.sum(picked.reshape(-1, size, 2, half), axis=0)
    for owner in range(size):
        rows_ref[owner * home_dev : (owner + 1) * home_dev] = gathered[owner]
        guest = jnp.concatenate([picked[owner, :1], picked[owner, 1:]], axis=1)
        rows_ref[homes + owner : homes + owner + 1] = guest[:, : width + LANES]
    norm = to_step(normed(rows_ref[:, :width], gain[...]))
    products = jnp.dot(norm, weight[...], preferred_element_type=jnp.float32)
    line = lax.broadcasted_iota(jnp.int32, (size * SUB, LANES), 0)
    ids = line // SUB * npages + line % SUB
    ids = jnp.where(line % SUB < npages, ids, -2).astype(jnp.float32)
    hits = sum(page_hits(plan[...], ids))[:, : norm.shape[0]]
    paged[...] = jnp.dot(
        hits.astype(jnp.bfloat16), products.astype(jnp.bfloat16), preferred_element_type=jnp.float32
    )
    for end, out in zip(targets(me, size), outs):
        start = pl.multiple_of(end * SUB, SUB)
        out[...] = paged[pl.ds(start, SUB)][:npages].astype(jnp.bfloat16)


def attend_kernel(size, top, *refs):
    blocks, refs = refs[:size], refs[size:]
    cache, rows_ref, plan_ref, _ = refs[:4]
    outs = refs[4 : 4 + size]
    gathered, terms = refs[4 + size :]
    me = lax.axis_index("tensor")
    npages, _, page_len, _ = cache.shape
    home_pages = npages - MAXP
    homes = home_pages // MAXP * size
    group = HEADS // KVH
    qwidth, kwidth = HEADS * HD, KVH * HD
    width = rows_ref.shape[1] - LANES
    for owner, block in zip(senders(me, size), blocks):
        gathered[pl.ds(owner, 1), :npages] = block[...].astype(jnp.float32)[None]
    joined = jnp.concatenate([gathered[owner] for owner in range(size)], axis=1)

    plan = plan_ref[...]
    line = lax.broadcasted_iota(jnp.int32, (SUB, LANES), 0)
    hits = page_hits(plan, (me * npages + line).astype(jnp.float32))
    left = sum(
        hit * (plan[MAXP : MAXP + 1] - float(place * page_len)) for place, hit in enumerate(hits)
    )
    left = jnp.sum(left, axis=1, keepdims=True)
    leads = jnp.sum(hits[0], axis=1, keepdims=True)
    tails = rows_ref[:, width:]
    place = lax.broadcasted_iota(jnp.int32, tails.shape, 0)
    numbers = jnp.sum(jnp.where(place == homes + me, tails, 0.0), axis=0, keepdims=True)
    lane = lax.broadcasted_iota(jnp.int32, (1, LANES), 1)
    near_len = at_lane(numbers, lane, top)
    line = line[:, :1]
    near_left, near_lead = jnp.zeros((SUB, 1), jnp.float32), None
    for place in range(MAXP):
        named = at_lane(numbers, lane, top + 1 + place) == line.astype(jnp.float32)
        near_left = jnp.where(named, near_len - float(place * page_len), near_left)
        if place == 0:
            near_lead = jnp.where(named, 1.0, 0.0)
    left = jnp.where(line < home_pages, left, near_left)
    leads = jnp.where(line < home_pages, leads, near_lead)
    row = lax.broadcasted_iota(jnp.int32, (SUB, npages * page_len), 0)
    spot = lax.broadcasted_iota(jnp.int32, (SUB, npages * page_len), 1)
    inside = (spot - row * page_len).astype(jnp.float32)
    usable = jnp.where((inside >= 0.0) & (inside < jnp.minimum(left, float(page_len))), 1.0, 0.0)
    usable = jnp.concatenate([usable] * HEADS, axis=0) > 0.5
    leads = jnp.concatenate([leads] * HEADS, axis=0) > 0.5

    query = jnp.concatenate([joined[:, h * HD : (h + 1) * HD] for h in range(HEADS)], axis=0)
    fresh_key, fresh_value = [
        jnp.concatenate(
            [joined[:, start + h // group * HD : start + (h // group + 1) * HD] for h in range(HEADS)],
            axis=0,
        )
        for start in (qwidth, qwidth + kwidth)
    ]
    lines = group * SUB
    narrow = query.astype(jnp.bfloat16)
    scores = []
    for kv in range(KVH):
        keys = cache[:, 0, :, kv * HD : (kv + 1) * HD].reshape(npages * page_len, HD)
        scores.append(
            lax.dot_general(
                narrow[kv * lines : (kv + 1) * lines],
                keys,
                (((1,), (1,)), ((), ())),
                preferred_element_type=jnp.float32,
            )
        )
    scores = jnp.concatenate(scores, axis=0) * HD ** (-0.5)
    scores = jnp.where(usable, scores, EMPTY)
    own = jnp.sum(query * fresh_key, axis=-1, keepdims=True) * HD ** (-0.5)
    own = jnp.where(leads, own, EMPTY)
    peak = jnp.maximum(jnp.max(scores, axis=-1, keepdims=True), own)
    weights = jnp.where(usable, jnp.exp(scores - peak), 0.0)
    newest = jnp.where(leads, jnp.exp(own - peak), 0.0)
    total = jnp.sum(weights, axis=-1, keepdims=True) + newest
    narrow = weights.astype(jnp.bfloat16)
    summed = []
    for kv in range(KVH):
        values = cache[:, 1, :, kv * HD : (kv + 1) * HD].reshape(npages * page_len, HD)
        summed.append(
            jnp.dot(
                narrow[kv * lines : (kv + 1) * lines], values, preferred_element_type=jnp.float32
            )
        )
    summed = jnp.concatenate(summed, axis=0) + newest * fresh_value
    used = total > 0.0
    safe = jnp.where(used, total, 1.0)
    mixed = summed / safe
    level = jnp.where(used, peak + jnp.log(safe), EMPTY)
    lane = lax.broadcasted_iota(jnp.int32, (SUB, LANES), 1)
    levels = jnp.zeros((SUB, LANES), jnp.float32)
    for h in range(HEADS):
        levels = jnp.where(lane % STEP == h, level[h * SUB : (h + 1) * SUB], levels)
    upper = levels.astype(jnp.bfloat16).astype(jnp.float32)
    rest = levels - upper
    middle = rest.astype(jnp.bfloat16).astype(jnp.float32)
    levels = jnp.where(lane < STEP, upper, jnp.where(lane < 2 * STEP, middle, rest - middle))
    levels = jnp.where(lane < 3 * STEP, levels, 0.0)
    mixes = jnp.concatenate([mixed[h * SUB : (h + 1) * SUB] for h in range(HEADS)], axis=1)
    chips = size // CORES
    part = qwidth // chips
    for chip in range(chips):
        terms[chip] = jnp.concatenate([mixes[:, chip * part : (chip + 1) * part], levels], axis=1)
    for end, out in zip(targets(me, size), outs):
        out[...] = terms[pl.ds(end // CORES, 1)][0, :npages].astype(jnp.bfloat16)


def out_kernel(size, npages, *refs):
    blocks, refs = refs[:size], refs[size:]
    weight, mate_weight, plan, _, out = refs
    me = lax.axis_index("tensor")
    part = CORES * weight.shape[0]
    terms, ids = [], []
    line = lax.broadcasted_iota(jnp.int32, (SUB, LANES), 0)
    filler = jnp.zeros((SUB - npages, part + LANES), jnp.float32)
    for owner, block in zip(senders(me, size), blocks):
        terms += [block[...].astype(jnp.float32), filler]
        ids.append(jnp.where(line < npages, owner * npages + line, -2))
    terms = jnp.concatenate(terms, axis=0).astype(jnp.bfloat16)
    ids = jnp.concatenate(ids, axis=0).astype(jnp.float32)
    spread = lax.broadcasted_iota(jnp.int32, (LANES, part), 0)
    head = (lax.broadcasted_iota(jnp.int32, (LANES, part), 1) + me // CORES * part) // HD
    spread = jnp.where((spread % STEP == head) & (spread < 3 * STEP), 1.0, 0.0)
    spread = spread.astype(jnp.bfloat16)
    count = out.shape[0]
    rows = count + -count % STEP
    mixes, levels = [], []
    for hit in page_hits(plan[...], ids):
        picked = lax.dot_general(
            hit[:, :rows].astype(jnp.bfloat16),
            terms,
            (((0,), (0,)), ((), ())),
            preferred_element_type=jnp.float32,
        )
        mixes.append(picked[:, :part])
        levels.append(
            jnp.dot(
                picked[:, part:].astype(jnp.bfloat16), spread, preferred_element_type=jnp.float32
            )
        )
    highest = functools.reduce(jnp.maximum, levels)
    factors = [jnp.exp(level - highest) for level in levels]
    mixed = sum(mix * factor for mix, factor in zip(mixes, factors)) / sum(factors)
    halves = mixed[:, : part // CORES], mixed[:, part // CORES :]
    first = lax.rem(me, CORES) == 0
    own = jnp.where(first, halves[0], halves[1]).astype(jnp.bfloat16)
    other = jnp.where(first, halves[1], halves[0]).astype(jnp.bfloat16)
    products = jnp.dot(own, weight[...], preferred_element_type=jnp.float32)
    products += jnp.dot(other, mate_weight[...], preferred_element_type=jnp.float32)
    out[...] = products[:count].astype(jnp.bfloat16)


def expert_kernel(size, top, experts, parts, lows, *refs):
    chips = size // CORES
    sums, refs = refs[:chips], refs[chips:]
    rows_ref, gain, router = refs[:3]
    gate_up, refs = refs[3 : 3 + parts], refs[3 + parts :]
    down, refs = refs[:lows], refs[lows:]
    units = sum(piece.shape[0] for piece in down)
    homes, guests, finished, ends_ref = refs[:size], refs[size], refs[size + 1], refs[size + 2]
    me = lax.axis_index("tensor")
    count = rows_ref.shape[0]
    width = rows_ref.shape[1] - LANES
    rows_dev = count // size
    total = functools.reduce(jnp.add, [piece[...].astype(jnp.float32) for piece in sums])
    hidden = (rows_ref[:, :width] + total).astype(jnp.bfloat16).astype(jnp.float32)
    norm = normed(hidden, gain[...])
    lane = lax.broadcasted_iota(jnp.int32, (count, LANES), 1)
    numbers = rows_ref[:, width:]
    logits = lax.dot_general(
        norm, router[...], (((1,), (1,)), ((), ())), preferred_element_type=jnp.float32
    )
    logits = jnp.concatenate(
        [logits, jnp.zeros((count, LANES - experts), jnp.float32)], axis=1
    )
    routed = jnp.zeros((count, LANES), jnp.float32)
    for place in range(top):
        route = at_lane(numbers, lane, place)
        routed = jnp.where(lane.astype(jnp.float32) == route, 1.0, routed)
    logits = jnp.where(routed > 0.5, logits, EMPTY)
    shares = jnp.where(
        routed > 0.5, jnp.exp(logits - jnp.max(logits, axis=-1, keepdims=True)), 0.0
    )
    shares = shares / jnp.sum(shares, axis=-1, keepdims=True)

    here = lax.broadcasted_iota(jnp.int32, (LANES, 2 * LANES), 0)
    there = lax.broadcasted_iota(jnp.int32, (LANES, 2 * LANES), 1)
    evens = jnp.where(there == 2 * here, 1.0, 0.0).astype(jnp.bfloat16)
    odds = jnp.where(there == 2 * here + 1, 1.0, 0.0).astype(jnp.bfloat16)
    wide = to_step(norm)
    padded = wide.shape[0]
    blocks = width // LANES
    tall = jnp.concatenate([wide[:, b * LANES : (b + 1) * LANES] for b in range(blocks)], axis=0)
    to_gate = jnp.dot(tall, evens, preferred_element_type=jnp.float32).astype(jnp.bfloat16)
    to_up = jnp.dot(tall, odds, preferred_element_type=jnp.float32).astype(jnp.bfloat16)
    left = []
    for b in range(blocks):
        lines = slice(b * padded, (b + 1) * padded)
        left.append(jnp.concatenate([to_gate[lines], to_up[lines]], axis=0))
    left = jnp.concatenate(left, axis=1)
    both = []
    for piece in gate_up:
        right = jnp.concatenate([piece[place] for place in range(piece.shape[0])], axis=1)
        both.append(jnp.dot(left, right, preferred_element_type=jnp.float32))
    both = jnp.concatenate(both, axis=1)
    gate, up = both[:count], both[padded : padded + count]
    activated = gate / (1.0 + jnp.exp(-gate)) * up
    step = min(units, MOE_FF)
    scaled = []
    for start in range(0, units, step):
        expert = (me * units + start) // MOE_FF
        share = at_lane(shares, lane, expert)
        scaled.append(activated[:, start : start + step] * share)
    scaled = jnp.concatenate(scaled, axis=1).astype(jnp.bfloat16)
    partial, start = 0.0, 0
    for piece in down:
        left = scaled[:, start : start + piece.shape[0]]
        partial += jnp.dot(left, piece[...], preferred_element_type=jnp.float32)
        start += piece.shape[0]
    home_dev = rows_dev - 1
    first = size * home_dev
    for owner in range(size):
        lines = slice(owner * home_dev, (owner + 1) * home_dev)
        mine = jnp.where(me == owner, 1.0, 0.0)
        finished[owner] = partial[lines] + hidden[lines] * mine
        line = slice(first + owner, first + owner + 1)
        ends_ref[owner : owner + 1] = partial[line] + hidden[line] * mine
    for end, out in zip(targets(me, size), homes):
        out[...] = finished[pl.ds(end, 1)][0].astype(jnp.bfloat16)
    half = width // 2
    for owner in range(size):
        guest = ends_ref[owner : owner + 1]
        block = jnp.concatenate([guest[:, :half], guest[:, half:]], axis=0).astype(jnp.bfloat16)
        for place in range(owner, guests.shape[0], size):
            guests[place] = block


def finish_kernel(size, spot, *refs):
    pieces, refs = refs[:size], refs[size:]
    guests, tail, out = refs
    homes = functools.reduce(jnp.add, [piece[...].astype(jnp.float32) for piece in pieces])
    came = guests[...].astype(jnp.float32)
    lane = lax.broadcasted_iota(jnp.int32, (1, LANES), 1)
    source = at_lane(tail[...], lane, spot).reshape(1, 1, 1)
    place = lax.broadcasted_iota(jnp.int32, (came.shape[0], 1, 1), 0) // size
    guest = jnp.sum(jnp.where(place.astype(jnp.float32) == source, came, 0.0), axis=0)
    guest = jnp.concatenate([guest[:1], guest[1:]], axis=1)
    out[...] = jnp.concatenate([homes, guest], axis=0).astype(jnp.bfloat16)


def shape(dims, dtype=jnp.float32):
    return jax.ShapeDtypeStruct(dims, dtype)


def shards(
    tokens,
    attn_gain,
    qkv_weight,
    out_weight,
    moe_gain,
    router,
    expert_gate_up,
    expert_down,
    kv_cache,
    page_table,
    home_len,
    guest_source,
    guest_pages,
    guest_len,
    routes,
):
    size = lax.axis_size("tensor")
    replicas = lax.axis_size("replica")
    rows_dev, width = tokens.shape
    npages = kv_cache.shape[0]
    top = routes.shape[1]
    units = expert_down.shape[0]
    part = out_weight.shape[0]
    columns = qkv_weight.shape[1]
    count = size * rows_dev
    home_dev = rows_dev - 1
    wide = width + LANES
    everyone = size * replicas
    blocks = units // LANES
    gate_up, down = [], []

    def load_more(after, ups, downs):
        first, last = ups[0] * blocks // 8, ups[1] * blocks // 8
        wanted = []
        if last > first:
            wanted.append((expert_gate_up, first, last - first))
        if downs[1] > downs[0]:
            wanted.append((expert_down, downs[0] * units // 8, (downs[1] - downs[0]) * units // 8))
        if not wanted:
            return after
        got = loaded(after, *wanted)
        for part in got:
            (gate_up if part.ndim == 3 else down).append(part)
        return got[0]

    packed = guest_source * FAR + guest_len
    offers, homes, plan, tail = pl.pallas_call(
        offer_kernel,
        out_shape=[
            pltpu.VMEM((everyone, 2, (wide + LANES) // 2), jnp.bfloat16),
            shape((home_dev, wide), jnp.bfloat16),
            shape((npages, LANES)),
            shape((1, LANES)),
        ],
        in_specs=[ANY] * 5 + [SMEM],
        out_specs=[VMEM] * 4,
        scratch_shapes=[
            pltpu.VMEM(tokens.shape, tokens.dtype),
            pltpu.SMEM(routes.T.shape, jnp.int32),
            pltpu.SMEM(guest_pages.shape, jnp.int32),
            pltpu.VMEM(page_table.T.shape, jnp.int32),
            pltpu.VMEM((1,) + home_len.shape, jnp.int32),
            pltpu.SemaphoreType.DMA((5,)),
        ],
        compiler_params=PARAMS,
        name="offer",
    )(far(tokens), far(routes.T), far(guest_pages), far(page_table.T), far(home_len), packed)
    came = lax.all_to_all(offers, ("replica", "tensor"), 0, 0, tiled=True)
    messages = exchanged([homes] * size)
    (qkv_near,) = loaded(homes, (qkv_weight, 0, width))

    rows, *projected = pl.pallas_call(
        functools.partial(project_kernel, size, npages, top),
        out_shape=[shape((count, wide))] + [shape((npages, columns), jnp.bfloat16)] * size,
        in_specs=[VMEM] * (size + 4),
        out_specs=[VMEM] * (size + 1),
        scratch_shapes=[
            pltpu.VMEM((size, home_dev, wide), jnp.float32),
            pltpu.VMEM((size * SUB, columns), jnp.float32),
        ],
        compiler_params=PARAMS,
        name="project",
    )(
        *messages,
        came,
        attn_gain.reshape(1, width),
        resident(qkv_near),
        plan,
    )
    joined = exchanged(projected)

    before = load_more(rows, (0, 2), (0, 2))
    late, _ = lax.optimization_barrier((out_weight, joined[1]))
    out_mate = lax.ppermute(late, "tensor", [(me, me ^ 1) for me in range(size)])
    terms = pl.pallas_call(
        functools.partial(attend_kernel, size, top),
        out_shape=[shape((npages, CORES * part + LANES), jnp.bfloat16)] * size,
        in_specs=[VMEM] * (size + 3) + [ANY],
        out_specs=[VMEM] * size,
        scratch_shapes=[
            pltpu.VMEM((size, SUB, columns), jnp.float32),
            pltpu.VMEM((size // CORES, SUB, CORES * part + LANES), jnp.float32),
        ],
        compiler_params=PARAMS,
        name="attend",
    )(*joined, resident(kv_cache), rows, plan, before)
    arrived = exchanged(terms)

    before = load_more(terms[0], (2, 5), (2, 4))
    partial = pl.pallas_call(
        functools.partial(out_kernel, size, npages),
        out_shape=shape((count, width), jnp.bfloat16),
        in_specs=[VMEM] * (size + 3) + [ANY],
        out_specs=VMEM,
        compiler_params=PARAMS,
        name="out",
    )(*arrived, resident(out_weight), resident(out_mate), plan, before)
    sums = across(partial, size)

    load_more(partial, (5, 8), (4, 8))
    *pieces, guests = pl.pallas_call(
        functools.partial(
            expert_kernel, size, top, router.shape[1], len(gate_up), len(down)
        ),
        out_shape=[shape((home_dev, width), jnp.bfloat16)] * size
        + [pltpu.VMEM((everyone, 2, width // 2), jnp.bfloat16)],
        in_specs=[VMEM] * (len(sums) + 3 + len(gate_up) + len(down)),
        out_specs=[VMEM] * (size + 1),
        scratch_shapes=[
            pltpu.VMEM((size, home_dev, width), jnp.float32),
            pltpu.VMEM((size, width), jnp.float32),
        ],
        compiler_params=PARAMS,
        name="experts",
    )(
        *sums,
        rows,
        moe_gain.reshape(1, width),
        router.T,
        *[resident(piece) for piece in gate_up + down],
    )
    guests = lax.all_to_all(guests, ("replica", "tensor"), 0, 0, tiled=True)
    pieces = exchanged(pieces)
    return pl.pallas_call(
        functools.partial(finish_kernel, size, top + 1 + MAXP),
        out_shape=shape((rows_dev, width), jnp.bfloat16),
        in_specs=[VMEM] * (size + 2),
        out_specs=VMEM,
        compiler_params=PARAMS,
        name="finish",
    )(*pieces, guests, tail)


def solution(mesh):
    placed = (
        P(("replica", "tensor"), None),
        P(),
        P(None, "tensor"),
        P("tensor", None),
        P(),
        P(),
        P(None, None, "tensor"),
        P("tensor", None),
        P(("replica", "tensor"), None, None, None),
        P("replica", None),
        P("replica"),
        P(("replica", "tensor")),
        P(("replica", "tensor"), None),
        P(("replica", "tensor")),
        P("replica", None),
    )
    return jax.shard_map(
        shards,
        mesh=mesh,
        in_specs=placed,
        out_specs=P(("replica", "tensor"), None),
        check_vma=False,
    )
```

```python
import functools

import jax
import jax.numpy as jnp
from jax import lax
from jax.experimental import pallas as pl
from jax.experimental.pallas import tpu as pltpu
from jax.sharding import PartitionSpec as P

HEADS = 12
KVH = 4
HD = 128
MOE_FF = 512
LANES = 128
SUB = 8
CORES = 2
FAR = 1024
EMPTY = -1e30
TENSOR = ("chip", "core")
STEP = 16
MAXP = 2

VMEM = pl.BlockSpec(memory_space=pltpu.VMEM)
SMEM = pl.BlockSpec(memory_space=pltpu.SMEM)
ANY = pl.BlockSpec(memory_space=pl.ANY)
PARAMS = pltpu.CompilerParams(vmem_limit_bytes=16 * 2**20)


def resident(array):
    return pltpu.with_memory_space_constraint(array, pltpu.VMEM)


def far(array):
    return pltpu.with_memory_space_constraint(array, pltpu.HBM)


def normed(values, gain):
    inverse = lax.rsqrt(jnp.mean(values * values, axis=-1, keepdims=True) + 1e-05)
    return (values * inverse * gain).astype(jnp.bfloat16)


def ways(size):
    return [(chips, core) for chips in range(size // CORES) for core in range(CORES)][1:]


def target(me, size, way):
    chip = lax.rem(me // CORES + way[0], size // CORES)
    return chip * CORES + lax.rem(me + way[1], CORES)


def sender(me, size, way):
    chip = lax.rem(me // CORES + size // CORES - way[0], size // CORES)
    return chip * CORES + lax.rem(me + way[1], CORES)


def senders(me, size):
    return [me] + [sender(me, size, way) for way in ways(size)]


def targets(me, size):
    return [me] + [target(me, size, way) for way in ways(size)]


def exchanged(blocks):
    size = len(blocks)
    arrived = [blocks[0]]
    for way, block in zip(ways(size), blocks[1:]):
        pairs = []
        for me in range(size):
            chip = (me // CORES + way[0]) % (size // CORES)
            pairs.append((me, chip * CORES + (me + way[1]) % CORES))
        arrived.append(lax.ppermute(block, TENSOR, pairs))
    return arrived


def to_step(rows):
    extra = -rows.shape[0] % STEP
    if not extra:
        return rows
    filler = jnp.zeros((extra, rows.shape[1]), jnp.float32)
    return jnp.concatenate([rows.astype(jnp.float32), filler], axis=0).astype(rows.dtype)


def lanes_of(numbers, lane):
    row = jnp.zeros(lane.shape, jnp.float32)
    for place, number in enumerate(numbers):
        row = jnp.where(lane == place, number.astype(jnp.float32), row)
    return row


def at_lane(rows, lane, place):
    return jnp.sum(jnp.where(lane == place, rows, 0.0), axis=-1, keepdims=True)


def across(block, size):
    arrived = [block]
    for chips in range(1, size // CORES):
        pairs = [(me, (me + chips * CORES) % size) for me in range(size)]
        arrived.append(lax.ppermute(block, TENSOR, pairs))
    return arrived


def to_mate(block, size):
    return lax.ppermute(block, TENSOR, [(me, me ^ 1) for me in range(size)])


def page_hits(plan, pages):
    return [jnp.where(plan[place : place + 1] == pages, 1.0, 0.0) for place in range(MAXP)]


def offer_kernel(tokens, paths, pages, table, lens, packed, *refs):
    offers, homes, plan, tail_out, rows, paths_s, pages_s, table_v, lens_v, sems = refs
    pairs = [
        (tokens, rows),
        (paths, paths_s),
        (pages, pages_s),
        (table, table_v),
        (lens, lens_v.at[0]),
    ]
    copies = [pltpu.make_async_copy(*pair, sems.at[i]) for i, pair in enumerate(pairs)]
    for copy in copies:
        copy.start()
    for copy in copies:
        copy.wait()
    me = lax.axis_index(TENSOR)
    rows_dev, width = rows.shape
    top = paths.shape[0]
    lane = lax.broadcasted_iota(jnp.int32, (1, LANES), 1)
    wide = rows[...].astype(jnp.float32)
    tails = []
    for slot in range(rows_dev):
        numbers = [paths_s[place, me * rows_dev + slot] for place in range(top)]
        if slot == rows_dev - 1:
            numbers += [packed[0] % FAR]
            numbers += [pages_s[0, place] for place in range(MAXP)]
            numbers += [packed[0] // FAR]
        tails.append(lanes_of(numbers, lane))
    tail_out[...] = tails[-1]
    full = jnp.concatenate([wide, jnp.concatenate(tails, axis=0)], axis=1)
    homes[...] = full[:-1].astype(jnp.bfloat16)
    guest = jnp.concatenate(
        [wide[-1:], tails[-1], jnp.zeros((1, LANES), jnp.float32)], axis=1
    )
    half = guest.shape[1] // 2
    block = jnp.concatenate([guest[:, :half], guest[:, half:]], axis=0).astype(jnp.bfloat16)
    for place in range(offers.shape[0]):
        offers[place] = block

    count = table.shape[1]
    npages = plan.shape[0]
    size = count * MAXP // (npages - MAXP)
    filler = jnp.zeros((1, LANES - count), jnp.float32)
    spots = lane - count
    lines = []
    for place in range(MAXP):
        ids = table_v[place : place + 1].astype(jnp.float32)
        ids = jnp.concatenate([ids, filler], axis=1)
        guests = (spots * npages + npages - MAXP + place).astype(jnp.float32)
        guests = jnp.where(spots < size, guests, -1.0)
        lines.append(jnp.where(spots < 0, ids, guests))
    lines.append(jnp.concatenate([lens_v[...].astype(jnp.float32), filler], axis=1))
    lines.append(jnp.zeros((npages - MAXP - 1, LANES), jnp.float32))
    plan[...] = jnp.concatenate(lines, axis=0)


def choose_kernel(chips, spot, offers, *refs):
    out = refs[-1]
    replica = lax.axis_index("replica").astype(jnp.float32)
    came = offers[...].astype(jnp.float32)
    half = came.shape[2]
    lane = lax.broadcasted_iota(jnp.int32, (1, 1, half), 2)
    source = jnp.sum(jnp.where(lane == spot - half, came[:, 1:], 0.0), axis=2, keepdims=True)
    picked = jnp.where(source == replica, came, 0.0)
    out[...] = jnp.sum(picked.reshape(-1, chips, 2, half), axis=0).astype(jnp.bfloat16)


def load_kernel(plans, *refs):
    sources, outs, sems = refs[1 : 1 + len(plans)], refs[1 + len(plans) : -1], refs[-1]
    copies = []

    def copy(source, out):
        copies.append(pltpu.make_async_copy(source, out, sems.at[len(copies)]))

    for (first, count, pieces), source, out in zip(plans, sources, outs):
        each = source.shape[0] // pieces if len(out.shape) == 4 else count // pieces
        for piece in range(pieces):
            lines = pl.ds(piece * each, each)
            if len(out.shape) == 4:
                for place in range(count):
                    columns = pl.ds((first + place) * LANES, LANES)
                    copy(source.at[lines, :, columns], out.at[place, lines])
            else:
                copy(source.at[pl.ds(first + piece * each, each)], out.at[lines])
    for made in copies:
        made.start()
    for made in copies:
        made.wait()


def loaded(after, *wanted):
    shapes, plans, copies = [], [], 0
    for array, first, count in wanted:
        if array.ndim == 3:
            shapes.append(shape((count,) + array.shape[:2] + (LANES,), array.dtype))
            plans.append((first, count, 2))
            copies += 2 * count
        else:
            shapes.append(shape((count, array.shape[1]), array.dtype))
            plans.append((first, count, 4))
            copies += 4
    parts = pl.pallas_call(
        functools.partial(load_kernel, tuple(plans)),
        out_shape=shapes,
        in_specs=[ANY] * (1 + len(wanted)),
        out_specs=[VMEM] * len(wanted),
        scratch_shapes=[pltpu.SemaphoreType.DMA((copies,))],
        compiler_params=PARAMS,
        cost_estimate=pl.CostEstimate(
            flops=0, bytes_accessed=sum(2 * part.size for part in shapes), transcendentals=0
        ),
        name="load",
    )(after, *[far(array) for array, _, _ in wanted])
    return [
        part.reshape(part.shape[0], -1, LANES) if part.ndim == 4 else part for part in parts
    ]


def project_kernel(size, npages, top, *refs):
    blocks, refs = refs[:size], refs[size:]
    own, other, gain, weight, plan, rows_ref = refs[:6]
    outs = refs[6 : 6 + size]
    gathered, paged = refs[6 + size :]
    me = lax.axis_index(TENSOR)
    home_dev = blocks[0].shape[0]
    homes = size * home_dev
    width, columns = weight.shape
    for owner, block in zip(senders(me, size), blocks):
        gathered[pl.ds(owner, 1)] = block[...].astype(jnp.float32)[None]
    own, other = own[...].astype(jnp.float32), other[...].astype(jnp.float32)
    first = lax.rem(me, CORES) == 0
    picked = jnp.where(first, own, other), jnp.where(first, other, own)
    for owner in range(size):
        rows_ref[owner * home_dev : (owner + 1) * home_dev] = gathered[owner]
        guest = picked[owner % CORES][owner // CORES]
        guest = jnp.concatenate([guest[:1], guest[1:]], axis=1)
        rows_ref[homes + owner : homes + owner + 1] = guest[:, : width + LANES]
    norm = to_step(normed(rows_ref[:, :width], gain[...]))
    products = jnp.dot(norm, weight[...], preferred_element_type=jnp.float32)
    line = lax.broadcasted_iota(jnp.int32, (size * SUB, LANES), 0)
    ids = line // SUB * npages + line % SUB
    ids = jnp.where(line % SUB < npages, ids, -2).astype(jnp.float32)
    hits = sum(page_hits(plan[...], ids))[:, : norm.shape[0]]
    paged[...] = jnp.dot(
        hits.astype(jnp.bfloat16), products.astype(jnp.bfloat16), preferred_element_type=jnp.float32
    )
    for end, out in zip(targets(me, size), outs):
        start = pl.multiple_of(end * SUB, SUB)
        out[...] = paged[pl.ds(start, SUB)][:npages].astype(jnp.bfloat16)


def attend_kernel(size, top, *refs):
    blocks, refs = refs[:size], refs[size:]
    cache, rows_ref, plan_ref, _ = refs[:4]
    outs = refs[4 : 4 + size]
    gathered, terms = refs[4 + size :]
    me = lax.axis_index(TENSOR)
    npages, _, page_len, _ = cache.shape
    home_pages = npages - MAXP
    homes = home_pages // MAXP * size
    group = HEADS // KVH
    qwidth, kwidth = HEADS * HD, KVH * HD
    width = rows_ref.shape[1] - LANES
    for owner, block in zip(senders(me, size), blocks):
        gathered[pl.ds(owner, 1), :npages] = block[...].astype(jnp.float32)[None]
    joined = jnp.concatenate([gathered[owner] for owner in range(size)], axis=1)

    plan = plan_ref[...]
    line = lax.broadcasted_iota(jnp.int32, (SUB, LANES), 0)
    hits = page_hits(plan, (me * npages + line).astype(jnp.float32))
    left = sum(
        hit * (plan[MAXP : MAXP + 1] - float(place * page_len)) for place, hit in enumerate(hits)
    )
    left = jnp.sum(left, axis=1, keepdims=True)
    leads = jnp.sum(hits[0], axis=1, keepdims=True)
    tails = rows_ref[:, width:]
    place = lax.broadcasted_iota(jnp.int32, tails.shape, 0)
    numbers = jnp.sum(jnp.where(place == homes + me, tails, 0.0), axis=0, keepdims=True)
    lane = lax.broadcasted_iota(jnp.int32, (1, LANES), 1)
    near_len = at_lane(numbers, lane, top)
    line = line[:, :1]
    near_left, near_lead = jnp.zeros((SUB, 1), jnp.float32), None
    for place in range(MAXP):
        named = at_lane(numbers, lane, top + 1 + place) == line.astype(jnp.float32)
        near_left = jnp.where(named, near_len - float(place * page_len), near_left)
        if place == 0:
            near_lead = jnp.where(named, 1.0, 0.0)
    left = jnp.where(line < home_pages, left, near_left)
    leads = jnp.where(line < home_pages, leads, near_lead)
    row = lax.broadcasted_iota(jnp.int32, (SUB, npages * page_len), 0)
    spot = lax.broadcasted_iota(jnp.int32, (SUB, npages * page_len), 1)
    inside = (spot - row * page_len).astype(jnp.float32)
    usable = jnp.where((inside >= 0.0) & (inside < jnp.minimum(left, float(page_len))), 1.0, 0.0)
    usable = jnp.concatenate([usable] * HEADS, axis=0) > 0.5
    leads = jnp.concatenate([leads] * HEADS, axis=0) > 0.5

    query = jnp.concatenate([joined[:, h * HD : (h + 1) * HD] for h in range(HEADS)], axis=0)
    fresh_key, fresh_value = [
        jnp.concatenate(
            [joined[:, start + h // group * HD : start + (h // group + 1) * HD] for h in range(HEADS)],
            axis=0,
        )
        for start in (qwidth, qwidth + kwidth)
    ]
    lines = group * SUB
    narrow = query.astype(jnp.bfloat16)
    scores = []
    for kv in range(KVH):
        keys = cache[:, 0, :, kv * HD : (kv + 1) * HD].reshape(npages * page_len, HD)
        scores.append(
            lax.dot_general(
                narrow[kv * lines : (kv + 1) * lines],
                keys,
                (((1,), (1,)), ((), ())),
                preferred_element_type=jnp.float32,
            )
        )
    scores = jnp.concatenate(scores, axis=0) * HD ** (-0.5)
    scores = jnp.where(usable, scores, EMPTY)
    own = jnp.sum(query * fresh_key, axis=-1, keepdims=True) * HD ** (-0.5)
    own = jnp.where(leads, own, EMPTY)
    peak = jnp.maximum(jnp.max(scores, axis=-1, keepdims=True), own)
    weights = jnp.where(usable, jnp.exp(scores - peak), 0.0)
    newest = jnp.where(leads, jnp.exp(own - peak), 0.0)
    total = jnp.sum(weights, axis=-1, keepdims=True) + newest
    narrow = weights.astype(jnp.bfloat16)
    summed = []
    for kv in range(KVH):
        values = cache[:, 1, :, kv * HD : (kv + 1) * HD].reshape(npages * page_len, HD)
        summed.append(
            jnp.dot(
                narrow[kv * lines : (kv + 1) * lines], values, preferred_element_type=jnp.float32
            )
        )
    summed = jnp.concatenate(summed, axis=0) + newest * fresh_value
    used = total > 0.0
    safe = jnp.where(used, total, 1.0)
    mixed = summed / safe
    level = jnp.where(used, peak + jnp.log(safe), EMPTY)
    lane = lax.broadcasted_iota(jnp.int32, (SUB, LANES), 1)
    levels = jnp.zeros((SUB, LANES), jnp.float32)
    for h in range(HEADS):
        levels = jnp.where(lane % STEP == h, level[h * SUB : (h + 1) * SUB], levels)
    upper = levels.astype(jnp.bfloat16).astype(jnp.float32)
    rest = levels - upper
    middle = rest.astype(jnp.bfloat16).astype(jnp.float32)
    levels = jnp.where(lane < STEP, upper, jnp.where(lane < 2 * STEP, middle, rest - middle))
    levels = jnp.where(lane < 3 * STEP, levels, 0.0)
    mixes = jnp.concatenate([mixed[h * SUB : (h + 1) * SUB] for h in range(HEADS)], axis=1)
    chips = size // CORES
    part = qwidth // chips
    for chip in range(chips):
        terms[chip] = jnp.concatenate([mixes[:, chip * part : (chip + 1) * part], levels], axis=1)
    for end, out in zip(targets(me, size), outs):
        out[...] = terms[pl.ds(end // CORES, 1)][0, :npages].astype(jnp.bfloat16)


def out_kernel(size, npages, *refs):
    blocks, refs = refs[:size], refs[size:]
    weight, mate_weight, plan, _, out = refs
    me = lax.axis_index(TENSOR)
    part = CORES * weight.shape[0]
    terms, ids = [], []
    line = lax.broadcasted_iota(jnp.int32, (SUB, LANES), 0)
    filler = jnp.zeros((SUB - npages, part + LANES), jnp.float32)
    for owner, block in zip(senders(me, size), blocks):
        terms += [block[...].astype(jnp.float32), filler]
        ids.append(jnp.where(line < npages, owner * npages + line, -2))
    terms = jnp.concatenate(terms, axis=0).astype(jnp.bfloat16)
    ids = jnp.concatenate(ids, axis=0).astype(jnp.float32)
    spread = lax.broadcasted_iota(jnp.int32, (LANES, part), 0)
    head = (lax.broadcasted_iota(jnp.int32, (LANES, part), 1) + me // CORES * part) // HD
    spread = jnp.where((spread % STEP == head) & (spread < 3 * STEP), 1.0, 0.0)
    spread = spread.astype(jnp.bfloat16)
    count = out.shape[0]
    rows = count + -count % STEP
    mixes, levels = [], []
    for hit in page_hits(plan[...], ids):
        picked = lax.dot_general(
            hit[:, :rows].astype(jnp.bfloat16),
            terms,
            (((0,), (0,)), ((), ())),
            preferred_element_type=jnp.float32,
        )
        mixes.append(picked[:, :part])
        levels.append(
            jnp.dot(
                picked[:, part:].astype(jnp.bfloat16), spread, preferred_element_type=jnp.float32
            )
        )
    highest = functools.reduce(jnp.maximum, levels)
    factors = [jnp.exp(level - highest) for level in levels]
    mixed = sum(mix * factor for mix, factor in zip(mixes, factors)) / sum(factors)
    halves = mixed[:, : part // CORES], mixed[:, part // CORES :]
    first = lax.rem(me, CORES) == 0
    own = jnp.where(first, halves[0], halves[1]).astype(jnp.bfloat16)
    other = jnp.where(first, halves[1], halves[0]).astype(jnp.bfloat16)
    products = jnp.dot(own, weight[...], preferred_element_type=jnp.float32)
    products += jnp.dot(other, mate_weight[...], preferred_element_type=jnp.float32)
    out[...] = products[:count].astype(jnp.bfloat16)


def expert_kernel(size, top, experts, parts, lows, *refs):
    chips = size // CORES
    sums, refs = refs[:chips], refs[chips:]
    rows_ref, gain, router = refs[:3]
    gate_up, refs = refs[3 : 3 + parts], refs[3 + parts :]
    down, refs = refs[:lows], refs[lows:]
    units = sum(piece.shape[0] for piece in down)
    homes, refs = refs[:size], refs[size:]
    keep, give, finished = refs
    me = lax.axis_index(TENSOR)
    count = rows_ref.shape[0]
    width = rows_ref.shape[1] - LANES
    rows_dev = count // size
    total = functools.reduce(jnp.add, [piece[...].astype(jnp.float32) for piece in sums])
    hidden = (rows_ref[:, :width] + total).astype(jnp.bfloat16).astype(jnp.float32)
    norm = normed(hidden, gain[...])
    lane = lax.broadcasted_iota(jnp.int32, (count, LANES), 1)
    numbers = rows_ref[:, width:]
    logits = lax.dot_general(
        norm, router[...], (((1,), (1,)), ((), ())), preferred_element_type=jnp.float32
    )
    logits = jnp.concatenate(
        [logits, jnp.zeros((count, LANES - experts), jnp.float32)], axis=1
    )
    routed = jnp.zeros((count, LANES), jnp.float32)
    for place in range(top):
        route = at_lane(numbers, lane, place)
        routed = jnp.where(lane.astype(jnp.float32) == route, 1.0, routed)
    logits = jnp.where(routed > 0.5, logits, EMPTY)
    shares = jnp.where(
        routed > 0.5, jnp.exp(logits - jnp.max(logits, axis=-1, keepdims=True)), 0.0
    )
    shares = shares / jnp.sum(shares, axis=-1, keepdims=True)

    here = lax.broadcasted_iota(jnp.int32, (LANES, 2 * LANES), 0)
    there = lax.broadcasted_iota(jnp.int32, (LANES, 2 * LANES), 1)
    evens = jnp.where(there == 2 * here, 1.0, 0.0).astype(jnp.bfloat16)
    odds = jnp.where(there == 2 * here + 1, 1.0, 0.0).astype(jnp.bfloat16)
    wide = to_step(norm)
    padded = wide.shape[0]
    blocks = width // LANES
    tall = jnp.concatenate([wide[:, b * LANES : (b + 1) * LANES] for b in range(blocks)], axis=0)
    to_gate = jnp.dot(tall, evens, preferred_element_type=jnp.float32).astype(jnp.bfloat16)
    to_up = jnp.dot(tall, odds, preferred_element_type=jnp.float32).astype(jnp.bfloat16)
    left = []
    for b in range(blocks):
        lines = slice(b * padded, (b + 1) * padded)
        left.append(jnp.concatenate([to_gate[lines], to_up[lines]], axis=0))
    left = jnp.concatenate(left, axis=1)
    both, right = [], []
    for piece in gate_up:
        right += [piece[place] for place in range(piece.shape[0])]
    for place in range(0, len(right), 2):
        pair = jnp.concatenate(right[place : place + 2], axis=1)
        both.append(jnp.dot(left, pair, preferred_element_type=jnp.float32))
    both = jnp.concatenate(both, axis=1)
    gate, up = both[:count], both[padded : padded + count]
    activated = gate / (1.0 + jnp.exp(-gate)) * up
    step = min(units, MOE_FF)
    scaled = []
    for start in range(0, units, step):
        expert = (me * units + start) // MOE_FF
        share = at_lane(shares, lane, expert)
        scaled.append(activated[:, start : start + step] * share)
    scaled = jnp.concatenate(scaled, axis=1).astype(jnp.bfloat16)
    partial, start = 0.0, 0
    for piece in down:
        left = scaled[:, start : start + piece.shape[0]]
        partial += jnp.dot(left, piece[...], preferred_element_type=jnp.float32)
        start += piece.shape[0]
    home_dev = rows_dev - 1
    first = size * home_dev
    ends = []
    for owner in range(size):
        lines = slice(owner * home_dev, (owner + 1) * home_dev)
        mine = jnp.where(me == owner, 1.0, 0.0)
        finished[owner] = partial[lines] + hidden[lines] * mine
        line = slice(first + owner, first + owner + 1)
        ends.append(partial[line] + hidden[line] * mine)
    for end, out in zip(targets(me, size), homes):
        out[...] = finished[pl.ds(end, 1)][0].astype(jnp.bfloat16)
    ends = jnp.concatenate(ends[0::2], axis=0), jnp.concatenate(ends[1::2], axis=0)
    first = lax.rem(me, CORES) == 0
    keep[...] = jnp.where(first, ends[0], ends[1])
    give[...] = jnp.where(first, ends[1], ends[0]).astype(jnp.bfloat16)


def spread_kernel(keep, came, out):
    total = keep[...] + came[...].astype(jnp.float32)
    chips, width = total.shape
    half = width // 2
    for chip in range(chips):
        guest = total[chip : chip + 1]
        block = jnp.concatenate([guest[:, :half], guest[:, half:]], axis=0).astype(jnp.bfloat16)
        for place in range(chip, out.shape[0], chips):
            out[place] = block


def finish_kernel(size, spot, *refs):
    pieces, refs = refs[:size], refs[size:]
    guests, tail, out = refs
    homes = functools.reduce(jnp.add, [piece[...].astype(jnp.float32) for piece in pieces])
    came = guests[...].astype(jnp.float32)
    lane = lax.broadcasted_iota(jnp.int32, (1, LANES), 1)
    source = at_lane(tail[...], lane, spot).reshape(1, 1, 1)
    place = lax.broadcasted_iota(jnp.int32, (came.shape[0], 1, 1), 0) // (size // CORES)
    guest = jnp.sum(jnp.where(place.astype(jnp.float32) == source, came, 0.0), axis=0)
    guest = jnp.concatenate([guest[:1], guest[1:]], axis=1)
    out[...] = jnp.concatenate([homes, guest], axis=0).astype(jnp.bfloat16)


def shape(dims, dtype=jnp.float32):
    return jax.ShapeDtypeStruct(dims, dtype)


def shards(
    tokens,
    attn_gain,
    qkv_weight,
    out_weight,
    moe_gain,
    router,
    expert_gate_up,
    expert_down,
    kv_cache,
    page_table,
    home_len,
    guest_source,
    guest_pages,
    guest_len,
    routes,
):
    size = lax.axis_size(TENSOR)
    replicas = lax.axis_size("replica")
    rows_dev, width = tokens.shape
    npages = kv_cache.shape[0]
    top = routes.shape[1]
    units = expert_down.shape[0]
    part = out_weight.shape[0]
    columns = qkv_weight.shape[1]
    count = size * rows_dev
    home_dev = rows_dev - 1
    wide = width + LANES
    chips = size // CORES
    everyone = chips * replicas
    blocks = units // LANES
    gate_up, down = [], []

    def load_more(after, ups, downs):
        first, last = ups[0] * blocks // 8, ups[1] * blocks // 8
        wanted = []
        if last > first:
            wanted.append((expert_gate_up, first, last - first))
        if downs[1] > downs[0]:
            wanted.append((expert_down, downs[0] * units // 8, (downs[1] - downs[0]) * units // 8))
        if not wanted:
            return after
        got = loaded(after, *wanted)
        for part in got:
            (gate_up if part.ndim == 3 else down).append(part)
        return got[0]

    packed = guest_source * FAR + guest_len
    offers, homes, plan, tail = pl.pallas_call(
        offer_kernel,
        out_shape=[
            shape((everyone, 2, (wide + LANES) // 2), jnp.bfloat16),
            shape((home_dev, wide), jnp.bfloat16),
            shape((npages, LANES)),
            shape((1, LANES)),
        ],
        in_specs=[ANY] * 5 + [SMEM],
        out_specs=[VMEM] * 4,
        scratch_shapes=[
            pltpu.VMEM(tokens.shape, tokens.dtype),
            pltpu.SMEM(routes.T.shape, jnp.int32),
            pltpu.SMEM(guest_pages.shape, jnp.int32),
            pltpu.VMEM(page_table.T.shape, jnp.int32),
            pltpu.VMEM((1,) + home_len.shape, jnp.int32),
            pltpu.SemaphoreType.DMA((5,)),
        ],
        compiler_params=PARAMS,
        name="offer",
    )(far(tokens), far(routes.T), far(guest_pages), far(page_table.T), far(home_len), packed)
    came = lax.all_to_all(offers, ("replica", "chip"), 0, 0, tiled=True)
    messages = exchanged([homes] * size)
    (qkv_near,) = loaded(homes, (qkv_weight, 0, width))
    own = pl.pallas_call(
        functools.partial(choose_kernel, chips, width + top + 1 + MAXP),
        out_shape=shape((chips, 2, (wide + LANES) // 2), jnp.bfloat16),
        in_specs=[VMEM] + [ANY] * size,
        out_specs=VMEM,
        compiler_params=PARAMS,
        name="choose",
    )(came, qkv_near, *messages[1:])
    other = to_mate(own, size)

    rows, *projected = pl.pallas_call(
        functools.partial(project_kernel, size, npages, top),
        out_shape=[shape((count, wide))] + [shape((npages, columns), jnp.bfloat16)] * size,
        in_specs=[VMEM] * (size + 5),
        out_specs=[VMEM] * (size + 1),
        scratch_shapes=[
            pltpu.VMEM((size, home_dev, wide), jnp.float32),
            pltpu.VMEM((size * SUB, columns), jnp.float32),
        ],
        compiler_params=PARAMS,
        name="project",
    )(
        *messages,
        own,
        other,
        attn_gain.reshape(1, width),
        resident(qkv_near),
        plan,
    )
    joined = exchanged(projected)

    before = load_more(rows, (0, 2), (0, 2))
    late, _ = lax.optimization_barrier((out_weight, rows))
    out_mate = to_mate(late, size)
    terms = pl.pallas_call(
        functools.partial(attend_kernel, size, top),
        out_shape=[shape((npages, CORES * part + LANES), jnp.bfloat16)] * size,
        in_specs=[VMEM] * (size + 3) + [ANY],
        out_specs=[VMEM] * size,
        scratch_shapes=[
            pltpu.VMEM((size, SUB, columns), jnp.float32),
            pltpu.VMEM((size // CORES, SUB, CORES * part + LANES), jnp.float32),
        ],
        compiler_params=PARAMS,
        name="attend",
    )(*joined, resident(kv_cache), rows, plan, before)
    arrived = exchanged(terms)

    before = load_more(terms[0], (2, 5), (2, 4))
    partial = pl.pallas_call(
        functools.partial(out_kernel, size, npages),
        out_shape=shape((count, width), jnp.bfloat16),
        in_specs=[VMEM] * (size + 3) + [ANY],
        out_specs=VMEM,
        compiler_params=PARAMS,
        name="out",
    )(*arrived, resident(out_weight), resident(out_mate), plan, before)
    sums = across(partial, size)

    load_more(partial, (5, 8), (4, 8))
    *pieces, keep, give = pl.pallas_call(
        functools.partial(
            expert_kernel, size, top, router.shape[1], len(gate_up), len(down)
        ),
        out_shape=[shape((home_dev, width), jnp.bfloat16)] * size
        + [shape((chips, width)), shape((chips, width), jnp.bfloat16)],
        in_specs=[VMEM] * (len(sums) + 3 + len(gate_up) + len(down)),
        out_specs=[VMEM] * (size + 2),
        scratch_shapes=[
            pltpu.VMEM((size, home_dev, width), jnp.float32),
        ],
        compiler_params=PARAMS,
        name="experts",
    )(
        *sums,
        rows,
        moe_gain.reshape(1, width),
        router.T,
        *[resident(piece) for piece in gate_up + down],
    )
    guests = pl.pallas_call(
        spread_kernel,
        out_shape=shape((everyone, 2, width // 2), jnp.bfloat16),
        in_specs=[VMEM, VMEM],
        out_specs=VMEM,
        compiler_params=PARAMS,
        name="spread",
    )(keep, to_mate(give, size))
    *pieces, guests = lax.optimization_barrier((*pieces, guests))
    guests = lax.all_to_all(guests, ("replica", "chip"), 0, 0, tiled=True)
    pieces = exchanged(pieces)
    return pl.pallas_call(
        functools.partial(finish_kernel, size, top + 1 + MAXP),
        out_shape=shape((rows_dev, width), jnp.bfloat16),
        in_specs=[VMEM] * (size + 2),
        out_specs=VMEM,
        compiler_params=PARAMS,
        name="finish",
    )(*pieces, guests, tail)


def solution(mesh):
    replicas, size = mesh.devices.shape
    devices = mesh.devices.reshape(replicas, size // CORES, CORES)
    everyone = ("replica",) + TENSOR
    placed = (
        P(everyone, None),
        P(),
        P(None, TENSOR),
        P(TENSOR, None),
        P(),
        P(),
        P(None, None, TENSOR),
        P(TENSOR, None),
        P(everyone, None, None, None),
        P("replica", None),
        P("replica"),
        P(everyone),
        P(everyone, None),
        P(everyone),
        P("replica", None),
    )
    return jax.shard_map(
        shards,
        mesh=jax.sharding.Mesh(devices, everyone),
        in_specs=placed,
        out_specs=P(everyone, None),
        check_vma=False,
    )
```

```python
import functools

import jax
import jax.numpy as jnp
from jax import lax
from jax.experimental import pallas as pl
from jax.experimental.pallas import tpu as pltpu
from jax.sharding import PartitionSpec as P

HEADS = 12
KVH = 4
HD = 128
MOE_FF = 512
LANES = 128
SUB = 8
CORES = 2
FAR = 1024
EMPTY = -1e30
STEP = 16
MAXP = 2

VMEM = pl.BlockSpec(memory_space=pltpu.VMEM)
SMEM = pl.BlockSpec(memory_space=pltpu.SMEM)
ANY = pl.BlockSpec(memory_space=pl.ANY)
PARAMS = pltpu.CompilerParams(vmem_limit_bytes=16 * 2**20)


def resident(array):
    return pltpu.with_memory_space_constraint(array, pltpu.VMEM)


def far(array):
    return pltpu.with_memory_space_constraint(array, pltpu.HBM)


def normed(values, gain):
    inverse = lax.rsqrt(jnp.mean(values * values, axis=-1, keepdims=True) + 1e-05)
    return (values * inverse * gain).astype(jnp.bfloat16)


def ways(size):
    return [(chips, core) for chips in range(size // CORES) for core in range(CORES)][1:]


def target(me, size, way):
    chip = lax.rem(me // CORES + way[0], size // CORES)
    return chip * CORES + lax.rem(me + way[1], CORES)


def sender(me, size, way):
    chip = lax.rem(me // CORES + size // CORES - way[0], size // CORES)
    return chip * CORES + lax.rem(me + way[1], CORES)


def senders(me, size):
    return [me] + [sender(me, size, way) for way in ways(size)]


def targets(me, size):
    return [me] + [target(me, size, way) for way in ways(size)]


def exchanged(blocks):
    size = len(blocks)
    arrived = [blocks[0]]
    for way, block in zip(ways(size), blocks[1:]):
        pairs = []
        for me in range(size):
            chip = (me // CORES + way[0]) % (size // CORES)
            pairs.append((me, chip * CORES + (me + way[1]) % CORES))
        arrived.append(lax.ppermute(block, "tensor", pairs))
    return arrived


def to_step(rows):
    extra = -rows.shape[0] % STEP
    if not extra:
        return rows
    filler = jnp.zeros((extra, rows.shape[1]), jnp.float32)
    return jnp.concatenate([rows.astype(jnp.float32), filler], axis=0).astype(rows.dtype)


def lanes_of(numbers, lane):
    row = jnp.zeros(lane.shape, jnp.float32)
    for place, number in enumerate(numbers):
        row = jnp.where(lane == place, number.astype(jnp.float32), row)
    return row


def at_lane(rows, lane, place):
    return jnp.sum(jnp.where(lane == place, rows, 0.0), axis=-1, keepdims=True)


def chip_of(me, size, chips):
    return lax.rem(me // CORES + chips + size // CORES, size // CORES) * CORES + lax.rem(me, CORES)


def across(blocks, size):
    arrived = [blocks[0]]
    for chips in range(1, size // CORES):
        pairs = [(me, (me + chips * CORES) % size) for me in range(size)]
        arrived.append(lax.ppermute(blocks[chips], "tensor", pairs))
    return arrived


def to_mate(block, size):
    return lax.ppermute(block, "tensor", [(me, me ^ 1) for me in range(size)])


def page_hits(plan, pages):
    return [jnp.where(plan[place : place + 1] == pages, 1.0, 0.0) for place in range(MAXP)]


def offer_kernel(tokens, paths, pages, table, lens, packed, *refs):
    offers, homes, plan, tail_out, rows, paths_s, pages_s, table_v, lens_v, sems = refs
    pairs = [
        (tokens, rows),
        (paths, paths_s),
        (pages, pages_s),
        (table, table_v),
        (lens, lens_v.at[0]),
    ]
    copies = [pltpu.make_async_copy(*pair, sems.at[i]) for i, pair in enumerate(pairs)]
    for copy in copies:
        copy.start()
    for copy in copies:
        copy.wait()
    me = lax.axis_index("tensor")
    rows_dev, width = rows.shape
    top = paths.shape[0]
    lane = lax.broadcasted_iota(jnp.int32, (1, LANES), 1)
    wide = rows[...].astype(jnp.float32)
    tails = []
    for slot in range(rows_dev):
        numbers = [paths_s[place, me * rows_dev + slot] for place in range(top)]
        if slot == rows_dev - 1:
            numbers += [packed[0] % FAR]
            numbers += [pages_s[0, place] for place in range(MAXP)]
            numbers += [packed[0] // FAR]
        tails.append(lanes_of(numbers, lane))
    tail_out[...] = tails[-1]
    full = jnp.concatenate([wide, jnp.concatenate(tails, axis=0)], axis=1)
    homes[...] = full[:-1].astype(jnp.bfloat16)
    guest = jnp.concatenate(
        [wide[-1:], tails[-1], jnp.zeros((1, LANES), jnp.float32)], axis=1
    )
    half = guest.shape[1] // 2
    block = jnp.concatenate([guest[:, :half], guest[:, half:]], axis=0).astype(jnp.bfloat16)
    for place in range(offers.shape[0]):
        offers[place] = block

    count = table.shape[1]
    npages = plan.shape[0]
    size = count * MAXP // (npages - MAXP)
    filler = jnp.zeros((1, LANES - count), jnp.float32)
    spots = lane - count
    lines = []
    for place in range(MAXP):
        ids = table_v[place : place + 1].astype(jnp.float32)
        ids = jnp.concatenate([ids, filler], axis=1)
        guests = (spots * npages + npages - MAXP + place).astype(jnp.float32)
        guests = jnp.where(spots < size, guests, -1.0)
        lines.append(jnp.where(spots < 0, ids, guests))
    lines.append(jnp.concatenate([lens_v[...].astype(jnp.float32), filler], axis=1))
    lines.append(jnp.zeros((npages - MAXP - 1, LANES), jnp.float32))
    plan[...] = jnp.concatenate(lines, axis=0)


def load_kernel(plans, *refs):
    sources, outs, sems = refs[1 : 1 + len(plans)], refs[1 + len(plans) : -1], refs[-1]
    copies = []

    def copy(source, out):
        copies.append(pltpu.make_async_copy(source, out, sems.at[len(copies)]))

    for (first, count, pieces), source, out in zip(plans, sources, outs):
        each = source.shape[0] // pieces if len(out.shape) == 4 else count // pieces
        for piece in range(pieces):
            lines = pl.ds(piece * each, each)
            if len(out.shape) == 4:
                for place in range(count):
                    columns = pl.ds((first + place) * LANES, LANES)
                    copy(source.at[lines, :, columns], out.at[place, lines])
            else:
                copy(source.at[pl.ds(first + piece * each, each)], out.at[lines])
    for made in copies:
        made.start()
    for made in copies:
        made.wait()


def loaded(after, *wanted):
    shapes, plans, copies = [], [], 0
    for array, first, count in wanted:
        if array.ndim == 3:
            shapes.append(shape((count,) + array.shape[:2] + (LANES,), array.dtype))
            plans.append((first, count, 2))
            copies += 2 * count
        else:
            shapes.append(shape((count, array.shape[1]), array.dtype))
            plans.append((first, count, 4))
            copies += 4
    parts = pl.pallas_call(
        functools.partial(load_kernel, tuple(plans)),
        out_shape=shapes,
        in_specs=[ANY] * (1 + len(wanted)),
        out_specs=[VMEM] * len(wanted),
        scratch_shapes=[pltpu.SemaphoreType.DMA((copies,))],
        compiler_params=PARAMS,
        cost_estimate=pl.CostEstimate(
            flops=0, bytes_accessed=sum(2 * part.size for part in shapes), transcendentals=0
        ),
        name="load",
    )(after, *[far(array) for array, _, _ in wanted])
    return [
        part.reshape(part.shape[0], -1, LANES) if part.ndim == 4 else part for part in parts
    ]


def project_kernel(size, npages, top, *refs):
    blocks, refs = refs[:size], refs[size:]
    offers, gain, weight, plan, rows_ref = refs[:5]
    outs = refs[5 : 5 + size]
    gathered, paged = refs[5 + size :]
    me = lax.axis_index("tensor")
    replica = lax.axis_index("replica").astype(jnp.float32)
    home_dev = blocks[0].shape[0]
    homes = size * home_dev
    width, columns = weight.shape
    for owner, block in zip(senders(me, size), blocks):
        gathered[pl.ds(owner, 1)] = block[...].astype(jnp.float32)[None]
    came = offers[...].astype(jnp.float32)
    half = came.shape[2]
    lane = lax.broadcasted_iota(jnp.int32, (1, 1, half), 2)
    spot = width + top + 1 + MAXP - half
    source = jnp.sum(jnp.where(lane == spot, came[:, 1:], 0.0), axis=2, keepdims=True)
    picked = jnp.where(source == replica, came, 0.0)
    picked = jnp.sum(picked.reshape(-1, size, 2, half), axis=0)
    for owner in range(size):
        rows_ref[owner * home_dev : (owner + 1) * home_dev] = gathered[owner]
        guest = jnp.concatenate([picked[owner, :1], picked[owner, 1:]], axis=1)
        rows_ref[homes + owner : homes + owner + 1] = guest[:, : width + LANES]
    norm = to_step(normed(rows_ref[:, :width], gain[...]))
    products = jnp.dot(norm, weight[...], preferred_element_type=jnp.float32)
    line = lax.broadcasted_iota(jnp.int32, (size * SUB, LANES), 0)
    ids = line // SUB * npages + line % SUB
    ids = jnp.where(line % SUB < npages, ids, -2).astype(jnp.float32)
    hits = sum(page_hits(plan[...], ids))[:, : norm.shape[0]]
    paged[...] = jnp.dot(
        hits.astype(jnp.bfloat16), products.astype(jnp.bfloat16), preferred_element_type=jnp.float32
    )
    for end, out in zip(targets(me, size), outs):
        start = pl.multiple_of(end // CORES * CORES * SUB, CORES * SUB)
        out[...] = paged[pl.ds(start, CORES * SUB)].astype(jnp.bfloat16)


def page_terms(rows, cache, left, leads):
    npages, _, page_len, _ = cache.shape
    group = HEADS // KVH
    qwidth, kwidth = HEADS * HD, KVH * HD
    row = lax.broadcasted_iota(jnp.int32, (SUB, npages * page_len), 0)
    spot = lax.broadcasted_iota(jnp.int32, (SUB, npages * page_len), 1)
    inside = (spot - row * page_len).astype(jnp.float32)
    usable = jnp.where((inside >= 0.0) & (inside < jnp.minimum(left, float(page_len))), 1.0, 0.0)
    usable = jnp.concatenate([usable] * HEADS, axis=0) > 0.5
    leads = jnp.concatenate([leads] * HEADS, axis=0) > 0.5

    query = jnp.concatenate([rows[:, h * HD : (h + 1) * HD] for h in range(HEADS)], axis=0)
    fresh_key, fresh_value = [
        jnp.concatenate(
            [rows[:, start + h // group * HD : start + (h // group + 1) * HD] for h in range(HEADS)],
            axis=0,
        )
        for start in (qwidth, qwidth + kwidth)
    ]
    lines = group * SUB
    narrow = query.astype(jnp.bfloat16)
    scores = []
    for kv in range(KVH):
        keys = cache[:, 0, :, kv * HD : (kv + 1) * HD].reshape(npages * page_len, HD)
        scores.append(
            lax.dot_general(
                narrow[kv * lines : (kv + 1) * lines],
                keys,
                (((1,), (1,)), ((), ())),
                preferred_element_type=jnp.float32,
            )
        )
    scores = jnp.concatenate(scores, axis=0) * HD ** (-0.5)
    scores = jnp.where(usable, scores, EMPTY)
    own = jnp.sum(query * fresh_key, axis=-1, keepdims=True) * HD ** (-0.5)
    own = jnp.where(leads, own, EMPTY)
    peak = jnp.maximum(jnp.max(scores, axis=-1, keepdims=True), own)
    weights = jnp.where(usable, jnp.exp(scores - peak), 0.0)
    newest = jnp.where(leads, jnp.exp(own - peak), 0.0)
    total = jnp.sum(weights, axis=-1, keepdims=True) + newest
    narrow = weights.astype(jnp.bfloat16)
    summed = []
    for kv in range(KVH):
        values = cache[:, 1, :, kv * HD : (kv + 1) * HD].reshape(npages * page_len, HD)
        summed.append(
            jnp.dot(
                narrow[kv * lines : (kv + 1) * lines], values, preferred_element_type=jnp.float32
            )
        )
    summed = jnp.concatenate(summed, axis=0) + newest * fresh_value
    used = total > 0.0
    safe = jnp.where(used, total, 1.0)
    return summed / safe, jnp.where(used, peak + jnp.log(safe), EMPTY)


def attend_kernel(size, top, *refs):
    blocks, refs = refs[:size], refs[size:]
    cache, mate_cache, rows_ref, plan_ref, _ = refs[:5]
    chips = size // CORES
    outs = refs[5 : 5 + chips]
    gathered, terms = refs[5 + chips :]
    me = lax.axis_index("tensor")
    npages, _, page_len, _ = cache.shape
    home_pages = npages - MAXP
    homes = home_pages // MAXP * size
    width = rows_ref.shape[1] - LANES
    for owner, block in zip(senders(me, size), blocks):
        gathered[pl.ds(owner, 1)] = block[...].astype(jnp.float32)[None]
    joined = jnp.concatenate([gathered[owner] for owner in range(size)], axis=1)
    first = lax.rem(me, CORES) == 0
    halves = joined[:SUB], joined[SUB:]
    mate = me + 1 - 2 * lax.rem(me, CORES)

    plan = plan_ref[...]
    lane = lax.broadcasted_iota(jnp.int32, (1, LANES), 1)
    part = HEADS * HD // chips
    for side, (device, pages) in enumerate(((me, cache), (mate, mate_cache))):
        line = lax.broadcasted_iota(jnp.int32, (SUB, LANES), 0)
        ids = jnp.where(line < npages, device * npages + line, -2)
        hits = page_hits(plan, ids.astype(jnp.float32))
        left = sum(
            hit * (plan[MAXP : MAXP + 1] - float(place * page_len))
            for place, hit in enumerate(hits)
        )
        left = jnp.sum(left, axis=1, keepdims=True)
        leads = jnp.sum(hits[0], axis=1, keepdims=True)
        tails = rows_ref[:, width:]
        place = lax.broadcasted_iota(jnp.int32, tails.shape, 0)
        numbers = jnp.sum(jnp.where(place == homes + device, tails, 0.0), axis=0, keepdims=True)
        near_len = at_lane(numbers, lane, top)
        line = line[:, :1]
        near_left, near_lead = jnp.zeros((SUB, 1), jnp.float32), None
        for place in range(MAXP):
            named = at_lane(numbers, lane, top + 1 + place) == line.astype(jnp.float32)
            near_left = jnp.where(named, near_len - float(place * page_len), near_left)
            if place == 0:
                near_lead = jnp.where(named, 1.0, 0.0)
        left = jnp.where(line < home_pages, left, near_left)
        leads = jnp.where(line < home_pages, leads, near_lead)
        rows = jnp.where(first, halves[side], halves[1 - side])
        mixed, level = page_terms(rows, pages, left, leads)

        spots = lax.broadcasted_iota(jnp.int32, (SUB, LANES), 1)
        levels = jnp.zeros((SUB, LANES), jnp.float32)
        for h in range(HEADS):
            levels = jnp.where(spots % STEP == h, level[h * SUB : (h + 1) * SUB], levels)
        upper = levels.astype(jnp.bfloat16).astype(jnp.float32)
        rest = levels - upper
        middle = rest.astype(jnp.bfloat16).astype(jnp.float32)
        levels = jnp.where(spots < STEP, upper, jnp.where(spots < 2 * STEP, middle, rest - middle))
        levels = jnp.where(spots < 3 * STEP, levels, 0.0)
        mixes = jnp.concatenate([mixed[h * SUB : (h + 1) * SUB] for h in range(HEADS)], axis=1)
        for chip in range(chips):
            columns = mixes[:, chip * part : (chip + 1) * part]
            terms[chip, side * SUB : (side + 1) * SUB] = jnp.concatenate([columns, levels], axis=1)
    for step, out in enumerate(outs):
        end = chip_of(me, size, step)
        out[...] = terms[pl.ds(end // CORES, 1)][0].astype(jnp.bfloat16)


def out_kernel(size, npages, *refs):
    chips = size // CORES
    blocks, refs = refs[:chips], refs[chips:]
    weight, mate_weight, plan, _, out = refs
    me = lax.axis_index("tensor")
    part = CORES * weight.shape[0]
    terms, ids = [], []
    line = lax.broadcasted_iota(jnp.int32, (SUB, LANES), 0)
    for step, block in enumerate(blocks):
        owner = chip_of(me, size, -step)
        terms.append(block[...])
        for device in (owner, owner + 1 - 2 * lax.rem(me, CORES)):
            ids.append(jnp.where(line < npages, device * npages + line, -2))
    terms = jnp.concatenate(terms, axis=0)
    ids = jnp.concatenate(ids, axis=0).astype(jnp.float32)
    spread = lax.broadcasted_iota(jnp.int32, (LANES, part), 0)
    head = (lax.broadcasted_iota(jnp.int32, (LANES, part), 1) + me // CORES * part) // HD
    spread = jnp.where((spread % STEP == head) & (spread < 3 * STEP), 1.0, 0.0)
    spread = spread.astype(jnp.bfloat16)
    count = out.shape[0]
    rows = count + -count % STEP
    mixes, levels = [], []
    for hit in page_hits(plan[...], ids):
        picked = lax.dot_general(
            hit[:, :rows].astype(jnp.bfloat16),
            terms,
            (((0,), (0,)), ((), ())),
            preferred_element_type=jnp.float32,
        )
        mixes.append(picked[:, :part])
        levels.append(
            jnp.dot(
                picked[:, part:].astype(jnp.bfloat16), spread, preferred_element_type=jnp.float32
            )
        )
    highest = functools.reduce(jnp.maximum, levels)
    factors = [jnp.exp(level - highest) for level in levels]
    mixed = sum(mix * factor for mix, factor in zip(mixes, factors)) / sum(factors)
    halves = mixed[:, : part // CORES], mixed[:, part // CORES :]
    first = lax.rem(me, CORES) == 0
    own = jnp.where(first, halves[0], halves[1]).astype(jnp.bfloat16)
    other = jnp.where(first, halves[1], halves[0]).astype(jnp.bfloat16)
    products = jnp.dot(own, weight[...], preferred_element_type=jnp.float32)
    products += jnp.dot(other, mate_weight[...], preferred_element_type=jnp.float32)
    out[...] = products[:count].astype(jnp.bfloat16)


def expert_kernel(size, top, experts, parts, lows, *refs):
    chips = size // CORES
    sums, refs = refs[:chips], refs[chips:]
    rows_ref, gain, router = refs[:3]
    gate_up, refs = refs[3 : 3 + parts], refs[3 + parts :]
    down, refs = refs[:lows], refs[lows:]
    units = sum(piece.shape[0] for piece in down)
    homes, guests, finished, ends_ref = refs[:size], refs[size], refs[size + 1], refs[size + 2]
    me = lax.axis_index("tensor")
    count = rows_ref.shape[0]
    width = rows_ref.shape[1] - LANES
    rows_dev = count // size
    total = functools.reduce(jnp.add, [piece[...].astype(jnp.float32) for piece in sums])
    hidden = (rows_ref[:, :width] + total).astype(jnp.bfloat16).astype(jnp.float32)
    norm = normed(hidden, gain[...])
    lane = lax.broadcasted_iota(jnp.int32, (count, LANES), 1)
    numbers = rows_ref[:, width:]
    logits = lax.dot_general(
        norm, router[...], (((1,), (1,)), ((), ())), preferred_element_type=jnp.float32
    )
    logits = jnp.concatenate(
        [logits, jnp.zeros((count, LANES - experts), jnp.float32)], axis=1
    )
    routed = jnp.zeros((count, LANES), jnp.float32)
    for place in range(top):
        route = at_lane(numbers, lane, place)
        routed = jnp.where(lane.astype(jnp.float32) == route, 1.0, routed)
    logits = jnp.where(routed > 0.5, logits, EMPTY)
    shares = jnp.where(
        routed > 0.5, jnp.exp(logits - jnp.max(logits, axis=-1, keepdims=True)), 0.0
    )
    shares = shares / jnp.sum(shares, axis=-1, keepdims=True)

    here = lax.broadcasted_iota(jnp.int32, (LANES, 2 * LANES), 0)
    there = lax.broadcasted_iota(jnp.int32, (LANES, 2 * LANES), 1)
    evens = jnp.where(there == 2 * here, 1.0, 0.0).astype(jnp.bfloat16)
    odds = jnp.where(there == 2 * here + 1, 1.0, 0.0).astype(jnp.bfloat16)
    wide = to_step(norm)
    padded = wide.shape[0]
    blocks = width // LANES
    tall = jnp.concatenate([wide[:, b * LANES : (b + 1) * LANES] for b in range(blocks)], axis=0)
    to_gate = jnp.dot(tall, evens, preferred_element_type=jnp.float32).astype(jnp.bfloat16)
    to_up = jnp.dot(tall, odds, preferred_element_type=jnp.float32).astype(jnp.bfloat16)
    left = []
    for b in range(blocks):
        lines = slice(b * padded, (b + 1) * padded)
        left.append(jnp.concatenate([to_gate[lines], to_up[lines]], axis=0))
    left = jnp.concatenate(left, axis=1)
    both, right = [], []
    for piece in gate_up:
        right += [piece[place] for place in range(piece.shape[0])]
    for place in range(0, len(right), 2):
        pair = jnp.concatenate(right[place : place + 2], axis=1)
        both.append(jnp.dot(left, pair, preferred_element_type=jnp.float32))
    both = jnp.concatenate(both, axis=1)
    gate, up = both[:count], both[padded : padded + count]
    activated = gate / (1.0 + jnp.exp(-gate)) * up
    step = min(units, MOE_FF)
    scaled = []
    for start in range(0, units, step):
        expert = (me * units + start) // MOE_FF
        share = at_lane(shares, lane, expert)
        scaled.append(activated[:, start : start + step] * share)
    scaled = jnp.concatenate(scaled, axis=1).astype(jnp.bfloat16)
    partial, start = 0.0, 0
    for piece in down:
        left = scaled[:, start : start + piece.shape[0]]
        partial += jnp.dot(left, piece[...], preferred_element_type=jnp.float32)
        start += piece.shape[0]
    home_dev = rows_dev - 1
    first = size * home_dev
    for owner in range(size):
        lines = slice(owner * home_dev, (owner + 1) * home_dev)
        mine = jnp.where(me == owner, 1.0, 0.0)
        finished[owner] = partial[lines] + hidden[lines] * mine
        line = slice(first + owner, first + owner + 1)
        ends_ref[owner : owner + 1] = partial[line] + hidden[line] * mine
    for end, out in zip(targets(me, size), homes):
        out[...] = finished[pl.ds(end, 1)][0].astype(jnp.bfloat16)
    half = width // 2
    for owner in range(size):
        guest = ends_ref[owner : owner + 1]
        block = jnp.concatenate([guest[:, :half], guest[:, half:]], axis=0).astype(jnp.bfloat16)
        for place in range(owner, guests.shape[0], size):
            guests[place] = block


def finish_kernel(size, spot, *refs):
    pieces, refs = refs[:size], refs[size:]
    guests, tail, out = refs
    homes = functools.reduce(jnp.add, [piece[...].astype(jnp.float32) for piece in pieces])
    came = guests[...].astype(jnp.float32)
    lane = lax.broadcasted_iota(jnp.int32, (1, LANES), 1)
    source = at_lane(tail[...], lane, spot).reshape(1, 1, 1)
    place = lax.broadcasted_iota(jnp.int32, (came.shape[0], 1, 1), 0) // size
    guest = jnp.sum(jnp.where(place.astype(jnp.float32) == source, came, 0.0), axis=0)
    guest = jnp.concatenate([guest[:1], guest[1:]], axis=1)
    out[...] = jnp.concatenate([homes, guest], axis=0).astype(jnp.bfloat16)


def shape(dims, dtype=jnp.float32):
    return jax.ShapeDtypeStruct(dims, dtype)


def shards(
    tokens,
    attn_gain,
    qkv_weight,
    out_weight,
    moe_gain,
    router,
    expert_gate_up,
    expert_down,
    kv_cache,
    page_table,
    home_len,
    guest_source,
    guest_pages,
    guest_len,
    routes,
):
    size = lax.axis_size("tensor")
    replicas = lax.axis_size("replica")
    rows_dev, width = tokens.shape
    npages = kv_cache.shape[0]
    top = routes.shape[1]
    units = expert_down.shape[0]
    part = out_weight.shape[0]
    columns = qkv_weight.shape[1]
    count = size * rows_dev
    chips = size // CORES
    home_dev = rows_dev - 1
    wide = width + LANES
    everyone = size * replicas
    blocks = units // LANES
    gate_up, down = [], []

    def load_more(after, ups, downs):
        first, last = ups[0] * blocks // 8, ups[1] * blocks // 8
        wanted = []
        if last > first:
            wanted.append((expert_gate_up, first, last - first))
        if downs[1] > downs[0]:
            wanted.append((expert_down, downs[0] * units // 8, (downs[1] - downs[0]) * units // 8))
        if not wanted:
            return after
        got = loaded(after, *wanted)
        for part in got:
            (gate_up if part.ndim == 3 else down).append(part)
        return got[0]

    packed = guest_source * FAR + guest_len
    offers, homes, plan, tail = pl.pallas_call(
        offer_kernel,
        out_shape=[
            shape((everyone, 2, (wide + LANES) // 2), jnp.bfloat16),
            shape((home_dev, wide), jnp.bfloat16),
            shape((npages, LANES)),
            shape((1, LANES)),
        ],
        in_specs=[ANY] * 5 + [SMEM],
        out_specs=[VMEM] * 4,
        scratch_shapes=[
            pltpu.VMEM(tokens.shape, tokens.dtype),
            pltpu.SMEM(routes.T.shape, jnp.int32),
            pltpu.SMEM(guest_pages.shape, jnp.int32),
            pltpu.VMEM(page_table.T.shape, jnp.int32),
            pltpu.VMEM((1,) + home_len.shape, jnp.int32),
            pltpu.SemaphoreType.DMA((5,)),
        ],
        compiler_params=PARAMS,
        name="offer",
    )(far(tokens), far(routes.T), far(guest_pages), far(page_table.T), far(home_len), packed)
    came = lax.all_to_all(offers, ("replica", "tensor"), 0, 0, tiled=True)
    messages = exchanged([homes] * size)
    (qkv_near,) = loaded(homes, (qkv_weight, 0, width))

    rows, *projected = pl.pallas_call(
        functools.partial(project_kernel, size, npages, top),
        out_shape=[shape((count, wide))] + [shape((CORES * SUB, columns), jnp.bfloat16)] * size,
        in_specs=[VMEM] * (size + 4),
        out_specs=[VMEM] * (size + 1),
        scratch_shapes=[
            pltpu.VMEM((size, home_dev, wide), jnp.float32),
            pltpu.VMEM((size * SUB, columns), jnp.float32),
        ],
        compiler_params=PARAMS,
        name="project",
    )(
        *messages,
        came,
        attn_gain.reshape(1, width),
        resident(qkv_near),
        plan,
    )
    joined = exchanged(projected)

    before = load_more(rows, (0, 2), (0, 2))
    late, _ = lax.optimization_barrier((out_weight, rows))
    out_mate = to_mate(late, size)
    cache_late, _ = lax.optimization_barrier((kv_cache, homes))
    cache_mate = to_mate(cache_late, size)
    terms = pl.pallas_call(
        functools.partial(attend_kernel, size, top),
        out_shape=[shape((CORES * SUB, CORES * part + LANES), jnp.bfloat16)] * chips,
        in_specs=[VMEM] * (size + 4) + [ANY],
        out_specs=[VMEM] * chips,
        scratch_shapes=[
            pltpu.VMEM((size, CORES * SUB, columns), jnp.float32),
            pltpu.VMEM((chips, CORES * SUB, CORES * part + LANES), jnp.float32),
        ],
        compiler_params=PARAMS,
        name="attend",
    )(*joined, resident(kv_cache), resident(cache_mate), rows, plan, before)
    arrived = across(terms, size)

    before = load_more(terms[0], (2, 5), (2, 4))
    partial = pl.pallas_call(
        functools.partial(out_kernel, size, npages),
        out_shape=shape((count, width), jnp.bfloat16),
        in_specs=[VMEM] * (chips + 3) + [ANY],
        out_specs=VMEM,
        compiler_params=PARAMS,
        name="out",
    )(*arrived, resident(out_weight), resident(out_mate), plan, before)
    sums = across([partial] * chips, size)

    load_more(partial, (5, 8), (4, 8))
    *pieces, guests = pl.pallas_call(
        functools.partial(
            expert_kernel, size, top, router.shape[1], len(gate_up), len(down)
        ),
        out_shape=[shape((home_dev, width), jnp.bfloat16)] * size
        + [shape((everyone, 2, width // 2), jnp.bfloat16)],
        in_specs=[VMEM] * (len(sums) + 3 + len(gate_up) + len(down)),
        out_specs=[VMEM] * (size + 1),
        scratch_shapes=[
            pltpu.VMEM((size, home_dev, width), jnp.float32),
            pltpu.VMEM((size, width), jnp.float32),
        ],
        compiler_params=PARAMS,
        name="experts",
    )(
        *sums,
        rows,
        moe_gain.reshape(1, width),
        router.T,
        *[resident(piece) for piece in gate_up + down],
    )
    guests = lax.all_to_all(guests, ("replica", "tensor"), 0, 0, tiled=True)
    pieces = exchanged(pieces)
    return pl.pallas_call(
        functools.partial(finish_kernel, size, top + 1 + MAXP),
        out_shape=shape((rows_dev, width), jnp.bfloat16),
        in_specs=[VMEM] * (size + 2),
        out_specs=VMEM,
        compiler_params=PARAMS,
        name="finish",
    )(*pieces, guests, tail)


def solution(mesh):
    placed = (
        P(("replica", "tensor"), None),
        P(),
        P(None, "tensor"),
        P("tensor", None),
        P(),
        P(),
        P(None, None, "tensor"),
        P("tensor", None),
        P(("replica", "tensor"), None, None, None),
        P("replica", None),
        P("replica"),
        P(("replica", "tensor")),
        P(("replica", "tensor"), None),
        P(("replica", "tensor")),
        P("replica", None),
    )
    return jax.shard_map(
        shards,
        mesh=mesh,
        in_specs=placed,
        out_specs=P(("replica", "tensor"), None),
        check_vma=False,
    )
```

```python
import functools

import jax
import jax.numpy as jnp
from jax import lax
from jax.experimental import pallas as pl
from jax.experimental.pallas import tpu as pltpu
from jax.sharding import PartitionSpec as P

HEADS = 12
KVH = 4
HD = 128
MOE_FF = 512
LANES = 128
SUB = 8
CORES = 2
FAR = 1024
EMPTY = -1e30
STEP = 16
MAXP = 2

VMEM = pl.BlockSpec(memory_space=pltpu.VMEM)
SMEM = pl.BlockSpec(memory_space=pltpu.SMEM)
ANY = pl.BlockSpec(memory_space=pl.ANY)
PARAMS = pltpu.CompilerParams(vmem_limit_bytes=16 * 2**20)


def resident(array):
    return pltpu.with_memory_space_constraint(array, pltpu.VMEM)


def far(array):
    return pltpu.with_memory_space_constraint(array, pltpu.HBM)


def normed(values, gain):
    inverse = lax.rsqrt(jnp.mean(values * values, axis=-1, keepdims=True) + 1e-05)
    return (values * inverse * gain).astype(jnp.bfloat16)


def ways(size):
    return [(chips, core) for chips in range(size // CORES) for core in range(CORES)][1:]


def target(me, size, way):
    chip = lax.rem(me // CORES + way[0], size // CORES)
    return chip * CORES + lax.rem(me + way[1], CORES)


def sender(me, size, way):
    chip = lax.rem(me // CORES + size // CORES - way[0], size // CORES)
    return chip * CORES + lax.rem(me + way[1], CORES)


def senders(me, size):
    return [me] + [sender(me, size, way) for way in ways(size)]


def targets(me, size):
    return [me] + [target(me, size, way) for way in ways(size)]


def exchanged(blocks):
    size = len(blocks)
    arrived = [blocks[0]]
    for way, block in zip(ways(size), blocks[1:]):
        pairs = []
        for me in range(size):
            chip = (me // CORES + way[0]) % (size // CORES)
            pairs.append((me, chip * CORES + (me + way[1]) % CORES))
        arrived.append(lax.ppermute(block, "tensor", pairs))
    return arrived


def to_step(rows):
    extra = -rows.shape[0] % STEP
    if not extra:
        return rows
    filler = jnp.zeros((extra, rows.shape[1]), jnp.float32)
    return jnp.concatenate([rows.astype(jnp.float32), filler], axis=0).astype(rows.dtype)


def lanes_of(numbers, lane):
    row = jnp.zeros(lane.shape, jnp.float32)
    for place, number in enumerate(numbers):
        row = jnp.where(lane == place, number.astype(jnp.float32), row)
    return row


def at_lane(rows, lane, place):
    return jnp.sum(jnp.where(lane == place, rows, 0.0), axis=-1, keepdims=True)


def across(block, size):
    arrived = [block]
    for chips in range(1, size // CORES):
        pairs = [(me, (me + chips * CORES) % size) for me in range(size)]
        arrived.append(lax.ppermute(block, "tensor", pairs))
    return arrived


def page_hits(plan, pages):
    return [jnp.where(plan[place : place + 1] == pages, 1.0, 0.0) for place in range(MAXP)]


def offer_kernel(tokens, paths, pages, table, lens, packed, *refs):
    offers, homes, plan, tail_out, rows, paths_s, pages_s, table_v, lens_v, sems = refs
    pairs = [
        (tokens, rows),
        (paths, paths_s),
        (pages, pages_s),
        (table, table_v),
        (lens, lens_v.at[0]),
    ]
    copies = [pltpu.make_async_copy(*pair, sems.at[i]) for i, pair in enumerate(pairs)]
    for copy in copies:
        copy.start()
    for copy in copies:
        copy.wait()
    me = lax.axis_index("tensor")
    rows_dev, width = rows.shape
    top = paths.shape[0]
    lane = lax.broadcasted_iota(jnp.int32, (1, LANES), 1)
    wide = rows[...].astype(jnp.float32)
    tails = []
    for slot in range(rows_dev):
        numbers = [paths_s[place, me * rows_dev + slot] for place in range(top)]
        if slot == rows_dev - 1:
            numbers += [packed[0] % FAR]
            numbers += [pages_s[0, place] for place in range(MAXP)]
            numbers += [packed[0] // FAR]
        tails.append(lanes_of(numbers, lane))
    tail_out[...] = tails[-1]
    full = jnp.concatenate([wide, jnp.concatenate(tails, axis=0)], axis=1)
    homes[...] = full[:-1].astype(jnp.bfloat16)
    guest = jnp.concatenate(
        [wide[-1:], tails[-1], jnp.zeros((1, LANES), jnp.float32)], axis=1
    )
    half = guest.shape[1] // 2
    block = jnp.concatenate([guest[:, :half], guest[:, half:]], axis=0).astype(jnp.bfloat16)
    for place in range(offers.shape[0]):
        offers[place] = block

    count = table.shape[1]
    npages = plan.shape[0]
    size = count * MAXP // (npages - MAXP)
    filler = jnp.zeros((1, LANES - count), jnp.float32)
    spots = lane - count
    lines = []
    for place in range(MAXP):
        ids = table_v[place : place + 1].astype(jnp.float32)
        ids = jnp.concatenate([ids, filler], axis=1)
        guests = (spots * npages + npages - MAXP + place).astype(jnp.float32)
        guests = jnp.where(spots < size, guests, -1.0)
        lines.append(jnp.where(spots < 0, ids, guests))
    lines.append(jnp.concatenate([lens_v[...].astype(jnp.float32), filler], axis=1))
    lines.append(jnp.zeros((npages - MAXP - 1, LANES), jnp.float32))
    plan[...] = jnp.concatenate(lines, axis=0)


def load_kernel(plans, *refs):
    sources, outs, sems = refs[1 : 1 + len(plans)], refs[1 + len(plans) : -1], refs[-1]
    copies = []

    def copy(source, out):
        copies.append(pltpu.make_async_copy(source, out, sems.at[len(copies)]))

    for (first, count, pieces), source, out in zip(plans, sources, outs):
        each = source.shape[0] // pieces if len(out.shape) == 4 else count // pieces
        for piece in range(pieces):
            lines = pl.ds(piece * each, each)
            if len(out.shape) == 4:
                for place in range(count):
                    columns = pl.ds((first + place) * LANES, LANES)
                    copy(source.at[lines, :, columns], out.at[place, lines])
            else:
                copy(source.at[pl.ds(first + piece * each, each)], out.at[lines])
    for made in copies:
        made.start()
    for made in copies:
        made.wait()


def loaded(after, *wanted):
    shapes, plans, copies = [], [], 0
    for array, first, count in wanted:
        if array.ndim == 3:
            shapes.append(shape((count,) + array.shape[:2] + (LANES,), array.dtype))
            plans.append((first, count, 2))
            copies += 2 * count
        else:
            shapes.append(shape((count, array.shape[1]), array.dtype))
            plans.append((first, count, 4))
            copies += 4
    parts = pl.pallas_call(
        functools.partial(load_kernel, tuple(plans)),
        out_shape=shapes,
        in_specs=[ANY] * (1 + len(wanted)),
        out_specs=[VMEM] * len(wanted),
        scratch_shapes=[pltpu.SemaphoreType.DMA((copies,))],
        compiler_params=PARAMS,
        cost_estimate=pl.CostEstimate(
            flops=0, bytes_accessed=sum(2 * part.size for part in shapes), transcendentals=0
        ),
        name="load",
    )(after, *[far(array) for array, _, _ in wanted])
    return [
        part.reshape(part.shape[0], -1, LANES) if part.ndim == 4 else part for part in parts
    ]


def project_kernel(size, npages, top, *refs):
    blocks, refs = refs[:size], refs[size:]
    offers, gain, weight, plan, rows_ref = refs[:5]
    outs = refs[5 : 5 + size]
    gathered, paged = refs[5 + size :]
    me = lax.axis_index("tensor")
    replica = lax.axis_index("replica").astype(jnp.float32)
    home_dev = blocks[0].shape[0]
    homes = size * home_dev
    width, columns = weight.shape
    for owner, block in zip(senders(me, size), blocks):
        gathered[pl.ds(owner, 1)] = block[...].astype(jnp.float32)[None]
    came = offers[...].astype(jnp.float32)
    half = came.shape[2]
    lane = lax.broadcasted_iota(jnp.int32, (1, 1, half), 2)
    spot = width + top + 1 + MAXP - half
    source = jnp.sum(jnp.where(lane == spot, came[:, 1:], 0.0), axis=2, keepdims=True)
    picked = jnp.where(source == replica, came, 0.0)
    picked = jnp.sum(picked.reshape(-1, size, 2, half), axis=0)
    for owner in range(size):
        rows_ref[owner * home_dev : (owner + 1) * home_dev] = gathered[owner]
        guest = jnp.concatenate([picked[owner, :1], picked[owner, 1:]], axis=1)
        rows_ref[homes + owner : homes + owner + 1] = guest[:, : width + LANES]
    norm = to_step(normed(rows_ref[:, :width], gain[...]))
    products = jnp.dot(norm, weight[...], preferred_element_type=jnp.float32)
    line = lax.broadcasted_iota(jnp.int32, (size * SUB, LANES), 0)
    ids = line // SUB * npages + line % SUB
    ids = jnp.where(line % SUB < npages, ids, -2).astype(jnp.float32)
    hits = sum(page_hits(plan[...], ids))[:, : norm.shape[0]]
    paged[...] = jnp.dot(
        hits.astype(jnp.bfloat16), products.astype(jnp.bfloat16), preferred_element_type=jnp.float32
    )
    for end, out in zip(targets(me, size), outs):
        start = pl.multiple_of(end * SUB, SUB)
        out[...] = paged[pl.ds(start, SUB)][:npages].astype(jnp.bfloat16)


def attend_kernel(size, top, *refs):
    blocks, refs = refs[:size], refs[size:]
    cache, rows_ref, plan_ref, _ = refs[:4]
    outs = refs[4 : 4 + size]
    gathered, terms = refs[4 + size :]
    me = lax.axis_index("tensor")
    npages, _, page_len, _ = cache.shape
    home_pages = npages - MAXP
    homes = home_pages // MAXP * size
    group = HEADS // KVH
    qwidth, kwidth = HEADS * HD, KVH * HD
    width = rows_ref.shape[1] - LANES
    for owner, block in zip(senders(me, size), blocks):
        gathered[pl.ds(owner, 1), :npages] = block[...].astype(jnp.float32)[None]
    joined = jnp.concatenate([gathered[owner] for owner in range(size)], axis=1)

    plan = plan_ref[...]
    line = lax.broadcasted_iota(jnp.int32, (SUB, LANES), 0)
    hits = page_hits(plan, (me * npages + line).astype(jnp.float32))
    left = sum(
        hit * (plan[MAXP : MAXP + 1] - float(place * page_len)) for place, hit in enumerate(hits)
    )
    left = jnp.sum(left, axis=1, keepdims=True)
    leads = jnp.sum(hits[0], axis=1, keepdims=True)
    tails = rows_ref[:, width:]
    place = lax.broadcasted_iota(jnp.int32, tails.shape, 0)
    numbers = jnp.sum(jnp.where(place == homes + me, tails, 0.0), axis=0, keepdims=True)
    lane = lax.broadcasted_iota(jnp.int32, (1, LANES), 1)
    near_len = at_lane(numbers, lane, top)
    line = line[:, :1]
    near_left, near_lead = jnp.zeros((SUB, 1), jnp.float32), None
    for place in range(MAXP):
        named = at_lane(numbers, lane, top + 1 + place) == line.astype(jnp.float32)
        near_left = jnp.where(named, near_len - float(place * page_len), near_left)
        if place == 0:
            near_lead = jnp.where(named, 1.0, 0.0)
    left = jnp.where(line < home_pages, left, near_left)
    leads = jnp.where(line < home_pages, leads, near_lead)
    row = lax.broadcasted_iota(jnp.int32, (SUB, npages * page_len), 0)
    spot = lax.broadcasted_iota(jnp.int32, (SUB, npages * page_len), 1)
    inside = (spot - row * page_len).astype(jnp.float32)
    usable = jnp.where((inside >= 0.0) & (inside < jnp.minimum(left, float(page_len))), 1.0, 0.0)
    usable = jnp.concatenate([usable] * HEADS, axis=0) > 0.5
    leads = jnp.concatenate([leads] * HEADS, axis=0) > 0.5

    query = jnp.concatenate([joined[:, h * HD : (h + 1) * HD] for h in range(HEADS)], axis=0)
    fresh_key, fresh_value = [
        jnp.concatenate(
            [joined[:, start + h // group * HD : start + (h // group + 1) * HD] for h in range(HEADS)],
            axis=0,
        )
        for start in (qwidth, qwidth + kwidth)
    ]
    lines = group * SUB
    narrow = query.astype(jnp.bfloat16)
    scores = []
    for kv in range(KVH):
        keys = cache[:, 0, :, kv * HD : (kv + 1) * HD].reshape(npages * page_len, HD)
        scores.append(
            lax.dot_general(
                narrow[kv * lines : (kv + 1) * lines],
                keys,
                (((1,), (1,)), ((), ())),
                preferred_element_type=jnp.float32,
            )
        )
    scores = jnp.concatenate(scores, axis=0) * HD ** (-0.5)
    scores = jnp.where(usable, scores, EMPTY)
    own = jnp.sum(query * fresh_key, axis=-1, keepdims=True) * HD ** (-0.5)
    own = jnp.where(leads, own, EMPTY)
    peak = jnp.maximum(jnp.max(scores, axis=-1, keepdims=True), own)
    weights = jnp.where(usable, jnp.exp(scores - peak), 0.0)
    newest = jnp.where(leads, jnp.exp(own - peak), 0.0)
    total = jnp.sum(weights, axis=-1, keepdims=True) + newest
    narrow = weights.astype(jnp.bfloat16)
    summed = []
    for kv in range(KVH):
        values = cache[:, 1, :, kv * HD : (kv + 1) * HD].reshape(npages * page_len, HD)
        summed.append(
            jnp.dot(
                narrow[kv * lines : (kv + 1) * lines], values, preferred_element_type=jnp.float32
            )
        )
    summed = jnp.concatenate(summed, axis=0) + newest * fresh_value
    used = total > 0.0
    safe = jnp.where(used, total, 1.0)
    mixed = summed / safe
    level = jnp.where(used, peak + jnp.log(safe), EMPTY)
    lane = lax.broadcasted_iota(jnp.int32, (SUB, LANES), 1)
    levels = jnp.zeros((SUB, LANES), jnp.float32)
    for h in range(HEADS):
        levels = jnp.where(lane % STEP == h, level[h * SUB : (h + 1) * SUB], levels)
    upper = levels.astype(jnp.bfloat16).astype(jnp.float32)
    rest = levels - upper
    middle = rest.astype(jnp.bfloat16).astype(jnp.float32)
    levels = jnp.where(lane < STEP, upper, jnp.where(lane < 2 * STEP, middle, rest - middle))
    levels = jnp.where(lane < 3 * STEP, levels, 0.0)
    mixes = jnp.concatenate([mixed[h * SUB : (h + 1) * SUB] for h in range(HEADS)], axis=1)
    chips = size // CORES
    part = qwidth // chips
    for chip in range(chips):
        terms[chip] = jnp.concatenate([mixes[:, chip * part : (chip + 1) * part], levels], axis=1)
    for end, out in zip(targets(me, size), outs):
        out[...] = terms[pl.ds(end // CORES, 1)][0, :npages].astype(jnp.bfloat16)


def out_kernel(size, npages, *refs):
    blocks, refs = refs[:size], refs[size:]
    weight, mate_weight, plan, _, out = refs
    me = lax.axis_index("tensor")
    part = CORES * weight.shape[0]
    terms, ids = [], []
    line = lax.broadcasted_iota(jnp.int32, (SUB, LANES), 0)
    filler = jnp.zeros((SUB - npages, part + LANES), jnp.float32)
    for owner, block in zip(senders(me, size), blocks):
        terms += [block[...].astype(jnp.float32), filler]
        ids.append(jnp.where(line < npages, owner * npages + line, -2))
    terms = jnp.concatenate(terms, axis=0).astype(jnp.bfloat16)
    ids = jnp.concatenate(ids, axis=0).astype(jnp.float32)
    spread = lax.broadcasted_iota(jnp.int32, (LANES, part), 0)
    head = (lax.broadcasted_iota(jnp.int32, (LANES, part), 1) + me // CORES * part) // HD
    spread = jnp.where((spread % STEP == head) & (spread < 3 * STEP), 1.0, 0.0)
    spread = spread.astype(jnp.bfloat16)
    count = out.shape[0]
    rows = count + -count % STEP
    mixes, levels = [], []
    for hit in page_hits(plan[...], ids):
        picked = lax.dot_general(
            hit[:, :rows].astype(jnp.bfloat16),
            terms,
            (((0,), (0,)), ((), ())),
            preferred_element_type=jnp.float32,
        )
        mixes.append(picked[:, :part])
        levels.append(
            jnp.dot(
                picked[:, part:].astype(jnp.bfloat16), spread, preferred_element_type=jnp.float32
            )
        )
    highest = functools.reduce(jnp.maximum, levels)
    factors = [jnp.exp(level - highest) for level in levels]
    mixed = sum(mix * factor for mix, factor in zip(mixes, factors)) / sum(factors)
    halves = mixed[:, : part // CORES], mixed[:, part // CORES :]
    first = lax.rem(me, CORES) == 0
    own = jnp.where(first, halves[0], halves[1]).astype(jnp.bfloat16)
    other = jnp.where(first, halves[1], halves[0]).astype(jnp.bfloat16)
    products = jnp.dot(own, weight[...], preferred_element_type=jnp.float32)
    products += jnp.dot(other, mate_weight[...], preferred_element_type=jnp.float32)
    out[...] = products[:count].astype(jnp.bfloat16)


def expert_kernel(size, top, experts, parts, lows, *refs):
    chips = size // CORES
    sums, refs = refs[:chips], refs[chips:]
    rows_ref, gain, router = refs[:3]
    gate_up, refs = refs[3 : 3 + parts], refs[3 + parts :]
    down, refs = refs[:lows], refs[lows:]
    units = sum(piece.shape[0] for piece in down)
    homes, guests, finished, ends_ref = refs[:size], refs[size], refs[size + 1], refs[size + 2]
    me = lax.axis_index("tensor")
    count = rows_ref.shape[0]
    width = rows_ref.shape[1] - LANES
    rows_dev = count // size
    total = functools.reduce(jnp.add, [piece[...].astype(jnp.float32) for piece in sums])
    hidden = (rows_ref[:, :width] + total).astype(jnp.bfloat16).astype(jnp.float32)
    norm = normed(hidden, gain[...])
    lane = lax.broadcasted_iota(jnp.int32, (count, LANES), 1)
    numbers = rows_ref[:, width:]
    logits = lax.dot_general(
        norm, router[...], (((1,), (1,)), ((), ())), preferred_element_type=jnp.float32
    )
    logits = jnp.concatenate(
        [logits, jnp.zeros((count, LANES - experts), jnp.float32)], axis=1
    )
    routed = jnp.zeros((count, LANES), jnp.float32)
    for place in range(top):
        route = at_lane(numbers, lane, place)
        routed = jnp.where(lane.astype(jnp.float32) == route, 1.0, routed)
    logits = jnp.where(routed > 0.5, logits, EMPTY)
    shares = jnp.where(
        routed > 0.5, jnp.exp(logits - jnp.max(logits, axis=-1, keepdims=True)), 0.0
    )
    shares = shares / jnp.sum(shares, axis=-1, keepdims=True)

    here = lax.broadcasted_iota(jnp.int32, (LANES, 2 * LANES), 0)
    there = lax.broadcasted_iota(jnp.int32, (LANES, 2 * LANES), 1)
    evens = jnp.where(there == 2 * here, 1.0, 0.0).astype(jnp.bfloat16)
    odds = jnp.where(there == 2 * here + 1, 1.0, 0.0).astype(jnp.bfloat16)
    wide = to_step(norm)
    padded = wide.shape[0]
    blocks = width // LANES
    tall = jnp.concatenate([wide[:, b * LANES : (b + 1) * LANES] for b in range(blocks)], axis=0)
    to_gate = jnp.dot(tall, evens, preferred_element_type=jnp.float32).astype(jnp.bfloat16)
    to_up = jnp.dot(tall, odds, preferred_element_type=jnp.float32).astype(jnp.bfloat16)
    left = []
    for b in range(blocks):
        lines = slice(b * padded, (b + 1) * padded)
        left.append(jnp.concatenate([to_gate[lines], to_up[lines]], axis=0))
    left = jnp.concatenate(left, axis=1)
    both, right = [], []
    for piece in gate_up:
        right += [piece[place] for place in range(piece.shape[0])]
    for place in range(0, len(right), 2):
        pair = jnp.concatenate(right[place : place + 2], axis=1)
        both.append(jnp.dot(left, pair, preferred_element_type=jnp.float32))
    both = jnp.concatenate(both, axis=1)
    gate, up = both[:count], both[padded : padded + count]
    activated = gate / (1.0 + jnp.exp(-gate)) * up
    step = min(units, MOE_FF)
    scaled = []
    for start in range(0, units, step):
        expert = (me * units + start) // MOE_FF
        share = at_lane(shares, lane, expert)
        scaled.append(activated[:, start : start + step] * share)
    scaled = jnp.concatenate(scaled, axis=1).astype(jnp.bfloat16)
    partial, start = 0.0, 0
    for piece in down:
        left = scaled[:, start : start + piece.shape[0]]
        partial += jnp.dot(left, piece[...], preferred_element_type=jnp.float32)
        start += piece.shape[0]
    home_dev = rows_dev - 1
    first = size * home_dev
    for owner in range(size):
        lines = slice(owner * home_dev, (owner + 1) * home_dev)
        mine = jnp.where(me == owner, 1.0, 0.0)
        finished[owner] = partial[lines] + hidden[lines] * mine
        line = slice(first + owner, first + owner + 1)
        ends_ref[owner : owner + 1] = partial[line] + hidden[line] * mine
    for end, out in zip(targets(me, size), homes):
        out[...] = finished[pl.ds(end, 1)][0].astype(jnp.bfloat16)
    half = width // 2
    for owner in range(size):
        guest = ends_ref[owner : owner + 1]
        block = jnp.concatenate([guest[:, :half], guest[:, half:]], axis=0).astype(jnp.bfloat16)
        for place in range(owner, guests.shape[0], size):
            guests[place] = block


def finish_kernel(size, spot, *refs):
    pieces, refs = refs[:size], refs[size:]
    guests, tail, out = refs
    homes = functools.reduce(jnp.add, [piece[...].astype(jnp.float32) for piece in pieces])
    came = guests[...].astype(jnp.float32)
    lane = lax.broadcasted_iota(jnp.int32, (1, LANES), 1)
    source = at_lane(tail[...], lane, spot).reshape(1, 1, 1)
    place = lax.broadcasted_iota(jnp.int32, (came.shape[0], 1, 1), 0) // size
    guest = jnp.sum(jnp.where(place.astype(jnp.float32) == source, came, 0.0), axis=0)
    guest = jnp.concatenate([guest[:1], guest[1:]], axis=1)
    out[...] = jnp.concatenate([homes, guest], axis=0).astype(jnp.bfloat16)


def shape(dims, dtype=jnp.float32):
    return jax.ShapeDtypeStruct(dims, dtype)


def shards(
    tokens,
    attn_gain,
    qkv_weight,
    out_weight,
    moe_gain,
    router,
    expert_gate_up,
    expert_down,
    kv_cache,
    page_table,
    home_len,
    guest_source,
    guest_pages,
    guest_len,
    routes,
):
    size = lax.axis_size("tensor")
    replicas = lax.axis_size("replica")
    rows_dev, width = tokens.shape
    npages = kv_cache.shape[0]
    top = routes.shape[1]
    units = expert_down.shape[0]
    part = out_weight.shape[0]
    columns = qkv_weight.shape[1]
    count = size * rows_dev
    home_dev = rows_dev - 1
    wide = width + LANES
    everyone = size * replicas
    blocks = units // LANES
    gate_up, down = [], []

    def load_more(after, ups, downs):
        first, last = ups[0] * blocks // 8, ups[1] * blocks // 8
        wanted = []
        if last > first:
            wanted.append((expert_gate_up, first, last - first))
        if downs[1] > downs[0]:
            wanted.append((expert_down, downs[0] * units // 8, (downs[1] - downs[0]) * units // 8))
        if not wanted:
            return after
        got = loaded(after, *wanted)
        for part in got:
            (gate_up if part.ndim == 3 else down).append(part)
        return got[0]

    packed = guest_source * FAR + guest_len
    offers, homes, plan, tail = pl.pallas_call(
        offer_kernel,
        out_shape=[
            shape((everyone, 2, (wide + LANES) // 2), jnp.bfloat16),
            shape((home_dev, wide), jnp.bfloat16),
            shape((npages, LANES)),
            shape((1, LANES)),
        ],
        in_specs=[ANY] * 5 + [SMEM],
        out_specs=[VMEM] * 4,
        scratch_shapes=[
            pltpu.VMEM(tokens.shape, tokens.dtype),
            pltpu.SMEM(routes.T.shape, jnp.int32),
            pltpu.SMEM(guest_pages.shape, jnp.int32),
            pltpu.VMEM(page_table.T.shape, jnp.int32),
            pltpu.VMEM((1,) + home_len.shape, jnp.int32),
            pltpu.SemaphoreType.DMA((5,)),
        ],
        compiler_params=PARAMS,
        name="offer",
    )(far(tokens), far(routes.T), far(guest_pages), far(page_table.T), far(home_len), packed)
    came = lax.all_to_all(offers, ("replica", "tensor"), 0, 0, tiled=True)
    messages = exchanged([homes] * size)
    (qkv_near,) = loaded(homes, (qkv_weight, 0, width))

    rows, *projected = pl.pallas_call(
        functools.partial(project_kernel, size, npages, top),
        out_shape=[shape((count, wide))] + [shape((npages, columns), jnp.bfloat16)] * size,
        in_specs=[VMEM] * (size + 4),
        out_specs=[VMEM] * (size + 1),
        scratch_shapes=[
            pltpu.VMEM((size, home_dev, wide), jnp.float32),
            pltpu.VMEM((size * SUB, columns), jnp.float32),
        ],
        compiler_params=PARAMS,
        name="project",
    )(
        *messages,
        came,
        attn_gain.reshape(1, width),
        resident(qkv_near),
        plan,
    )
    joined = exchanged(projected)

    before = load_more(rows, (0, 2), (0, 4))
    late, _ = lax.optimization_barrier((out_weight, rows))
    out_mate = lax.ppermute(late, "tensor", [(me, me ^ 1) for me in range(size)])
    terms = pl.pallas_call(
        functools.partial(attend_kernel, size, top),
        out_shape=[shape((npages, CORES * part + LANES), jnp.bfloat16)] * size,
        in_specs=[VMEM] * (size + 3) + [ANY],
        out_specs=[VMEM] * size,
        scratch_shapes=[
            pltpu.VMEM((size, SUB, columns), jnp.float32),
            pltpu.VMEM((size // CORES, SUB, CORES * part + LANES), jnp.float32),
        ],
        compiler_params=PARAMS,
        name="attend",
    )(*joined, resident(kv_cache), rows, plan, before)
    arrived = exchanged(terms)

    before = load_more(terms[0], (2, 5), (4, 6))
    partial = pl.pallas_call(
        functools.partial(out_kernel, size, npages),
        out_shape=shape((count, width), jnp.bfloat16),
        in_specs=[VMEM] * (size + 3) + [ANY],
        out_specs=VMEM,
        compiler_params=PARAMS,
        name="out",
    )(*arrived, resident(out_weight), resident(out_mate), plan, before)
    sums = across(partial, size)

    load_more(partial, (5, 8), (6, 8))
    *pieces, guests = pl.pallas_call(
        functools.partial(
            expert_kernel, size, top, router.shape[1], len(gate_up), len(down)
        ),
        out_shape=[shape((home_dev, width), jnp.bfloat16)] * size
        + [shape((everyone, 2, width // 2), jnp.bfloat16)],
        in_specs=[VMEM] * (len(sums) + 3 + len(gate_up) + len(down)),
        out_specs=[VMEM] * (size + 1),
        scratch_shapes=[
            pltpu.VMEM((size, home_dev, width), jnp.float32),
            pltpu.VMEM((size, width), jnp.float32),
        ],
        compiler_params=PARAMS,
        name="experts",
    )(
        *sums,
        rows,
        moe_gain.reshape(1, width),
        router.T,
        *[resident(piece) for piece in gate_up + down],
    )
    guests = lax.all_to_all(guests, ("replica", "tensor"), 0, 0, tiled=True)
    pieces = exchanged(pieces)
    return pl.pallas_call(
        functools.partial(finish_kernel, size, top + 1 + MAXP),
        out_shape=shape((rows_dev, width), jnp.bfloat16),
        in_specs=[VMEM] * (size + 2),
        out_specs=VMEM,
        compiler_params=PARAMS,
        name="finish",
    )(*pieces, guests, tail)


def solution(mesh):
    placed = (
        P(("replica", "tensor"), None),
        P(),
        P(None, "tensor"),
        P("tensor", None),
        P(),
        P(),
        P(None, None, "tensor"),
        P("tensor", None),
        P(("replica", "tensor"), None, None, None),
        P("replica", None),
        P("replica"),
        P(("replica", "tensor")),
        P(("replica", "tensor"), None),
        P(("replica", "tensor")),
        P("replica", None),
    )
    return jax.shard_map(
        shards,
        mesh=mesh,
        in_specs=placed,
        out_specs=P(("replica", "tensor"), None),
        check_vma=False,
    )
```

```python
import functools

import jax
import jax.numpy as jnp
from jax import lax
from jax.experimental import pallas as pl
from jax.experimental.pallas import tpu as pltpu
from jax.sharding import PartitionSpec as P

HEADS = 12
KVH = 4
HD = 128
MOE_FF = 512
LANES = 128
SUB = 8
CORES = 2
FAR = 1024
EMPTY = -1e30
STEP = 16
MAXP = 2

VMEM = pl.BlockSpec(memory_space=pltpu.VMEM)
SMEM = pl.BlockSpec(memory_space=pltpu.SMEM)
ANY = pl.BlockSpec(memory_space=pl.ANY)
PARAMS = pltpu.CompilerParams(vmem_limit_bytes=16 * 2**20)


def resident(array):
    return pltpu.with_memory_space_constraint(array, pltpu.VMEM)


def far(array):
    return pltpu.with_memory_space_constraint(array, pltpu.HBM)


def normed(values, gain):
    inverse = lax.rsqrt(jnp.mean(values * values, axis=-1, keepdims=True) + 1e-05)
    return (values * inverse * gain).astype(jnp.bfloat16)


def ways(size):
    return [(chips, core) for chips in range(size // CORES) for core in range(CORES)][1:]


def target(me, size, way):
    chip = lax.rem(me // CORES + way[0], size // CORES)
    return chip * CORES + lax.rem(me + way[1], CORES)


def sender(me, size, way):
    chip = lax.rem(me // CORES + size // CORES - way[0], size // CORES)
    return chip * CORES + lax.rem(me + way[1], CORES)


def senders(me, size):
    return [me] + [sender(me, size, way) for way in ways(size)]


def targets(me, size):
    return [me] + [target(me, size, way) for way in ways(size)]


def exchanged(blocks):
    size = len(blocks)
    arrived = [blocks[0]]
    for way, block in zip(ways(size), blocks[1:]):
        pairs = []
        for me in range(size):
            chip = (me // CORES + way[0]) % (size // CORES)
            pairs.append((me, chip * CORES + (me + way[1]) % CORES))
        arrived.append(lax.ppermute(block, "tensor", pairs))
    return arrived


def to_step(rows):
    extra = -rows.shape[0] % STEP
    if not extra:
        return rows
    filler = jnp.zeros((extra, rows.shape[1]), jnp.float32)
    return jnp.concatenate([rows.astype(jnp.float32), filler], axis=0).astype(rows.dtype)


def lanes_of(numbers, lane):
    row = jnp.zeros(lane.shape, jnp.float32)
    for place, number in enumerate(numbers):
        row = jnp.where(lane == place, number.astype(jnp.float32), row)
    return row


def at_lane(rows, lane, place):
    return jnp.sum(jnp.where(lane == place, rows, 0.0), axis=-1, keepdims=True)


def across(block, size):
    arrived = [block]
    for chips in range(1, size // CORES):
        pairs = [(me, (me + chips * CORES) % size) for me in range(size)]
        arrived.append(lax.ppermute(block, "tensor", pairs))
    return arrived


def to_everyone(blocks):
    order = tuple(reversed(range(blocks.shape[0])))
    return lax.all_to_all(
        blocks, ("replica", "tensor"), 0, 0, axis_index_groups=[order], tiled=True
    )


def page_hits(plan, pages):
    return [jnp.where(plan[place : place + 1] == pages, 1.0, 0.0) for place in range(MAXP)]


def offer_kernel(tokens, paths, pages, table, lens, packed, *refs):
    offers, homes, plan, tail_out, rows, paths_s, pages_s, table_v, lens_v, sems = refs
    pairs = [
        (tokens, rows),
        (paths, paths_s),
        (pages, pages_s),
        (table, table_v),
        (lens, lens_v.at[0]),
    ]
    copies = [pltpu.make_async_copy(*pair, sems.at[i]) for i, pair in enumerate(pairs)]
    for copy in copies:
        copy.start()
    for copy in copies:
        copy.wait()
    me = lax.axis_index("tensor")
    rows_dev, width = rows.shape
    top = paths.shape[0]
    lane = lax.broadcasted_iota(jnp.int32, (1, LANES), 1)
    wide = rows[...].astype(jnp.float32)
    tails = []
    for slot in range(rows_dev):
        numbers = [paths_s[place, me * rows_dev + slot] for place in range(top)]
        if slot == rows_dev - 1:
            numbers += [packed[0] % FAR]
            numbers += [pages_s[0, place] for place in range(MAXP)]
            numbers += [packed[0] // FAR]
        tails.append(lanes_of(numbers, lane))
    tail_out[...] = tails[-1]
    full = jnp.concatenate([wide, jnp.concatenate(tails, axis=0)], axis=1)
    homes[...] = full[:-1].astype(jnp.bfloat16)
    guest = jnp.concatenate(
        [wide[-1:], tails[-1], jnp.zeros((1, LANES), jnp.float32)], axis=1
    )
    half = guest.shape[1] // 2
    block = jnp.concatenate([guest[:, :half], guest[:, half:]], axis=0).astype(jnp.bfloat16)
    for place in range(offers.shape[0]):
        offers[place] = block

    count = table.shape[1]
    npages = plan.shape[0]
    size = count * MAXP // (npages - MAXP)
    filler = jnp.zeros((1, LANES - count), jnp.float32)
    spots = lane - count
    lines = []
    for place in range(MAXP):
        ids = table_v[place : place + 1].astype(jnp.float32)
        ids = jnp.concatenate([ids, filler], axis=1)
        guests = (spots * npages + npages - MAXP + place).astype(jnp.float32)
        guests = jnp.where(spots < size, guests, -1.0)
        lines.append(jnp.where(spots < 0, ids, guests))
    lines.append(jnp.concatenate([lens_v[...].astype(jnp.float32), filler], axis=1))
    lines.append(jnp.zeros((npages - MAXP - 1, LANES), jnp.float32))
    plan[...] = jnp.concatenate(lines, axis=0)


def load_kernel(plans, *refs):
    sources, outs, sems = refs[1 : 1 + len(plans)], refs[1 + len(plans) : -1], refs[-1]
    copies = []

    def copy(source, out):
        copies.append(pltpu.make_async_copy(source, out, sems.at[len(copies)]))

    for (first, count, pieces), source, out in zip(plans, sources, outs):
        each = source.shape[0] // pieces if len(out.shape) == 4 else count // pieces
        for piece in range(pieces):
            lines = pl.ds(piece * each, each)
            if len(out.shape) == 4:
                for place in range(count):
                    columns = pl.ds((first + place) * LANES, LANES)
                    copy(source.at[lines, :, columns], out.at[place, lines])
            else:
                copy(source.at[pl.ds(first + piece * each, each)], out.at[lines])
    for made in copies:
        made.start()
    for made in copies:
        made.wait()


def loaded(after, *wanted):
    shapes, plans, copies = [], [], 0
    for array, first, count in wanted:
        if array.ndim == 3:
            shapes.append(shape((count,) + array.shape[:2] + (LANES,), array.dtype))
            plans.append((first, count, 2))
            copies += 2 * count
        else:
            shapes.append(shape((count, array.shape[1]), array.dtype))
            plans.append((first, count, 4))
            copies += 4
    parts = pl.pallas_call(
        functools.partial(load_kernel, tuple(plans)),
        out_shape=shapes,
        in_specs=[ANY] * (1 + len(wanted)),
        out_specs=[VMEM] * len(wanted),
        scratch_shapes=[pltpu.SemaphoreType.DMA((copies,))],
        compiler_params=PARAMS,
        cost_estimate=pl.CostEstimate(
            flops=0, bytes_accessed=sum(2 * part.size for part in shapes), transcendentals=0
        ),
        name="load",
    )(after, *[far(array) for array, _, _ in wanted])
    return [
        part.reshape(part.shape[0], -1, LANES) if part.ndim == 4 else part for part in parts
    ]


def project_kernel(size, npages, top, *refs):
    blocks, refs = refs[:size], refs[size:]
    offers, gain, weight, plan, rows_ref = refs[:5]
    outs = refs[5 : 5 + size]
    gathered, paged = refs[5 + size :]
    me = lax.axis_index("tensor")
    replica = lax.axis_index("replica").astype(jnp.float32)
    home_dev = blocks[0].shape[0]
    homes = size * home_dev
    width, columns = weight.shape
    for owner, block in zip(senders(me, size), blocks):
        gathered[pl.ds(owner, 1)] = block[...].astype(jnp.float32)[None]
    came = offers[...].astype(jnp.float32)
    half = came.shape[2]
    lane = lax.broadcasted_iota(jnp.int32, (1, 1, half), 2)
    spot = width + top + 1 + MAXP - half
    source = jnp.sum(jnp.where(lane == spot, came[:, 1:], 0.0), axis=2, keepdims=True)
    picked = jnp.where(source == replica, came, 0.0)
    picked = jnp.sum(picked.reshape(-1, size, 2, half), axis=0)
    for owner in range(size):
        rows_ref[owner * home_dev : (owner + 1) * home_dev] = gathered[owner]
        place = size - 1 - owner
        guest = jnp.concatenate([picked[place, :1], picked[place, 1:]], axis=1)
        rows_ref[homes + owner : homes + owner + 1] = guest[:, : width + LANES]
    norm = to_step(normed(rows_ref[:, :width], gain[...]))
    products = jnp.dot(norm, weight[...], preferred_element_type=jnp.float32)
    line = lax.broadcasted_iota(jnp.int32, (size * SUB, LANES), 0)
    ids = line // SUB * npages + line % SUB
    ids = jnp.where(line % SUB < npages, ids, -2).astype(jnp.float32)
    hits = sum(page_hits(plan[...], ids))[:, : norm.shape[0]]
    paged[...] = jnp.dot(
        hits.astype(jnp.bfloat16), products.astype(jnp.bfloat16), preferred_element_type=jnp.float32
    )
    for end, out in zip(targets(me, size), outs):
        start = pl.multiple_of(end * SUB, SUB)
        out[...] = paged[pl.ds(start, SUB)][:npages].astype(jnp.bfloat16)


def attend_kernel(size, top, *refs):
    blocks, refs = refs[:size], refs[size:]
    cache, rows_ref, plan_ref, _ = refs[:4]
    outs = refs[4 : 4 + size]
    gathered, terms = refs[4 + size :]
    me = lax.axis_index("tensor")
    npages, _, page_len, _ = cache.shape
    home_pages = npages - MAXP
    homes = home_pages // MAXP * size
    group = HEADS // KVH
    qwidth, kwidth = HEADS * HD, KVH * HD
    width = rows_ref.shape[1] - LANES
    for owner, block in zip(senders(me, size), blocks):
        gathered[pl.ds(owner, 1), :npages] = block[...].astype(jnp.float32)[None]
    joined = jnp.concatenate([gathered[owner] for owner in range(size)], axis=1)

    plan = plan_ref[...]
    line = lax.broadcasted_iota(jnp.int32, (SUB, LANES), 0)
    hits = page_hits(plan, (me * npages + line).astype(jnp.float32))
    left = sum(
        hit * (plan[MAXP : MAXP + 1] - float(place * page_len)) for place, hit in enumerate(hits)
    )
    left = jnp.sum(left, axis=1, keepdims=True)
    leads = jnp.sum(hits[0], axis=1, keepdims=True)
    tails = rows_ref[:, width:]
    place = lax.broadcasted_iota(jnp.int32, tails.shape, 0)
    numbers = jnp.sum(jnp.where(place == homes + me, tails, 0.0), axis=0, keepdims=True)
    lane = lax.broadcasted_iota(jnp.int32, (1, LANES), 1)
    near_len = at_lane(numbers, lane, top)
    line = line[:, :1]
    near_left, near_lead = jnp.zeros((SUB, 1), jnp.float32), None
    for place in range(MAXP):
        named = at_lane(numbers, lane, top + 1 + place) == line.astype(jnp.float32)
        near_left = jnp.where(named, near_len - float(place * page_len), near_left)
        if place == 0:
            near_lead = jnp.where(named, 1.0, 0.0)
    left = jnp.where(line < home_pages, left, near_left)
    leads = jnp.where(line < home_pages, leads, near_lead)
    row = lax.broadcasted_iota(jnp.int32, (SUB, npages * page_len), 0)
    spot = lax.broadcasted_iota(jnp.int32, (SUB, npages * page_len), 1)
    inside = (spot - row * page_len).astype(jnp.float32)
    usable = jnp.where((inside >= 0.0) & (inside < jnp.minimum(left, float(page_len))), 1.0, 0.0)
    usable = jnp.concatenate([usable] * HEADS, axis=0) > 0.5
    leads = jnp.concatenate([leads] * HEADS, axis=0) > 0.5

    query = jnp.concatenate([joined[:, h * HD : (h + 1) * HD] for h in range(HEADS)], axis=0)
    fresh_key, fresh_value = [
        jnp.concatenate(
            [joined[:, start + h // group * HD : start + (h // group + 1) * HD] for h in range(HEADS)],
            axis=0,
        )
        for start in (qwidth, qwidth + kwidth)
    ]
    lines = group * SUB
    narrow = query.astype(jnp.bfloat16)
    scores = []
    for kv in range(KVH):
        keys = cache[:, 0, :, kv * HD : (kv + 1) * HD].reshape(npages * page_len, HD)
        scores.append(
            lax.dot_general(
                narrow[kv * lines : (kv + 1) * lines],
                keys,
                (((1,), (1,)), ((), ())),
                preferred_element_type=jnp.float32,
            )
        )
    scores = jnp.concatenate(scores, axis=0) * HD ** (-0.5)
    scores = jnp.where(usable, scores, EMPTY)
    own = jnp.sum(query * fresh_key, axis=-1, keepdims=True) * HD ** (-0.5)
    own = jnp.where(leads, own, EMPTY)
    peak = jnp.maximum(jnp.max(scores, axis=-1, keepdims=True), own)
    weights = jnp.where(usable, jnp.exp(scores - peak), 0.0)
    newest = jnp.where(leads, jnp.exp(own - peak), 0.0)
    total = jnp.sum(weights, axis=-1, keepdims=True) + newest
    narrow = weights.astype(jnp.bfloat16)
    summed = []
    for kv in range(KVH):
        values = cache[:, 1, :, kv * HD : (kv + 1) * HD].reshape(npages * page_len, HD)
        summed.append(
            jnp.dot(
                narrow[kv * lines : (kv + 1) * lines], values, preferred_element_type=jnp.float32
            )
        )
    summed = jnp.concatenate(summed, axis=0) + newest * fresh_value
    used = total > 0.0
    safe = jnp.where(used, total, 1.0)
    mixed = summed / safe
    level = jnp.where(used, peak + jnp.log(safe), EMPTY)
    lane = lax.broadcasted_iota(jnp.int32, (SUB, LANES), 1)
    levels = jnp.zeros((SUB, LANES), jnp.float32)
    for h in range(HEADS):
        levels = jnp.where(lane % STEP == h, level[h * SUB : (h + 1) * SUB], levels)
    upper = levels.astype(jnp.bfloat16).astype(jnp.float32)
    rest = levels - upper
    middle = rest.astype(jnp.bfloat16).astype(jnp.float32)
    levels = jnp.where(lane < STEP, upper, jnp.where(lane < 2 * STEP, middle, rest - middle))
    levels = jnp.where(lane < 3 * STEP, levels, 0.0)
    mixes = jnp.concatenate([mixed[h * SUB : (h + 1) * SUB] for h in range(HEADS)], axis=1)
    chips = size // CORES
    part = qwidth // chips
    for chip in range(chips):
        terms[chip] = jnp.concatenate([mixes[:, chip * part : (chip + 1) * part], levels], axis=1)
    for end, out in zip(targets(me, size), outs):
        out[...] = terms[pl.ds(end // CORES, 1)][0, :npages].astype(jnp.bfloat16)


def out_kernel(size, npages, *refs):
    blocks, refs = refs[:size], refs[size:]
    weight, mate_weight, plan, _, out = refs
    me = lax.axis_index("tensor")
    part = CORES * weight.shape[0]
    terms, ids = [], []
    line = lax.broadcasted_iota(jnp.int32, (SUB, LANES), 0)
    filler = jnp.zeros((SUB - npages, part + LANES), jnp.float32)
    for owner, block in zip(senders(me, size), blocks):
        terms += [block[...].astype(jnp.float32), filler]
        ids.append(jnp.where(line < npages, owner * npages + line, -2))
    terms = jnp.concatenate(terms, axis=0).astype(jnp.bfloat16)
    ids = jnp.concatenate(ids, axis=0).astype(jnp.float32)
    spread = lax.broadcasted_iota(jnp.int32, (LANES, part), 0)
    head = (lax.broadcasted_iota(jnp.int32, (LANES, part), 1) + me // CORES * part) // HD
    spread = jnp.where((spread % STEP == head) & (spread < 3 * STEP), 1.0, 0.0)
    spread = spread.astype(jnp.bfloat16)
    count = out.shape[0]
    rows = count + -count % STEP
    mixes, levels = [], []
    for hit in page_hits(plan[...], ids):
        picked = lax.dot_general(
            hit[:, :rows].astype(jnp.bfloat16),
            terms,
            (((0,), (0,)), ((), ())),
            preferred_element_type=jnp.float32,
        )
        mixes.append(picked[:, :part])
        levels.append(
            jnp.dot(
                picked[:, part:].astype(jnp.bfloat16), spread, preferred_element_type=jnp.float32
            )
        )
    highest = functools.reduce(jnp.maximum, levels)
    factors = [jnp.exp(level - highest) for level in levels]
    mixed = sum(mix * factor for mix, factor in zip(mixes, factors)) / sum(factors)
    halves = mixed[:, : part // CORES], mixed[:, part // CORES :]
    first = lax.rem(me, CORES) == 0
    own = jnp.where(first, halves[0], halves[1]).astype(jnp.bfloat16)
    other = jnp.where(first, halves[1], halves[0]).astype(jnp.bfloat16)
    products = jnp.dot(own, weight[...], preferred_element_type=jnp.float32)
    products += jnp.dot(other, mate_weight[...], preferred_element_type=jnp.float32)
    out[...] = products[:count].astype(jnp.bfloat16)


def expert_kernel(size, top, experts, parts, lows, *refs):
    chips = size // CORES
    sums, refs = refs[:chips], refs[chips:]
    rows_ref, gain, router = refs[:3]
    gate_up, refs = refs[3 : 3 + parts], refs[3 + parts :]
    down, refs = refs[:lows], refs[lows:]
    units = sum(piece.shape[0] for piece in down)
    homes, guests, finished, ends_ref = refs[:size], refs[size], refs[size + 1], refs[size + 2]
    me = lax.axis_index("tensor")
    count = rows_ref.shape[0]
    width = rows_ref.shape[1] - LANES
    rows_dev = count // size
    total = functools.reduce(jnp.add, [piece[...].astype(jnp.float32) for piece in sums])
    hidden = (rows_ref[:, :width] + total).astype(jnp.bfloat16).astype(jnp.float32)
    norm = normed(hidden, gain[...])
    lane = lax.broadcasted_iota(jnp.int32, (count, LANES), 1)
    numbers = rows_ref[:, width:]
    logits = lax.dot_general(
        norm, router[...], (((1,), (1,)), ((), ())), preferred_element_type=jnp.float32
    )
    logits = jnp.concatenate(
        [logits, jnp.zeros((count, LANES - experts), jnp.float32)], axis=1
    )
    routed = jnp.zeros((count, LANES), jnp.float32)
    for place in range(top):
        route = at_lane(numbers, lane, place)
        routed = jnp.where(lane.astype(jnp.float32) == route, 1.0, routed)
    logits = jnp.where(routed > 0.5, logits, EMPTY)
    shares = jnp.where(
        routed > 0.5, jnp.exp(logits - jnp.max(logits, axis=-1, keepdims=True)), 0.0
    )
    shares = shares / jnp.sum(shares, axis=-1, keepdims=True)

    here = lax.broadcasted_iota(jnp.int32, (LANES, 2 * LANES), 0)
    there = lax.broadcasted_iota(jnp.int32, (LANES, 2 * LANES), 1)
    evens = jnp.where(there == 2 * here, 1.0, 0.0).astype(jnp.bfloat16)
    odds = jnp.where(there == 2 * here + 1, 1.0, 0.0).astype(jnp.bfloat16)
    wide = to_step(norm)
    padded = wide.shape[0]
    blocks = width // LANES
    tall = jnp.concatenate([wide[:, b * LANES : (b + 1) * LANES] for b in range(blocks)], axis=0)
    to_gate = jnp.dot(tall, evens, preferred_element_type=jnp.float32).astype(jnp.bfloat16)
    to_up = jnp.dot(tall, odds, preferred_element_type=jnp.float32).astype(jnp.bfloat16)
    left = []
    for b in range(blocks):
        lines = slice(b * padded, (b + 1) * padded)
        left.append(jnp.concatenate([to_gate[lines], to_up[lines]], axis=0))
    left = jnp.concatenate(left, axis=1)
    both, right = [], []
    for piece in gate_up:
        right += [piece[place] for place in range(piece.shape[0])]
    for place in range(0, len(right), 2):
        pair = jnp.concatenate(right[place : place + 2], axis=1)
        both.append(jnp.dot(left, pair, preferred_element_type=jnp.float32))
    both = jnp.concatenate(both, axis=1)
    gate, up = both[:count], both[padded : padded + count]
    activated = gate / (1.0 + jnp.exp(-gate)) * up
    step = min(units, MOE_FF)
    scaled = []
    for start in range(0, units, step):
        expert = (me * units + start) // MOE_FF
        share = at_lane(shares, lane, expert)
        scaled.append(activated[:, start : start + step] * share)
    scaled = jnp.concatenate(scaled, axis=1).astype(jnp.bfloat16)
    partial, start = 0.0, 0
    for piece in down:
        left = scaled[:, start : start + piece.shape[0]]
        partial += jnp.dot(left, piece[...], preferred_element_type=jnp.float32)
        start += piece.shape[0]
    home_dev = rows_dev - 1
    first = size * home_dev
    for owner in range(size):
        lines = slice(owner * home_dev, (owner + 1) * home_dev)
        mine = jnp.where(me == owner, 1.0, 0.0)
        finished[owner] = partial[lines] + hidden[lines] * mine
        line = slice(first + owner, first + owner + 1)
        ends_ref[owner : owner + 1] = partial[line] + hidden[line] * mine
    for end, out in zip(targets(me, size), homes):
        out[...] = finished[pl.ds(end, 1)][0].astype(jnp.bfloat16)
    half = width // 2
    for owner in range(size):
        guest = ends_ref[owner : owner + 1]
        block = jnp.concatenate([guest[:, :half], guest[:, half:]], axis=0).astype(jnp.bfloat16)
        for place in range(owner, guests.shape[0], size):
            guests[guests.shape[0] - 1 - place] = block


def finish_kernel(size, spot, *refs):
    pieces, refs = refs[:size], refs[size:]
    guests, tail, out = refs
    homes = functools.reduce(jnp.add, [piece[...].astype(jnp.float32) for piece in pieces])
    came = guests[...].astype(jnp.float32)
    lane = lax.broadcasted_iota(jnp.int32, (1, LANES), 1)
    source = at_lane(tail[...], lane, spot).reshape(1, 1, 1)
    place = lax.broadcasted_iota(jnp.int32, (came.shape[0], 1, 1), 0)
    place = (came.shape[0] - 1 - place) // size
    guest = jnp.sum(jnp.where(place.astype(jnp.float32) == source, came, 0.0), axis=0)
    guest = jnp.concatenate([guest[:1], guest[1:]], axis=1)
    out[...] = jnp.concatenate([homes, guest], axis=0).astype(jnp.bfloat16)


def shape(dims, dtype=jnp.float32):
    return jax.ShapeDtypeStruct(dims, dtype)


def shards(
    tokens,
    attn_gain,
    qkv_weight,
    out_weight,
    moe_gain,
    router,
    expert_gate_up,
    expert_down,
    kv_cache,
    page_table,
    home_len,
    guest_source,
    guest_pages,
    guest_len,
    routes,
):
    size = lax.axis_size("tensor")
    replicas = lax.axis_size("replica")
    rows_dev, width = tokens.shape
    npages = kv_cache.shape[0]
    top = routes.shape[1]
    units = expert_down.shape[0]
    part = out_weight.shape[0]
    columns = qkv_weight.shape[1]
    count = size * rows_dev
    home_dev = rows_dev - 1
    wide = width + LANES
    everyone = size * replicas
    blocks = units // LANES
    gate_up, down = [], []

    def load_more(after, ups, downs):
        first, last = ups[0] * blocks // 8, ups[1] * blocks // 8
        wanted = []
        if last > first:
            wanted.append((expert_gate_up, first, last - first))
        if downs[1] > downs[0]:
            wanted.append((expert_down, downs[0] * units // 8, (downs[1] - downs[0]) * units // 8))
        if not wanted:
            return after
        got = loaded(after, *wanted)
        for part in got:
            (gate_up if part.ndim == 3 else down).append(part)
        return got[0]

    packed = guest_source * FAR + guest_len
    offers, homes, plan, tail = pl.pallas_call(
        offer_kernel,
        out_shape=[
            shape((everyone, 2, (wide + LANES) // 2), jnp.bfloat16),
            shape((home_dev, wide), jnp.bfloat16),
            shape((npages, LANES)),
            shape((1, LANES)),
        ],
        in_specs=[ANY] * 5 + [SMEM],
        out_specs=[VMEM] * 4,
        scratch_shapes=[
            pltpu.VMEM(tokens.shape, tokens.dtype),
            pltpu.SMEM(routes.T.shape, jnp.int32),
            pltpu.SMEM(guest_pages.shape, jnp.int32),
            pltpu.VMEM(page_table.T.shape, jnp.int32),
            pltpu.VMEM((1,) + home_len.shape, jnp.int32),
            pltpu.SemaphoreType.DMA((5,)),
        ],
        compiler_params=PARAMS,
        name="offer",
    )(far(tokens), far(routes.T), far(guest_pages), far(page_table.T), far(home_len), packed)
    came = to_everyone(offers)
    messages = exchanged([homes] * size)
    (qkv_near,) = loaded(homes, (qkv_weight, 0, width))

    rows, *projected = pl.pallas_call(
        functools.partial(project_kernel, size, npages, top),
        out_shape=[shape((count, wide))] + [shape((npages, columns), jnp.bfloat16)] * size,
        in_specs=[VMEM] * (size + 4),
        out_specs=[VMEM] * (size + 1),
        scratch_shapes=[
            pltpu.VMEM((size, home_dev, wide), jnp.float32),
            pltpu.VMEM((size * SUB, columns), jnp.float32),
        ],
        compiler_params=PARAMS,
        name="project",
    )(
        *messages,
        came,
        attn_gain.reshape(1, width),
        resident(qkv_near),
        plan,
    )
    joined = exchanged(projected)

    before = load_more(rows, (0, 2), (0, 4))
    late, _ = lax.optimization_barrier((out_weight, rows))
    out_mate = lax.ppermute(late, "tensor", [(me, me ^ 1) for me in range(size)])
    terms = pl.pallas_call(
        functools.partial(attend_kernel, size, top),
        out_shape=[shape((npages, CORES * part + LANES), jnp.bfloat16)] * size,
        in_specs=[VMEM] * (size + 3) + [ANY],
        out_specs=[VMEM] * size,
        scratch_shapes=[
            pltpu.VMEM((size, SUB, columns), jnp.float32),
            pltpu.VMEM((size // CORES, SUB, CORES * part + LANES), jnp.float32),
        ],
        compiler_params=PARAMS,
        name="attend",
    )(*joined, resident(kv_cache), rows, plan, before)
    arrived = exchanged(terms)

    before = load_more(terms[0], (2, 5), (4, 6))
    partial = pl.pallas_call(
        functools.partial(out_kernel, size, npages),
        out_shape=shape((count, width), jnp.bfloat16),
        in_specs=[VMEM] * (size + 3) + [ANY],
        out_specs=VMEM,
        compiler_params=PARAMS,
        name="out",
    )(*arrived, resident(out_weight), resident(out_mate), plan, before)
    sums = across(partial, size)

    load_more(partial, (5, 8), (6, 8))
    *pieces, guests = pl.pallas_call(
        functools.partial(
            expert_kernel, size, top, router.shape[1], len(gate_up), len(down)
        ),
        out_shape=[shape((home_dev, width), jnp.bfloat16)] * size
        + [shape((everyone, 2, width // 2), jnp.bfloat16)],
        in_specs=[VMEM] * (len(sums) + 3 + len(gate_up) + len(down)),
        out_specs=[VMEM] * (size + 1),
        scratch_shapes=[
            pltpu.VMEM((size, home_dev, width), jnp.float32),
            pltpu.VMEM((size, width), jnp.float32),
        ],
        compiler_params=PARAMS,
        name="experts",
    )(
        *sums,
        rows,
        moe_gain.reshape(1, width),
        router.T,
        *[resident(piece) for piece in gate_up + down],
    )
    guests = to_everyone(guests)
    pieces = exchanged(pieces)
    return pl.pallas_call(
        functools.partial(finish_kernel, size, top + 1 + MAXP),
        out_shape=shape((rows_dev, width), jnp.bfloat16),
        in_specs=[VMEM] * (size + 2),
        out_specs=VMEM,
        compiler_params=PARAMS,
        name="finish",
    )(*pieces, guests, tail)


def solution(mesh):
    placed = (
        P(("replica", "tensor"), None),
        P(),
        P(None, "tensor"),
        P("tensor", None),
        P(),
        P(),
        P(None, None, "tensor"),
        P("tensor", None),
        P(("replica", "tensor"), None, None, None),
        P("replica", None),
        P("replica"),
        P(("replica", "tensor")),
        P(("replica", "tensor"), None),
        P(("replica", "tensor")),
        P("replica", None),
    )
    return jax.shard_map(
        shards,
        mesh=mesh,
        in_specs=placed,
        out_specs=P(("replica", "tensor"), None),
        check_vma=False,
    )
```

```python
import functools

import jax
import jax.numpy as jnp
from jax import lax
from jax.experimental import pallas as pl
from jax.experimental.pallas import tpu as pltpu
from jax.sharding import PartitionSpec as P

HEADS = 12
KVH = 4
HD = 128
MOE_FF = 512
LANES = 128
SUB = 8
CORES = 2
FAR = 1024
EMPTY = -1e30
STEP = 16
MAXP = 2

VMEM = pl.BlockSpec(memory_space=pltpu.VMEM)
SMEM = pl.BlockSpec(memory_space=pltpu.SMEM)
ANY = pl.BlockSpec(memory_space=pl.ANY)
PARAMS = pltpu.CompilerParams(vmem_limit_bytes=16 * 2**20)


def resident(array):
    return pltpu.with_memory_space_constraint(array, pltpu.VMEM)


def far(array):
    return pltpu.with_memory_space_constraint(array, pltpu.HBM)


def normed(values, gain):
    inverse = lax.rsqrt(jnp.mean(values * values, axis=-1, keepdims=True) + 1e-05)
    return (values * inverse * gain).astype(jnp.bfloat16)


def ways(size):
    return [(chips, core) for chips in range(size // CORES) for core in range(CORES)][1:]


def target(me, size, way):
    chip = lax.rem(me // CORES + way[0], size // CORES)
    return chip * CORES + lax.rem(me + way[1], CORES)


def sender(me, size, way):
    chip = lax.rem(me // CORES + size // CORES - way[0], size // CORES)
    return chip * CORES + lax.rem(me + way[1], CORES)


def senders(me, size):
    return [me] + [sender(me, size, way) for way in ways(size)]


def targets(me, size):
    return [me] + [target(me, size, way) for way in ways(size)]


def exchanged(blocks):
    size = len(blocks)
    arrived = [blocks[0]]
    for way, block in zip(ways(size), blocks[1:]):
        pairs = []
        for me in range(size):
            chip = (me // CORES + way[0]) % (size // CORES)
            pairs.append((me, chip * CORES + (me + way[1]) % CORES))
        arrived.append(lax.ppermute(block, "tensor", pairs))
    return arrived


def to_step(rows):
    extra = -rows.shape[0] % STEP
    if not extra:
        return rows
    filler = jnp.zeros((extra, rows.shape[1]), jnp.float32)
    return jnp.concatenate([rows.astype(jnp.float32), filler], axis=0).astype(rows.dtype)


def at_lane(rows, lane, place):
    return jnp.sum(jnp.where(lane == place, rows, 0.0), axis=-1, keepdims=True)


def across(block, size):
    arrived = [block]
    for chips in range(1, size // CORES):
        pairs = [(me, (me + chips * CORES) % size) for me in range(size)]
        arrived.append(lax.ppermute(block, "tensor", pairs))
    return arrived


def page_hits(plan, pages):
    return [jnp.where(plan[place : place + 1] == pages, 1.0, 0.0) for place in range(MAXP)]


def offer_kernel(tokens, paths, pages, table, lens, packed, *refs):
    offers, homes, plan, tail_out, rows, paths_v, pages_v, table_v, lens_v, sems = refs
    pairs = [
        (tokens, rows),
        (paths, paths_v),
        (pages, pages_v),
        (table, table_v),
        (lens, lens_v.at[0]),
    ]
    copies = [pltpu.make_async_copy(*pair, sems.at[i]) for i, pair in enumerate(pairs)]
    for copy in copies:
        copy.start()
    for copy in copies:
        copy.wait()
    me = lax.axis_index("tensor")
    rows_dev, width = rows.shape
    top = paths.shape[0]
    lane = lax.broadcasted_iota(jnp.int32, (1, LANES), 1)
    wide = rows[...].astype(jnp.float32)
    routes = paths_v[...].astype(jnp.float32)
    spot = lax.broadcasted_iota(jnp.int32, routes.shape, 1)
    diagonal = (top, LANES)
    diagonal = lax.broadcasted_iota(jnp.int32, diagonal, 0) == lax.broadcasted_iota(
        jnp.int32, diagonal, 1
    )
    tails = []
    for slot in range(rows_dev):
        chosen = jnp.where(spot == me * rows_dev + slot, routes, 0.0)
        chosen = jnp.where(diagonal, jnp.sum(chosen, axis=1, keepdims=True), 0.0)
        tails.append(jnp.sum(chosen, axis=0, keepdims=True))
    numbers = [packed[0] % FAR, packed[0] // FAR]
    for place, number in zip((top, top + 1 + MAXP), numbers):
        tails[-1] = jnp.where(lane == place, number.astype(jnp.float32), tails[-1])
    named = pages_v[...].astype(jnp.float32)
    for place in range(MAXP):
        tails[-1] = jnp.where(lane == top + 1 + place, named[:, place : place + 1], tails[-1])
    tail_out[...] = tails[-1]
    full = jnp.concatenate([wide, jnp.concatenate(tails, axis=0)], axis=1)
    homes[...] = full[:-1].astype(jnp.bfloat16)
    guest = jnp.concatenate(
        [wide[-1:], tails[-1], jnp.zeros((1, LANES), jnp.float32)], axis=1
    )
    half = guest.shape[1] // 2
    block = jnp.concatenate([guest[:, :half], guest[:, half:]], axis=0).astype(jnp.bfloat16)
    for place in range(offers.shape[0]):
        offers[place] = block

    count = table.shape[1]
    npages = plan.shape[0]
    size = count * MAXP // (npages - MAXP)
    filler = jnp.zeros((1, LANES - count), jnp.float32)
    spots = lane - count
    lines = []
    for place in range(MAXP):
        ids = table_v[place : place + 1].astype(jnp.float32)
        ids = jnp.concatenate([ids, filler], axis=1)
        guests = (spots * npages + npages - MAXP + place).astype(jnp.float32)
        guests = jnp.where(spots < size, guests, -1.0)
        lines.append(jnp.where(spots < 0, ids, guests))
    lines.append(jnp.concatenate([lens_v[...].astype(jnp.float32), filler], axis=1))
    lines.append(jnp.zeros((npages - MAXP - 1, LANES), jnp.float32))
    plan[...] = jnp.concatenate(lines, axis=0)


def load_kernel(plans, *refs):
    sources, outs, sems = refs[1 : 1 + len(plans)], refs[1 + len(plans) : -1], refs[-1]
    copies = []

    def copy(source, out):
        copies.append(pltpu.make_async_copy(source, out, sems.at[len(copies)]))

    for (first, count, pieces), source, out in zip(plans, sources, outs):
        each = source.shape[0] // pieces if len(out.shape) == 4 else count // pieces
        for piece in range(pieces):
            lines = pl.ds(piece * each, each)
            if len(out.shape) == 4:
                for place in range(count):
                    columns = pl.ds((first + place) * LANES, LANES)
                    copy(source.at[lines, :, columns], out.at[place, lines])
            else:
                copy(source.at[pl.ds(first + piece * each, each)], out.at[lines])
    for made in copies:
        made.start()
    for made in copies:
        made.wait()


def loaded(after, *wanted):
    shapes, plans, copies = [], [], 0
    for array, first, count in wanted:
        if array.ndim == 3:
            shapes.append(shape((count,) + array.shape[:2] + (LANES,), array.dtype))
            plans.append((first, count, 2))
            copies += 2 * count
        else:
            shapes.append(shape((count, array.shape[1]), array.dtype))
            plans.append((first, count, 4))
            copies += 4
    parts = pl.pallas_call(
        functools.partial(load_kernel, tuple(plans)),
        out_shape=shapes,
        in_specs=[ANY] * (1 + len(wanted)),
        out_specs=[VMEM] * len(wanted),
        scratch_shapes=[pltpu.SemaphoreType.DMA((copies,))],
        compiler_params=PARAMS,
        cost_estimate=pl.CostEstimate(
            flops=0, bytes_accessed=sum(2 * part.size for part in shapes), transcendentals=0
        ),
        name="load",
    )(after, *[far(array) for array, _, _ in wanted])
    return [
        part.reshape(part.shape[0], -1, LANES) if part.ndim == 4 else part for part in parts
    ]


def project_kernel(size, npages, top, *refs):
    blocks, refs = refs[:size], refs[size:]
    offers, gain, weight, plan, rows_ref = refs[:5]
    outs = refs[5 : 5 + size]
    gathered, paged = refs[5 + size :]
    me = lax.axis_index("tensor")
    replica = lax.axis_index("replica").astype(jnp.float32)
    home_dev = blocks[0].shape[0]
    homes = size * home_dev
    width, columns = weight.shape
    for owner, block in zip(senders(me, size), blocks):
        gathered[pl.ds(owner, 1)] = block[...].astype(jnp.float32)[None]
    came = offers[...].astype(jnp.float32)
    half = came.shape[2]
    lane = lax.broadcasted_iota(jnp.int32, (1, 1, half), 2)
    spot = width + top + 1 + MAXP - half
    source = jnp.sum(jnp.where(lane == spot, came[:, 1:], 0.0), axis=2, keepdims=True)
    picked = jnp.where(source == replica, came, 0.0)
    picked = jnp.sum(picked.reshape(-1, size, 2, half), axis=0)
    for owner in range(size):
        rows_ref[owner * home_dev : (owner + 1) * home_dev] = gathered[owner]
        guest = jnp.concatenate([picked[owner, :1], picked[owner, 1:]], axis=1)
        rows_ref[homes + owner : homes + owner + 1] = guest[:, : width + LANES]
    norm = to_step(normed(rows_ref[:, :width], gain[...]))
    products = jnp.dot(norm, weight[...], preferred_element_type=jnp.float32)
    line = lax.broadcasted_iota(jnp.int32, (size * SUB, LANES), 0)
    ids = line // SUB * npages + line % SUB
    ids = jnp.where(line % SUB < npages, ids, -2).astype(jnp.float32)
    hits = sum(page_hits(plan[...], ids))[:, : norm.shape[0]]
    paged[...] = jnp.dot(
        hits.astype(jnp.bfloat16), products.astype(jnp.bfloat16), preferred_element_type=jnp.float32
    )
    for end, out in zip(targets(me, size), outs):
        start = pl.multiple_of(end * SUB, SUB)
        out[...] = paged[pl.ds(start, SUB)][:npages].astype(jnp.bfloat16)


def attend_kernel(size, top, *refs):
    blocks, refs = refs[:size], refs[size:]
    cache, rows_ref, plan_ref, _ = refs[:4]
    outs = refs[4 : 4 + size]
    gathered, terms = refs[4 + size :]
    me = lax.axis_index("tensor")
    npages, _, page_len, _ = cache.shape
    home_pages = npages - MAXP
    homes = home_pages // MAXP * size
    group = HEADS // KVH
    qwidth, kwidth = HEADS * HD, KVH * HD
    width = rows_ref.shape[1] - LANES
    for owner, block in zip(senders(me, size), blocks):
        gathered[pl.ds(owner, 1), :npages] = block[...].astype(jnp.float32)[None]
    joined = jnp.concatenate([gathered[owner] for owner in range(size)], axis=1)

    plan = plan_ref[...]
    line = lax.broadcasted_iota(jnp.int32, (SUB, LANES), 0)
    hits = page_hits(plan, (me * npages + line).astype(jnp.float32))
    left = sum(
        hit * (plan[MAXP : MAXP + 1] - float(place * page_len)) for place, hit in enumerate(hits)
    )
    left = jnp.sum(left, axis=1, keepdims=True)
    leads = jnp.sum(hits[0], axis=1, keepdims=True)
    tails = rows_ref[:, width:]
    place = lax.broadcasted_iota(jnp.int32, tails.shape, 0)
    numbers = jnp.sum(jnp.where(place == homes + me, tails, 0.0), axis=0, keepdims=True)
    lane = lax.broadcasted_iota(jnp.int32, (1, LANES), 1)
    near_len = at_lane(numbers, lane, top)
    line = line[:, :1]
    near_left, near_lead = jnp.zeros((SUB, 1), jnp.float32), None
    for place in range(MAXP):
        named = at_lane(numbers, lane, top + 1 + place) == line.astype(jnp.float32)
        near_left = jnp.where(named, near_len - float(place * page_len), near_left)
        if place == 0:
            near_lead = jnp.where(named, 1.0, 0.0)
    left = jnp.where(line < home_pages, left, near_left)
    leads = jnp.where(line < home_pages, leads, near_lead)
    row = lax.broadcasted_iota(jnp.int32, (SUB, npages * page_len), 0)
    spot = lax.broadcasted_iota(jnp.int32, (SUB, npages * page_len), 1)
    inside = (spot - row * page_len).astype(jnp.float32)
    usable = jnp.where((inside >= 0.0) & (inside < jnp.minimum(left, float(page_len))), 1.0, 0.0)
    usable = jnp.concatenate([usable] * HEADS, axis=0) > 0.5
    leads = jnp.concatenate([leads] * HEADS, axis=0) > 0.5

    query = jnp.concatenate([joined[:, h * HD : (h + 1) * HD] for h in range(HEADS)], axis=0)
    fresh_key, fresh_value = [
        jnp.concatenate(
            [joined[:, start + h // group * HD : start + (h // group + 1) * HD] for h in range(HEADS)],
            axis=0,
        )
        for start in (qwidth, qwidth + kwidth)
    ]
    lines = group * SUB
    narrow = query.astype(jnp.bfloat16)
    scores = []
    for kv in range(KVH):
        keys = cache[:, 0, :, kv * HD : (kv + 1) * HD].reshape(npages * page_len, HD)
        scores.append(
            lax.dot_general(
                narrow[kv * lines : (kv + 1) * lines],
                keys,
                (((1,), (1,)), ((), ())),
                preferred_element_type=jnp.float32,
            )
        )
    scores = jnp.concatenate(scores, axis=0) * HD ** (-0.5)
    scores = jnp.where(usable, scores, EMPTY)
    own = jnp.sum(query * fresh_key, axis=-1, keepdims=True) * HD ** (-0.5)
    own = jnp.where(leads, own, EMPTY)
    peak = jnp.maximum(jnp.max(scores, axis=-1, keepdims=True), own)
    weights = jnp.where(usable, jnp.exp(scores - peak), 0.0)
    newest = jnp.where(leads, jnp.exp(own - peak), 0.0)
    total = jnp.sum(weights, axis=-1, keepdims=True) + newest
    narrow = weights.astype(jnp.bfloat16)
    summed = []
    for kv in range(KVH):
        values = cache[:, 1, :, kv * HD : (kv + 1) * HD].reshape(npages * page_len, HD)
        summed.append(
            jnp.dot(
                narrow[kv * lines : (kv + 1) * lines], values, preferred_element_type=jnp.float32
            )
        )
    summed = jnp.concatenate(summed, axis=0) + newest * fresh_value
    used = total > 0.0
    safe = jnp.where(used, total, 1.0)
    mixed = summed / safe
    level = jnp.where(used, peak + jnp.log(safe), EMPTY)
    lane = lax.broadcasted_iota(jnp.int32, (SUB, LANES), 1)
    levels = jnp.zeros((SUB, LANES), jnp.float32)
    for h in range(HEADS):
        levels = jnp.where(lane % STEP == h, level[h * SUB : (h + 1) * SUB], levels)
    upper = levels.astype(jnp.bfloat16).astype(jnp.float32)
    rest = levels - upper
    middle = rest.astype(jnp.bfloat16).astype(jnp.float32)
    levels = jnp.where(lane < STEP, upper, jnp.where(lane < 2 * STEP, middle, rest - middle))
    levels = jnp.where(lane < 3 * STEP, levels, 0.0)
    mixes = jnp.concatenate([mixed[h * SUB : (h + 1) * SUB] for h in range(HEADS)], axis=1)
    chips = size // CORES
    part = qwidth // chips
    for chip in range(chips):
        terms[chip] = jnp.concatenate([mixes[:, chip * part : (chip + 1) * part], levels], axis=1)
    for end, out in zip(targets(me, size), outs):
        out[...] = terms[pl.ds(end // CORES, 1)][0, :npages].astype(jnp.bfloat16)


def out_kernel(size, npages, *refs):
    blocks, refs = refs[:size], refs[size:]
    weight, mate_weight, plan, _, out = refs
    me = lax.axis_index("tensor")
    part = CORES * weight.shape[0]
    terms, ids = [], []
    line = lax.broadcasted_iota(jnp.int32, (SUB, LANES), 0)
    filler = jnp.zeros((SUB - npages, part + LANES), jnp.float32)
    for owner, block in zip(senders(me, size), blocks):
        terms += [block[...].astype(jnp.float32), filler]
        ids.append(jnp.where(line < npages, owner * npages + line, -2))
    terms = jnp.concatenate(terms, axis=0).astype(jnp.bfloat16)
    ids = jnp.concatenate(ids, axis=0).astype(jnp.float32)
    spread = lax.broadcasted_iota(jnp.int32, (LANES, part), 0)
    head = (lax.broadcasted_iota(jnp.int32, (LANES, part), 1) + me // CORES * part) // HD
    spread = jnp.where((spread % STEP == head) & (spread < 3 * STEP), 1.0, 0.0)
    spread = spread.astype(jnp.bfloat16)
    count = out.shape[0]
    rows = count + -count % STEP
    mixes, levels = [], []
    for hit in page_hits(plan[...], ids):
        picked = lax.dot_general(
            hit[:, :rows].astype(jnp.bfloat16),
            terms,
            (((0,), (0,)), ((), ())),
            preferred_element_type=jnp.float32,
        )
        mixes.append(picked[:, :part])
        levels.append(
            jnp.dot(
                picked[:, part:].astype(jnp.bfloat16), spread, preferred_element_type=jnp.float32
            )
        )
    highest = functools.reduce(jnp.maximum, levels)
    factors = [jnp.exp(level - highest) for level in levels]
    mixed = sum(mix * factor for mix, factor in zip(mixes, factors)) / sum(factors)
    halves = mixed[:, : part // CORES], mixed[:, part // CORES :]
    first = lax.rem(me, CORES) == 0
    own = jnp.where(first, halves[0], halves[1]).astype(jnp.bfloat16)
    other = jnp.where(first, halves[1], halves[0]).astype(jnp.bfloat16)
    products = jnp.dot(own, weight[...], preferred_element_type=jnp.float32)
    products += jnp.dot(other, mate_weight[...], preferred_element_type=jnp.float32)
    out[...] = products[:count].astype(jnp.bfloat16)


def expert_kernel(size, top, experts, parts, lows, *refs):
    chips = size // CORES
    sums, refs = refs[:chips], refs[chips:]
    rows_ref, gain, router = refs[:3]
    gate_up, refs = refs[3 : 3 + parts], refs[3 + parts :]
    down, refs = refs[:lows], refs[lows:]
    units = sum(piece.shape[0] for piece in down)
    homes, guests, finished, ends_ref = refs[:size], refs[size], refs[size + 1], refs[size + 2]
    me = lax.axis_index("tensor")
    count = rows_ref.shape[0]
    width = rows_ref.shape[1] - LANES
    rows_dev = count // size
    total = functools.reduce(jnp.add, [piece[...].astype(jnp.float32) for piece in sums])
    hidden = (rows_ref[:, :width] + total).astype(jnp.bfloat16).astype(jnp.float32)
    norm = normed(hidden, gain[...])
    lane = lax.broadcasted_iota(jnp.int32, (count, LANES), 1)
    numbers = rows_ref[:, width:]
    logits = lax.dot_general(
        norm, router[...], (((1,), (1,)), ((), ())), preferred_element_type=jnp.float32
    )
    logits = jnp.concatenate(
        [logits, jnp.zeros((count, LANES - experts), jnp.float32)], axis=1
    )
    routed = jnp.zeros((count, LANES), jnp.float32)
    for place in range(top):
        route = at_lane(numbers, lane, place)
        routed = jnp.where(lane.astype(jnp.float32) == route, 1.0, routed)
    logits = jnp.where(routed > 0.5, logits, EMPTY)
    shares = jnp.where(
        routed > 0.5, jnp.exp(logits - jnp.max(logits, axis=-1, keepdims=True)), 0.0
    )
    shares = shares / jnp.sum(shares, axis=-1, keepdims=True)

    here = lax.broadcasted_iota(jnp.int32, (LANES, 2 * LANES), 0)
    there = lax.broadcasted_iota(jnp.int32, (LANES, 2 * LANES), 1)
    evens = jnp.where(there == 2 * here, 1.0, 0.0).astype(jnp.bfloat16)
    odds = jnp.where(there == 2 * here + 1, 1.0, 0.0).astype(jnp.bfloat16)
    wide = to_step(norm)
    padded = wide.shape[0]
    blocks = width // LANES
    tall = jnp.concatenate([wide[:, b * LANES : (b + 1) * LANES] for b in range(blocks)], axis=0)
    to_gate = jnp.dot(tall, evens, preferred_element_type=jnp.float32).astype(jnp.bfloat16)
    to_up = jnp.dot(tall, odds, preferred_element_type=jnp.float32).astype(jnp.bfloat16)
    left = []
    for b in range(blocks):
        lines = slice(b * padded, (b + 1) * padded)
        left.append(jnp.concatenate([to_gate[lines], to_up[lines]], axis=0))
    left = jnp.concatenate(left, axis=1)
    both, right = [], []
    for piece in gate_up:
        right += [piece[place] for place in range(piece.shape[0])]
    for place in range(0, len(right), 2):
        pair = jnp.concatenate(right[place : place + 2], axis=1)
        both.append(jnp.dot(left, pair, preferred_element_type=jnp.float32))
    both = jnp.concatenate(both, axis=1)
    gate, up = both[:count], both[padded : padded + count]
    activated = gate / (1.0 + jnp.exp(-gate)) * up
    step = min(units, MOE_FF)
    scaled = []
    for start in range(0, units, step):
        expert = (me * units + start) // MOE_FF
        share = at_lane(shares, lane, expert)
        scaled.append(activated[:, start : start + step] * share)
    scaled = jnp.concatenate(scaled, axis=1).astype(jnp.bfloat16)
    partial, start = 0.0, 0
    for piece in down:
        left = scaled[:, start : start + piece.shape[0]]
        partial += jnp.dot(left, piece[...], preferred_element_type=jnp.float32)
        start += piece.shape[0]
    home_dev = rows_dev - 1
    first = size * home_dev
    for owner in range(size):
        lines = slice(owner * home_dev, (owner + 1) * home_dev)
        mine = jnp.where(me == owner, 1.0, 0.0)
        finished[owner] = partial[lines] + hidden[lines] * mine
        line = slice(first + owner, first + owner + 1)
        ends_ref[owner : owner + 1] = partial[line] + hidden[line] * mine
    for end, out in zip(targets(me, size), homes):
        out[...] = finished[pl.ds(end, 1)][0].astype(jnp.bfloat16)
    half = width // 2
    for owner in range(size):
        guest = ends_ref[owner : owner + 1]
        block = jnp.concatenate([guest[:, :half], guest[:, half:]], axis=0).astype(jnp.bfloat16)
        for place in range(owner, guests.shape[0], size):
            guests[place] = block


def finish_kernel(size, spot, *refs):
    pieces, refs = refs[:size], refs[size:]
    guests, tail, out = refs
    homes = functools.reduce(jnp.add, [piece[...].astype(jnp.float32) for piece in pieces])
    came = guests[...].astype(jnp.float32)
    lane = lax.broadcasted_iota(jnp.int32, (1, LANES), 1)
    source = at_lane(tail[...], lane, spot).reshape(1, 1, 1)
    place = lax.broadcasted_iota(jnp.int32, (came.shape[0], 1, 1), 0) // size
    guest = jnp.sum(jnp.where(place.astype(jnp.float32) == source, came, 0.0), axis=0)
    guest = jnp.concatenate([guest[:1], guest[1:]], axis=1)
    out[...] = jnp.concatenate([homes, guest], axis=0).astype(jnp.bfloat16)


def shape(dims, dtype=jnp.float32):
    return jax.ShapeDtypeStruct(dims, dtype)


def shards(
    tokens,
    attn_gain,
    qkv_weight,
    out_weight,
    moe_gain,
    router,
    expert_gate_up,
    expert_down,
    kv_cache,
    page_table,
    home_len,
    guest_source,
    guest_pages,
    guest_len,
    routes,
):
    size = lax.axis_size("tensor")
    replicas = lax.axis_size("replica")
    rows_dev, width = tokens.shape
    npages = kv_cache.shape[0]
    top = routes.shape[1]
    units = expert_down.shape[0]
    part = out_weight.shape[0]
    columns = qkv_weight.shape[1]
    count = size * rows_dev
    home_dev = rows_dev - 1
    wide = width + LANES
    everyone = size * replicas
    blocks = units // LANES
    gate_up, down = [], []

    def load_more(after, ups, downs):
        first, last = ups[0] * blocks // 8, ups[1] * blocks // 8
        wanted = []
        if last > first:
            wanted.append((expert_gate_up, first, last - first))
        if downs[1] > downs[0]:
            wanted.append((expert_down, downs[0] * units // 8, (downs[1] - downs[0]) * units // 8))
        if not wanted:
            return after
        got = loaded(after, *wanted)
        for part in got:
            (gate_up if part.ndim == 3 else down).append(part)
        return got[0]

    packed = guest_source * FAR + guest_len
    offers, homes, plan, tail = pl.pallas_call(
        offer_kernel,
        out_shape=[
            shape((everyone, 2, (wide + LANES) // 2), jnp.bfloat16),
            shape((home_dev, wide), jnp.bfloat16),
            shape((npages, LANES)),
            shape((1, LANES)),
        ],
        in_specs=[ANY] * 5 + [SMEM],
        out_specs=[VMEM] * 4,
        scratch_shapes=[
            pltpu.VMEM(tokens.shape, tokens.dtype),
            pltpu.VMEM(routes.T.shape, jnp.int32),
            pltpu.VMEM(guest_pages.shape, jnp.int32),
            pltpu.VMEM(page_table.T.shape, jnp.int32),
            pltpu.VMEM((1,) + home_len.shape, jnp.int32),
            pltpu.SemaphoreType.DMA((5,)),
        ],
        compiler_params=PARAMS,
        name="offer",
    )(far(tokens), far(routes.T), far(guest_pages), far(page_table.T), far(home_len), packed)
    came = lax.all_to_all(offers, ("replica", "tensor"), 0, 0, tiled=True)
    messages = exchanged([homes] * size)
    (qkv_near,) = loaded(homes, (qkv_weight, 0, width))

    rows, *projected = pl.pallas_call(
        functools.partial(project_kernel, size, npages, top),
        out_shape=[shape((count, wide))] + [shape((npages, columns), jnp.bfloat16)] * size,
        in_specs=[VMEM] * (size + 4),
        out_specs=[VMEM] * (size + 1),
        scratch_shapes=[
            pltpu.VMEM((size, home_dev, wide), jnp.float32),
            pltpu.VMEM((size * SUB, columns), jnp.float32),
        ],
        compiler_params=PARAMS,
        name="project",
    )(
        *messages,
        came,
        attn_gain.reshape(1, width),
        resident(qkv_near),
        plan,
    )
    joined = exchanged(projected)

    before = load_more(rows, (0, 2), (0, 4))
    late, _ = lax.optimization_barrier((out_weight, rows))
    out_mate = lax.ppermute(late, "tensor", [(me, me ^ 1) for me in range(size)])
    terms = pl.pallas_call(
        functools.partial(attend_kernel, size, top),
        out_shape=[shape((npages, CORES * part + LANES), jnp.bfloat16)] * size,
        in_specs=[VMEM] * (size + 3) + [ANY],
        out_specs=[VMEM] * size,
        scratch_shapes=[
            pltpu.VMEM((size, SUB, columns), jnp.float32),
            pltpu.VMEM((size // CORES, SUB, CORES * part + LANES), jnp.float32),
        ],
        compiler_params=PARAMS,
        name="attend",
    )(*joined, resident(kv_cache), rows, plan, before)
    arrived = exchanged(terms)

    before = load_more(terms[0], (2, 5), (4, 6))
    partial = pl.pallas_call(
        functools.partial(out_kernel, size, npages),
        out_shape=shape((count, width), jnp.bfloat16),
        in_specs=[VMEM] * (size + 3) + [ANY],
        out_specs=VMEM,
        compiler_params=PARAMS,
        name="out",
    )(*arrived, resident(out_weight), resident(out_mate), plan, before)
    sums = across(partial, size)

    load_more(partial, (5, 8), (6, 8))
    *pieces, guests = pl.pallas_call(
        functools.partial(
            expert_kernel, size, top, router.shape[1], len(gate_up), len(down)
        ),
        out_shape=[shape((home_dev, width), jnp.bfloat16)] * size
        + [shape((everyone, 2, width // 2), jnp.bfloat16)],
        in_specs=[VMEM] * (len(sums) + 3 + len(gate_up) + len(down)),
        out_specs=[VMEM] * (size + 1),
        scratch_shapes=[
            pltpu.VMEM((size, home_dev, width), jnp.float32),
            pltpu.VMEM((size, width), jnp.float32),
        ],
        compiler_params=PARAMS,
        name="experts",
    )(
        *sums,
        rows,
        moe_gain.reshape(1, width),
        router.T,
        *[resident(piece) for piece in gate_up + down],
    )
    guests = lax.all_to_all(guests, ("replica", "tensor"), 0, 0, tiled=True)
    pieces = exchanged(pieces)
    return pl.pallas_call(
        functools.partial(finish_kernel, size, top + 1 + MAXP),
        out_shape=shape((rows_dev, width), jnp.bfloat16),
        in_specs=[VMEM] * (size + 2),
        out_specs=VMEM,
        compiler_params=PARAMS,
        name="finish",
    )(*pieces, guests, tail)


def solution(mesh):
    placed = (
        P(("replica", "tensor"), None),
        P(),
        P(None, "tensor"),
        P("tensor", None),
        P(),
        P(),
        P(None, None, "tensor"),
        P("tensor", None),
        P(("replica", "tensor"), None, None, None),
        P("replica", None),
        P("replica"),
        P(("replica", "tensor")),
        P(("replica", "tensor"), None),
        P(("replica", "tensor")),
        P("replica", None),
    )
    return jax.shard_map(
        shards,
        mesh=mesh,
        in_specs=placed,
        out_specs=P(("replica", "tensor"), None),
        check_vma=False,
    )
```

```python
import functools

import jax
import jax.numpy as jnp
from jax import lax
from jax.experimental import pallas as pl
from jax.experimental.pallas import tpu as pltpu
from jax.sharding import PartitionSpec as P

HEADS = 12
KVH = 4
HD = 128
MOE_FF = 512
LANES = 128
SUB = 8
CORES = 2
FAR = 1024
EMPTY = -1e30
STEP = 16
MAXP = 2

VMEM = pl.BlockSpec(memory_space=pltpu.VMEM)
SMEM = pl.BlockSpec(memory_space=pltpu.SMEM)
ANY = pl.BlockSpec(memory_space=pl.ANY)
PARAMS = pltpu.CompilerParams(vmem_limit_bytes=16 * 2**20)


def resident(array):
    return pltpu.with_memory_space_constraint(array, pltpu.VMEM)


def far(array):
    return pltpu.with_memory_space_constraint(array, pltpu.HBM)


def normed(values, gain):
    inverse = lax.rsqrt(jnp.mean(values * values, axis=-1, keepdims=True) + 1e-05)
    return (values * inverse * gain).astype(jnp.bfloat16)


def ways(size):
    return [(chips, core) for chips in range(size // CORES) for core in range(CORES)][1:]


def target(me, size, way):
    chip = lax.rem(me // CORES + way[0], size // CORES)
    return chip * CORES + lax.rem(me + way[1], CORES)


def sender(me, size, way):
    chip = lax.rem(me // CORES + size // CORES - way[0], size // CORES)
    return chip * CORES + lax.rem(me + way[1], CORES)


def senders(me, size):
    return [me] + [sender(me, size, way) for way in ways(size)]


def targets(me, size):
    return [me] + [target(me, size, way) for way in ways(size)]


def exchanged(blocks):
    size = len(blocks)
    arrived = [blocks[0]]
    for way, block in zip(ways(size), blocks[1:]):
        pairs = []
        for me in range(size):
            chip = (me // CORES + way[0]) % (size // CORES)
            pairs.append((me, chip * CORES + (me + way[1]) % CORES))
        arrived.append(lax.ppermute(block, "tensor", pairs))
    return arrived


def to_step(rows):
    extra = -rows.shape[0] % STEP
    if not extra:
        return rows
    filler = jnp.zeros((extra, rows.shape[1]), jnp.float32)
    return jnp.concatenate([rows.astype(jnp.float32), filler], axis=0).astype(rows.dtype)


def at_lane(rows, lane, place):
    return jnp.sum(jnp.where(lane == place, rows, 0.0), axis=-1, keepdims=True)


def across(block, size):
    arrived = [block]
    for chips in range(1, size // CORES):
        pairs = [(me, (me + chips * CORES) % size) for me in range(size)]
        arrived.append(lax.ppermute(block, "tensor", pairs))
    return arrived


def page_hits(plan, pages):
    return [jnp.where(plan[place : place + 1] == pages, 1.0, 0.0) for place in range(MAXP)]


def offer_kernel(tokens, paths, pages, packed, *refs):
    offers, homes, tail_out, rows, paths_v, pages_v, sems = refs
    pairs = [
        (tokens, rows),
        (paths, paths_v),
        (pages, pages_v),
    ]
    copies = [pltpu.make_async_copy(*pair, sems.at[i]) for i, pair in enumerate(pairs)]
    for copy in copies:
        copy.start()
    for copy in copies:
        copy.wait()
    me = lax.axis_index("tensor")
    rows_dev, width = rows.shape
    top = paths.shape[0]
    lane = lax.broadcasted_iota(jnp.int32, (1, LANES), 1)
    wide = rows[...].astype(jnp.float32)
    routes = paths_v[...].astype(jnp.float32)
    spot = lax.broadcasted_iota(jnp.int32, routes.shape, 1)
    diagonal = (top, LANES)
    diagonal = lax.broadcasted_iota(jnp.int32, diagonal, 0) == lax.broadcasted_iota(
        jnp.int32, diagonal, 1
    )
    tails = []
    for slot in range(rows_dev):
        chosen = jnp.where(spot == me * rows_dev + slot, routes, 0.0)
        chosen = jnp.where(diagonal, jnp.sum(chosen, axis=1, keepdims=True), 0.0)
        tails.append(jnp.sum(chosen, axis=0, keepdims=True))
    numbers = [packed[0] % FAR, packed[0] // FAR]
    for place, number in zip((top, top + 1 + MAXP), numbers):
        tails[-1] = jnp.where(lane == place, number.astype(jnp.float32), tails[-1])
    named = pages_v[...].astype(jnp.float32)
    for place in range(MAXP):
        tails[-1] = jnp.where(lane == top + 1 + place, named[:, place : place + 1], tails[-1])
    tail_out[...] = tails[-1]
    full = jnp.concatenate([wide, jnp.concatenate(tails, axis=0)], axis=1)
    homes[...] = full[:-1].astype(jnp.bfloat16)
    guest = jnp.concatenate(
        [wide[-1:], tails[-1], jnp.zeros((1, LANES), jnp.float32)], axis=1
    )
    half = guest.shape[1] // 2
    block = jnp.concatenate([guest[:, :half], guest[:, half:]], axis=0).astype(jnp.bfloat16)
    for place in range(offers.shape[0]):
        offers[place] = block


def plan_kernel(_, table, lens, plan, table_v, lens_v, sems):
    copies = [
        pltpu.make_async_copy(table, table_v, sems.at[0]),
        pltpu.make_async_copy(lens, lens_v.at[0], sems.at[1]),
    ]
    for copy in copies:
        copy.start()
    for copy in copies:
        copy.wait()
    lane = lax.broadcasted_iota(jnp.int32, (1, LANES), 1)
    count = table.shape[1]
    npages = plan.shape[0]
    size = count * MAXP // (npages - MAXP)
    filler = jnp.zeros((1, LANES - count), jnp.float32)
    spots = lane - count
    lines = []
    for place in range(MAXP):
        ids = table_v[place : place + 1].astype(jnp.float32)
        ids = jnp.concatenate([ids, filler], axis=1)
        guests = (spots * npages + npages - MAXP + place).astype(jnp.float32)
        guests = jnp.where(spots < size, guests, -1.0)
        lines.append(jnp.where(spots < 0, ids, guests))
    lines.append(jnp.concatenate([lens_v[...].astype(jnp.float32), filler], axis=1))
    lines.append(jnp.zeros((npages - MAXP - 1, LANES), jnp.float32))
    plan[...] = jnp.concatenate(lines, axis=0)


def load_kernel(plans, *refs):
    sources, outs, sems = refs[1 : 1 + len(plans)], refs[1 + len(plans) : -1], refs[-1]
    copies = []

    def copy(source, out):
        copies.append(pltpu.make_async_copy(source, out, sems.at[len(copies)]))

    for (first, count, pieces), source, out in zip(plans, sources, outs):
        each = source.shape[0] // pieces if len(out.shape) == 4 else count // pieces
        for piece in range(pieces):
            lines = pl.ds(piece * each, each)
            if len(out.shape) == 4:
                for place in range(count):
                    columns = pl.ds((first + place) * LANES, LANES)
                    copy(source.at[lines, :, columns], out.at[place, lines])
            else:
                copy(source.at[pl.ds(first + piece * each, each)], out.at[lines])
    for made in copies:
        made.start()
    for made in copies:
        made.wait()


def loaded(after, *wanted):
    shapes, plans, copies = [], [], 0
    for array, first, count in wanted:
        if array.ndim == 3:
            shapes.append(shape((count,) + array.shape[:2] + (LANES,), array.dtype))
            plans.append((first, count, 2))
            copies += 2 * count
        else:
            shapes.append(shape((count, array.shape[1]), array.dtype))
            plans.append((first, count, 4))
            copies += 4
    parts = pl.pallas_call(
        functools.partial(load_kernel, tuple(plans)),
        out_shape=shapes,
        in_specs=[ANY] * (1 + len(wanted)),
        out_specs=[VMEM] * len(wanted),
        scratch_shapes=[pltpu.SemaphoreType.DMA((copies,))],
        compiler_params=PARAMS,
        cost_estimate=pl.CostEstimate(
            flops=0, bytes_accessed=sum(2 * part.size for part in shapes), transcendentals=0
        ),
        name="load",
    )(after, *[far(array) for array, _, _ in wanted])
    return [
        part.reshape(part.shape[0], -1, LANES) if part.ndim == 4 else part for part in parts
    ]


def project_kernel(size, npages, top, *refs):
    blocks, refs = refs[:size], refs[size:]
    offers, gain, weight, plan, rows_ref = refs[:5]
    outs = refs[5 : 5 + size]
    gathered, paged = refs[5 + size :]
    me = lax.axis_index("tensor")
    replica = lax.axis_index("replica").astype(jnp.float32)
    home_dev = blocks[0].shape[0]
    homes = size * home_dev
    width, columns = weight.shape
    for owner, block in zip(senders(me, size), blocks):
        gathered[pl.ds(owner, 1)] = block[...].astype(jnp.float32)[None]
    came = offers[...].astype(jnp.float32)
    half = came.shape[2]
    lane = lax.broadcasted_iota(jnp.int32, (1, 1, half), 2)
    spot = width + top + 1 + MAXP - half
    source = jnp.sum(jnp.where(lane == spot, came[:, 1:], 0.0), axis=2, keepdims=True)
    picked = jnp.where(source == replica, came, 0.0)
    picked = jnp.sum(picked.reshape(-1, size, 2, half), axis=0)
    for owner in range(size):
        rows_ref[owner * home_dev : (owner + 1) * home_dev] = gathered[owner]
        guest = jnp.concatenate([picked[owner, :1], picked[owner, 1:]], axis=1)
        rows_ref[homes + owner : homes + owner + 1] = guest[:, : width + LANES]
    norm = to_step(normed(rows_ref[:, :width], gain[...]))
    products = jnp.dot(norm, weight[...], preferred_element_type=jnp.float32)
    line = lax.broadcasted_iota(jnp.int32, (size * SUB, LANES), 0)
    ids = line // SUB * npages + line % SUB
    ids = jnp.where(line % SUB < npages, ids, -2).astype(jnp.float32)
    hits = sum(page_hits(plan[...], ids))[:, : norm.shape[0]]
    paged[...] = jnp.dot(
        hits.astype(jnp.bfloat16), products.astype(jnp.bfloat16), preferred_element_type=jnp.float32
    )
    for end, out in zip(targets(me, size), outs):
        start = pl.multiple_of(end * SUB, SUB)
        out[...] = paged[pl.ds(start, SUB)][:npages].astype(jnp.bfloat16)


def attend_kernel(size, top, *refs):
    blocks, refs = refs[:size], refs[size:]
    cache, rows_ref, plan_ref, _ = refs[:4]
    outs = refs[4 : 4 + size]
    gathered, terms = refs[4 + size :]
    me = lax.axis_index("tensor")
    npages, _, page_len, _ = cache.shape
    home_pages = npages - MAXP
    homes = home_pages // MAXP * size
    group = HEADS // KVH
    qwidth, kwidth = HEADS * HD, KVH * HD
    width = rows_ref.shape[1] - LANES
    for owner, block in zip(senders(me, size), blocks):
        gathered[pl.ds(owner, 1), :npages] = block[...].astype(jnp.float32)[None]
    joined = jnp.concatenate([gathered[owner] for owner in range(size)], axis=1)

    plan = plan_ref[...]
    line = lax.broadcasted_iota(jnp.int32, (SUB, LANES), 0)
    hits = page_hits(plan, (me * npages + line).astype(jnp.float32))
    left = sum(
        hit * (plan[MAXP : MAXP + 1] - float(place * page_len)) for place, hit in enumerate(hits)
    )
    left = jnp.sum(left, axis=1, keepdims=True)
    leads = jnp.sum(hits[0], axis=1, keepdims=True)
    tails = rows_ref[:, width:]
    place = lax.broadcasted_iota(jnp.int32, tails.shape, 0)
    numbers = jnp.sum(jnp.where(place == homes + me, tails, 0.0), axis=0, keepdims=True)
    lane = lax.broadcasted_iota(jnp.int32, (1, LANES), 1)
    near_len = at_lane(numbers, lane, top)
    line = line[:, :1]
    near_left, near_lead = jnp.zeros((SUB, 1), jnp.float32), None
    for place in range(MAXP):
        named = at_lane(numbers, lane, top + 1 + place) == line.astype(jnp.float32)
        near_left = jnp.where(named, near_len - float(place * page_len), near_left)
        if place == 0:
            near_lead = jnp.where(named, 1.0, 0.0)
    left = jnp.where(line < home_pages, left, near_left)
    leads = jnp.where(line < home_pages, leads, near_lead)
    row = lax.broadcasted_iota(jnp.int32, (SUB, npages * page_len), 0)
    spot = lax.broadcasted_iota(jnp.int32, (SUB, npages * page_len), 1)
    inside = (spot - row * page_len).astype(jnp.float32)
    usable = jnp.where((inside >= 0.0) & (inside < jnp.minimum(left, float(page_len))), 1.0, 0.0)
    usable = jnp.concatenate([usable] * HEADS, axis=0) > 0.5
    leads = jnp.concatenate([leads] * HEADS, axis=0) > 0.5

    query = jnp.concatenate([joined[:, h * HD : (h + 1) * HD] for h in range(HEADS)], axis=0)
    fresh_key, fresh_value = [
        jnp.concatenate(
            [joined[:, start + h // group * HD : start + (h // group + 1) * HD] for h in range(HEADS)],
            axis=0,
        )
        for start in (qwidth, qwidth + kwidth)
    ]
    lines = group * SUB
    narrow = query.astype(jnp.bfloat16)
    scores = []
    for kv in range(KVH):
        keys = cache[:, 0, :, kv * HD : (kv + 1) * HD].reshape(npages * page_len, HD)
        scores.append(
            lax.dot_general(
                narrow[kv * lines : (kv + 1) * lines],
                keys,
                (((1,), (1,)), ((), ())),
                preferred_element_type=jnp.float32,
            )
        )
    scores = jnp.concatenate(scores, axis=0) * HD ** (-0.5)
    scores = jnp.where(usable, scores, EMPTY)
    own = jnp.sum(query * fresh_key, axis=-1, keepdims=True) * HD ** (-0.5)
    own = jnp.where(leads, own, EMPTY)
    peak = jnp.maximum(jnp.max(scores, axis=-1, keepdims=True), own)
    weights = jnp.where(usable, jnp.exp(scores - peak), 0.0)
    newest = jnp.where(leads, jnp.exp(own - peak), 0.0)
    total = jnp.sum(weights, axis=-1, keepdims=True) + newest
    narrow = weights.astype(jnp.bfloat16)
    summed = []
    for kv in range(KVH):
        values = cache[:, 1, :, kv * HD : (kv + 1) * HD].reshape(npages * page_len, HD)
        summed.append(
            jnp.dot(
                narrow[kv * lines : (kv + 1) * lines], values, preferred_element_type=jnp.float32
            )
        )
    summed = jnp.concatenate(summed, axis=0) + newest * fresh_value
    used = total > 0.0
    safe = jnp.where(used, total, 1.0)
    mixed = summed / safe
    level = jnp.where(used, peak + jnp.log(safe), EMPTY)
    lane = lax.broadcasted_iota(jnp.int32, (SUB, LANES), 1)
    levels = jnp.zeros((SUB, LANES), jnp.float32)
    for h in range(HEADS):
        levels = jnp.where(lane % STEP == h, level[h * SUB : (h + 1) * SUB], levels)
    upper = levels.astype(jnp.bfloat16).astype(jnp.float32)
    rest = levels - upper
    middle = rest.astype(jnp.bfloat16).astype(jnp.float32)
    levels = jnp.where(lane < STEP, upper, jnp.where(lane < 2 * STEP, middle, rest - middle))
    levels = jnp.where(lane < 3 * STEP, levels, 0.0)
    mixes = jnp.concatenate([mixed[h * SUB : (h + 1) * SUB] for h in range(HEADS)], axis=1)
    chips = size // CORES
    part = qwidth // chips
    for chip in range(chips):
        terms[chip] = jnp.concatenate([mixes[:, chip * part : (chip + 1) * part], levels], axis=1)
    for end, out in zip(targets(me, size), outs):
        out[...] = terms[pl.ds(end // CORES, 1)][0, :npages].astype(jnp.bfloat16)


def out_kernel(size, npages, *refs):
    blocks, refs = refs[:size], refs[size:]
    weight, mate_weight, plan, _, out = refs
    me = lax.axis_index("tensor")
    part = CORES * weight.shape[0]
    terms, ids = [], []
    line = lax.broadcasted_iota(jnp.int32, (SUB, LANES), 0)
    filler = jnp.zeros((SUB - npages, part + LANES), jnp.float32)
    for owner, block in zip(senders(me, size), blocks):
        terms += [block[...].astype(jnp.float32), filler]
        ids.append(jnp.where(line < npages, owner * npages + line, -2))
    terms = jnp.concatenate(terms, axis=0).astype(jnp.bfloat16)
    ids = jnp.concatenate(ids, axis=0).astype(jnp.float32)
    spread = lax.broadcasted_iota(jnp.int32, (LANES, part), 0)
    head = (lax.broadcasted_iota(jnp.int32, (LANES, part), 1) + me // CORES * part) // HD
    spread = jnp.where((spread % STEP == head) & (spread < 3 * STEP), 1.0, 0.0)
    spread = spread.astype(jnp.bfloat16)
    count = out.shape[0]
    rows = count + -count % STEP
    mixes, levels = [], []
    for hit in page_hits(plan[...], ids):
        picked = lax.dot_general(
            hit[:, :rows].astype(jnp.bfloat16),
            terms,
            (((0,), (0,)), ((), ())),
            preferred_element_type=jnp.float32,
        )
        mixes.append(picked[:, :part])
        levels.append(
            jnp.dot(
                picked[:, part:].astype(jnp.bfloat16), spread, preferred_element_type=jnp.float32
            )
        )
    highest = functools.reduce(jnp.maximum, levels)
    factors = [jnp.exp(level - highest) for level in levels]
    mixed = sum(mix * factor for mix, factor in zip(mixes, factors)) / sum(factors)
    halves = mixed[:, : part // CORES], mixed[:, part // CORES :]
    first = lax.rem(me, CORES) == 0
    own = jnp.where(first, halves[0], halves[1]).astype(jnp.bfloat16)
    other = jnp.where(first, halves[1], halves[0]).astype(jnp.bfloat16)
    products = jnp.dot(own, weight[...], preferred_element_type=jnp.float32)
    products += jnp.dot(other, mate_weight[...], preferred_element_type=jnp.float32)
    out[...] = products[:count].astype(jnp.bfloat16)


def expert_kernel(size, top, experts, parts, lows, *refs):
    chips = size // CORES
    sums, refs = refs[:chips], refs[chips:]
    rows_ref, gain, router = refs[:3]
    gate_up, refs = refs[3 : 3 + parts], refs[3 + parts :]
    down, refs = refs[:lows], refs[lows:]
    units = sum(piece.shape[0] for piece in down)
    homes, guests, finished, ends_ref = refs[:size], refs[size], refs[size + 1], refs[size + 2]
    me = lax.axis_index("tensor")
    count = rows_ref.shape[0]
    width = rows_ref.shape[1] - LANES
    rows_dev = count // size
    total = functools.reduce(jnp.add, [piece[...].astype(jnp.float32) for piece in sums])
    hidden = (rows_ref[:, :width] + total).astype(jnp.bfloat16).astype(jnp.float32)
    norm = normed(hidden, gain[...])
    lane = lax.broadcasted_iota(jnp.int32, (count, LANES), 1)
    numbers = rows_ref[:, width:]
    logits = lax.dot_general(
        norm, router[...], (((1,), (1,)), ((), ())), preferred_element_type=jnp.float32
    )
    logits = jnp.concatenate(
        [logits, jnp.zeros((count, LANES - experts), jnp.float32)], axis=1
    )
    routed = jnp.zeros((count, LANES), jnp.float32)
    for place in range(top):
        route = at_lane(numbers, lane, place)
        routed = jnp.where(lane.astype(jnp.float32) == route, 1.0, routed)
    logits = jnp.where(routed > 0.5, logits, EMPTY)
    shares = jnp.where(
        routed > 0.5, jnp.exp(logits - jnp.max(logits, axis=-1, keepdims=True)), 0.0
    )
    shares = shares / jnp.sum(shares, axis=-1, keepdims=True)

    here = lax.broadcasted_iota(jnp.int32, (LANES, 2 * LANES), 0)
    there = lax.broadcasted_iota(jnp.int32, (LANES, 2 * LANES), 1)
    evens = jnp.where(there == 2 * here, 1.0, 0.0).astype(jnp.bfloat16)
    odds = jnp.where(there == 2 * here + 1, 1.0, 0.0).astype(jnp.bfloat16)
    wide = to_step(norm)
    padded = wide.shape[0]
    blocks = width // LANES
    tall = jnp.concatenate([wide[:, b * LANES : (b + 1) * LANES] for b in range(blocks)], axis=0)
    to_gate = jnp.dot(tall, evens, preferred_element_type=jnp.float32).astype(jnp.bfloat16)
    to_up = jnp.dot(tall, odds, preferred_element_type=jnp.float32).astype(jnp.bfloat16)
    left = []
    for b in range(blocks):
        lines = slice(b * padded, (b + 1) * padded)
        left.append(jnp.concatenate([to_gate[lines], to_up[lines]], axis=0))
    left = jnp.concatenate(left, axis=1)
    both, right = [], []
    for piece in gate_up:
        right += [piece[place] for place in range(piece.shape[0])]
    for place in range(0, len(right), 2):
        pair = jnp.concatenate(right[place : place + 2], axis=1)
        both.append(jnp.dot(left, pair, preferred_element_type=jnp.float32))
    both = jnp.concatenate(both, axis=1)
    gate, up = both[:count], both[padded : padded + count]
    activated = gate / (1.0 + jnp.exp(-gate)) * up
    step = min(units, MOE_FF)
    scaled = []
    for start in range(0, units, step):
        expert = (me * units + start) // MOE_FF
        share = at_lane(shares, lane, expert)
        scaled.append(activated[:, start : start + step] * share)
    scaled = jnp.concatenate(scaled, axis=1).astype(jnp.bfloat16)
    partial, start = 0.0, 0
    for piece in down:
        left = scaled[:, start : start + piece.shape[0]]
        partial += jnp.dot(left, piece[...], preferred_element_type=jnp.float32)
        start += piece.shape[0]
    home_dev = rows_dev - 1
    first = size * home_dev
    for owner in range(size):
        lines = slice(owner * home_dev, (owner + 1) * home_dev)
        mine = jnp.where(me == owner, 1.0, 0.0)
        finished[owner] = partial[lines] + hidden[lines] * mine
        line = slice(first + owner, first + owner + 1)
        ends_ref[owner : owner + 1] = partial[line] + hidden[line] * mine
    for end, out in zip(targets(me, size), homes):
        out[...] = finished[pl.ds(end, 1)][0].astype(jnp.bfloat16)
    half = width // 2
    for owner in range(size):
        guest = ends_ref[owner : owner + 1]
        block = jnp.concatenate([guest[:, :half], guest[:, half:]], axis=0).astype(jnp.bfloat16)
        for place in range(owner, guests.shape[0], size):
            guests[place] = block


def finish_kernel(size, spot, *refs):
    pieces, refs = refs[:size], refs[size:]
    guests, tail, out = refs
    homes = functools.reduce(jnp.add, [piece[...].astype(jnp.float32) for piece in pieces])
    came = guests[...].astype(jnp.float32)
    lane = lax.broadcasted_iota(jnp.int32, (1, LANES), 1)
    source = at_lane(tail[...], lane, spot).reshape(1, 1, 1)
    place = lax.broadcasted_iota(jnp.int32, (came.shape[0], 1, 1), 0) // size
    guest = jnp.sum(jnp.where(place.astype(jnp.float32) == source, came, 0.0), axis=0)
    guest = jnp.concatenate([guest[:1], guest[1:]], axis=1)
    out[...] = jnp.concatenate([homes, guest], axis=0).astype(jnp.bfloat16)


def shape(dims, dtype=jnp.float32):
    return jax.ShapeDtypeStruct(dims, dtype)


def shards(
    tokens,
    attn_gain,
    qkv_weight,
    out_weight,
    moe_gain,
    router,
    expert_gate_up,
    expert_down,
    kv_cache,
    page_table,
    home_len,
    guest_source,
    guest_pages,
    guest_len,
    routes,
):
    size = lax.axis_size("tensor")
    replicas = lax.axis_size("replica")
    rows_dev, width = tokens.shape
    npages = kv_cache.shape[0]
    top = routes.shape[1]
    units = expert_down.shape[0]
    part = out_weight.shape[0]
    columns = qkv_weight.shape[1]
    count = size * rows_dev
    home_dev = rows_dev - 1
    wide = width + LANES
    everyone = size * replicas
    blocks = units // LANES
    gate_up, down = [], []

    def load_more(after, ups, downs):
        first, last = ups[0] * blocks // 8, ups[1] * blocks // 8
        wanted = []
        if last > first:
            wanted.append((expert_gate_up, first, last - first))
        if downs[1] > downs[0]:
            wanted.append((expert_down, downs[0] * units // 8, (downs[1] - downs[0]) * units // 8))
        if not wanted:
            return after
        got = loaded(after, *wanted)
        for part in got:
            (gate_up if part.ndim == 3 else down).append(part)
        return got[0]

    packed = guest_source * FAR + guest_len
    offers, homes, tail = pl.pallas_call(
        offer_kernel,
        out_shape=[
            shape((everyone, 2, (wide + LANES) // 2), jnp.bfloat16),
            shape((home_dev, wide), jnp.bfloat16),
            shape((1, LANES)),
        ],
        in_specs=[ANY] * 3 + [SMEM],
        out_specs=[VMEM] * 3,
        scratch_shapes=[
            pltpu.VMEM(tokens.shape, tokens.dtype),
            pltpu.VMEM(routes.T.shape, jnp.int32),
            pltpu.VMEM(guest_pages.shape, jnp.int32),
            pltpu.SemaphoreType.DMA((3,)),
        ],
        compiler_params=PARAMS,
        name="offer",
    )(far(tokens), far(routes.T), far(guest_pages), packed)
    plan = pl.pallas_call(
        plan_kernel,
        out_shape=shape((npages, LANES)),
        in_specs=[ANY] * 3,
        out_specs=VMEM,
        scratch_shapes=[
            pltpu.VMEM(page_table.T.shape, jnp.int32),
            pltpu.VMEM((1,) + home_len.shape, jnp.int32),
            pltpu.SemaphoreType.DMA((2,)),
        ],
        compiler_params=PARAMS,
        name="plan",
    )(homes, far(page_table.T), far(home_len))
    came = lax.all_to_all(offers, ("replica", "tensor"), 0, 0, tiled=True)
    messages = exchanged([homes] * size)
    (qkv_near,) = loaded(homes, (qkv_weight, 0, width))

    rows, *projected = pl.pallas_call(
        functools.partial(project_kernel, size, npages, top),
        out_shape=[shape((count, wide))] + [shape((npages, columns), jnp.bfloat16)] * size,
        in_specs=[VMEM] * (size + 4),
        out_specs=[VMEM] * (size + 1),
        scratch_shapes=[
            pltpu.VMEM((size, home_dev, wide), jnp.float32),
            pltpu.VMEM((size * SUB, columns), jnp.float32),
        ],
        compiler_params=PARAMS,
        name="project",
    )(
        *messages,
        came,
        attn_gain.reshape(1, width),
        resident(qkv_near),
        plan,
    )
    joined = exchanged(projected)

    before = load_more(rows, (0, 2), (0, 4))
    late, _ = lax.optimization_barrier((out_weight, rows))
    out_mate = lax.ppermute(late, "tensor", [(me, me ^ 1) for me in range(size)])
    terms = pl.pallas_call(
        functools.partial(attend_kernel, size, top),
        out_shape=[shape((npages, CORES * part + LANES), jnp.bfloat16)] * size,
        in_specs=[VMEM] * (size + 3) + [ANY],
        out_specs=[VMEM] * size,
        scratch_shapes=[
            pltpu.VMEM((size, SUB, columns), jnp.float32),
            pltpu.VMEM((size // CORES, SUB, CORES * part + LANES), jnp.float32),
        ],
        compiler_params=PARAMS,
        name="attend",
    )(*joined, resident(kv_cache), rows, plan, before)
    arrived = exchanged(terms)

    before = load_more(terms[0], (2, 5), (4, 6))
    partial = pl.pallas_call(
        functools.partial(out_kernel, size, npages),
        out_shape=shape((count, width), jnp.bfloat16),
        in_specs=[VMEM] * (size + 3) + [ANY],
        out_specs=VMEM,
        compiler_params=PARAMS,
        name="out",
    )(*arrived, resident(out_weight), resident(out_mate), plan, before)
    sums = across(partial, size)

    load_more(partial, (5, 8), (6, 8))
    *pieces, guests = pl.pallas_call(
        functools.partial(
            expert_kernel, size, top, router.shape[1], len(gate_up), len(down)
        ),
        out_shape=[shape((home_dev, width), jnp.bfloat16)] * size
        + [shape((everyone, 2, width // 2), jnp.bfloat16)],
        in_specs=[VMEM] * (len(sums) + 3 + len(gate_up) + len(down)),
        out_specs=[VMEM] * (size + 1),
        scratch_shapes=[
            pltpu.VMEM((size, home_dev, width), jnp.float32),
            pltpu.VMEM((size, width), jnp.float32),
        ],
        compiler_params=PARAMS,
        name="experts",
    )(
        *sums,
        rows,
        moe_gain.reshape(1, width),
        router.T,
        *[resident(piece) for piece in gate_up + down],
    )
    guests = lax.all_to_all(guests, ("replica", "tensor"), 0, 0, tiled=True)
    pieces = exchanged(pieces)
    return pl.pallas_call(
        functools.partial(finish_kernel, size, top + 1 + MAXP),
        out_shape=shape((rows_dev, width), jnp.bfloat16),
        in_specs=[VMEM] * (size + 2),
        out_specs=VMEM,
        compiler_params=PARAMS,
        name="finish",
    )(*pieces, guests, tail)


def solution(mesh):
    placed = (
        P(("replica", "tensor"), None),
        P(),
        P(None, "tensor"),
        P("tensor", None),
        P(),
        P(),
        P(None, None, "tensor"),
        P("tensor", None),
        P(("replica", "tensor"), None, None, None),
        P("replica", None),
        P("replica"),
        P(("replica", "tensor")),
        P(("replica", "tensor"), None),
        P(("replica", "tensor")),
        P("replica", None),
    )
    return jax.shard_map(
        shards,
        mesh=mesh,
        in_specs=placed,
        out_specs=P(("replica", "tensor"), None),
        check_vma=False,
    )
```
